32 devices in a mesh: dp: 4 (over y, x), rows: 8 (over z, core).
Axes of the slice: x: 2, y: 2, z: 4, core: 2. Of those that a mesh axis runs over, the one named last changes fastest.
Arguments:
- latents: bfloat16 [8, 512, 1024], P('dp'), may hold values from -6 to 6
- pixels: bfloat16 [8, 12544, 261], P('dp', 'rows'), may hold values from -6 to 6
- pix_counts: int32 [8], P('dp'), may hold values from 1024 to 12544, as said below
- cotangent: bfloat16 [8, 512, 1024], P('dp'), may hold values from -6 to 6
- weight_mats: float32 [10, 1024, 1024], P(None, ('dp', 'rows'))
- kv_weights: float32 [2, 261, 1024], P(None, None, ('dp', 'rows')), may hold values from -0.375 to 0.375
- norm_gains: float32 [4, 1024], P(None, ('dp', 'rows')), may hold values from 0.5 to 1.5
- input_gain: float32 [261], replicated, may hold values from 0.5 to 1.5
- mats_first: float32 [10, 1024, 1024], P(None, ('dp', 'rows'))
- mats_second: float32 [10, 1024, 1024], P(None, ('dp', 'rows')), may hold values from 1 to 100
- kv_first: float32 [2, 261, 1024], P(None, None, ('dp', 'rows')), may hold values from -6 to 6
- kv_second: float32 [2, 261, 1024], P(None, None, ('dp', 'rows')), may hold values from 1 to 100
- gains_first: float32 [4, 1024], P(None, ('dp', 'rows')), may hold values from -6 to 6
- gains_second: float32 [4, 1024], P(None, ('dp', 'rows')), may hold values from 1 to 100
- input_first: float32 [261], replicated, may hold values from -6 to 6
- input_second: float32 [261], replicated, may hold values from 1 to 100
Outputs:
- block_out: bfloat16 [8, 512, 1024], P('dp', 'rows')
- latent_grad: float32 [8, 512, 1024], P('dp', 'rows')
- pixel_grad: float32 [8, 12544, 261], P('dp', 'rows')
- mats_grad: float32 [10, 1024, 1024], P(None, ('dp', 'rows'))
- kv_grad: float32 [2, 261, 1024], P(None, None, ('dp', 'rows'))
- gains_grad: float32 [4, 1024], P(None, ('dp', 'rows'))
- input_grad: float32 [261], replicated
- mats_new: float32 [10, 1024, 1024], P(None, ('dp', 'rows'))
- mats_first_new: float32 [10, 1024, 1024], P(None, ('dp', 'rows'))
- mats_second_new: float32 [10, 1024, 1024], P(None, ('dp', 'rows'))
- kv_new: float32 [2, 261, 1024], P(None, None, ('dp', 'rows'))
- kv_first_new: float32 [2, 261, 1024], P(None, None, ('dp', 'rows'))
- kv_second_new: float32 [2, 261, 1024], P(None, None, ('dp', 'rows'))
- gains_new: float32 [4, 1024], P(None, ('dp', 'rows'))
- gains_first_new: float32 [4, 1024], P(None, ('dp', 'rows'))
- gains_second_new: float32 [4, 1024], P(None, ('dp', 'rows'))
- input_new: float32 [261], replicated
- input_first_new: float32 [261], replicated
- input_second_new: float32 [261], replicated
The draws below stay inside these ranges and needn't reach their ends.
Inputs may be any that keep to these rules, and one draw needn't show every extreme that they name: The first pix_counts[i] pixel rows of item i are valid, the rest padding; in each group of 2 items on one index of dp, one item drawn from the seed has all 12544 rows valid.
All inputs are finite; a program needn't handle non-finite values.
Results may differ from the reference program's by a relative error of at most 0.025.
Values may be sent and summed in bfloat16 or wider, within the bound.
A program may use at most 320 MiB of HBM per device.

```python
import math
import jax
import jax.numpy as jnp
from jax import lax

D = 1024
C = 261
LAT = 512
HEADS = 8
HD = 128
ITEMS_DEV = 2
PIX_DEV = 1568
MINPIX = 1024
ITEMS = 8
PIX = 12544
N_DP = 4
N_ROWS = 8


def draw_pix_counts(key, part):
    key = jax.random.fold_in(key, 7)
    spin_key, pick_key = jax.random.split(key)
    full_len = PIX_DEV * N_ROWS
    level = jax.random.randint(spin_key, (ITEMS,), 0, 1024)
    bent_level = level * level // 1024 * level // 1024
    drawn_len = MINPIX + (full_len - MINPIX) * bent_level // 1023
    chosen = jax.random.randint(pick_key, (N_DP,), 0, ITEMS_DEV)
    slot_index = jnp.arange(ITEMS) % ITEMS_DEV
    group_pick = jnp.repeat(chosen, ITEMS_DEV)
    return jnp.where(slot_index == group_pick, full_len, drawn_len).astype(jnp.int32)


def row_ramp(start_log, end_log):
    place = jnp.arange(D, dtype=jnp.float32) / (D - 1.0)
    return jnp.exp(start_log + (end_log - start_log) * place)


def draw_weight_mats(key, part):
    key = jax.random.fold_in(key, 11)
    drawn_draw = jax.random.truncated_normal(key, -6.0, 6.0, (10, D, D), jnp.float32) * D ** (-0.5)
    slot_index = jnp.arange(10)
    cross_lift = (PIX_DEV * N_ROWS * MINPIX) ** 0.25 / 2.0
    self_lift = (LAT / 4.0) ** 0.5
    lift_factor = jnp.where(slot_index == 1, cross_lift, jnp.where(slot_index == 7, self_lift, 1.0))
    ramp = row_ramp(-0.6931, 0.6931)
    return drawn_draw * lift_factor[:, None, None] * ramp[None, :, None]


def draw_mats_first(key, part):
    key = jax.random.fold_in(key, 13)
    drawn_draw = jax.random.truncated_normal(key, -6.0, 6.0, (10, D, D), jnp.float32)
    ramp = row_ramp(0.6931, -0.6931)
    return drawn_draw * ramp[None, :, None]


def level_of(key, shape, cuts, least, top_value):
    level = 1.0
    for position, blocks in cuts:
        heights = jax.random.uniform(jax.random.fold_in(jax.random.fold_in(key, 6), position), (blocks,), jnp.float32, least / len(cuts), top_value / len(cuts))
        level = level * jnp.repeat(jnp.exp(heights), shape[position] // blocks).reshape((-1,) + (1,) * (len(shape) - 1 - position))
    return level


def scatter_about(key, extent, scale, reach, cuts=(), held_as=jnp.bfloat16):
    factor_of = level_of(key, extent, cuts, -0.22, 0.18) if cuts else 1.0
    drawn = jax.random.normal(key, extent, jnp.float32) * scale * factor_of
    return jnp.minimum(jnp.maximum(drawn, -reach), reach).astype(held_as)


def setup_inputs(seed: int = 0) -> dict:
    splits = jax.random.split(jax.random.key(seed), 17)
    latents = scatter_about(splits[0], (ITEMS, LAT, D), 1.0, 6.0, ((0, 4),))
    pixels = scatter_about(splits[1], (ITEMS, PIX, C), 1.0, 6.0, ((0, 4), (1, 8)))
    pix_counts = draw_pix_counts(jax.random.fold_in(splits[16], 71), 0)
    cotangent = scatter_about(splits[3], (ITEMS, LAT, D), 1.0, 6.0, ((0, 4),))
    weight_mats = draw_weight_mats(jax.random.fold_in(splits[16], 71), 0)
    kv_weights = scatter_about(splits[5], (2, C, D), C ** -0.5, 0.375, ((2, 32),), jnp.float32)
    norm_gains = jnp.clip(1.0 + 0.1 * jax.random.normal(splits[6], (4, D), jnp.float32), 0.5, 1.5)
    input_gain = jnp.clip(1.0 + 0.1 * jax.random.normal(splits[7], (C,), jnp.float32), 0.5, 1.5)
    mats_first = draw_mats_first(jax.random.fold_in(splits[16], 71), 0)
    mats_second = jnp.clip(jnp.exp(math.log(100.0) - 4.6051702 * jax.random.uniform(splits[9], (10, D, D), jnp.float32) ** level_of(splits[9], (10, D, D), ((1, 32),), -0.2, 0.2)), 1.0, 100.0)
    kv_first = scatter_about(splits[10], (2, C, D), 1.0, 6.0, ((2, 32),), jnp.float32)
    kv_second = jnp.clip(jnp.exp(math.log(100.0) - 4.6051702 * jax.random.uniform(splits[11], (2, C, D), jnp.float32) ** level_of(splits[11], (2, C, D), ((2, 32),), -0.2, 0.2)), 1.0, 100.0)
    gains_first = scatter_about(splits[12], (4, D), 1.0, 6.0, ((1, 32),), jnp.float32)
    gains_second = jnp.clip(jnp.exp(math.log(100.0) - 4.6051702 * jax.random.uniform(splits[13], (4, D), jnp.float32) ** level_of(splits[13], (4, D), ((1, 32),), -0.2, 0.2)), 1.0, 100.0)
    input_first = scatter_about(splits[14], (C,), 1.0, 6.0, (), jnp.float32)
    input_second = jnp.clip(jnp.exp(jax.random.uniform(splits[15], (C,), jnp.float32, math.log(1.0), math.log(100.0))), 1.0, 100.0)
    return {"latents": latents, "pixels": pixels, "pix_counts": pix_counts, "cotangent": cotangent, "weight_mats": weight_mats, "kv_weights": kv_weights, "norm_gains": norm_gains, "input_gain": input_gain, "mats_first": mats_first, "mats_second": mats_second, "kv_first": kv_first, "kv_second": kv_second, "gains_first": gains_first, "gains_second": gains_second, "input_first": input_first, "input_second": input_second}


@jax.custom_vjp
def low(v):
    return lax.optimization_barrier(v.astype(jnp.bfloat16)).astype(jnp.float32)

@jax.custom_vjp
def low_back(v):
    return v

def low_keep(v):
    return (low(v), None)

def low_pass(kept, grad):
    return (grad,)

def back_keep(v):
    return (v, None)

def back_low(kept, grad):
    return (low(grad),)
low.defvjp(low_keep, low_pass)
low_back.defvjp(back_keep, back_low)
highest = lax.Precision.HIGHEST
first_fix = 1.0 - 0.9 ** 10
second_fix = 1.0 - 0.999 ** 10
step_rate = 0.25
decay_rate = 0.01

def both_ways(values):
    return low(low_back(values))

def matmul(left_side, right_side):
    return jnp.dot(left_side, right_side, precision=highest, preferred_element_type=jnp.float32)

def standard(values):
    centred = values - lax.optimization_barrier(jnp.mean(values, -1, keepdims=True))
    return centred * lax.rsqrt(lax.optimization_barrier(jnp.mean(centred * centred, -1, keepdims=True)) + 1e-05)

def softmax_rows(scores):
    exp_scores = jnp.exp(scores - lax.optimization_barrier(jnp.max(scores, -1, keepdims=True)))
    return exp_scores / lax.optimization_barrier(jnp.sum(exp_scores, -1, keepdims=True))

def item_pass(rounded, weight_in, lat_in, pix_in, item_len):
    w_mats, w_pairs, w_gains = rounded
    norm_a = low(standard(lat_in) * w_gains[0])
    queries = both_ways(matmul(norm_a, w_mats[0]))
    norm_p = low(standard(pix_in) * weight_in)
    key_rows = both_ways(matmul(norm_p, w_pairs[0]))
    value_rows = both_ways(matmul(norm_p, w_pairs[1]))
    scores = low_back(matmul(queries, key_rows.T) * D ** (-0.5))
    valid_rows = jnp.arange(PIX) < item_len
    scores = jnp.where(valid_rows[None, :], scores, -1e+30)
    attn_probs = low(softmax_rows(scores))
    attended = both_ways(matmul(attn_probs, value_rows))
    after_cross = lat_in + low_back(matmul(attended, w_mats[1]))
    norm_c = low(standard(after_cross) * w_gains[1])
    up_cross = low_back(matmul(norm_c, w_mats[2]))
    gelu_cross = low(jax.nn.gelu(up_cross))
    after_mlp = after_cross + low_back(matmul(gelu_cross, w_mats[3]))
    norm_s = low(standard(after_mlp) * w_gains[2])
    q_self = both_ways(matmul(norm_s, w_mats[4])).reshape(LAT, HEADS, HD)
    k_self = both_ways(matmul(norm_s, w_mats[5])).reshape(LAT, HEADS, HD)
    v_self = both_ways(matmul(norm_s, w_mats[6])).reshape(LAT, HEADS, HD)
    self_scores = low_back(jnp.einsum('qhd,khd->hqk', q_self, k_self, precision=highest) * HD ** (-0.5))
    self_probs = low(softmax_rows(self_scores))
    mixed_heads = both_ways(jnp.einsum('hqk,khd->qhd', self_probs, v_self, precision=highest).reshape(LAT, D))
    after_self = after_mlp + low_back(matmul(mixed_heads, w_mats[7]))
    norm_f = low(standard(after_self) * w_gains[3])
    up_self = low_back(matmul(norm_f, w_mats[8]))
    gelu_self = low(jax.nn.gelu(up_self))
    return after_self + low_back(matmul(gelu_self, w_mats[9]))

def lamb(weight, gradient, first_mom, second, sum_axes):
    first_new = 0.9 * first_mom + 0.1 * gradient
    second_new = 0.999 * second + 0.001 * gradient * gradient
    update = first_new / first_fix / (jnp.sqrt(second_new / second_fix) + 1e-06) + decay_rate * weight
    weight_norm = jnp.sqrt(lax.optimization_barrier(jnp.sum(weight * weight, sum_axes, keepdims=True)))
    update_norm = jnp.sqrt(lax.optimization_barrier(jnp.sum(update * update, sum_axes, keepdims=True)))
    trust = weight_norm / (update_norm + 1e-06)
    return (weight - step_rate * trust * update, first_new, second_new)

def reference(latents, pixels, pix_counts, cotangent, weight_mats, kv_weights, norm_gains, input_gain, mats_first, mats_second, kv_first, kv_second, gains_first, gains_second, input_first, input_second):

    def forward(lat_all, pix_all, mats_in, pairs_in, gains_in, gain_pix):
        rounded = (low(mats_in), low(pairs_in), low(gains_in))

        def per_item(pieces):
            return item_pass(rounded, gain_pix, pieces[0], pieces[1], pieces[2])
        return lax.map(jax.checkpoint(per_item), (lat_all, pix_all, pix_counts))
    block_f, pull_back = jax.vjp(forward, latents.astype(jnp.float32), pixels.astype(jnp.float32), weight_mats, kv_weights, norm_gains, input_gain)
    latent_grad, pixel_grad, mats_grad, kv_grad, gains_grad, input_grad = pull_back(cotangent.astype(jnp.float32))
    mats_new, mats_first_new, mats_second_new = lamb(weight_mats, mats_grad, mats_first, mats_second, (1, 2))
    kv_new, kv_first_new, kv_second_new = lamb(kv_weights, kv_grad, kv_first, kv_second, (1, 2))
    gains_new, gains_first_new, gains_second_new = lamb(norm_gains, gains_grad, gains_first, gains_second, (1,))
    input_new, input_first_new, input_second_new = lamb(input_gain, input_grad, input_first, input_second, (0,))
    return (block_f.astype(jnp.bfloat16), latent_grad, pixel_grad, mats_grad, kv_grad, gains_grad, input_grad, mats_new, mats_first_new, mats_second_new, kv_new, kv_first_new, kv_second_new, gains_new, gains_first_new, gains_second_new, input_new, input_first_new, input_second_new)
```

```python
import jax
import jax.numpy as jnp
from jax import lax
from jax.sharding import Mesh, PartitionSpec as P

HEADS = 8
first_fix = 1.0 - 0.9**10
second_fix = 1.0 - 0.999**10
step_rate = 0.25
decay_rate = 0.01
bf_type = jnp.bfloat16
fl_type = jnp.float32
ALL = ("dp", "z", "core")


def standard(values):
    centred = values - jnp.mean(values, -1, keepdims=True)
    return centred * lax.rsqrt(jnp.mean(centred * centred, -1, keepdims=True) + 1e-05)


def standard_parts(values):
    centred = values - jnp.mean(values, -1, keepdims=True)
    inv = lax.rsqrt(jnp.mean(centred * centred, -1, keepdims=True) + 1e-05)
    return centred * inv, inv


def pull(hat, inv, grad):
    return (
        grad - jnp.mean(grad, -1, keepdims=True) - hat * jnp.mean(grad * hat, -1, keepdims=True)
    ) * inv


def softmax_rows(scores):
    exp_scores = jnp.exp(scores - jnp.max(scores, -1, keepdims=True))
    return exp_scores / jnp.sum(exp_scores, -1, keepdims=True)


def product(left_side, right_side):
    return jnp.dot(left_side, right_side, preferred_element_type=fl_type)


def product_tn(left_side, right_side):
    return lax.dot_general(
        left_side, right_side, (((0,), (0,)), ((), ())), preferred_element_type=fl_type
    )


def product_nt(left_side, right_side):
    return lax.dot_general(
        left_side, right_side, (((1,), (1,)), ((), ())), preferred_element_type=fl_type
    )


def moments(weight, gradient, first_mom, second, sum_axes):
    first_new = 0.9 * first_mom + 0.1 * gradient
    second_new = 0.999 * second + 0.001 * gradient * gradient
    update = (
        first_new / first_fix / (jnp.sqrt(second_new / second_fix) + 1e-06) + decay_rate * weight
    )
    return (
        first_new,
        second_new,
        update,
        jnp.sum(weight * weight, sum_axes),
        jnp.sum(update * update, sum_axes),
    )


def swap(value):
    return lax.ppermute(value, "core", [(0, 1), (1, 0)])


def local(
    latents,
    pixels,
    pix_counts,
    cotangent,
    weight_mats,
    kv_weights,
    norm_gains,
    input_gain,
    mats_first,
    mats_second,
    kv_first,
    kv_second,
    gains_first,
    gains_second,
    input_first,
    input_second,
):
    item_count, lat_len, model_width = latents.shape
    pix_dev, pix_width = pixels.shape[1:]
    n_mats, own_width = weight_mats.shape[:2]
    n_dp, n_z = lax.axis_size("dp"), lax.axis_size("z")
    z_rank, core = lax.axis_index("z"), lax.axis_index("core")
    pad_width = -(-(pix_width + 4) // 128) * 128
    head_dim = model_width // HEADS

    kv_cols = jnp.swapaxes(kv_weights, 1, 2)
    first_block = jnp.concatenate(
        [
            weight_mats[0],
            jnp.pad(kv_cols[0], ((0, 0), (0, pad_width - pix_width))),
            kv_cols[1],
            norm_gains.T,
            jnp.zeros((own_width, pad_width - pix_width - 4), fl_type),
        ],
        axis=1,
    ).astype(bf_type)
    first_all = lax.all_gather(first_block, ALL, axis=0, tiled=True)
    w_rest = lax.all_gather(weight_mats[1:].astype(bf_type), ALL, axis=1, tiled=True)
    w_zero = first_all[:, :model_width]
    kt_zero = first_all[:, model_width : model_width + pix_width]
    kt_one = first_all[:, model_width + pad_width : model_width + pad_width + pix_width]
    gain_rows = first_all[
        :, model_width + pad_width + pix_width : model_width + pad_width + pix_width + 4
    ].T.astype(fl_type)

    def w_mat(index):
        return w_zero if index == 0 else w_rest[index - 1]

    lat_both = latents.astype(fl_type).reshape(item_count * lat_len, model_width)
    hat_both, inv_both = standard_parts(lat_both)
    norm_both = (hat_both * gain_rows[0]).astype(bf_type)
    q_both = product(norm_both, w_zero).astype(bf_type)
    cross_scale = model_width ** (-0.5)
    qk_both = (
        (product(q_both, kt_zero) * cross_scale)
        .astype(bf_type)
        .reshape(item_count, lat_len, pix_width)
    )
    hat_pix, inv_pix = standard_parts(pixels.astype(fl_type))
    norm_pix = (hat_pix * input_gain).astype(bf_type)
    scores = jnp.einsum("iqc,ipc->iqp", qk_both, norm_pix, preferred_element_type=fl_type)
    pix_place = (z_rank * 2 + core) * pix_dev + lax.iota(jnp.int32, pix_dev)
    valid_rows = pix_place[None, :] < pix_counts[:, None]
    scores = jnp.where(valid_rows[:, None, :], scores, -1e30)
    peak_loc = jnp.max(scores, -1)
    exp_scores = jnp.exp(scores - peak_loc[:, :, None])
    exp_low = exp_scores.astype(bf_type)
    total_loc = jnp.sum(exp_scores, -1)
    part_loc = jnp.einsum("iqp,ipc->iqc", exp_low, norm_pix, preferred_element_type=fl_type)
    packed = jnp.concatenate(
        [
            part_loc,
            peak_loc[:, :, None],
            total_loc[:, :, None],
            jnp.zeros((item_count, lat_len, pad_width - pix_width - 2), fl_type),
        ],
        axis=2,
    )

    def own_of(both):
        return lax.dynamic_index_in_dim(both, core, 0, keepdims=False)

    def other_of(both):
        return lax.dynamic_index_in_dim(both, 1 - core, 0, keepdims=False)

    def by_item(own, other):
        return jnp.where(core == 0, jnp.stack([own, other]), jnp.stack([other, own]))

    pair = jnp.stack([own_of(packed), swap(other_of(packed))])
    everyone = lax.all_gather(pair, "z", axis=0, tiled=True)
    peaks = everyone[:, :, pix_width]
    peak = jnp.max(peaks, 0)
    shares = jnp.exp(peaks - peak)
    total = jnp.sum(shares * everyone[:, :, pix_width + 1], 0)
    mixed_pix = jnp.sum(shares[:, :, None] * everyone[:, :, :pix_width], 0) / total[:, None]
    mixed_low = mixed_pix.astype(bf_type)

    lat_own = own_of(latents).astype(fl_type)
    hat_a = own_of(hat_both.reshape(item_count, lat_len, model_width))
    inv_a = own_of(inv_both.reshape(item_count, lat_len, 1))
    norm_a = own_of(norm_both.reshape(item_count, lat_len, model_width))
    q_own = own_of(q_both.reshape(item_count, lat_len, model_width))
    att_low = product_nt(mixed_low, kt_one).astype(bf_type)
    after_cross = lat_own + product(att_low, w_mat(1))
    hat_c, inv_c = standard_parts(after_cross)
    norm_c = (hat_c * gain_rows[1]).astype(bf_type)
    gelu_c, pull_gelu_c = jax.vjp(jax.nn.gelu, product(norm_c, w_mat(2)))
    gelu_c_low = gelu_c.astype(bf_type)
    after_mlp = after_cross + product(gelu_c_low, w_mat(3))
    hat_s, inv_s = standard_parts(after_mlp)
    norm_s = (hat_s * gain_rows[2]).astype(bf_type)
    head_shape = (lat_len, HEADS, head_dim)
    q_self = product(norm_s, w_mat(4)).astype(bf_type).reshape(head_shape)
    k_self = product(norm_s, w_mat(5)).astype(bf_type).reshape(head_shape)
    v_self = product(norm_s, w_mat(6)).astype(bf_type).reshape(head_shape)
    head_scale = head_dim ** (-0.5)
    self_probs = softmax_rows(
        jnp.einsum("qhd,khd->hqk", q_self, k_self, preferred_element_type=fl_type) * head_scale
    )
    self_low = self_probs.astype(bf_type)
    mixed_heads = (
        jnp.einsum("hqk,khd->qhd", self_low, v_self, preferred_element_type=fl_type)
        .astype(bf_type)
        .reshape(lat_len, model_width)
    )
    after_self = after_mlp + product(mixed_heads, w_mat(7))
    hat_f, inv_f = standard_parts(after_self)
    norm_f = (hat_f * gain_rows[3]).astype(bf_type)
    gelu_f, pull_gelu_f = jax.vjp(jax.nn.gelu, product(norm_f, w_mat(8)))
    gelu_f_low = gelu_f.astype(bf_type)
    z_share = lat_len // n_z

    def z_rows(values):
        return lax.dynamic_slice_in_dim(values, z_rank * z_share, z_share, 0)

    def exchange_rows(values):
        halves = values.reshape(2, z_share // 2, model_width)
        return by_item(own_of(halves), swap(other_of(halves)))

    block_out = exchange_rows(
        (z_rows(after_self) + product(z_rows(gelu_f_low), w_mat(9))).astype(bf_type)
    )

    pair_width = 2 * own_width
    n_cols = n_dp * pair_width
    wanted = lax.iota(jnp.int32, n_cols)
    wanted = ((wanted // pair_width) * n_z + z_rank) * pair_width + wanted % pair_width
    select = (lax.iota(jnp.int32, model_width)[:, None] == wanted[None, :]).astype(bf_type)

    def chosen(values):
        return product(values, select).astype(bf_type)

    def chosen_sum(values):
        total_cols = jnp.sum(values, 0).reshape(n_dp, n_z, pair_width)
        return lax.dynamic_index_in_dim(total_cols, z_rank, 1, keepdims=False).reshape(n_cols)

    grad_out = own_of(cotangent).astype(fl_type)
    grad_nine = own_of(cotangent)
    terms = {}
    gain_terms = {}
    terms[9] = product_tn(chosen(gelu_f_low), grad_nine)
    grad_up_f = pull_gelu_f(product_nt(grad_nine, w_mat(9)))[0].astype(bf_type)
    terms[8] = product_tn(chosen(norm_f), grad_up_f)
    grad_norm_f = product_nt(grad_up_f, w_mat(8))
    gain_terms[3] = chosen_sum(hat_f * grad_norm_f)
    grad_self = grad_out + pull(hat_f, inv_f, grad_norm_f * gain_rows[3])
    grad_seven = grad_self.astype(bf_type)
    terms[7] = product_tn(chosen(mixed_heads), grad_seven)
    grad_mixed = product_nt(grad_seven, w_mat(7)).astype(bf_type).reshape(head_shape)
    grad_self_probs = jnp.einsum("qhd,khd->hqk", grad_mixed, v_self, preferred_element_type=fl_type)
    grad_self_scores = (
        self_probs * (grad_self_probs - jnp.sum(self_probs * grad_self_probs, -1, keepdims=True))
    ).astype(bf_type)
    grad_q_self = (
        (
            jnp.einsum("hqk,khd->qhd", grad_self_scores, k_self, preferred_element_type=fl_type)
            * head_scale
        )
        .astype(bf_type)
        .reshape(lat_len, model_width)
    )
    grad_k_self = (
        (
            jnp.einsum("hqk,qhd->khd", grad_self_scores, q_self, preferred_element_type=fl_type)
            * head_scale
        )
        .astype(bf_type)
        .reshape(lat_len, model_width)
    )
    grad_v_self = (
        jnp.einsum("hqk,qhd->khd", self_low, grad_mixed, preferred_element_type=fl_type)
        .astype(bf_type)
        .reshape(lat_len, model_width)
    )
    norm_s_chosen = chosen(norm_s)
    terms[4] = product_tn(norm_s_chosen, grad_q_self)
    terms[5] = product_tn(norm_s_chosen, grad_k_self)
    terms[6] = product_tn(norm_s_chosen, grad_v_self)
    grad_norm_s = (
        product_nt(grad_q_self, w_mat(4))
        + product_nt(grad_k_self, w_mat(5))
        + product_nt(grad_v_self, w_mat(6))
    )
    gain_terms[2] = chosen_sum(hat_s * grad_norm_s)
    grad_mlp = grad_self + pull(hat_s, inv_s, grad_norm_s * gain_rows[2])
    grad_three = grad_mlp.astype(bf_type)
    terms[3] = product_tn(chosen(gelu_c_low), grad_three)
    grad_up_c = pull_gelu_c(product_nt(grad_three, w_mat(3)))[0].astype(bf_type)
    terms[2] = product_tn(chosen(norm_c), grad_up_c)
    grad_norm_c = product_nt(grad_up_c, w_mat(2))
    gain_terms[1] = chosen_sum(hat_c * grad_norm_c)
    grad_cross = grad_mlp + pull(hat_c, inv_c, grad_norm_c * gain_rows[1])
    grad_one = grad_cross.astype(bf_type)
    terms[1] = product_tn(chosen(att_low), grad_one)
    grad_att = product_nt(grad_one, w_mat(1)).astype(bf_type)
    gk_own = product(grad_att, kt_one).astype(bf_type)
    dot_own = jnp.sum(gk_own.astype(fl_type) * mixed_pix, -1)
    term_k_one = product_tn(chosen(grad_att), mixed_low)

    early = jnp.stack([terms[index] for index in range(1, 10)])
    early = early.reshape(9, n_dp * 2, own_width, model_width).swapaxes(0, 1)
    early = early.reshape(n_dp * 2 * 9 * own_width, model_width).astype(bf_type)
    early_sum = lax.psum_scatter(early, ("dp", "core"), scatter_dimension=0, tiled=True)
    early_grad = early_sum.astype(fl_type).reshape(9, own_width, model_width)

    stats_own = jnp.stack([peak, total, dot_own])
    stats = by_item(stats_own, swap(stats_own))
    gk_both = by_item(gk_own, swap(gk_own))
    probs = exp_low.astype(fl_type) * (jnp.exp(peak_loc - stats[:, 0]) / stats[:, 1])[:, :, None]
    grad_probs = jnp.einsum("iqc,ipc->iqp", gk_both, norm_pix, preferred_element_type=fl_type)
    grad_scores = (probs * (grad_probs - stats[:, 2][:, :, None])).astype(bf_type)
    probs_low = probs.astype(bf_type)
    query_part = jnp.einsum("iqp,ipc->iqc", grad_scores, norm_pix, preferred_element_type=fl_type)
    query_own = own_of(query_part) + swap(other_of(query_part))
    query_sum = lax.psum(query_own, "z")
    grad_norm_p = jnp.einsum(
        "iqp,iqc->ipc", grad_scores, qk_both, preferred_element_type=fl_type
    ) + jnp.einsum("iqp,iqc->ipc", probs_low, gk_both, preferred_element_type=fl_type)
    input_part = jnp.sum(hat_pix * grad_norm_p, (0, 1))
    pixel_grad = pull(hat_pix, inv_pix, grad_norm_p * input_gain)

    query_low = query_sum.astype(bf_type)
    grad_query = (product_nt(query_low, kt_zero) * cross_scale).astype(bf_type)
    term_zero = product_tn(chosen(norm_a), grad_query)
    grad_norm_a = product_nt(grad_query, w_zero)
    gain_terms[0] = chosen_sum(hat_a * grad_norm_a)
    latent_grad = exchange_rows(
        z_rows(grad_cross)
        + pull(z_rows(hat_a), z_rows(inv_a), z_rows(grad_norm_a) * gain_rows[0])
    )
    term_k_zero = product_tn(chosen(q_own), query_low) * cross_scale
    gains_cols = jnp.stack([gain_terms[index] for index in range(4)], axis=1)
    late = jnp.concatenate(
        [
            term_zero,
            jnp.pad(term_k_zero, ((0, 0), (0, pad_width - pix_width))),
            term_k_one,
            gains_cols,
            jnp.zeros((n_cols, pad_width - pix_width - 4), fl_type),
        ],
        axis=1,
    ).astype(bf_type)
    late_sum = lax.psum_scatter(late, ("dp", "core"), scatter_dimension=0, tiled=True).astype(
        fl_type
    )
    wide_grad = jnp.concatenate([late_sum[None, :, :model_width], early_grad], axis=0)
    kv_grad = jnp.stack(
        [
            late_sum[:, model_width : model_width + pix_width].T,
            late_sum[:, model_width + pad_width : model_width + pad_width + pix_width].T,
        ]
    )
    gains_grad = late_sum[
        :, model_width + pad_width + pix_width : model_width + pad_width + pix_width + 4
    ].T

    mats_first_new, mats_second_new, mats_update, mats_wsum, mats_usum = moments(
        weight_mats, wide_grad, mats_first, mats_second, (1, 2)
    )
    kv_first_new, kv_second_new, kv_update, kv_wsum, kv_usum = moments(
        kv_weights, kv_grad, kv_first, kv_second, (1, 2)
    )
    gains_first_new, gains_second_new, gains_update, gains_wsum, gains_usum = moments(
        norm_gains, gains_grad, gains_first, gains_second, (1,)
    )
    small = jnp.concatenate(
        [mats_wsum, kv_wsum, gains_wsum, mats_usum, kv_usum, gains_usum, input_part]
    )
    small = lax.psum(small, ALL)
    square_w, square_u, input_grad = small[:16], small[16:32], small[32:]
    trust = jnp.sqrt(square_w) / (jnp.sqrt(square_u) + 1e-06)
    mats_new = weight_mats - step_rate * trust[0:10, None, None] * mats_update
    kv_new = kv_weights - step_rate * trust[10:12, None, None] * kv_update
    gains_new = norm_gains - step_rate * trust[12:16, None] * gains_update
    input_first_new, input_second_new, input_update, input_wsum, input_usum = moments(
        input_gain, input_grad, input_first, input_second, (0,)
    )
    input_trust = jnp.sqrt(input_wsum) / (jnp.sqrt(input_usum) + 1e-06)
    input_new = input_gain - step_rate * input_trust * input_update
    return (
        block_out,
        latent_grad,
        pixel_grad,
        wide_grad,
        kv_grad,
        gains_grad,
        input_grad,
        mats_new,
        mats_first_new,
        mats_second_new,
        kv_new,
        kv_first_new,
        kv_second_new,
        gains_new,
        gains_first_new,
        gains_second_new,
        input_new,
        input_first_new,
        input_second_new,
    )


def solution(mesh):
    n_dp, n_rows = mesh.devices.shape
    split_mesh = Mesh(mesh.devices.reshape(n_dp, n_rows // 2, 2), ALL)
    rows = ("z", "core")
    items = P("dp", None, None)
    pix = P("dp", rows, None)
    mats = P(None, ALL, None)
    pairs = P(None, None, ALL)
    gains = P(None, ALL)
    in_specs = (
        items,
        pix,
        P("dp"),
        items,
        mats,
        pairs,
        gains,
        P(),
        mats,
        mats,
        pairs,
        pairs,
        gains,
        gains,
        P(),
        P(),
    )
    out_specs = (
        pix,
        pix,
        pix,
        mats,
        pairs,
        gains,
        P(),
        mats,
        mats,
        mats,
        pairs,
        pairs,
        pairs,
        gains,
        gains,
        gains,
        P(),
        P(),
        P(),
    )
    return jax.shard_map(
        local, mesh=split_mesh, in_specs=in_specs, out_specs=out_specs, check_vma=False
    )
```

```python
import functools

import jax
import jax.numpy as jnp
from jax import lax
from jax.experimental import pallas as pl
from jax.experimental.pallas import tpu as pltpu
from jax.sharding import Mesh, PartitionSpec as P

HEADS = 8
first_fix = 1.0 - 0.9**10
second_fix = 1.0 - 0.999**10
step_rate = 0.25
decay_rate = 0.01
bf_type = jnp.bfloat16
fl_type = jnp.float32
ALL = ("dp", "z", "core")

NT = (((1,), (1,)), ((), ()))
TN = (((0,), (0,)), ((), ()))
NN = (((1,), (0,)), ((), ()))
MESH = pl.DeviceIdType.MESH
PIECES = ((0, 3), (3, 6), (6, 9))


def dot(left_side, right_side, dims=NN):
    return lax.dot_general(left_side, right_side, dims, preferred_element_type=fl_type)


def round_up(value, unit):
    return -(-value // unit) * unit


def tile_of(rows, unit, most):
    best = unit
    for size in range(unit, most + 1, unit):
        if rows % size == 0:
            best = size
    return best


def meet(peers):
    barrier = pltpu.get_barrier_semaphore()
    for peer in peers:
        pl.semaphore_signal(barrier, inc=1, device_id=peer, device_id_type=MESH)
    pl.semaphore_wait(barrier, len(peers))


class Gather:
    def __init__(self, mine, place, sems, n_z):
        self.mine, self.place, self.sems, self.n_z = mine, place, sems, n_z
        self.d, self.z, self.c = (lax.axis_index(name) for name in ALL)
        self.z_from = [lax.rem(self.z + n_z - i, n_z) for i in range(n_z)]
        self.z_to = [lax.rem(self.z + i, n_z) for i in range(n_z)]
        self.sent = []

    def slot(self, d, z, c):
        return self.place((d * self.n_z + z) * 2 + c)

    def copy(self, src, shard, kind, index, peer):
        return pltpu.make_async_remote_copy(
            src_ref=src,
            dst_ref=self.slot(*shard),
            send_sem=self.sems.at[0, kind, index],
            recv_sem=self.sems.at[1, kind, index],
            device_id=peer,
            device_id_type=MESH,
        )

    def send(self, src, shard, kind, index, peer):
        copy = self.copy(src, shard, kind, index, peer)
        copy.start()
        self.sent.append(copy)

    def arrived(self, shard, kind, index):
        self.copy(self.mine, shard, kind, index, (self.d, self.z, 1 - self.c)).wait_recv()

    def start(self, local_sem):
        d, z, c = self.d, self.z, self.c
        shard = (d, z, c)
        for i in range(1, self.n_z):
            self.send(self.mine, shard, 0, i, (d, self.z_to[i], c))
        self.send(self.mine, shard, 1, 0, (d ^ 1, z, c))
        self.send(self.mine, shard, 2, 0, (d ^ 2, z, c))
        self.send(self.mine, shard, 4, 0, (d, z, 1 - c))
        self.own = pltpu.make_async_copy(self.mine, self.slot(*shard), local_sem)
        self.own.start()

    def relay_z(self):
        d, z, c = self.d, self.z, self.c
        for i in range(1, self.n_z):
            shard = (d, self.z_from[i], c)
            self.arrived(shard, 0, i)
            src = self.slot(*shard)
            self.send(src, shard, 1, i, (d ^ 1, z, c))
            self.send(src, shard, 2, i, (d ^ 2, z, c))
            self.send(src, shard, 4, i, (d, z, 1 - c))

    def relay_plane(self):
        d, z, c = self.d, self.z, self.c
        for i in range(self.n_z):
            for kind, flip, onward in ((1, 1, 2), (2, 2, 1)):
                shard = (d ^ flip, self.z_from[i], c)
                self.arrived(shard, kind, i)
                src = self.slot(*shard)
                if (i < self.n_z // 2) == (kind == 1):
                    self.send(src, shard, 3, i, (d ^ onward, z, c))
                self.send(src, shard, 4 + kind, i, (d, z, 1 - c))

    def relay_far(self):
        d, z, c = self.d, self.z, self.c
        for i in range(self.n_z):
            shard = (d ^ 3, self.z_from[i], c)
            self.arrived(shard, 3, i)
            self.send(self.slot(*shard), shard, 7, i, (d, z, 1 - c))

    def finish(self):
        self.own.wait()
        for i in range(self.n_z):
            for kind, flip in ((4, 0), (5, 1), (6, 2), (7, 3)):
                self.arrived((self.d ^ flip, self.z_from[i], 1 - self.c), kind, i)

    def drain(self):
        for copy in self.sent:
            copy.wait_send()


def pixels_forward(
    n_z,
    gathers,
    pix_width,
    chunk,
    counts,
    first_ref,
    *refs,
):
    refs = list(refs)
    rest_ref = refs.pop(0) if gathers else None
    pix_ref, lat_ref, gain_ref = refs[:3]
    refs = refs[3:]
    first_out = refs.pop(0) if gathers else None
    rest_out = refs.pop(0) if gathers else None
    xn_ref, pt_ref, peak_ref, qk_ref, q_ref, gains_ref, mean_ref, stat_ref = refs[:8]
    refs = refs[8:]
    (
        first_all,
        q_all,
        s_buf,
        px_own,
        px_tx,
        px_rx,
        st_tx,
        st_rx,
        px2_tx,
        px2_rx,
        st2_tx,
        st2_rx,
        fin_tx,
        fin_rx,
        col_sems,
        local_sems,
    ) = refs[:16]
    gather_sems = refs[16:]
    d, z, c = (lax.axis_index(name) for name in ALL)
    peers = [(d, lax.rem(z + i, n_z), c) for i in range(1, n_z)] + [(d, z, 1 - c)]
    if gathers:
        peers += [(d ^ 1, z, c), (d ^ 2, z, c)]
    meet(peers)
    if gathers:
        own = first_ref.shape[0]

        def first_place(rank):
            return first_all.at[pl.ds(pl.multiple_of(rank * own, own), own)]

        def rest_place(low, high):
            def place(rank):
                return rest_out.at[low:high, pl.ds(pl.multiple_of(rank * own, own), own)]

            return place

        first = Gather(first_ref, first_place, gather_sems[0], n_z)
        first.start(local_sems.at[0])
        rest = [
            Gather(
                rest_ref.at[low:high],
                rest_place(low, high),
                gather_sems[1 + index],
                n_z,
            )
            for index, (low, high) in enumerate(PIECES)
        ]
        for index, piece in enumerate(rest):
            piece.start(local_sems.at[1 + index])
    else:
        rest = []
        load = pltpu.make_async_copy(first_ref, first_all, local_sems.at[0])
        load.start()

    n_items, pix_dev, _ = pix_ref.shape
    lat_len, width = lat_ref.shape[1:]
    pad_width = xn_ref.shape[2]
    rows = tile_of(pix_dev, 16, 256)
    tiles = pix_dev // rows
    held = chunk * n_z

    def normalise(item):
        def body(t, _):
            at = pl.ds(pl.multiple_of(t * rows, rows), rows)
            values = pix_ref[item, at, :].astype(fl_type)
            centred = values - jnp.sum(values, -1, keepdims=True) * (1.0 / pix_width)
            var = jnp.sum(centred * centred, -1, keepdims=True) * (1.0 / pix_width)
            normal = centred * lax.rsqrt(var + 1e-05) * gain_ref[...]
            xn_ref[item, at, pad_width - 128 :] = jnp.zeros((rows, 128), bf_type)
            xn_ref[item, at, :pix_width] = normal.astype(bf_type)
            return 0

        lax.fori_loop(0, tiles, body, 0)

    normalise(0)
    if gathers:
        first.relay_z()
    for item in range(1, n_items):
        normalise(item)
    if gathers:
        first.relay_plane()
        rest[0].relay_z()
        first.relay_far()
        first.finish()
    else:
        load.wait()

    gain_at = round_up(pix_width, 8) - (pad_width - 128)
    tail = first_all[:, width + 2 * pad_width - 128 :].astype(fl_type).T
    gains_ref[...] = tail[gain_at : gain_at + 8]
    lat_rows = tile_of(lat_len, 16, 256)
    for item in range(n_items):

        def queries(t, _, item=item):
            at = pl.ds(pl.multiple_of(t * lat_rows, lat_rows), lat_rows)
            values = lat_ref[item, at, :].astype(fl_type)
            centred = values - jnp.mean(values, -1, keepdims=True)
            var = jnp.mean(centred * centred, -1, keepdims=True)
            normal = (centred * lax.rsqrt(var + 1e-05) * gains_ref[:1]).astype(bf_type)
            q_low = dot(normal, first_all[:, :width]).astype(bf_type)
            q_all[item, at, :] = q_low
            raw = dot(q_low, first_all[:, width : width + pad_width])
            qk_ref[item, at, :] = (raw * width**-0.5).astype(bf_type)
            return 0

        lax.fori_loop(0, lat_len // lat_rows, queries, 0)
    if gathers:
        rest[0].relay_plane()
        rest[1].relay_z()

    base = (z * 2 + c) * pix_dev
    for item in range(n_items):
        valid = counts[item] - base

        def score(t, most, item=item, valid=valid):
            at = pl.ds(pl.multiple_of(t * rows, rows), rows)
            values = dot(xn_ref[item, at, :], qk_ref[item], NT)
            place = lax.broadcasted_iota(jnp.int32, values.shape, 0) + t * rows
            values = jnp.where(place < valid, values, -1e30)
            s_buf[at, :] = values
            return jnp.maximum(most, jnp.max(values.reshape(rows // 8, 8, lat_len), 0))

        most = lax.fori_loop(0, tiles, score, jnp.full((8, lat_len), -1e30, fl_type))
        peak = jnp.max(most, 0, keepdims=True)

        def weigh(t, total, item=item, peak=peak):
            at = pl.ds(pl.multiple_of(t * rows, rows), rows)
            values = jnp.exp(s_buf[at, :] - peak)
            pt_ref[item, at, :] = values.astype(bf_type)
            return total + jnp.sum(values.reshape(rows // 8, 8, lat_len), 0)

        total = lax.fori_loop(0, tiles, weigh, jnp.zeros((8, lat_len), fl_type))
        total = jnp.sum(total, 0, keepdims=True)
        peak_ref[item] = jnp.broadcast_to(peak, (8, lat_len))
        st_tx[item, :8] = jnp.broadcast_to(peak, (8, lat_len))
        st_tx[item, 8:] = jnp.broadcast_to(total, (8, lat_len))
        part = dot(xn_ref[item], pt_ref[item], TN)
        px_own[item, : part.shape[0]] = part
        if held > part.shape[0]:
            px_own[item, part.shape[0] :] = jnp.zeros((px_own.shape[1] - part.shape[0], lat_len), fl_type)
        px_tx[item] = px_own[item, :held].astype(bf_type)

    def column_copy(src, dst, index, peer):
        return pltpu.make_async_remote_copy(
            src_ref=src,
            dst_ref=dst,
            send_sem=col_sems.at[0, index],
            recv_sem=col_sems.at[1, index],
            device_id=peer,
            device_id_type=MESH,
        )

    pair = [
        column_copy(px_tx.at[1 - c], px_rx, 0, (d, z, 1 - c)),
        column_copy(st_tx.at[1 - c], st_rx, 1, (d, z, 1 - c)),
    ]
    for copy in pair:
        copy.start()
    if gathers:
        rest[0].relay_far()
    q_ref[...] = q_all[c]
    for copy in pair:
        copy.wait()
    peak_own, peak_rx = st_tx[c, :1], st_rx[:1]
    peak = jnp.maximum(peak_own, peak_rx)
    scale_own, scale_rx = jnp.exp(peak_own - peak), jnp.exp(peak_rx - peak)
    st2_tx[:8] = jnp.broadcast_to(peak, (8, lat_len))
    st2_tx[8:] = jnp.broadcast_to(scale_own * st_tx[c, 8:9] + scale_rx * st_rx[8:9], (8, lat_len))
    both = px_own[c, :held] * scale_own + px_rx[...].astype(fl_type) * scale_rx
    px2_tx[...] = both.astype(bf_type).reshape(n_z, chunk, lat_len)
    copies = []
    for i in range(1, n_z):
        to = lax.rem(z + i, n_z)
        copies.append(column_copy(px2_tx.at[to], px2_rx.at[z], 2 * i, (d, to, c)))
        copies.append(column_copy(st2_tx, st2_rx.at[z], 2 * i + 1, (d, to, c)))
    for copy in copies:
        copy.start()
    for copy in copies:
        copy.wait()
    peak = st2_tx[:1]
    froms = [lax.rem(z + n_z - i, n_z) for i in range(1, n_z)]
    for other in froms:
        peak = jnp.maximum(peak, st2_rx[other, :1])
    scale = jnp.exp(st2_tx[:1] - peak)
    total = scale * st2_tx[8:9]
    mean = scale * px2_tx[z].astype(fl_type)
    for other in froms:
        scale = jnp.exp(st2_rx[other, :1] - peak)
        total = total + scale * st2_rx[other, 8:9]
        mean = mean + scale * px2_rx[other].astype(fl_type)
    stat_ref[:8] = jnp.broadcast_to(peak, (8, lat_len))
    stat_ref[8:] = jnp.broadcast_to(total, (8, lat_len))
    fin_tx[...] = (mean / total).astype(bf_type)
    copies = []
    for i in range(1, n_z):
        to = lax.rem(z + i, n_z)
        copies.append(column_copy(fin_tx, fin_rx.at[z], 2 * n_z + i, (d, to, c)))
    for copy in copies:
        copy.start()
    if gathers:
        rest[1].relay_plane()
        rest[2].relay_z()
    for copy in copies:
        copy.wait()
    for other in froms:
        mean_ref[pl.ds(other * chunk, chunk)] = fin_rx[other]
    mean_ref[pl.ds(z * chunk, chunk)] = fin_tx[...]
    if gathers:
        out = pltpu.make_async_copy(first_all, first_out, local_sems.at[4])
        out.start()
        rest[1].relay_far()
        rest[2].relay_plane()
        rest[2].relay_far()
        for piece in rest:
            piece.finish()
        for piece in [first] + rest:
            piece.drain()
        out.wait()


def forward_call(first_block, rest_block, pixels, latents, counts, input_gain, n_z, n_dev):
    gathers = rest_block is not None
    own, block_width = first_block.shape
    n_items, pix_dev, pix_width = pixels.shape
    lat_len, width = latents.shape[1:]
    pad_width = (block_width - width) // 2
    whole_rows = own * n_dev if gathers else own
    chunk = round_up(-(-pix_width // n_z), 16)
    held = chunk * n_z
    vmem, hbm = pl.BlockSpec(memory_space=pltpu.VMEM), pl.BlockSpec(memory_space=pl.ANY)
    shape = jax.ShapeDtypeStruct
    in_specs = [pl.BlockSpec(memory_space=pltpu.SMEM), hbm] + [hbm] * gathers + [vmem] * 3
    out_shape = [
        shape((n_items, pix_dev, pad_width), bf_type),
        shape((n_items, pix_dev, lat_len), bf_type),
        shape((n_items, 8, lat_len), fl_type),
        shape((n_items, lat_len, pad_width), bf_type),
        shape((lat_len, width), bf_type),
        shape((8, width), fl_type),
        shape((held, lat_len), bf_type),
        shape((16, lat_len), fl_type),
    ]
    out_specs = [vmem] * len(out_shape)
    if gathers:
        out_shape = [
            shape((whole_rows, block_width), bf_type),
            shape((rest_block.shape[0], whole_rows, width), bf_type),
        ] + out_shape
        out_specs = [hbm, hbm] + out_specs
    scratch = [
        pltpu.VMEM((whole_rows, block_width), bf_type),
        pltpu.VMEM((n_items, lat_len, width), bf_type),
        pltpu.VMEM((pix_dev, lat_len), fl_type),
        pltpu.VMEM((n_items, max(held, pad_width), lat_len), fl_type),
        pltpu.VMEM((n_items, held, lat_len), bf_type),
        pltpu.VMEM((held, lat_len), bf_type),
        pltpu.VMEM((n_items, 16, lat_len), fl_type),
        pltpu.VMEM((16, lat_len), fl_type),
        pltpu.VMEM((n_z, chunk, lat_len), bf_type),
        pltpu.VMEM((n_z, chunk, lat_len), bf_type),
        pltpu.VMEM((16, lat_len), fl_type),
        pltpu.VMEM((n_z, 16, lat_len), fl_type),
        pltpu.VMEM((chunk, lat_len), bf_type),
        pltpu.VMEM((n_z, chunk, lat_len), bf_type),
        pltpu.SemaphoreType.DMA((2, 3 * n_z)),
        pltpu.SemaphoreType.DMA((5,)),
    ]
    if gathers:
        scratch += [pltpu.SemaphoreType.DMA((2, 8, n_z))] * (1 + len(PIECES))
    args = [counts, first_block] + ([rest_block] if gathers else [])
    args += [pixels, latents, input_gain.reshape(1, pix_width)]
    outs = pl.pallas_call(
        functools.partial(pixels_forward, n_z, gathers, pix_width, chunk),
        out_shape=out_shape,
        in_specs=in_specs,
        out_specs=out_specs,
        scratch_shapes=scratch,
        compiler_params=pltpu.CompilerParams(
            collective_id=0, has_side_effects=True, vmem_limit_bytes=60 * 2**20
        ),
        name="pixels_forward",
    )(*args)
    return outs if gathers else [first_block, None] + list(outs)


def standard(values):
    centred = values - jnp.mean(values, -1, keepdims=True)
    return centred * lax.rsqrt(jnp.mean(centred * centred, -1, keepdims=True) + 1e-05)


def standard_parts(values):
    centred = values - jnp.mean(values, -1, keepdims=True)
    inv = lax.rsqrt(jnp.mean(centred * centred, -1, keepdims=True) + 1e-05)
    return centred * inv, inv


def pull(hat, inv, grad):
    return (
        grad - jnp.mean(grad, -1, keepdims=True) - hat * jnp.mean(grad * hat, -1, keepdims=True)
    ) * inv


def softmax_rows(scores):
    exp_scores = jnp.exp(scores - jnp.max(scores, -1, keepdims=True))
    return exp_scores / jnp.sum(exp_scores, -1, keepdims=True)


def product(left_side, right_side):
    return jnp.dot(left_side, right_side, preferred_element_type=fl_type)


def product_tn(left_side, right_side):
    return lax.dot_general(
        left_side, right_side, (((0,), (0,)), ((), ())), preferred_element_type=fl_type
    )


def product_nt(left_side, right_side):
    return lax.dot_general(
        left_side, right_side, (((1,), (1,)), ((), ())), preferred_element_type=fl_type
    )


def moments(weight, gradient, first_mom, second, sum_axes):
    first_new = 0.9 * first_mom + 0.1 * gradient
    second_new = 0.999 * second + 0.001 * gradient * gradient
    update = (
        first_new / first_fix / (jnp.sqrt(second_new / second_fix) + 1e-06) + decay_rate * weight
    )
    return (
        first_new,
        second_new,
        update,
        jnp.sum(weight * weight, sum_axes),
        jnp.sum(update * update, sum_axes),
    )


def swap(value):
    return lax.ppermute(value, "core", [(0, 1), (1, 0)])


def local(
    latents,
    pixels,
    pix_counts,
    cotangent,
    weight_mats,
    kv_weights,
    norm_gains,
    input_gain,
    mats_first,
    mats_second,
    kv_first,
    kv_second,
    gains_first,
    gains_second,
    input_first,
    input_second,
):
    item_count, lat_len, model_width = latents.shape
    pix_dev, pix_width = pixels.shape[1:]
    n_mats, own_width = weight_mats.shape[:2]
    n_dp, n_z = lax.axis_size("dp"), lax.axis_size("z")
    z_rank, core = lax.axis_index("z"), lax.axis_index("core")
    pad_width = round_up(round_up(pix_width, 8) + 8, 128)
    head_dim = model_width // HEADS

    kv_cols = jnp.swapaxes(kv_weights, 1, 2)
    gain_at = round_up(pix_width, 8)
    first_block = jnp.concatenate(
        [
            weight_mats[0],
            jnp.pad(kv_cols[0], ((0, 0), (0, pad_width - pix_width))),
            jnp.pad(kv_cols[1], ((0, 0), (0, gain_at - pix_width))),
            norm_gains.T,
            jnp.zeros((own_width, pad_width - gain_at - 4), fl_type),
        ],
        axis=1,
    ).astype(bf_type)
    rest_block = weight_mats[1:].astype(bf_type)
    if own_width % 16:
        first_block = lax.all_gather(first_block, ALL, axis=0, tiled=True)
        w_rest = lax.all_gather(rest_block, ALL, axis=1, tiled=True)
        rest_block = None
    outs = forward_call(
        first_block, rest_block, pixels, latents, pix_counts, input_gain, n_z, n_dp * n_z * 2
    )
    first_all, gathered = outs[:2]
    xn, exp_low, peak_loc, qk_both, q_own, gain_rows, mean_rows, stat_rows = outs[2:]
    if gathered is not None:
        w_rest = gathered
    w_zero = first_all[:, :model_width]
    kt_zero = first_all[:, model_width : model_width + pix_width]
    kt_one = first_all[:, model_width + pad_width : model_width + pad_width + pix_width]
    norm_pix = xn[:, :, :pix_width]
    qk_both = qk_both[:, :, :pix_width]
    peak_loc = peak_loc[:, 0]
    mixed_low = mean_rows[:pix_width].T
    mixed_pix = mixed_low.astype(fl_type)
    peak, total = stat_rows[0], stat_rows[8]
    cross_scale = model_width ** (-0.5)

    def w_mat(index):
        return w_zero if index == 0 else w_rest[index - 1]

    def own_of(both):
        return lax.dynamic_index_in_dim(both, core, 0, keepdims=False)

    def other_of(both):
        return lax.dynamic_index_in_dim(both, 1 - core, 0, keepdims=False)

    def by_item(own, other):
        return jnp.where(core == 0, jnp.stack([own, other]), jnp.stack([other, own]))

    lat_own = own_of(latents).astype(fl_type)
    hat_a, inv_a = standard_parts(lat_own)
    norm_a = (hat_a * gain_rows[0]).astype(bf_type)
    att_low = product_nt(mixed_low, kt_one).astype(bf_type)
    after_cross = lat_own + product(att_low, w_mat(1))
    hat_c, inv_c = standard_parts(after_cross)
    norm_c = (hat_c * gain_rows[1]).astype(bf_type)
    gelu_c, pull_gelu_c = jax.vjp(jax.nn.gelu, product(norm_c, w_mat(2)))
    gelu_c_low = gelu_c.astype(bf_type)
    after_mlp = after_cross + product(gelu_c_low, w_mat(3))
    hat_s, inv_s = standard_parts(after_mlp)
    norm_s = (hat_s * gain_rows[2]).astype(bf_type)
    head_shape = (lat_len, HEADS, head_dim)
    q_self = product(norm_s, w_mat(4)).astype(bf_type).reshape(head_shape)
    k_self = product(norm_s, w_mat(5)).astype(bf_type).reshape(head_shape)
    v_self = product(norm_s, w_mat(6)).astype(bf_type).reshape(head_shape)
    head_scale = head_dim ** (-0.5)
    self_probs = softmax_rows(
        jnp.einsum("qhd,khd->hqk", q_self, k_self, preferred_element_type=fl_type) * head_scale
    )
    self_low = self_probs.astype(bf_type)
    mixed_heads = (
        jnp.einsum("hqk,khd->qhd", self_low, v_self, preferred_element_type=fl_type)
        .astype(bf_type)
        .reshape(lat_len, model_width)
    )
    after_self = after_mlp + product(mixed_heads, w_mat(7))
    hat_f, inv_f = standard_parts(after_self)
    norm_f = (hat_f * gain_rows[3]).astype(bf_type)
    gelu_f, pull_gelu_f = jax.vjp(jax.nn.gelu, product(norm_f, w_mat(8)))
    gelu_f_low = gelu_f.astype(bf_type)
    z_share = lat_len // n_z

    def z_rows(values):
        return lax.dynamic_slice_in_dim(values, z_rank * z_share, z_share, 0)

    def exchange_rows(values):
        halves = values.reshape(2, z_share // 2, model_width)
        return by_item(own_of(halves), swap(other_of(halves)))

    block_out = exchange_rows(
        (z_rows(after_self) + product(z_rows(gelu_f_low), w_mat(9))).astype(bf_type)
    )

    pair_width = 2 * own_width
    n_cols = n_dp * pair_width
    wanted = lax.iota(jnp.int32, n_cols)
    wanted = ((wanted // pair_width) * n_z + z_rank) * pair_width + wanted % pair_width
    select = (lax.iota(jnp.int32, model_width)[:, None] == wanted[None, :]).astype(bf_type)

    def chosen(values):
        return product(values, select).astype(bf_type)

    def chosen_sum(values):
        total_cols = jnp.sum(values, 0).reshape(n_dp, n_z, pair_width)
        return lax.dynamic_index_in_dim(total_cols, z_rank, 1, keepdims=False).reshape(n_cols)

    grad_out = own_of(cotangent).astype(fl_type)
    grad_nine = own_of(cotangent)
    terms = {}
    gain_terms = {}
    terms[9] = product_tn(chosen(gelu_f_low), grad_nine)
    grad_up_f = pull_gelu_f(product_nt(grad_nine, w_mat(9)))[0].astype(bf_type)
    terms[8] = product_tn(chosen(norm_f), grad_up_f)
    grad_norm_f = product_nt(grad_up_f, w_mat(8))
    gain_terms[3] = chosen_sum(hat_f * grad_norm_f)
    grad_self = grad_out + pull(hat_f, inv_f, grad_norm_f * gain_rows[3])
    grad_seven = grad_self.astype(bf_type)
    terms[7] = product_tn(chosen(mixed_heads), grad_seven)
    grad_mixed = product_nt(grad_seven, w_mat(7)).astype(bf_type).reshape(head_shape)
    grad_self_probs = jnp.einsum("qhd,khd->hqk", grad_mixed, v_self, preferred_element_type=fl_type)
    grad_self_scores = (
        self_probs * (grad_self_probs - jnp.sum(self_probs * grad_self_probs, -1, keepdims=True))
    ).astype(bf_type)
    grad_q_self = (
        (
            jnp.einsum("hqk,khd->qhd", grad_self_scores, k_self, preferred_element_type=fl_type)
            * head_scale
        )
        .astype(bf_type)
        .reshape(lat_len, model_width)
    )
    grad_k_self = (
        (
            jnp.einsum("hqk,qhd->khd", grad_self_scores, q_self, preferred_element_type=fl_type)
            * head_scale
        )
        .astype(bf_type)
        .reshape(lat_len, model_width)
    )
    grad_v_self = (
        jnp.einsum("hqk,qhd->khd", self_low, grad_mixed, preferred_element_type=fl_type)
        .astype(bf_type)
        .reshape(lat_len, model_width)
    )
    norm_s_chosen = chosen(norm_s)
    terms[4] = product_tn(norm_s_chosen, grad_q_self)
    terms[5] = product_tn(norm_s_chosen, grad_k_self)
    terms[6] = product_tn(norm_s_chosen, grad_v_self)
    grad_norm_s = (
        product_nt(grad_q_self, w_mat(4))
        + product_nt(grad_k_self, w_mat(5))
        + product_nt(grad_v_self, w_mat(6))
    )
    gain_terms[2] = chosen_sum(hat_s * grad_norm_s)
    grad_mlp = grad_self + pull(hat_s, inv_s, grad_norm_s * gain_rows[2])
    grad_three = grad_mlp.astype(bf_type)
    terms[3] = product_tn(chosen(gelu_c_low), grad_three)
    grad_up_c = pull_gelu_c(product_nt(grad_three, w_mat(3)))[0].astype(bf_type)
    terms[2] = product_tn(chosen(norm_c), grad_up_c)
    grad_norm_c = product_nt(grad_up_c, w_mat(2))
    gain_terms[1] = chosen_sum(hat_c * grad_norm_c)
    grad_cross = grad_mlp + pull(hat_c, inv_c, grad_norm_c * gain_rows[1])
    grad_one = grad_cross.astype(bf_type)
    terms[1] = product_tn(chosen(att_low), grad_one)
    grad_att = product_nt(grad_one, w_mat(1)).astype(bf_type)
    gk_own = product(grad_att, kt_one).astype(bf_type)
    dot_own = jnp.sum(gk_own.astype(fl_type) * mixed_pix, -1)
    term_k_one = product_tn(chosen(grad_att), mixed_low)

    early = jnp.stack([terms[index] for index in range(1, 10)])
    early = early.reshape(9, n_dp * 2, own_width, model_width).swapaxes(0, 1)
    early = early.reshape(n_dp * 2 * 9 * own_width, model_width).astype(bf_type)
    early_sum = lax.psum_scatter(early, ("dp", "core"), scatter_dimension=0, tiled=True)
    early_grad = early_sum.astype(fl_type).reshape(9, own_width, model_width)

    hat_pix, inv_pix = standard_parts(pixels.astype(fl_type))
    stats_own = jnp.stack([peak, total, dot_own])
    stats = by_item(stats_own, swap(stats_own))
    gk_both = by_item(gk_own, swap(gk_own))
    probs = exp_low.astype(fl_type) * (jnp.exp(peak_loc - stats[:, 0]) / stats[:, 1])[:, None, :]
    grad_probs = jnp.einsum("ipc,iqc->ipq", norm_pix, gk_both, preferred_element_type=fl_type)
    grad_scores = (probs * (grad_probs - stats[:, 2][:, None, :])).astype(bf_type)
    probs_low = probs.astype(bf_type)
    query_part = jnp.einsum("ipq,ipc->iqc", grad_scores, norm_pix, preferred_element_type=fl_type)
    query_own = own_of(query_part) + swap(other_of(query_part))
    query_sum = lax.psum(query_own, "z")
    grad_norm_p = jnp.einsum(
        "ipq,iqc->ipc", grad_scores, qk_both, preferred_element_type=fl_type
    ) + jnp.einsum("ipq,iqc->ipc", probs_low, gk_both, preferred_element_type=fl_type)
    input_part = jnp.sum(hat_pix * grad_norm_p, (0, 1))
    pixel_grad = pull(hat_pix, inv_pix, grad_norm_p * input_gain)

    query_low = query_sum.astype(bf_type)
    grad_query = (product_nt(query_low, kt_zero) * cross_scale).astype(bf_type)
    term_zero = product_tn(chosen(norm_a), grad_query)
    grad_norm_a = product_nt(grad_query, w_zero)
    gain_terms[0] = chosen_sum(hat_a * grad_norm_a)
    latent_grad = exchange_rows(
        z_rows(grad_cross)
        + pull(z_rows(hat_a), z_rows(inv_a), z_rows(grad_norm_a) * gain_rows[0])
    )
    term_k_zero = product_tn(chosen(q_own), query_low) * cross_scale
    gains_cols = jnp.stack([gain_terms[index] for index in range(4)], axis=1)
    late = jnp.concatenate(
        [
            term_zero,
            jnp.pad(term_k_zero, ((0, 0), (0, pad_width - pix_width))),
            term_k_one,
            gains_cols,
            jnp.zeros((n_cols, pad_width - pix_width - 4), fl_type),
        ],
        axis=1,
    ).astype(bf_type)
    late_sum = lax.psum_scatter(late, ("dp", "core"), scatter_dimension=0, tiled=True).astype(
        fl_type
    )
    wide_grad = jnp.concatenate([late_sum[None, :, :model_width], early_grad], axis=0)
    kv_grad = jnp.stack(
        [
            late_sum[:, model_width : model_width + pix_width].T,
            late_sum[:, model_width + pad_width : model_width + pad_width + pix_width].T,
        ]
    )
    gains_grad = late_sum[
        :, model_width + pad_width + pix_width : model_width + pad_width + pix_width + 4
    ].T

    mats_first_new, mats_second_new, mats_update, mats_wsum, mats_usum = moments(
        weight_mats, wide_grad, mats_first, mats_second, (1, 2)
    )
    kv_first_new, kv_second_new, kv_update, kv_wsum, kv_usum = moments(
        kv_weights, kv_grad, kv_first, kv_second, (1, 2)
    )
    gains_first_new, gains_second_new, gains_update, gains_wsum, gains_usum = moments(
        norm_gains, gains_grad, gains_first, gains_second, (1,)
    )
    small = jnp.concatenate(
        [mats_wsum, kv_wsum, gains_wsum, mats_usum, kv_usum, gains_usum, input_part]
    )
    small = lax.psum(small, ALL)
    square_w, square_u, input_grad = small[:16], small[16:32], small[32:]
    trust = jnp.sqrt(square_w) / (jnp.sqrt(square_u) + 1e-06)
    mats_new = weight_mats - step_rate * trust[0:10, None, None] * mats_update
    kv_new = kv_weights - step_rate * trust[10:12, None, None] * kv_update
    gains_new = norm_gains - step_rate * trust[12:16, None] * gains_update
    input_first_new, input_second_new, input_update, input_wsum, input_usum = moments(
        input_gain, input_grad, input_first, input_second, (0,)
    )
    input_trust = jnp.sqrt(input_wsum) / (jnp.sqrt(input_usum) + 1e-06)
    input_new = input_gain - step_rate * input_trust * input_update
    return (
        block_out,
        latent_grad,
        pixel_grad,
        wide_grad,
        kv_grad,
        gains_grad,
        input_grad,
        mats_new,
        mats_first_new,
        mats_second_new,
        kv_new,
        kv_first_new,
        kv_second_new,
        gains_new,
        gains_first_new,
        gains_second_new,
        input_new,
        input_first_new,
        input_second_new,
    )


def solution(mesh):
    n_dp, n_rows = mesh.devices.shape
    split_mesh = Mesh(mesh.devices.reshape(n_dp, n_rows // 2, 2), ALL)
    rows = ("z", "core")
    items = P("dp", None, None)
    pix = P("dp", rows, None)
    mats = P(None, ALL, None)
    pairs = P(None, None, ALL)
    gains = P(None, ALL)
    in_specs = (
        items,
        pix,
        P("dp"),
        items,
        mats,
        pairs,
        gains,
        P(),
        mats,
        mats,
        pairs,
        pairs,
        gains,
        gains,
        P(),
        P(),
    )
    out_specs = (
        pix,
        pix,
        pix,
        mats,
        pairs,
        gains,
        P(),
        mats,
        mats,
        mats,
        pairs,
        pairs,
        pairs,
        gains,
        gains,
        gains,
        P(),
        P(),
        P(),
    )
    return jax.shard_map(
        local, mesh=split_mesh, in_specs=in_specs, out_specs=out_specs, check_vma=False
    )
```

```python
import functools

import jax
import jax.numpy as jnp
from jax import lax
from jax.experimental import pallas as pl
from jax.experimental.pallas import tpu as pltpu
from jax.sharding import Mesh, PartitionSpec as P

HEADS = 8
first_fix = 1.0 - 0.9**10
second_fix = 1.0 - 0.999**10
step_rate = 0.25
decay_rate = 0.01
bf_type = jnp.bfloat16
fl_type = jnp.float32
ALL = ("dp", "z", "core")

NT = (((1,), (1,)), ((), ()))
TN = (((0,), (0,)), ((), ()))
NN = (((1,), (0,)), ((), ()))
MESH = pl.DeviceIdType.MESH
PIECES = ((0, 3), (3, 6), (6, 9))


def dot(left_side, right_side, dims=NN):
    return lax.dot_general(left_side, right_side, dims, preferred_element_type=fl_type)


def round_up(value, unit):
    return -(-value // unit) * unit


def tile_of(rows, unit, most):
    best = unit
    for size in range(unit, most + 1, unit):
        if rows % size == 0:
            best = size
    return best


def meet(peers):
    barrier = pltpu.get_barrier_semaphore()
    for peer in peers:
        pl.semaphore_signal(barrier, inc=1, device_id=peer, device_id_type=MESH)
    pl.semaphore_wait(barrier, len(peers))


class Gather:
    def __init__(self, mine, place, sems, n_z):
        self.mine, self.place, self.sems, self.n_z = mine, place, sems, n_z
        self.d, self.z, self.c = (lax.axis_index(name) for name in ALL)
        self.z_from = [lax.rem(self.z + n_z - i, n_z) for i in range(n_z)]
        self.z_to = [lax.rem(self.z + i, n_z) for i in range(n_z)]
        self.sent = []

    def slot(self, d, z, c):
        return self.place((d * self.n_z + z) * 2 + c)

    def copy(self, src, shard, kind, index, peer):
        return pltpu.make_async_remote_copy(
            src_ref=src,
            dst_ref=self.slot(*shard),
            send_sem=self.sems.at[0, kind, index],
            recv_sem=self.sems.at[1, kind, index],
            device_id=peer,
            device_id_type=MESH,
        )

    def send(self, src, shard, kind, index, peer):
        copy = self.copy(src, shard, kind, index, peer)
        copy.start()
        self.sent.append(copy)

    def arrived(self, shard, kind, index):
        self.copy(self.mine, shard, kind, index, (self.d, self.z, 1 - self.c)).wait_recv()

    def start(self, local_sem):
        d, z, c = self.d, self.z, self.c
        shard = (d, z, c)
        for i in range(1, self.n_z):
            self.send(self.mine, shard, 0, i, (d, self.z_to[i], c))
        self.send(self.mine, shard, 1, 0, (d ^ 1, z, c))
        self.send(self.mine, shard, 2, 0, (d ^ 2, z, c))
        self.send(self.mine, shard, 4, 0, (d, z, 1 - c))
        self.own = pltpu.make_async_copy(self.mine, self.slot(*shard), local_sem)
        self.own.start()

    def relay_z(self):
        d, z, c = self.d, self.z, self.c
        for i in range(1, self.n_z):
            shard = (d, self.z_from[i], c)
            self.arrived(shard, 0, i)
            src = self.slot(*shard)
            self.send(src, shard, 1, i, (d ^ 1, z, c))
            self.send(src, shard, 2, i, (d ^ 2, z, c))
            self.send(src, shard, 4, i, (d, z, 1 - c))

    def relay_plane(self):
        d, z, c = self.d, self.z, self.c
        for i in range(self.n_z):
            for kind, flip, onward in ((1, 1, 2), (2, 2, 1)):
                shard = (d ^ flip, self.z_from[i], c)
                self.arrived(shard, kind, i)
                src = self.slot(*shard)
                if (i < self.n_z // 2) == (kind == 1):
                    self.send(src, shard, 3, i, (d ^ onward, z, c))
                self.send(src, shard, 4 + kind, i, (d, z, 1 - c))

    def relay_far(self):
        d, z, c = self.d, self.z, self.c
        for i in range(self.n_z):
            shard = (d ^ 3, self.z_from[i], c)
            self.arrived(shard, 3, i)
            self.send(self.slot(*shard), shard, 7, i, (d, z, 1 - c))

    def finish(self):
        self.own.wait()
        for i in range(self.n_z):
            for kind, flip in ((4, 0), (5, 1), (6, 2), (7, 3)):
                self.arrived((self.d ^ flip, self.z_from[i], 1 - self.c), kind, i)

    def drain(self):
        for copy in self.sent:
            copy.wait_send()


def pixels_forward(
    n_z,
    gathers,
    pix_width,
    chunk,
    counts,
    first_ref,
    *refs,
):
    refs = list(refs)
    rest_ref = refs.pop(0) if gathers else None
    pix_ref, lat_ref, gain_ref = refs[:3]
    refs = refs[3:]
    first_out = refs.pop(0) if gathers else None
    rest_out = refs.pop(0) if gathers else None
    xn_ref, pt_ref, peak_ref, qk_ref, q_ref, gains_ref, mean_ref, stat_ref = refs[:8]
    refs = refs[8:]
    (
        first_all,
        q_all,
        s_buf,
        px_own,
        px_tx,
        px_rx,
        st_tx,
        st_rx,
        px2_tx,
        px2_rx,
        st2_tx,
        st2_rx,
        fin_tx,
        fin_rx,
        col_sems,
        local_sems,
    ) = refs[:16]
    gather_sems = refs[16:]
    d, z, c = (lax.axis_index(name) for name in ALL)
    peers = [(d, lax.rem(z + i, n_z), c) for i in range(1, n_z)] + [(d, z, 1 - c)]
    if gathers:
        peers += [(d ^ 1, z, c), (d ^ 2, z, c)]
    meet(peers)
    if gathers:
        own = first_ref.shape[0]

        def first_place(rank):
            return first_all.at[pl.ds(pl.multiple_of(rank * own, own), own)]

        def rest_place(low, high):
            def place(rank):
                return rest_out.at[low:high, pl.ds(pl.multiple_of(rank * own, own), own)]

            return place

        first = Gather(first_ref, first_place, gather_sems[0], n_z)
        first.start(local_sems.at[0])
        rest = [
            Gather(
                rest_ref.at[low:high],
                rest_place(low, high),
                gather_sems[1 + index],
                n_z,
            )
            for index, (low, high) in enumerate(PIECES)
        ]
        for index, piece in enumerate(rest):
            piece.start(local_sems.at[1 + index])
    else:
        rest = []
        load = pltpu.make_async_copy(first_ref, first_all, local_sems.at[0])
        load.start()

    n_items, pix_dev, _ = pix_ref.shape
    lat_len, width = lat_ref.shape[1:]
    pad_width = xn_ref.shape[2]
    rows = tile_of(pix_dev, 16, 256)
    tiles = pix_dev // rows
    held = chunk * n_z

    def normalise(item):
        def body(t, _):
            at = pl.ds(pl.multiple_of(t * rows, rows), rows)
            values = pix_ref[item, at, :].astype(fl_type)
            centred = values - jnp.sum(values, -1, keepdims=True) * (1.0 / pix_width)
            var = jnp.sum(centred * centred, -1, keepdims=True) * (1.0 / pix_width)
            normal = centred * lax.rsqrt(var + 1e-05) * gain_ref[...]
            xn_ref[item, at, pad_width - 128 :] = jnp.zeros((rows, 128), bf_type)
            xn_ref[item, at, :pix_width] = normal.astype(bf_type)
            return 0

        lax.fori_loop(0, tiles, body, 0)

    normalise(0)
    if gathers:
        first.relay_z()
    for item in range(1, n_items):
        normalise(item)
    if gathers:
        first.relay_plane()
        rest[0].relay_z()
        first.relay_far()
        first.finish()
    else:
        load.wait()

    gain_at = round_up(pix_width, 8) - (pad_width - 128)
    tail = first_all[:, width + 2 * pad_width - 128 :].astype(fl_type).T
    gains_ref[...] = tail[gain_at : gain_at + 8]
    lat_rows = tile_of(lat_len, 16, 256)
    for item in range(n_items):

        def queries(t, _, item=item):
            at = pl.ds(pl.multiple_of(t * lat_rows, lat_rows), lat_rows)
            values = lat_ref[item, at, :].astype(fl_type)
            centred = values - jnp.mean(values, -1, keepdims=True)
            var = jnp.mean(centred * centred, -1, keepdims=True)
            normal = (centred * lax.rsqrt(var + 1e-05) * gains_ref[:1]).astype(bf_type)
            q_low = dot(normal, first_all[:, :width]).astype(bf_type)
            q_all[item, at, :] = q_low
            raw = dot(q_low, first_all[:, width : width + pad_width])
            qk_ref[item, at, :] = (raw * width**-0.5).astype(bf_type)
            return 0

        lax.fori_loop(0, lat_len // lat_rows, queries, 0)
    if gathers:
        rest[0].relay_plane()
        rest[1].relay_z()

    base = (z * 2 + c) * pix_dev
    for item in range(n_items):
        valid = counts[item] - base

        def score(t, most, item=item, valid=valid):
            at = pl.ds(pl.multiple_of(t * rows, rows), rows)
            values = dot(xn_ref[item, at, :], qk_ref[item], NT)
            place = lax.broadcasted_iota(jnp.int32, values.shape, 0) + t * rows
            values = jnp.where(place < valid, values, -1e30)
            s_buf[at, :] = values
            return jnp.maximum(most, jnp.max(values.reshape(rows // 8, 8, lat_len), 0))

        most = lax.fori_loop(0, tiles, score, jnp.full((8, lat_len), -1e30, fl_type))
        peak = jnp.max(most, 0, keepdims=True)

        def weigh(t, total, item=item, peak=peak):
            at = pl.ds(pl.multiple_of(t * rows, rows), rows)
            values = jnp.exp(s_buf[at, :] - peak)
            pt_ref[item, at, :] = values.astype(bf_type)
            return total + jnp.sum(values.reshape(rows // 8, 8, lat_len), 0)

        total = lax.fori_loop(0, tiles, weigh, jnp.zeros((8, lat_len), fl_type))
        total = jnp.sum(total, 0, keepdims=True)
        peak_ref[item] = jnp.broadcast_to(peak, (8, lat_len))
        st_tx[item, :8] = jnp.broadcast_to(peak, (8, lat_len))
        st_tx[item, 8:] = jnp.broadcast_to(total, (8, lat_len))
        part = dot(xn_ref[item], pt_ref[item], TN)
        px_own[item, : part.shape[0]] = part
        if held > part.shape[0]:
            px_own[item, part.shape[0] :] = jnp.zeros((px_own.shape[1] - part.shape[0], lat_len), fl_type)
        px_tx[item] = px_own[item, :held].astype(bf_type)

    def column_copy(src, dst, index, peer):
        return pltpu.make_async_remote_copy(
            src_ref=src,
            dst_ref=dst,
            send_sem=col_sems.at[0, index],
            recv_sem=col_sems.at[1, index],
            device_id=peer,
            device_id_type=MESH,
        )

    pair = [
        column_copy(px_tx.at[1 - c], px_rx, 0, (d, z, 1 - c)),
        column_copy(st_tx.at[1 - c], st_rx, 1, (d, z, 1 - c)),
    ]
    for copy in pair:
        copy.start()
    if gathers:
        rest[0].relay_far()
    q_ref[...] = q_all[c]
    for copy in pair:
        copy.wait()
    peak_own, peak_rx = st_tx[c, :1], st_rx[:1]
    peak = jnp.maximum(peak_own, peak_rx)
    scale_own, scale_rx = jnp.exp(peak_own - peak), jnp.exp(peak_rx - peak)
    st2_tx[:8] = jnp.broadcast_to(peak, (8, lat_len))
    st2_tx[8:] = jnp.broadcast_to(scale_own * st_tx[c, 8:9] + scale_rx * st_rx[8:9], (8, lat_len))
    both = px_own[c, :held] * scale_own + px_rx[...].astype(fl_type) * scale_rx
    px2_tx[...] = both.astype(bf_type).reshape(n_z, chunk, lat_len)
    copies = []
    for i in range(1, n_z):
        to = lax.rem(z + i, n_z)
        copies.append(column_copy(px2_tx.at[to], px2_rx.at[z], 2 * i, (d, to, c)))
        copies.append(column_copy(st2_tx, st2_rx.at[z], 2 * i + 1, (d, to, c)))
    for copy in copies:
        copy.start()
    for copy in copies:
        copy.wait()
    peak = st2_tx[:1]
    froms = [lax.rem(z + n_z - i, n_z) for i in range(1, n_z)]
    for other in froms:
        peak = jnp.maximum(peak, st2_rx[other, :1])
    scale = jnp.exp(st2_tx[:1] - peak)
    total = scale * st2_tx[8:9]
    mean = scale * px2_tx[z].astype(fl_type)
    for other in froms:
        scale = jnp.exp(st2_rx[other, :1] - peak)
        total = total + scale * st2_rx[other, 8:9]
        mean = mean + scale * px2_rx[other].astype(fl_type)
    stat_ref[:8] = jnp.broadcast_to(peak, (8, lat_len))
    stat_ref[8:] = jnp.broadcast_to(total, (8, lat_len))
    fin_tx[...] = (mean / total).astype(bf_type)
    copies = []
    for i in range(1, n_z):
        to = lax.rem(z + i, n_z)
        copies.append(column_copy(fin_tx, fin_rx.at[z], 2 * n_z + i, (d, to, c)))
    for copy in copies:
        copy.start()
    if gathers:
        rest[1].relay_plane()
        rest[2].relay_z()
    for copy in copies:
        copy.wait()
    for other in froms:
        mean_ref[pl.ds(other * chunk, chunk)] = fin_rx[other]
    mean_ref[pl.ds(z * chunk, chunk)] = fin_tx[...]
    if gathers:
        out = pltpu.make_async_copy(first_all, first_out, local_sems.at[4])
        out.start()
        rest[1].relay_far()
        rest[2].relay_plane()
        rest[2].relay_far()
        for piece in rest:
            piece.finish()
        for piece in [first] + rest:
            piece.drain()
        out.wait()


def forward_call(first_block, rest_block, pixels, latents, counts, input_gain, n_z, n_dev):
    gathers = rest_block is not None
    own, block_width = first_block.shape
    n_items, pix_dev, pix_width = pixels.shape
    lat_len, width = latents.shape[1:]
    pad_width = (block_width - width) // 2
    whole_rows = own * n_dev if gathers else own
    chunk = round_up(-(-pix_width // n_z), 16)
    held = chunk * n_z
    vmem, hbm = pl.BlockSpec(memory_space=pltpu.VMEM), pl.BlockSpec(memory_space=pl.ANY)
    shape = jax.ShapeDtypeStruct
    in_specs = [pl.BlockSpec(memory_space=pltpu.SMEM), hbm] + [hbm] * gathers + [vmem] * 3
    out_shape = [
        shape((n_items, pix_dev, pad_width), bf_type),
        shape((n_items, pix_dev, lat_len), bf_type),
        shape((n_items, 8, lat_len), fl_type),
        shape((n_items, lat_len, pad_width), bf_type),
        shape((lat_len, width), bf_type),
        shape((8, width), fl_type),
        shape((held, lat_len), bf_type),
        shape((16, lat_len), fl_type),
    ]
    out_specs = [vmem] * len(out_shape)
    if gathers:
        out_shape = [
            shape((whole_rows, block_width), bf_type),
            shape((rest_block.shape[0], whole_rows, width), bf_type),
        ] + out_shape
        out_specs = [hbm, hbm] + out_specs
    scratch = [
        pltpu.VMEM((whole_rows, block_width), bf_type),
        pltpu.VMEM((n_items, lat_len, width), bf_type),
        pltpu.VMEM((pix_dev, lat_len), fl_type),
        pltpu.VMEM((n_items, max(held, pad_width), lat_len), fl_type),
        pltpu.VMEM((n_items, held, lat_len), bf_type),
        pltpu.VMEM((held, lat_len), bf_type),
        pltpu.VMEM((n_items, 16, lat_len), fl_type),
        pltpu.VMEM((16, lat_len), fl_type),
        pltpu.VMEM((n_z, chunk, lat_len), bf_type),
        pltpu.VMEM((n_z, chunk, lat_len), bf_type),
        pltpu.VMEM((16, lat_len), fl_type),
        pltpu.VMEM((n_z, 16, lat_len), fl_type),
        pltpu.VMEM((chunk, lat_len), bf_type),
        pltpu.VMEM((n_z, chunk, lat_len), bf_type),
        pltpu.SemaphoreType.DMA((2, 3 * n_z)),
        pltpu.SemaphoreType.DMA((5,)),
    ]
    if gathers:
        scratch += [pltpu.SemaphoreType.DMA((2, 8, n_z))] * (1 + len(PIECES))
    args = [counts, first_block] + ([rest_block] if gathers else [])
    args += [pixels, latents, input_gain.reshape(1, pix_width)]
    outs = pl.pallas_call(
        functools.partial(pixels_forward, n_z, gathers, pix_width, chunk),
        out_shape=out_shape,
        in_specs=in_specs,
        out_specs=out_specs,
        scratch_shapes=scratch,
        compiler_params=pltpu.CompilerParams(
            collective_id=0, has_side_effects=True, vmem_limit_bytes=60 * 2**20
        ),
        name="pixels_forward",
    )(*args)
    return outs if gathers else [first_block, None] + list(outs)


def remote(src, dst, sems, index, peer):
    return pltpu.make_async_remote_copy(
        src_ref=src,
        dst_ref=dst,
        send_sem=sems.at[0, index],
        recv_sem=sems.at[1, index],
        device_id=peer,
        device_id_type=MESH,
    )


def backward(n_z, n_dp, pix_width, chunk, *refs):
    (
        gk_ref,
        stats_ref,
        early_ref,
        block_ref,
        xn_hbm,
        pt_hbm,
        peak_ref,
        qk_ref,
        pix_hbm,
        gain_ref,
        lat_hbm,
        first_hbm,
        gains_ref,
        q_hbm,
        cross_ref,
        k_one_ref,
        gterm_ref,
        mats_hbm,
        mfirst_hbm,
        msecond_hbm,
        kv_ref,
        kfirst_ref,
        ksecond_ref,
        ng_ref,
        gfirst_ref,
        gsecond_ref,
        block_out,
        lat_out,
        pix_out,
        mats_out,
        kv_out,
        gains_out,
        small_out,
        xn,
        pt,
        pix,
        lat,
        first,
        q_own,
        mats,
        mfirst,
        msecond,
        gk_rx,
        stats_rx,
        ds,
        pl_low,
        part_tx,
        part_own,
        part_rx,
        col_tx,
        col_rx,
        fin_tx,
        fin_rx,
        dst_full,
        early_own,
        early_rx,
        early_tx,
        early_sum,
        early_far,
        pix_buf,
        hat,
        inv,
        norm,
        dq,
        da,
        sel,
        lat_tx,
        late,
        late_rx,
        late_tx,
        late_own,
        late_far,
        small_tx,
        small_col,
        small_far_tx,
        small_far,
        input_acc,
        sems,
        loads,
    ) = refs
    d, z, c = (lax.axis_index(name) for name in ALL)
    oc = 1 - c
    n_items, pix_dev, pad_width = xn.shape
    lat_len, width = lat.shape[1:]
    own = kv_out.shape[2]
    far = [lax.rem(d + i, n_dp) for i in range(1, n_dp)]
    far_from = [lax.rem(d + n_dp - i, n_dp) for i in range(1, n_dp)]
    z_to = [lax.rem(z + i, n_z) for i in range(1, n_z)]
    z_from = [lax.rem(z + n_z - i, n_z) for i in range(1, n_z)]
    partner = (d, z, oc)
    column = [(i, 0) for i in range(1, n_z)] + [(i, 1) for i in range(n_z)]

    def in_column(i, j):
        return (d, lax.rem(z + i, n_z), lax.rem(c + j, 2))

    meet([in_column(i, j) for i, j in column] + [(to, z, c) for to in far])

    slot = iter(range(1000))

    def send(src, dst, peer):
        copy = remote(src, dst, sems, next(slot), peer)
        copy.start()
        return copy

    pair = [
        send(gk_ref, gk_rx, partner),
        send(stats_ref, stats_rx, partner),
    ]
    out_pair = send(block_ref.at[oc], block_out.at[c], partner)
    early_pair = send(early_ref.at[:, oc], early_rx, partner)
    load_slot = iter(range(1000))

    def load(src, dst):
        copy = pltpu.make_async_copy(src, dst, loads.at[next(load_slot)])
        copy.start()
        return copy

    l_xn = load(xn_hbm, xn)
    l_pt = load(pt_hbm, pt)
    l_pix = load(pix_hbm, pix)
    l_lat = load(lat_hbm.at[c], lat.at[0])
    l_first = load(first_hbm, first)
    l_q = load(q_hbm, q_own)
    l_early = load(early_ref.at[:, c], early_own)
    l_mats = [load(mats_hbm, mats), load(mfirst_hbm, mfirst), load(msecond_hbm, msecond)]
    block_out[c] = block_ref[c]

    rows = tile_of(pix_dev, 16, 256)
    tiles = pix_dev // rows
    held = chunk * n_z
    l_pt.wait()
    l_xn.wait()
    for copy in pair:
        copy.wait()

    def score_side(item, gk, stats):
        scale = jnp.exp(peak_ref[item, :1] - stats[0, :1]) / stats[1, :1]
        delta = stats[2, :1]

        def body(t, _):
            at = pl.ds(pl.multiple_of(t * rows, rows), rows)
            probs = pt[item, at, :].astype(fl_type) * scale
            grad_probs = dot(xn[item, at, :], gk[...], NT)
            ds[item, at, :] = (probs * (grad_probs - delta)).astype(bf_type)
            pl_low[item, at, :] = probs.astype(bf_type)
            return 0

        lax.fori_loop(0, tiles, body, 0)
        return dot(xn[item], ds[item], TN)

    part_tx[...] = score_side(oc, gk_rx, stats_rx)[: part_tx.shape[0]].astype(part_tx.dtype)
    px_pair = send(part_tx, part_rx, partner)
    part_own[...] = score_side(c, gk_ref, stats_ref)
    l_early.wait()
    early_pair.wait()

    n_rows = early_own.shape[1]

    def pair_sum(t, _):
        both = early_own[t].astype(fl_type) + early_rx[t].astype(fl_type)
        early_tx[t] = both.astype(early_tx.dtype)
        return 0

    lax.fori_loop(0, n_dp, pair_sum, 0)
    early_sum[...] = early_own[d].astype(fl_type) + early_rx[d].astype(fl_type)
    px_pair.wait()
    both = part_own[: part_rx.shape[0]] + part_rx[...].astype(fl_type)
    if held > both.shape[0]:
        both = jnp.concatenate([both, jnp.zeros((held - both.shape[0], lat_len), fl_type)], 0)
    col_tx[...] = both[:held].astype(col_tx.dtype).reshape(n_z, chunk, lat_len)
    col = [
        send(col_tx.at[to], col_rx.at[z], (d, to, c)) for to in z_to
    ]
    early_out = [send(early_tx.at[to], early_far.at[d], (to, z, c)) for to in far]

    l_pix.wait()
    input_acc[...] = jnp.zeros(input_acc.shape, fl_type)

    def pixel_side(item, gk):
        def body(t, _):
            at = pl.ds(pl.multiple_of(t * rows, rows), rows)
            grad = dot(ds[item, at, :], qk_ref[item]) + dot(pl_low[item, at, :], gk[...])
            grad = grad[:, :pix_width]
            values = pix[item, at, :].astype(fl_type)
            centred = values - jnp.sum(values, -1, keepdims=True) * (1.0 / pix_width)
            var = jnp.sum(centred * centred, -1, keepdims=True) * (1.0 / pix_width)
            scale = lax.rsqrt(var + 1e-05)
            normal = centred * scale
            input_acc[...] += jnp.sum((normal * grad).reshape(rows // 8, 8, pix_width), 0)
            grad = grad * gain_ref[...]
            mean = jnp.sum(grad, -1, keepdims=True) * (1.0 / pix_width)
            along = jnp.sum(grad * normal, -1, keepdims=True) * (1.0 / pix_width)
            pix_buf[item, at, :] = (grad - mean - normal * along) * scale
            return 0

        lax.fori_loop(0, tiles, body, 0)
        return load(pix_buf.at[item], pix_out.at[item])

    stores = [pixel_side(c, gk_ref)]

    for copy in col:
        copy.wait()
    mean = col_tx[z].astype(fl_type)
    for other in z_from:
        mean = mean + col_rx[other].astype(fl_type)
    fin_tx[...] = mean.astype(fin_tx.dtype)
    fin = [send(fin_tx, fin_rx.at[z], (d, to, c)) for to in z_to]

    stores.append(pixel_side(oc, gk_rx))

    l_lat.wait()
    l_first.wait()
    l_q.wait()
    pair_width = 2 * own
    n_cols = n_dp * pair_width
    wanted = lax.broadcasted_iota(jnp.int32, (width, n_cols), 1)
    wanted = (lax.div(wanted, pair_width) * n_z + z) * pair_width + lax.rem(wanted, pair_width)
    place = lax.broadcasted_iota(jnp.int32, (width, n_cols), 0)
    sel[...] = jnp.where(place == wanted, 1.0, 0.0).astype(bf_type)
    values = lat[0].astype(fl_type)
    centred = values - jnp.mean(values, -1, keepdims=True)
    scale = lax.rsqrt(jnp.mean(centred * centred, -1, keepdims=True) + 1e-05)
    hat[...] = centred * scale
    inv[...] = jnp.broadcast_to(scale, inv.shape)
    norm[...] = dot((hat[...] * gains_ref[:1]).astype(bf_type), sel[...]).astype(bf_type)

    for copy in fin:
        copy.wait()
    dst_full[...] = jnp.zeros(dst_full.shape, fl_type)
    for other in z_from:
        dst_full[pl.ds(other * chunk, chunk)] = fin_rx[other].astype(fl_type)
    dst_full[pl.ds(z * chunk, chunk)] = fin_tx[...].astype(fl_type)
    summed = dst_full[:pad_width].T.astype(bf_type)
    kt_zero = first[:, width : width + pad_width]
    dq[...] = (dot(summed, kt_zero, NT) * width**-0.5).astype(bf_type)
    da[...] = dot(dq[...], first[:, :width], NT)
    term_zero = dot(norm[...], dq[...], TN)
    q_sel = dot(q_own[...], sel[...]).astype(bf_type)
    term_k = dot(q_sel, summed, TN) * width**-0.5
    gain_at = round_up(pix_width, 8) - (pad_width - 128)
    gain_zero = jnp.sum(hat[...] * da[...], 0, keepdims=True)
    place = lax.broadcasted_iota(jnp.int32, (8, width), 0)
    gain_sums = jnp.where(place == 0, gain_zero, gterm_ref[...]).astype(bf_type)
    gain_cols = dot(gain_sums, sel[...])
    gain_cols = jnp.concatenate(
        [
            jnp.zeros((gain_at, n_cols), fl_type),
            gain_cols,
            jnp.zeros((128 - gain_at - 8, n_cols), fl_type),
        ],
        0,
    ).T
    late_shape = (n_dp, 2, own, -1)
    late[:, :, :, :width] = term_zero.astype(late.dtype).reshape(n_dp, 2, own, width)
    late[:, :, :, width : width + pad_width] = term_k.astype(late.dtype).reshape(
        n_dp, 2, own, pad_width
    )
    ones = k_one_ref[...]
    late[:, :, :, width + pad_width : width + 2 * pad_width - 128] = (
        ones[:, : pad_width - 128].astype(late.dtype).reshape(n_dp, 2, own, pad_width - 128)
    )
    late[:, :, :, width + 2 * pad_width - 128 :] = (
        (ones[:, pad_width - 128 :] + gain_cols).astype(late.dtype).reshape(n_dp, 2, own, 128)
    )
    late_pair = send(late.at[:, oc], late_rx, partner)

    z_share = lat_len // n_z
    at = pl.ds(pl.multiple_of(z * z_share, z_share), z_share)
    grad = da[at, :] * gains_ref[:1]
    normal = hat[at, :]
    mean = jnp.mean(grad, -1, keepdims=True)
    along = jnp.mean(grad * normal, -1, keepdims=True)
    lat_grad = cross_ref[...] + (grad - mean - normal * along) * inv[at, :1]
    lat_tx[...] = lat_grad.reshape(2, z_share // 2, width)
    lat_pair = send(lat_tx.at[oc], lat_out.at[c], partner)
    lat_out[c] = lat_tx[c]

    late_pair.wait()
    late_sum = late[:, c].astype(fl_type) + late_rx[...].astype(fl_type)
    late_tx[...] = late_sum.astype(late_tx.dtype)
    late_out = [send(late_tx.at[to], late_far.at[d], (to, z, c)) for to in far]
    late_own[...] = late[d, c].astype(fl_type) + late_rx[d].astype(fl_type)

    for copy in early_out:
        copy.wait()
    for copy in l_mats:
        copy.wait()
    lane = lax.broadcasted_iota(jnp.int32, (1, 128), 1)

    def norms(weight, gradient, first_mom, second):
        first_new = 0.9 * first_mom + 0.1 * gradient
        second_new = 0.999 * second + 0.001 * gradient * gradient
        update = (
            first_new / first_fix / (jnp.sqrt(second_new / second_fix) + 1e-06)
            + decay_rate * weight
        )
        return (weight * weight, update * update)

    def total(values):
        return jnp.sum(jnp.sum(values, 0, keepdims=True), 1, keepdims=True)

    def matrix(k, sums):
        at = pl.ds(pl.multiple_of((k - 1) * own, own), own)
        gradient = early_sum[at, :]
        for other in far_from:
            gradient = gradient + early_far[other, at, :].astype(fl_type)
        mats_out[k] = gradient
        w_sq, u_sq = norms(mats[k], gradient, mfirst[k], msecond[k])
        here = lane == k
        return (
            sums[0] + jnp.where(here, total(w_sq), 0.0),
            sums[1] + jnp.where(here, total(u_sq), 0.0),
        )

    zero = jnp.zeros((1, 128), fl_type)
    sums = lax.fori_loop(1, mats.shape[0], matrix, (zero, zero))

    for copy in late_out:
        copy.wait()
    for other in far_from:
        late_own[...] += late_far[other].astype(fl_type)
    mats_out[0] = late_own[:, :width]
    grads = [(mats[0], late_own[:, :width], mfirst[0], msecond[0], 0)]
    for k in range(2):
        cols = late_own[:, width + k * pad_width : width + (k + 1) * pad_width].T
        kv_out[k] = cols[:pix_width]
        grads.append((kv_ref[k], cols[:pix_width], kfirst_ref[k], ksecond_ref[k], 10 + k))
    at = pad_width - 128 + gain_at
    gain_grad = cols[at : at + 8]
    gains_out[...] = gain_grad[:4]
    w_sum, u_sum = sums
    for weight, gradient, first_mom, second, k in grads:
        w_sq, u_sq = norms(weight, gradient, first_mom, second)
        w_sum = w_sum + jnp.where(lane == k, total(w_sq), 0.0)
        u_sum = u_sum + jnp.where(lane == k, total(u_sq), 0.0)
    w_sq, u_sq = norms(ng_ref[...], gain_grad[:4], gfirst_ref[...], gsecond_ref[...])
    w_sq, u_sq = jnp.sum(w_sq, 1, keepdims=True), jnp.sum(u_sq, 1, keepdims=True)
    for k in range(4):
        w_sum = w_sum + jnp.where(lane == 12 + k, w_sq[k : k + 1], 0.0)
        u_sum = u_sum + jnp.where(lane == 12 + k, u_sq[k : k + 1], 0.0)
    small_tx[...] = jnp.zeros(small_tx.shape, fl_type)
    small_tx[0:1, :128] = w_sum
    small_tx[1:2, :128] = u_sum
    small_tx[2:3, :pix_width] = jnp.sum(input_acc[...], 0, keepdims=True)
    copies = [
        send(small_tx, small_col.at[n], in_column(i, j)) for n, (i, j) in enumerate(column)
    ]
    for copy in copies:
        copy.wait()
    all_sum = small_tx[...]
    for n in range(len(column)):
        all_sum = all_sum + small_col[n]
    small_far_tx[...] = all_sum
    copies = [
        send(small_far_tx, small_far.at[n], (to, z, c)) for n, to in enumerate(far)
    ]
    for copy in copies:
        copy.wait()
    for n in range(len(far)):
        all_sum = all_sum + small_far[n]
    small_out[...] = all_sum
    for copy in [out_pair, lat_pair] + stores:
        copy.wait()


def backward_call(n_z, n_dp, args):
    (gk, stats, early, block, xn, pt, _, qk, pixels, _, latents, first) = args[:12]
    mats, kv, gains = args[17], args[20], args[23]
    n_items, pix_dev, pix_width = pixels.shape
    lat_len, width = latents.shape[1:]
    pad_width = xn.shape[2]
    own = mats.shape[1]
    early_rows = early.shape[2]
    wire = early.dtype
    chunk = round_up(-(-pix_width // n_z), 16)
    held = chunk * n_z
    cut = min(held, pad_width)
    z_share = lat_len // n_z
    n_cols = n_dp * 2 * own
    vmem, hbm = pl.BlockSpec(memory_space=pltpu.VMEM), pl.BlockSpec(memory_space=pl.ANY)
    in_hbm = {"early": 2, "xn": 4, "pt": 5, "pix": 8, "lat": 10, "first": 11, "q": 13}
    places = set(in_hbm.values()) | {17, 18, 19}
    in_specs = [hbm if index in places else vmem for index in range(len(args))]
    shape, buf = jax.ShapeDtypeStruct, pltpu.VMEM
    out_shape = [
        shape((n_items, z_share // 2, width), bf_type),
        shape((n_items, z_share // 2, width), fl_type),
        shape(pixels.shape, fl_type),
        shape(mats.shape, fl_type),
        shape(kv.shape, fl_type),
        shape(gains.shape, fl_type),
        shape((8, pad_width), fl_type),
    ]
    out_specs = [vmem, vmem, hbm, vmem, vmem, vmem, vmem]
    late_width = width + 2 * pad_width
    scratch = [
        buf(xn.shape, bf_type),
        buf(pt.shape, bf_type),
        buf(pixels.shape, bf_type),
        buf((1, lat_len, width), bf_type),
        buf(first.shape, bf_type),
        buf((lat_len, width), bf_type),
        buf(mats.shape, fl_type),
        buf(mats.shape, fl_type),
        buf(mats.shape, fl_type),
        buf(gk.shape, bf_type),
        buf(stats.shape, fl_type),
        buf(pt.shape, bf_type),
        buf(pt.shape, bf_type),
        buf((cut, lat_len), bf_type),
        buf((pad_width, lat_len), fl_type),
        buf((cut, lat_len), bf_type),
        buf((n_z, chunk, lat_len), bf_type),
        buf((n_z, chunk, lat_len), bf_type),
        buf((chunk, lat_len), bf_type),
        buf((n_z, chunk, lat_len), bf_type),
        buf((max(held, pad_width), lat_len), fl_type),
        buf((n_dp, early_rows, width), wire),
        buf((n_dp, early_rows, width), wire),
        buf((n_dp, early_rows, width), wire),
        buf((early_rows, width), fl_type),
        buf((n_dp, early_rows, width), wire),
        buf(pixels.shape, fl_type),
        buf((lat_len, width), fl_type),
        buf((lat_len, 128), fl_type),
        buf((lat_len, n_cols), bf_type),
        buf((lat_len, width), bf_type),
        buf((lat_len, width), fl_type),
        buf((width, n_cols), bf_type),
        buf((2, z_share // 2, width), fl_type),
        buf((n_dp, 2, own, late_width), wire),
        buf((n_dp, own, late_width), wire),
        buf((n_dp, own, late_width), wire),
        buf((own, late_width), fl_type),
        buf((n_dp, own, late_width), wire),
        buf((8, pad_width), fl_type),
        buf((2 * n_z - 1, 8, pad_width), fl_type),
        buf((8, pad_width), fl_type),
        buf((n_dp - 1, 8, pad_width), fl_type),
        buf((8, pix_width), fl_type),
        pltpu.SemaphoreType.DMA((2, 20 + 6 * n_z + 3 * n_dp)),
        pltpu.SemaphoreType.DMA((16,)),
    ]
    return pl.pallas_call(
        functools.partial(backward, n_z, n_dp, pix_width, chunk),
        out_shape=out_shape,
        in_specs=in_specs,
        out_specs=out_specs,
        scratch_shapes=scratch,
        compiler_params=pltpu.CompilerParams(
            collective_id=1, has_side_effects=True, vmem_limit_bytes=60 * 2**20
        ),
        name="backward",
    )(*args)


def standard(values):
    centred = values - jnp.mean(values, -1, keepdims=True)
    return centred * lax.rsqrt(jnp.mean(centred * centred, -1, keepdims=True) + 1e-05)


def standard_parts(values):
    centred = values - jnp.mean(values, -1, keepdims=True)
    inv = lax.rsqrt(jnp.mean(centred * centred, -1, keepdims=True) + 1e-05)
    return centred * inv, inv


def pull(hat, inv, grad):
    return (
        grad - jnp.mean(grad, -1, keepdims=True) - hat * jnp.mean(grad * hat, -1, keepdims=True)
    ) * inv


def softmax_rows(scores):
    exp_scores = jnp.exp(scores - jnp.max(scores, -1, keepdims=True))
    return exp_scores / jnp.sum(exp_scores, -1, keepdims=True)


def product(left_side, right_side):
    return jnp.dot(left_side, right_side, preferred_element_type=fl_type)


def product_tn(left_side, right_side):
    return lax.dot_general(
        left_side, right_side, (((0,), (0,)), ((), ())), preferred_element_type=fl_type
    )


def product_nt(left_side, right_side):
    return lax.dot_general(
        left_side, right_side, (((1,), (1,)), ((), ())), preferred_element_type=fl_type
    )


def moments(weight, gradient, first_mom, second, sum_axes):
    first_new = 0.9 * first_mom + 0.1 * gradient
    second_new = 0.999 * second + 0.001 * gradient * gradient
    update = (
        first_new / first_fix / (jnp.sqrt(second_new / second_fix) + 1e-06) + decay_rate * weight
    )
    return (
        first_new,
        second_new,
        update,
        jnp.sum(weight * weight, sum_axes),
        jnp.sum(update * update, sum_axes),
    )


def local(
    latents,
    pixels,
    pix_counts,
    cotangent,
    weight_mats,
    kv_weights,
    norm_gains,
    input_gain,
    mats_first,
    mats_second,
    kv_first,
    kv_second,
    gains_first,
    gains_second,
    input_first,
    input_second,
):
    item_count, lat_len, model_width = latents.shape
    pix_dev, pix_width = pixels.shape[1:]
    n_mats, own_width = weight_mats.shape[:2]
    n_dp, n_z = lax.axis_size("dp"), lax.axis_size("z")
    z_rank, core = lax.axis_index("z"), lax.axis_index("core")
    pad_width = round_up(round_up(pix_width, 8) + 8, 128)
    head_dim = model_width // HEADS

    kv_cols = jnp.swapaxes(kv_weights, 1, 2)
    gain_at = round_up(pix_width, 8)
    first_block = jnp.concatenate(
        [
            weight_mats[0],
            jnp.pad(kv_cols[0], ((0, 0), (0, pad_width - pix_width))),
            jnp.pad(kv_cols[1], ((0, 0), (0, gain_at - pix_width))),
            norm_gains.T,
            jnp.zeros((own_width, pad_width - gain_at - 4), fl_type),
        ],
        axis=1,
    ).astype(bf_type)
    rest_block = weight_mats[1:].astype(bf_type)
    if own_width % 16:
        first_block = lax.all_gather(first_block, ALL, axis=0, tiled=True)
        w_rest = lax.all_gather(rest_block, ALL, axis=1, tiled=True)
        rest_block = None
    outs = forward_call(
        first_block, rest_block, pixels, latents, pix_counts, input_gain, n_z, n_dp * n_z * 2
    )
    first_all, gathered = outs[:2]
    xn, exp_low, peak_loc, qk_both, q_own, gain_rows, mean_rows, stat_rows = outs[2:]
    if gathered is not None:
        w_rest = gathered
    w_zero = first_all[:, :model_width]
    kt_zero = first_all[:, model_width : model_width + pix_width]
    kt_one = first_all[:, model_width + pad_width : model_width + pad_width + pix_width]
    mixed_low = mean_rows[:pix_width].T
    mixed_pix = mixed_low.astype(fl_type)
    peak, total = stat_rows[0], stat_rows[8]

    def w_mat(index):
        return w_zero if index == 0 else w_rest[index - 1]

    def own_of(both):
        return lax.dynamic_index_in_dim(both, core, 0, keepdims=False)

    def other_of(both):
        return lax.dynamic_index_in_dim(both, 1 - core, 0, keepdims=False)

    lat_own = own_of(latents).astype(fl_type)
    hat_a, inv_a = standard_parts(lat_own)
    norm_a = (hat_a * gain_rows[0]).astype(bf_type)
    att_low = product_nt(mixed_low, kt_one).astype(bf_type)
    after_cross = lat_own + product(att_low, w_mat(1))
    hat_c, inv_c = standard_parts(after_cross)
    norm_c = (hat_c * gain_rows[1]).astype(bf_type)
    gelu_c, pull_gelu_c = jax.vjp(jax.nn.gelu, product(norm_c, w_mat(2)))
    gelu_c_low = gelu_c.astype(bf_type)
    after_mlp = after_cross + product(gelu_c_low, w_mat(3))
    hat_s, inv_s = standard_parts(after_mlp)
    norm_s = (hat_s * gain_rows[2]).astype(bf_type)
    head_shape = (lat_len, HEADS, head_dim)
    q_self = product(norm_s, w_mat(4)).astype(bf_type).reshape(head_shape)
    k_self = product(norm_s, w_mat(5)).astype(bf_type).reshape(head_shape)
    v_self = product(norm_s, w_mat(6)).astype(bf_type).reshape(head_shape)
    head_scale = head_dim ** (-0.5)
    self_probs = softmax_rows(
        jnp.einsum("qhd,khd->hqk", q_self, k_self, preferred_element_type=fl_type) * head_scale
    )
    self_low = self_probs.astype(bf_type)
    mixed_heads = (
        jnp.einsum("hqk,khd->qhd", self_low, v_self, preferred_element_type=fl_type)
        .astype(bf_type)
        .reshape(lat_len, model_width)
    )
    after_self = after_mlp + product(mixed_heads, w_mat(7))
    hat_f, inv_f = standard_parts(after_self)
    norm_f = (hat_f * gain_rows[3]).astype(bf_type)
    gelu_f, pull_gelu_f = jax.vjp(jax.nn.gelu, product(norm_f, w_mat(8)))
    gelu_f_low = gelu_f.astype(bf_type)
    z_share = lat_len // n_z

    def z_rows(values):
        return lax.dynamic_slice_in_dim(values, z_rank * z_share, z_share, 0)

    block_rows = (z_rows(after_self) + product(z_rows(gelu_f_low), w_mat(9))).astype(bf_type)
    block_rows = block_rows.reshape(2, z_share // 2, model_width)

    pair_width = 2 * own_width
    n_cols = n_dp * pair_width
    wanted = lax.iota(jnp.int32, n_cols)
    wanted = ((wanted // pair_width) * n_z + z_rank) * pair_width + wanted % pair_width
    select = (lax.iota(jnp.int32, model_width)[:, None] == wanted[None, :]).astype(bf_type)

    def col_sum(values):
        return jnp.sum(values, 0)

    def chosen(values):
        return product(values, select).astype(bf_type)


    grad_out = own_of(cotangent).astype(fl_type)
    grad_nine = own_of(cotangent)
    terms = {}
    gain_terms = {}
    terms[9] = product_tn(chosen(gelu_f_low), grad_nine)
    grad_up_f = pull_gelu_f(product_nt(grad_nine, w_mat(9)))[0].astype(bf_type)
    terms[8] = product_tn(chosen(norm_f), grad_up_f)
    grad_norm_f = product_nt(grad_up_f, w_mat(8))
    gain_terms[3] = col_sum(hat_f * grad_norm_f)
    grad_self = grad_out + pull(hat_f, inv_f, grad_norm_f * gain_rows[3])
    grad_seven = grad_self.astype(bf_type)
    terms[7] = product_tn(chosen(mixed_heads), grad_seven)
    grad_mixed = product_nt(grad_seven, w_mat(7)).astype(bf_type).reshape(head_shape)
    grad_self_probs = jnp.einsum("qhd,khd->hqk", grad_mixed, v_self, preferred_element_type=fl_type)
    grad_self_scores = (
        self_probs * (grad_self_probs - jnp.sum(self_probs * grad_self_probs, -1, keepdims=True))
    ).astype(bf_type)
    grad_q_self = (
        (
            jnp.einsum("hqk,khd->qhd", grad_self_scores, k_self, preferred_element_type=fl_type)
            * head_scale
        )
        .astype(bf_type)
        .reshape(lat_len, model_width)
    )
    grad_k_self = (
        (
            jnp.einsum("hqk,qhd->khd", grad_self_scores, q_self, preferred_element_type=fl_type)
            * head_scale
        )
        .astype(bf_type)
        .reshape(lat_len, model_width)
    )
    grad_v_self = (
        jnp.einsum("hqk,qhd->khd", self_low, grad_mixed, preferred_element_type=fl_type)
        .astype(bf_type)
        .reshape(lat_len, model_width)
    )
    norm_s_chosen = chosen(norm_s)
    terms[4] = product_tn(norm_s_chosen, grad_q_self)
    terms[5] = product_tn(norm_s_chosen, grad_k_self)
    terms[6] = product_tn(norm_s_chosen, grad_v_self)
    grad_norm_s = (
        product_nt(grad_q_self, w_mat(4))
        + product_nt(grad_k_self, w_mat(5))
        + product_nt(grad_v_self, w_mat(6))
    )
    gain_terms[2] = col_sum(hat_s * grad_norm_s)
    grad_mlp = grad_self + pull(hat_s, inv_s, grad_norm_s * gain_rows[2])
    grad_three = grad_mlp.astype(bf_type)
    terms[3] = product_tn(chosen(gelu_c_low), grad_three)
    grad_up_c = pull_gelu_c(product_nt(grad_three, w_mat(3)))[0].astype(bf_type)
    terms[2] = product_tn(chosen(norm_c), grad_up_c)
    grad_norm_c = product_nt(grad_up_c, w_mat(2))
    gain_terms[1] = col_sum(hat_c * grad_norm_c)
    grad_cross = grad_mlp + pull(hat_c, inv_c, grad_norm_c * gain_rows[1])
    grad_one = grad_cross.astype(bf_type)
    terms[1] = product_tn(chosen(att_low), grad_one)
    grad_att = product_nt(grad_one, w_mat(1)).astype(bf_type)
    gk_own = product(grad_att, kt_one).astype(bf_type)
    dot_own = jnp.sum(gk_own.astype(fl_type) * mixed_pix, -1)
    gk_own = jnp.pad(gk_own, ((0, 0), (0, pad_width - pix_width)))
    term_k_one = product_tn(chosen(grad_att), mixed_low)
    term_k_one = jnp.pad(term_k_one, ((0, 0), (0, pad_width - pix_width)))

    wire = bf_type if own_width % 16 == 0 else fl_type
    early = jnp.stack([terms[index] for index in range(1, 10)]).astype(wire)
    early = early.reshape(9, n_dp, 2, own_width, model_width).transpose(1, 2, 0, 3, 4)
    early = early.reshape(n_dp, 2, 9 * own_width, model_width)
    stats_own = jnp.broadcast_to(
        jnp.stack([peak, total, dot_own])[:, None, :], (3, 8, lat_len)
    )
    gain_sums = jnp.stack([gain_terms[index] for index in range(1, 4)])
    gain_sums = jnp.pad(gain_sums, ((1, 4), (0, 0)))
    block_out, latent_grad, pixel_grad, wide_grad, kv_grad, gains_grad, small = backward_call(
        n_z,
        n_dp,
        (
            gk_own,
            stats_own,
            early,
            block_rows,
            xn,
            exp_low,
            peak_loc,
            qk_both,
            pixels,
            input_gain.reshape(1, pix_width),
            latents,
            first_all,
            gain_rows,
            q_own,
            z_rows(grad_cross),
            term_k_one,
            gain_sums,
            weight_mats,
            mats_first,
            mats_second,
            kv_weights,
            kv_first,
            kv_second,
            norm_gains,
            gains_first,
            gains_second,
        ),
    )

    mats_first_new, mats_second_new, mats_update, mats_wsum, mats_usum = moments(
        weight_mats, wide_grad, mats_first, mats_second, (1, 2)
    )
    kv_first_new, kv_second_new, kv_update, kv_wsum, kv_usum = moments(
        kv_weights, kv_grad, kv_first, kv_second, (1, 2)
    )
    gains_first_new, gains_second_new, gains_update, gains_wsum, gains_usum = moments(
        norm_gains, gains_grad, gains_first, gains_second, (1,)
    )
    square_w, square_u, input_grad = small[0, :16], small[1, :16], small[2, :pix_width]
    trust = jnp.sqrt(square_w) / (jnp.sqrt(square_u) + 1e-06)
    mats_new = weight_mats - step_rate * trust[0:10, None, None] * mats_update
    kv_new = kv_weights - step_rate * trust[10:12, None, None] * kv_update
    gains_new = norm_gains - step_rate * trust[12:16, None] * gains_update
    input_first_new, input_second_new, input_update, input_wsum, input_usum = moments(
        input_gain, input_grad, input_first, input_second, (0,)
    )
    input_trust = jnp.sqrt(input_wsum) / (jnp.sqrt(input_usum) + 1e-06)
    input_new = input_gain - step_rate * input_trust * input_update
    return (
        block_out,
        latent_grad,
        pixel_grad,
        wide_grad,
        kv_grad,
        gains_grad,
        input_grad,
        mats_new,
        mats_first_new,
        mats_second_new,
        kv_new,
        kv_first_new,
        kv_second_new,
        gains_new,
        gains_first_new,
        gains_second_new,
        input_new,
        input_first_new,
        input_second_new,
    )


def solution(mesh):
    n_dp, n_rows = mesh.devices.shape
    split_mesh = Mesh(mesh.devices.reshape(n_dp, n_rows // 2, 2), ALL)
    rows = ("z", "core")
    items = P("dp", None, None)
    pix = P("dp", rows, None)
    mats = P(None, ALL, None)
    pairs = P(None, None, ALL)
    gains = P(None, ALL)
    in_specs = (
        items,
        pix,
        P("dp"),
        items,
        mats,
        pairs,
        gains,
        P(),
        mats,
        mats,
        pairs,
        pairs,
        gains,
        gains,
        P(),
        P(),
    )
    out_specs = (
        pix,
        pix,
        pix,
        mats,
        pairs,
        gains,
        P(),
        mats,
        mats,
        mats,
        pairs,
        pairs,
        pairs,
        gains,
        gains,
        gains,
        P(),
        P(),
        P(),
    )
    return jax.shard_map(
        local, mesh=split_mesh, in_specs=in_specs, out_specs=out_specs, check_vma=False
    )
```

```python
import functools
import math

import jax
import jax.numpy as jnp
from jax import lax
from jax.experimental import pallas as pl
from jax.experimental.pallas import tpu as pltpu
from jax.sharding import Mesh, PartitionSpec as P

HEADS = 8
first_fix = 1.0 - 0.9**10
second_fix = 1.0 - 0.999**10
step_rate = 0.25
decay_rate = 0.01
bf_type = jnp.bfloat16
fl_type = jnp.float32
ALL = ("dp", "z", "core")

NT = (((1,), (1,)), ((), ()))
TN = (((0,), (0,)), ((), ()))
NN = (((1,), (0,)), ((), ()))
MESH = pl.DeviceIdType.MESH
PIECES = ((0, 3), (3, 6), (6, 9))


def dot(left_side, right_side, dims=NN):
    return lax.dot_general(left_side, right_side, dims, preferred_element_type=fl_type)


def round_up(value, unit):
    return -(-value // unit) * unit


def tile_of(rows, unit, most):
    best = unit
    for size in range(unit, most + 1, unit):
        if rows % size == 0:
            best = size
    return best


def meet(peers):
    barrier = pltpu.get_barrier_semaphore()
    for peer in peers:
        pl.semaphore_signal(barrier, inc=1, device_id=peer, device_id_type=MESH)
    pl.semaphore_wait(barrier, len(peers))


class Gather:
    def __init__(self, mine, place, sems, n_z):
        self.mine, self.place, self.sems, self.n_z = mine, place, sems, n_z
        self.d, self.z, self.c = (lax.axis_index(name) for name in ALL)
        self.z_from = [lax.rem(self.z + n_z - i, n_z) for i in range(n_z)]
        self.z_to = [lax.rem(self.z + i, n_z) for i in range(n_z)]
        self.sent = []

    def slot(self, d, z, c):
        return self.place((d * self.n_z + z) * 2 + c)

    def copy(self, src, shard, kind, index, peer):
        return pltpu.make_async_remote_copy(
            src_ref=src,
            dst_ref=self.slot(*shard),
            send_sem=self.sems.at[0, kind, index],
            recv_sem=self.sems.at[1, kind, index],
            device_id=peer,
            device_id_type=MESH,
        )

    def send(self, src, shard, kind, index, peer):
        copy = self.copy(src, shard, kind, index, peer)
        copy.start()
        self.sent.append(copy)

    def arrived(self, shard, kind, index):
        self.copy(self.mine, shard, kind, index, (self.d, self.z, 1 - self.c)).wait_recv()

    def start(self, local_sem):
        d, z, c = self.d, self.z, self.c
        shard = (d, z, c)
        for i in range(1, self.n_z):
            self.send(self.mine, shard, 0, i, (d, self.z_to[i], c))
        self.send(self.mine, shard, 1, 0, (d ^ 1, z, c))
        self.send(self.mine, shard, 2, 0, (d ^ 2, z, c))
        self.send(self.mine, shard, 4, 0, (d, z, 1 - c))
        self.own = pltpu.make_async_copy(self.mine, self.slot(*shard), local_sem)
        self.own.start()

    def relay_z(self):
        d, z, c = self.d, self.z, self.c
        for i in range(1, self.n_z):
            shard = (d, self.z_from[i], c)
            self.arrived(shard, 0, i)
            src = self.slot(*shard)
            self.send(src, shard, 1, i, (d ^ 1, z, c))
            self.send(src, shard, 2, i, (d ^ 2, z, c))
            self.send(src, shard, 4, i, (d, z, 1 - c))

    def relay_plane(self):
        d, z, c = self.d, self.z, self.c
        for i in range(self.n_z):
            for kind, flip, onward in ((1, 1, 2), (2, 2, 1)):
                shard = (d ^ flip, self.z_from[i], c)
                self.arrived(shard, kind, i)
                src = self.slot(*shard)
                if (i < self.n_z // 2) == (kind == 1):
                    self.send(src, shard, 3, i, (d ^ onward, z, c))
                self.send(src, shard, 4 + kind, i, (d, z, 1 - c))

    def relay_far(self):
        d, z, c = self.d, self.z, self.c
        for i in range(self.n_z):
            shard = (d ^ 3, self.z_from[i], c)
            self.arrived(shard, 3, i)
            self.send(self.slot(*shard), shard, 7, i, (d, z, 1 - c))

    def finish(self):
        self.own.wait()
        for i in range(self.n_z):
            for kind, flip in ((4, 0), (5, 1), (6, 2), (7, 3)):
                self.arrived((self.d ^ flip, self.z_from[i], 1 - self.c), kind, i)

    def drain(self):
        for copy in self.sent:
            copy.wait_send()


def pixels_forward(
    n_z,
    gathers,
    pix_width,
    chunk,
    counts,
    first_ref,
    *refs,
):
    refs = list(refs)
    rest_ref = refs.pop(0) if gathers else None
    pix_ref, lat_ref, gain_ref = refs[:3]
    refs = refs[3:]
    first_out = refs.pop(0) if gathers else None
    rest_out = refs.pop(0) if gathers else None
    xn_ref, pt_ref, peak_ref, qk_ref, q_ref, gains_ref, mean_ref, stat_ref = refs[:8]
    refs = refs[8:]
    (
        first_all,
        q_all,
        s_buf,
        px_own,
        px_tx,
        px_rx,
        st_tx,
        st_rx,
        px2_tx,
        px2_rx,
        st2_tx,
        st2_rx,
        fin_tx,
        fin_rx,
        col_sems,
        local_sems,
    ) = refs[:16]
    gather_sems = refs[16:]
    d, z, c = (lax.axis_index(name) for name in ALL)
    peers = [(d, lax.rem(z + i, n_z), c) for i in range(1, n_z)] + [(d, z, 1 - c)]
    if gathers:
        peers += [(d ^ 1, z, c), (d ^ 2, z, c)]
    meet(peers)
    if gathers:
        own = first_ref.shape[0]

        def first_place(rank):
            return first_all.at[pl.ds(pl.multiple_of(rank * own, own), own)]

        def rest_place(low, high):
            def place(rank):
                return rest_out.at[low:high, pl.ds(pl.multiple_of(rank * own, own), own)]

            return place

        first = Gather(first_ref, first_place, gather_sems[0], n_z)
        first.start(local_sems.at[0])
        rest = [
            Gather(
                rest_ref.at[low:high],
                rest_place(low, high),
                gather_sems[1 + index],
                n_z,
            )
            for index, (low, high) in enumerate(PIECES)
        ]
        for index, piece in enumerate(rest):
            piece.start(local_sems.at[1 + index])
    else:
        rest = []
        load = pltpu.make_async_copy(first_ref, first_all, local_sems.at[0])
        load.start()

    n_items, pix_dev, _ = pix_ref.shape
    lat_len, width = lat_ref.shape[1:]
    pad_width = xn_ref.shape[2]
    rows = tile_of(pix_dev, 16, 256)
    tiles = pix_dev // rows
    held = chunk * n_z

    def normalise(item):
        def body(t, _):
            at = pl.ds(pl.multiple_of(t * rows, rows), rows)
            values = pix_ref[item, at, :].astype(fl_type)
            centred = values - jnp.sum(values, -1, keepdims=True) * (1.0 / pix_width)
            var = jnp.sum(centred * centred, -1, keepdims=True) * (1.0 / pix_width)
            normal = centred * lax.rsqrt(var + 1e-05) * gain_ref[...]
            xn_ref[item, at, pad_width - 128 :] = jnp.zeros((rows, 128), bf_type)
            xn_ref[item, at, :pix_width] = normal.astype(bf_type)
            return 0

        lax.fori_loop(0, tiles, body, 0)

    normalise(0)
    if gathers:
        first.relay_z()
    for item in range(1, n_items):
        normalise(item)
    if gathers:
        first.relay_plane()
        rest[0].relay_z()
        first.relay_far()
        first.finish()
    else:
        load.wait()

    gain_at = round_up(pix_width, 8) - (pad_width - 128)
    tail = first_all[:, width + 2 * pad_width - 128 :].astype(fl_type).T
    gains_ref[...] = tail[gain_at : gain_at + 8]
    lat_rows = tile_of(lat_len, 16, 256)
    for item in range(n_items):

        def queries(t, _, item=item):
            at = pl.ds(pl.multiple_of(t * lat_rows, lat_rows), lat_rows)
            values = lat_ref[item, at, :].astype(fl_type)
            centred = values - jnp.mean(values, -1, keepdims=True)
            var = jnp.mean(centred * centred, -1, keepdims=True)
            normal = (centred * lax.rsqrt(var + 1e-05) * gains_ref[:1]).astype(bf_type)
            q_low = dot(normal, first_all[:, :width]).astype(bf_type)
            q_all[item, at, :] = q_low
            raw = dot(q_low, first_all[:, width : width + pad_width])
            qk_ref[item, at, :] = (raw * width**-0.5).astype(bf_type)
            return 0

        lax.fori_loop(0, lat_len // lat_rows, queries, 0)
    if gathers:
        rest[0].relay_plane()
        rest[1].relay_z()

    base = (z * 2 + c) * pix_dev
    for item in range(n_items):
        valid = counts[item] - base

        def score(t, most, item=item, valid=valid):
            at = pl.ds(pl.multiple_of(t * rows, rows), rows)
            values = dot(xn_ref[item, at, :], qk_ref[item], NT)
            place = lax.broadcasted_iota(jnp.int32, values.shape, 0) + t * rows
            values = jnp.where(place < valid, values, -1e30)
            s_buf[at, :] = values
            return jnp.maximum(most, jnp.max(values.reshape(rows // 8, 8, lat_len), 0))

        most = lax.fori_loop(0, tiles, score, jnp.full((8, lat_len), -1e30, fl_type))
        peak = jnp.max(most, 0, keepdims=True)

        def weigh(t, total, item=item, peak=peak):
            at = pl.ds(pl.multiple_of(t * rows, rows), rows)
            values = jnp.exp(s_buf[at, :] - peak)
            pt_ref[item, at, :] = values.astype(bf_type)
            return total + jnp.sum(values.reshape(rows // 8, 8, lat_len), 0)

        total = lax.fori_loop(0, tiles, weigh, jnp.zeros((8, lat_len), fl_type))
        total = jnp.sum(total, 0, keepdims=True)
        peak_ref[item] = jnp.broadcast_to(peak, (8, lat_len))
        st_tx[item, :8] = jnp.broadcast_to(peak, (8, lat_len))
        st_tx[item, 8:] = jnp.broadcast_to(total, (8, lat_len))
        part = dot(xn_ref[item], pt_ref[item], TN)
        px_own[item, : part.shape[0]] = part
        if held > part.shape[0]:
            px_own[item, part.shape[0] :] = jnp.zeros((px_own.shape[1] - part.shape[0], lat_len), fl_type)
        px_tx[item] = px_own[item, :held].astype(bf_type)

    def column_copy(src, dst, index, peer):
        return pltpu.make_async_remote_copy(
            src_ref=src,
            dst_ref=dst,
            send_sem=col_sems.at[0, index],
            recv_sem=col_sems.at[1, index],
            device_id=peer,
            device_id_type=MESH,
        )

    pair = [
        column_copy(px_tx.at[1 - c], px_rx, 0, (d, z, 1 - c)),
        column_copy(st_tx.at[1 - c], st_rx, 1, (d, z, 1 - c)),
    ]
    for copy in pair:
        copy.start()
    if gathers:
        rest[0].relay_far()
    q_ref[...] = q_all[c]
    for copy in pair:
        copy.wait()
    peak_own, peak_rx = st_tx[c, :1], st_rx[:1]
    peak = jnp.maximum(peak_own, peak_rx)
    scale_own, scale_rx = jnp.exp(peak_own - peak), jnp.exp(peak_rx - peak)
    st2_tx[:8] = jnp.broadcast_to(peak, (8, lat_len))
    st2_tx[8:] = jnp.broadcast_to(scale_own * st_tx[c, 8:9] + scale_rx * st_rx[8:9], (8, lat_len))
    both = px_own[c, :held] * scale_own + px_rx[...].astype(fl_type) * scale_rx
    px2_tx[...] = both.astype(bf_type).reshape(n_z, chunk, lat_len)
    copies = []
    for i in range(1, n_z):
        to = lax.rem(z + i, n_z)
        copies.append(column_copy(px2_tx.at[to], px2_rx.at[z], 2 * i, (d, to, c)))
        copies.append(column_copy(st2_tx, st2_rx.at[z], 2 * i + 1, (d, to, c)))
    for copy in copies:
        copy.start()
    for copy in copies:
        copy.wait()
    peak = st2_tx[:1]
    froms = [lax.rem(z + n_z - i, n_z) for i in range(1, n_z)]
    for other in froms:
        peak = jnp.maximum(peak, st2_rx[other, :1])
    scale = jnp.exp(st2_tx[:1] - peak)
    total = scale * st2_tx[8:9]
    mean = scale * px2_tx[z].astype(fl_type)
    for other in froms:
        scale = jnp.exp(st2_rx[other, :1] - peak)
        total = total + scale * st2_rx[other, 8:9]
        mean = mean + scale * px2_rx[other].astype(fl_type)
    stat_ref[:8] = jnp.broadcast_to(peak, (8, lat_len))
    stat_ref[8:] = jnp.broadcast_to(total, (8, lat_len))
    fin_tx[...] = (mean / total).astype(bf_type)
    copies = []
    for i in range(1, n_z):
        to = lax.rem(z + i, n_z)
        copies.append(column_copy(fin_tx, fin_rx.at[z], 2 * n_z + i, (d, to, c)))
    for copy in copies:
        copy.start()
    if gathers:
        rest[1].relay_plane()
        rest[2].relay_z()
    for copy in copies:
        copy.wait()
    for other in froms:
        mean_ref[pl.ds(other * chunk, chunk)] = fin_rx[other]
    mean_ref[pl.ds(z * chunk, chunk)] = fin_tx[...]
    if gathers:
        out = pltpu.make_async_copy(first_all, first_out, local_sems.at[4])
        out.start()
        rest[1].relay_far()
        rest[2].relay_plane()
        rest[2].relay_far()
        for piece in rest:
            piece.finish()
        for piece in [first] + rest:
            piece.drain()
        out.wait()


def forward_call(first_block, rest_block, pixels, latents, counts, input_gain, n_z, n_dev):
    gathers = rest_block is not None
    own, block_width = first_block.shape
    n_items, pix_dev, pix_width = pixels.shape
    lat_len, width = latents.shape[1:]
    pad_width = (block_width - width) // 2
    whole_rows = own * n_dev if gathers else own
    chunk = round_up(-(-pix_width // n_z), 16)
    held = chunk * n_z
    vmem, hbm = pl.BlockSpec(memory_space=pltpu.VMEM), pl.BlockSpec(memory_space=pl.ANY)
    shape = jax.ShapeDtypeStruct
    in_specs = [pl.BlockSpec(memory_space=pltpu.SMEM), hbm] + [hbm] * gathers + [vmem] * 3
    out_shape = [
        shape((n_items, pix_dev, pad_width), bf_type),
        shape((n_items, pix_dev, lat_len), bf_type),
        shape((n_items, 8, lat_len), fl_type),
        shape((n_items, lat_len, pad_width), bf_type),
        shape((lat_len, width), bf_type),
        shape((8, width), fl_type),
        shape((held, lat_len), bf_type),
        shape((16, lat_len), fl_type),
    ]
    out_specs = [vmem] * len(out_shape)
    if gathers:
        out_shape = [
            shape((whole_rows, block_width), bf_type),
            shape((rest_block.shape[0], whole_rows, width), bf_type),
        ] + out_shape
        out_specs = [hbm, hbm] + out_specs
    scratch = [
        pltpu.VMEM((whole_rows, block_width), bf_type),
        pltpu.VMEM((n_items, lat_len, width), bf_type),
        pltpu.VMEM((pix_dev, lat_len), fl_type),
        pltpu.VMEM((n_items, max(held, pad_width), lat_len), fl_type),
        pltpu.VMEM((n_items, held, lat_len), bf_type),
        pltpu.VMEM((held, lat_len), bf_type),
        pltpu.VMEM((n_items, 16, lat_len), fl_type),
        pltpu.VMEM((16, lat_len), fl_type),
        pltpu.VMEM((n_z, chunk, lat_len), bf_type),
        pltpu.VMEM((n_z, chunk, lat_len), bf_type),
        pltpu.VMEM((16, lat_len), fl_type),
        pltpu.VMEM((n_z, 16, lat_len), fl_type),
        pltpu.VMEM((chunk, lat_len), bf_type),
        pltpu.VMEM((n_z, chunk, lat_len), bf_type),
        pltpu.SemaphoreType.DMA((2, 3 * n_z)),
        pltpu.SemaphoreType.DMA((5,)),
    ]
    if gathers:
        scratch += [pltpu.SemaphoreType.DMA((2, 8, n_z))] * (1 + len(PIECES))
    args = [counts, first_block] + ([rest_block] if gathers else [])
    args += [pixels, latents, input_gain.reshape(1, pix_width)]
    outs = pl.pallas_call(
        functools.partial(pixels_forward, n_z, gathers, pix_width, chunk),
        out_shape=out_shape,
        in_specs=in_specs,
        out_specs=out_specs,
        scratch_shapes=scratch,
        compiler_params=pltpu.CompilerParams(
            collective_id=0, has_side_effects=True, vmem_limit_bytes=60 * 2**20
        ),
        name="pixels_forward",
    )(*args)
    return outs if gathers else [first_block, None] + list(outs)


def remote(src, dst, sems, index, peer):
    return pltpu.make_async_remote_copy(
        src_ref=src,
        dst_ref=dst,
        send_sem=sems.at[0, index],
        recv_sem=sems.at[1, index],
        device_id=peer,
        device_id_type=MESH,
    )


def backward(n_z, n_dp, pix_width, chunk, *refs):
    (
        gk_ref,
        stats_ref,
        early_ref,
        block_ref,
        xn_hbm,
        pt_hbm,
        peak_ref,
        qk_ref,
        pix_hbm,
        gain_ref,
        lat_hbm,
        first_hbm,
        gains_ref,
        q_hbm,
        cross_ref,
        k_one_ref,
        gterm_ref,
        mats_hbm,
        mfirst_hbm,
        msecond_hbm,
        kv_ref,
        kfirst_ref,
        ksecond_ref,
        ng_ref,
        gfirst_ref,
        gsecond_ref,
        block_out,
        lat_out,
        pix_out,
        mats_out,
        kv_out,
        gains_out,
        small_out,
        xn,
        pt,
        pix,
        lat,
        first,
        q_own,
        mats,
        mfirst,
        msecond,
        gk_rx,
        stats_rx,
        ds,
        pl_low,
        part_tx,
        part_own,
        part_rx,
        col_tx,
        col_rx,
        fin_tx,
        fin_rx,
        dst_full,
        early_own,
        early_rx,
        early_tx,
        early_sum,
        early_far,
        pix_buf,
        hat,
        inv,
        norm,
        dq,
        da,
        sel,
        lat_tx,
        late,
        late_rx,
        late_tx,
        late_own,
        late_far,
        small_tx,
        small_col,
        small_far_tx,
        small_far,
        input_acc,
        sems,
        loads,
    ) = refs
    d, z, c = (lax.axis_index(name) for name in ALL)
    oc = 1 - c
    n_items, pix_dev, pad_width = xn.shape
    lat_len, width = lat.shape[1:]
    own = kv_out.shape[2]
    far = [lax.rem(d + i, n_dp) for i in range(1, n_dp)]
    far_from = [lax.rem(d + n_dp - i, n_dp) for i in range(1, n_dp)]
    z_to = [lax.rem(z + i, n_z) for i in range(1, n_z)]
    z_from = [lax.rem(z + n_z - i, n_z) for i in range(1, n_z)]
    partner = (d, z, oc)
    column = [(i, 0) for i in range(1, n_z)] + [(i, 1) for i in range(n_z)]

    def in_column(i, j):
        return (d, lax.rem(z + i, n_z), lax.rem(c + j, 2))

    meet([in_column(i, j) for i, j in column] + [(to, z, c) for to in far])

    slot = iter(range(1000))

    def send(src, dst, peer):
        copy = remote(src, dst, sems, next(slot), peer)
        copy.start()
        return copy

    pair = [
        send(gk_ref, gk_rx, partner),
        send(stats_ref, stats_rx, partner),
    ]
    out_pair = send(block_ref.at[oc], block_out.at[c], partner)
    early_pair = send(early_ref.at[:, oc], early_rx, partner)
    load_slot = iter(range(1000))

    def load(src, dst):
        copy = pltpu.make_async_copy(src, dst, loads.at[next(load_slot)])
        copy.start()
        return copy

    l_xn = load(xn_hbm, xn)
    l_pt = load(pt_hbm, pt)
    l_pix = load(pix_hbm, pix)
    l_lat = load(lat_hbm.at[c], lat.at[0])
    l_first = load(first_hbm, first)
    l_q = load(q_hbm, q_own)
    l_early = load(early_ref.at[:, c], early_own)
    l_mats = [load(mats_hbm, mats), load(mfirst_hbm, mfirst), load(msecond_hbm, msecond)]
    block_out[c] = block_ref[c]

    rows = tile_of(pix_dev, 16, 256)
    tiles = pix_dev // rows
    held = chunk * n_z
    l_pt.wait()
    l_xn.wait()
    for copy in pair:
        copy.wait()

    def score_side(item, gk, stats):
        scale = jnp.exp(peak_ref[item, :1] - stats[0, :1]) / stats[1, :1]
        delta = stats[2, :1]

        def body(t, _):
            at = pl.ds(pl.multiple_of(t * rows, rows), rows)
            probs = pt[item, at, :].astype(fl_type) * scale
            grad_probs = dot(xn[item, at, :], gk[...], NT)
            ds[item, at, :] = (probs * (grad_probs - delta)).astype(bf_type)
            pl_low[item, at, :] = probs.astype(bf_type)
            return 0

        lax.fori_loop(0, tiles, body, 0)
        return dot(xn[item], ds[item], TN)

    part_tx[...] = score_side(oc, gk_rx, stats_rx)[: part_tx.shape[0]].astype(part_tx.dtype)
    px_pair = send(part_tx, part_rx, partner)
    part_own[...] = score_side(c, gk_ref, stats_ref)
    l_early.wait()
    early_pair.wait()

    n_rows = early_own.shape[1]

    def pair_sum(t, _):
        both = early_own[t].astype(fl_type) + early_rx[t].astype(fl_type)
        early_tx[t] = both.astype(early_tx.dtype)
        return 0

    lax.fori_loop(0, n_dp, pair_sum, 0)
    early_sum[...] = early_own[d].astype(fl_type) + early_rx[d].astype(fl_type)
    px_pair.wait()
    both = part_own[: part_rx.shape[0]] + part_rx[...].astype(fl_type)
    if held > both.shape[0]:
        both = jnp.concatenate([both, jnp.zeros((held - both.shape[0], lat_len), fl_type)], 0)
    col_tx[...] = both[:held].astype(col_tx.dtype).reshape(n_z, chunk, lat_len)
    col = [
        send(col_tx.at[to], col_rx.at[z], (d, to, c)) for to in z_to
    ]
    early_out = [send(early_tx.at[to], early_far.at[d], (to, z, c)) for to in far]

    l_pix.wait()
    input_acc[...] = jnp.zeros(input_acc.shape, fl_type)

    def pixel_side(item, gk):
        def body(t, _):
            at = pl.ds(pl.multiple_of(t * rows, rows), rows)
            grad = dot(ds[item, at, :], qk_ref[item]) + dot(pl_low[item, at, :], gk[...])
            grad = grad[:, :pix_width]
            values = pix[item, at, :].astype(fl_type)
            centred = values - jnp.sum(values, -1, keepdims=True) * (1.0 / pix_width)
            var = jnp.sum(centred * centred, -1, keepdims=True) * (1.0 / pix_width)
            scale = lax.rsqrt(var + 1e-05)
            normal = centred * scale
            input_acc[...] += jnp.sum((normal * grad).reshape(rows // 8, 8, pix_width), 0)
            grad = grad * gain_ref[...]
            mean = jnp.sum(grad, -1, keepdims=True) * (1.0 / pix_width)
            along = jnp.sum(grad * normal, -1, keepdims=True) * (1.0 / pix_width)
            pix_buf[item, at, :] = (grad - mean - normal * along) * scale
            return 0

        lax.fori_loop(0, tiles, body, 0)
        return load(pix_buf.at[item], pix_out.at[item])

    stores = [pixel_side(c, gk_ref)]

    for copy in col:
        copy.wait()
    mean = col_tx[z].astype(fl_type)
    for other in z_from:
        mean = mean + col_rx[other].astype(fl_type)
    fin_tx[...] = mean.astype(fin_tx.dtype)
    fin = [send(fin_tx, fin_rx.at[z], (d, to, c)) for to in z_to]

    stores.append(pixel_side(oc, gk_rx))

    l_lat.wait()
    l_first.wait()
    l_q.wait()
    pair_width = 2 * own
    n_cols = n_dp * pair_width
    wanted = lax.broadcasted_iota(jnp.int32, (width, n_cols), 1)
    wanted = (lax.div(wanted, pair_width) * n_z + z) * pair_width + lax.rem(wanted, pair_width)
    place = lax.broadcasted_iota(jnp.int32, (width, n_cols), 0)
    sel[...] = jnp.where(place == wanted, 1.0, 0.0).astype(bf_type)
    values = lat[0].astype(fl_type)
    centred = values - jnp.mean(values, -1, keepdims=True)
    scale = lax.rsqrt(jnp.mean(centred * centred, -1, keepdims=True) + 1e-05)
    hat[...] = centred * scale
    inv[...] = jnp.broadcast_to(scale, inv.shape)
    norm[...] = dot((hat[...] * gains_ref[:1]).astype(bf_type), sel[...]).astype(bf_type)

    for copy in fin:
        copy.wait()
    dst_full[...] = jnp.zeros(dst_full.shape, fl_type)
    for other in z_from:
        dst_full[pl.ds(other * chunk, chunk)] = fin_rx[other].astype(fl_type)
    dst_full[pl.ds(z * chunk, chunk)] = fin_tx[...].astype(fl_type)
    summed = dst_full[:pad_width].T.astype(bf_type)
    kt_zero = first[:, width : width + pad_width]
    dq[...] = (dot(summed, kt_zero, NT) * width**-0.5).astype(bf_type)
    da[...] = dot(dq[...], first[:, :width], NT)
    term_zero = dot(norm[...], dq[...], TN)
    q_sel = dot(q_own[...], sel[...]).astype(bf_type)
    term_k = dot(q_sel, summed, TN) * width**-0.5
    gain_at = round_up(pix_width, 8) - (pad_width - 128)
    gain_zero = jnp.sum(hat[...] * da[...], 0, keepdims=True)
    place = lax.broadcasted_iota(jnp.int32, (8, width), 0)
    gain_sums = jnp.where(place == 0, gain_zero, gterm_ref[...]).astype(bf_type)
    gain_cols = dot(gain_sums, sel[...])
    gain_cols = jnp.concatenate(
        [
            jnp.zeros((gain_at, n_cols), fl_type),
            gain_cols,
            jnp.zeros((128 - gain_at - 8, n_cols), fl_type),
        ],
        0,
    ).T
    late_shape = (n_dp, 2, own, -1)
    late[:, :, :, :width] = term_zero.astype(late.dtype).reshape(n_dp, 2, own, width)
    late[:, :, :, width : width + pad_width] = term_k.astype(late.dtype).reshape(
        n_dp, 2, own, pad_width
    )
    ones = k_one_ref[...]
    late[:, :, :, width + pad_width : width + 2 * pad_width - 128] = (
        ones[:, : pad_width - 128].astype(late.dtype).reshape(n_dp, 2, own, pad_width - 128)
    )
    late[:, :, :, width + 2 * pad_width - 128 :] = (
        (ones[:, pad_width - 128 :] + gain_cols).astype(late.dtype).reshape(n_dp, 2, own, 128)
    )
    late_pair = send(late.at[:, oc], late_rx, partner)

    z_share = lat_len // n_z
    at = pl.ds(pl.multiple_of(z * z_share, z_share), z_share)
    grad = da[at, :] * gains_ref[:1]
    normal = hat[at, :]
    mean = jnp.mean(grad, -1, keepdims=True)
    along = jnp.mean(grad * normal, -1, keepdims=True)
    lat_grad = cross_ref[...] + (grad - mean - normal * along) * inv[at, :1]
    lat_tx[...] = lat_grad.reshape(2, z_share // 2, width)
    lat_pair = send(lat_tx.at[oc], lat_out.at[c], partner)
    lat_out[c] = lat_tx[c]

    late_pair.wait()
    late_sum = late[:, c].astype(fl_type) + late_rx[...].astype(fl_type)
    late_tx[...] = late_sum.astype(late_tx.dtype)
    late_out = [send(late_tx.at[to], late_far.at[d], (to, z, c)) for to in far]
    late_own[...] = late[d, c].astype(fl_type) + late_rx[d].astype(fl_type)

    for copy in early_out:
        copy.wait()
    for copy in l_mats:
        copy.wait()
    lane = lax.broadcasted_iota(jnp.int32, (1, 128), 1)

    def norms(weight, gradient, first_mom, second):
        first_new = 0.9 * first_mom + 0.1 * gradient
        second_new = 0.999 * second + 0.001 * gradient * gradient
        update = (
            first_new / first_fix / (jnp.sqrt(second_new / second_fix) + 1e-06)
            + decay_rate * weight
        )
        return (weight * weight, update * update)

    def total(values):
        return jnp.sum(jnp.sum(values, 0, keepdims=True), 1, keepdims=True)

    def matrix(k, sums):
        at = pl.ds(pl.multiple_of((k - 1) * own, own), own)
        gradient = early_sum[at, :]
        for other in far_from:
            gradient = gradient + early_far[other, at, :].astype(fl_type)
        mats_out[k] = gradient
        w_sq, u_sq = norms(mats[k], gradient, mfirst[k], msecond[k])
        here = lane == k
        return (
            sums[0] + jnp.where(here, total(w_sq), 0.0),
            sums[1] + jnp.where(here, total(u_sq), 0.0),
        )

    zero = jnp.zeros((1, 128), fl_type)
    sums = lax.fori_loop(1, mats.shape[0], matrix, (zero, zero))

    for copy in late_out:
        copy.wait()
    for other in far_from:
        late_own[...] += late_far[other].astype(fl_type)
    mats_out[0] = late_own[:, :width]
    grads = [(mats[0], late_own[:, :width], mfirst[0], msecond[0], 0)]
    for k in range(2):
        cols = late_own[:, width + k * pad_width : width + (k + 1) * pad_width].T
        kv_out[k] = cols[:pix_width]
        grads.append((kv_ref[k], cols[:pix_width], kfirst_ref[k], ksecond_ref[k], 10 + k))
    at = pad_width - 128 + gain_at
    gain_grad = cols[at : at + 8]
    gains_out[...] = gain_grad[:4]
    w_sum, u_sum = sums
    for weight, gradient, first_mom, second, k in grads:
        w_sq, u_sq = norms(weight, gradient, first_mom, second)
        w_sum = w_sum + jnp.where(lane == k, total(w_sq), 0.0)
        u_sum = u_sum + jnp.where(lane == k, total(u_sq), 0.0)
    w_sq, u_sq = norms(ng_ref[...], gain_grad[:4], gfirst_ref[...], gsecond_ref[...])
    w_sq, u_sq = jnp.sum(w_sq, 1, keepdims=True), jnp.sum(u_sq, 1, keepdims=True)
    for k in range(4):
        w_sum = w_sum + jnp.where(lane == 12 + k, w_sq[k : k + 1], 0.0)
        u_sum = u_sum + jnp.where(lane == 12 + k, u_sq[k : k + 1], 0.0)
    small_tx[...] = jnp.zeros(small_tx.shape, fl_type)
    small_tx[0:1, :128] = w_sum
    small_tx[1:2, :128] = u_sum
    small_tx[2:3, :pix_width] = jnp.sum(input_acc[...], 0, keepdims=True)
    copies = [
        send(small_tx, small_col.at[n], in_column(i, j)) for n, (i, j) in enumerate(column)
    ]
    for copy in copies:
        copy.wait()
    all_sum = small_tx[...]
    for n in range(len(column)):
        all_sum = all_sum + small_col[n]
    small_far_tx[...] = all_sum
    copies = [
        send(small_far_tx, small_far.at[n], (to, z, c)) for n, to in enumerate(far)
    ]
    for copy in copies:
        copy.wait()
    for n in range(len(far)):
        all_sum = all_sum + small_far[n]
    small_out[...] = all_sum
    for copy in [out_pair, lat_pair] + stores:
        copy.wait()


def backward_call(n_z, n_dp, args):
    (gk, stats, early, block, xn, pt, _, qk, pixels, _, latents, first) = args[:12]
    mats, kv, gains = args[17], args[20], args[23]
    n_items, pix_dev, pix_width = pixels.shape
    lat_len, width = latents.shape[1:]
    pad_width = xn.shape[2]
    own = mats.shape[1]
    early_rows = early.shape[2]
    wire = early.dtype
    chunk = round_up(-(-pix_width // n_z), 16)
    held = chunk * n_z
    cut = min(held, pad_width)
    z_share = lat_len // n_z
    n_cols = n_dp * 2 * own
    vmem, hbm = pl.BlockSpec(memory_space=pltpu.VMEM), pl.BlockSpec(memory_space=pl.ANY)
    in_hbm = {"early": 2, "xn": 4, "pt": 5, "pix": 8, "lat": 10, "first": 11, "q": 13}
    places = set(in_hbm.values()) | {17, 18, 19}
    in_specs = [hbm if index in places else vmem for index in range(len(args))]
    shape, buf = jax.ShapeDtypeStruct, pltpu.VMEM
    out_shape = [
        shape((n_items, z_share // 2, width), bf_type),
        shape((n_items, z_share // 2, width), fl_type),
        shape(pixels.shape, fl_type),
        shape(mats.shape, fl_type),
        shape(kv.shape, fl_type),
        shape(gains.shape, fl_type),
        shape((8, pad_width), fl_type),
    ]
    out_specs = [vmem, vmem, hbm, vmem, vmem, vmem, vmem]
    late_width = width + 2 * pad_width
    scratch = [
        buf(xn.shape, bf_type),
        buf(pt.shape, bf_type),
        buf(pixels.shape, bf_type),
        buf((1, lat_len, width), bf_type),
        buf(first.shape, bf_type),
        buf((lat_len, width), bf_type),
        buf(mats.shape, fl_type),
        buf(mats.shape, fl_type),
        buf(mats.shape, fl_type),
        buf(gk.shape, bf_type),
        buf(stats.shape, fl_type),
        buf(pt.shape, bf_type),
        buf(pt.shape, bf_type),
        buf((cut, lat_len), bf_type),
        buf((pad_width, lat_len), fl_type),
        buf((cut, lat_len), bf_type),
        buf((n_z, chunk, lat_len), bf_type),
        buf((n_z, chunk, lat_len), bf_type),
        buf((chunk, lat_len), bf_type),
        buf((n_z, chunk, lat_len), bf_type),
        buf((max(held, pad_width), lat_len), fl_type),
        buf((n_dp, early_rows, width), wire),
        buf((n_dp, early_rows, width), wire),
        buf((n_dp, early_rows, width), wire),
        buf((early_rows, width), fl_type),
        buf((n_dp, early_rows, width), wire),
        buf(pixels.shape, fl_type),
        buf((lat_len, width), fl_type),
        buf((lat_len, 128), fl_type),
        buf((lat_len, n_cols), bf_type),
        buf((lat_len, width), bf_type),
        buf((lat_len, width), fl_type),
        buf((width, n_cols), bf_type),
        buf((2, z_share // 2, width), fl_type),
        buf((n_dp, 2, own, late_width), wire),
        buf((n_dp, own, late_width), wire),
        buf((n_dp, own, late_width), wire),
        buf((own, late_width), fl_type),
        buf((n_dp, own, late_width), wire),
        buf((8, pad_width), fl_type),
        buf((2 * n_z - 1, 8, pad_width), fl_type),
        buf((8, pad_width), fl_type),
        buf((n_dp - 1, 8, pad_width), fl_type),
        buf((8, pix_width), fl_type),
        pltpu.SemaphoreType.DMA((2, 20 + 6 * n_z + 3 * n_dp)),
        pltpu.SemaphoreType.DMA((16,)),
    ]
    return pl.pallas_call(
        functools.partial(backward, n_z, n_dp, pix_width, chunk),
        out_shape=out_shape,
        in_specs=in_specs,
        out_specs=out_specs,
        scratch_shapes=scratch,
        compiler_params=pltpu.CompilerParams(
            collective_id=1, has_side_effects=True, vmem_limit_bytes=60 * 2**20
        ),
        name="backward",
    )(*args)


def row_loop(total, body, rows=32):
    def step(t, _):
        body(pl.ds(pl.multiple_of(t * rows, rows), rows))
        return 0

    lax.fori_loop(0, total // rows, step, 0)


def tanh_gelu(values):
    factor, cubic = (2.0 / math.pi) ** 0.5, 0.044715
    square = values * values
    bent = jnp.tanh(factor * values * (1.0 + cubic * square))
    half = 0.5 * (1.0 + bent)
    slope = half + 0.5 * values * (1.0 - bent * bent) * factor * (1.0 + 3.0 * cubic * square)
    return values * half, slope


def choose(sel_ref, n_dp, n_z, pair_width):
    width, n_cols = sel_ref.shape
    z = lax.axis_index("z")
    wanted = lax.broadcasted_iota(jnp.int32, (width, n_cols), 1)
    wanted = (lax.div(wanted, pair_width) * n_z + z) * pair_width + lax.rem(wanted, pair_width)
    place = lax.broadcasted_iota(jnp.int32, (width, n_cols), 0)
    sel_ref[...] = jnp.where(place == wanted, 1.0, 0.0).astype(bf_type)


def latent_chain(n_z, n_dp, own, weight, kt_one, lat, cot, gains, mean_ref, stat_ref, outs, bufs):
    early_put, block_ref, gk_ref, stats_ref, cross_ref, k_one_ref, gterm_ref = outs
    (
        run, x_buf, hat_c, hat_s, hat_f, inv, slope_c, slope_f,
        att, norm_c, gelu_c, norm_s, q_s, k_s, v_s, mixed, norm_f, gelu_f, tmp, probs, sel, mean_pad,
    ) = bufs
    lat_len, width = lat.shape
    pad_width = kt_one.shape[1]
    head_dim = width // HEADS
    z = lax.axis_index("z")
    z_share = lat_len // n_z
    z_rows = pl.ds(pl.multiple_of(z * z_share, z_share), z_share)
    choose(sel, n_dp, n_z, 2 * own)

    def add_norm(base, gain, hat, which, normal):
        def body(at):
            values = base(at) + x_buf[at, :]
            run[at, :] = values
            centred = values - jnp.mean(values, -1, keepdims=True)
            scale = lax.rsqrt(jnp.mean(centred * centred, -1, keepdims=True) + 1e-05)
            standard_values = centred * scale
            hat[at, :] = standard_values
            inv[which, at, :] = jnp.broadcast_to(scale, (scale.shape[0], 128))
            normal[at, :] = (standard_values * gains[gain : gain + 1]).astype(bf_type)

        row_loop(lat_len, body)

    def activate(slope, low):
        def body(at):
            value, grad = tanh_gelu(x_buf[at, :])
            low[at, :] = value.astype(bf_type)
            slope[at, :] = grad

        row_loop(lat_len, body)

    def times_slope(slope, low):
        def body(at):
            low[at, :] = (x_buf[at, :] * slope[at, :]).astype(bf_type)

        row_loop(lat_len, body)

    def pull_norm(base, gain, hat, which, low):
        def body(t, sums):
            at = pl.ds(pl.multiple_of(t * 32, 32), 32)
            grad = x_buf[at, :]
            normal = hat[at, :]
            sums = sums + jnp.sum((normal * grad).reshape(4, 8, width), 0)
            grad = grad * gains[gain : gain + 1]
            mean = jnp.mean(grad, -1, keepdims=True)
            along = jnp.mean(grad * normal, -1, keepdims=True)
            value = base(at) + (grad - mean - normal * along) * inv[which, at, :1]
            run[at, :] = value
            low[at, :] = value.astype(bf_type)
            return sums

        sums = lax.fori_loop(0, lat_len // 32, body, jnp.zeros((8, width), fl_type))
        gterm_ref[gain : gain + 1] = jnp.sum(sums, 0, keepdims=True)

    def matrix_term(k, left, right):
        early_put(k, dot(dot(left[...], sel[...]).astype(bf_type), right[...], TN))

    def head(h):
        return pl.ds(pl.multiple_of(h * head_dim, head_dim), head_dim)

    head_scale = head_dim**-0.5
    gterm_ref[...] = jnp.zeros(gterm_ref.shape, fl_type)

    mean_pad[...] = jnp.zeros(mean_pad.shape, bf_type)
    held = min(mean_ref.shape[0], pad_width)
    mean_pad[:, :held] = mean_ref[:held].astype(fl_type).T.astype(bf_type)
    att[...] = dot(mean_pad[...], kt_one[...], NT).astype(bf_type)
    x_buf[...] = dot(att[...], weight(1)[...])
    add_norm(lambda at: lat[at, :].astype(fl_type), 1, hat_c, 0, norm_c)
    x_buf[...] = dot(norm_c[...], weight(2)[...])
    activate(slope_c, gelu_c)
    x_buf[...] = dot(gelu_c[...], weight(3)[...])
    add_norm(lambda at: run[at, :], 2, hat_s, 1, norm_s)
    q_s[...] = dot(norm_s[...], weight(4)[...]).astype(bf_type)
    k_s[...] = dot(norm_s[...], weight(5)[...]).astype(bf_type)
    v_s[...] = dot(norm_s[...], weight(6)[...]).astype(bf_type)

    def attend(h, _):
        at = head(h)
        scores = dot(k_s[:, at], q_s[:, at], NT) * head_scale
        weights = jnp.exp(scores - jnp.max(scores, 0, keepdims=True))
        weights = weights * (1.0 / jnp.sum(weights, 0, keepdims=True))
        low = weights.astype(bf_type)
        probs[h] = low
        mixed[:, at] = dot(low, v_s[:, at], TN).astype(bf_type)
        return 0

    lax.fori_loop(0, HEADS, attend, 0)
    x_buf[...] = dot(mixed[...], weight(7)[...])
    add_norm(lambda at: run[at, :], 3, hat_f, 2, norm_f)
    x_buf[...] = dot(norm_f[...], weight(8)[...])
    activate(slope_f, gelu_f)
    final = run[z_rows, :] + dot(gelu_f[z_rows, :], weight(9)[...])
    block_ref[...] = final.astype(bf_type).reshape(block_ref.shape)

    matrix_term(9, gelu_f, cot)
    x_buf[...] = dot(cot[...], weight(9)[...], NT)
    times_slope(slope_f, tmp)
    matrix_term(8, norm_f, tmp)
    x_buf[...] = dot(tmp[...], weight(8)[...], NT)
    pull_norm(lambda at: cot[at, :].astype(fl_type), 3, hat_f, 2, tmp)
    matrix_term(7, mixed, tmp)
    grad_mixed = gelu_f
    grad_mixed[...] = dot(tmp[...], weight(7)[...], NT).astype(bf_type)

    def attend_back(h, _):
        at = head(h)
        q_h, k_h, v_h, grad_h = q_s[:, at], k_s[:, at], v_s[:, at], grad_mixed[:, at]
        low = probs[h]
        weights = low.astype(fl_type)
        grad_weights = dot(v_h, grad_h, NT)
        along = jnp.sum(weights * grad_weights, 0, keepdims=True)
        grad_scores = (weights * (grad_weights - along)).astype(bf_type)
        q_s[:, at] = (dot(grad_scores, k_h, TN) * head_scale).astype(bf_type)
        k_s[:, at] = (dot(grad_scores, q_h) * head_scale).astype(bf_type)
        v_s[:, at] = dot(low, grad_h).astype(bf_type)
        return 0

    lax.fori_loop(0, HEADS, attend_back, 0)
    matrix_term(4, norm_s, q_s)
    matrix_term(5, norm_s, k_s)
    matrix_term(6, norm_s, v_s)
    x_buf[...] = dot(q_s[...], weight(4)[...], NT)
    x_buf[...] += dot(k_s[...], weight(5)[...], NT)
    x_buf[...] += dot(v_s[...], weight(6)[...], NT)
    pull_norm(lambda at: run[at, :], 2, hat_s, 1, tmp)
    matrix_term(3, gelu_c, tmp)
    x_buf[...] = dot(tmp[...], weight(3)[...], NT)
    times_slope(slope_c, tmp)
    matrix_term(2, norm_c, tmp)
    x_buf[...] = dot(tmp[...], weight(2)[...], NT)
    pull_norm(lambda at: run[at, :], 1, hat_c, 0, tmp)
    matrix_term(1, att, tmp)
    cross_ref[...] = run[z_rows, :]
    grad_att = gelu_f
    grad_att[...] = dot(tmp[...], weight(1)[...], NT).astype(bf_type)
    low = dot(grad_att[...], kt_one[...]).astype(bf_type)
    gk_ref[...] = low
    delta = jnp.sum(low.astype(fl_type).T[:held] * mean_ref[:held].astype(fl_type), 0, keepdims=True)
    stats_ref[0] = stat_ref[:8]
    stats_ref[1] = stat_ref[8:]
    stats_ref[2] = jnp.broadcast_to(delta, stats_ref.shape[1:])
    k_one_ref[...] = dot(dot(grad_att[...], sel[...]).astype(bf_type), mean_pad[...], TN)


def chain_bufs(lat_len, width, pad_width, n_cols):
    wide = pltpu.VMEM((lat_len, width), fl_type)
    low = pltpu.VMEM((lat_len, width), bf_type)
    return (
        [wide] * 5
        + [pltpu.VMEM((3, lat_len, 128), fl_type)]
        + [wide] * 2
        + [low] * 11
        + [
            pltpu.VMEM((HEADS, lat_len, lat_len), bf_type),
            pltpu.VMEM((width, n_cols), bf_type),
            pltpu.VMEM((lat_len, pad_width), bf_type),
        ]
    )


def chain_kernel(n_z, n_dp, own, *refs):
    mats_hbm, kt_one, lat, cot, gains, mean_ref, stat_ref = refs[:7]
    early_ref, block_ref, gk_ref, stats_ref, cross_ref, k_one_ref, gterm_ref = refs[7:14]
    mats, stage, loads, puts = refs[14:18]
    bufs = refs[18:]
    copies = [
        pltpu.make_async_copy(mats_hbm.at[k], mats.at[k], loads.at[k])
        for k in range(mats.shape[0])
    ]
    for copy in copies:
        copy.start()
    here = set()

    def weight(k):
        if k not in here:
            copies[k - 1].wait()
            here.add(k)
        return mats.at[k - 1]

    flying = {}

    def early_put(k, term):
        buffer = len(flying) % 2
        if len(flying) >= 2:
            flying[len(flying) - 2].wait()
        stage[buffer] = term.astype(stage.dtype).reshape(stage.shape[1:])
        copy = pltpu.make_async_copy(
            stage.at[buffer], early_ref.at[:, :, pl.ds((k - 1) * own, own)], puts.at[buffer]
        )
        copy.start()
        flying[len(flying)] = copy

    outs = (early_put, block_ref, gk_ref, stats_ref, cross_ref, k_one_ref, gterm_ref)
    latent_chain(n_z, n_dp, own, weight, kt_one, lat, cot, gains, mean_ref, stat_ref, outs, bufs)
    for index in range(max(0, len(flying) - 2), len(flying)):
        flying[index].wait()


def chain_call(n_z, n_dp, own, mats, kt_one, lat, cot, gains, mean_rows, stat_rows):
    lat_len, width = lat.shape
    pad_width = kt_one.shape[1]
    n_cols = n_dp * 2 * own
    wire = bf_type if own % 16 == 0 else fl_type
    vmem, hbm = pl.BlockSpec(memory_space=pltpu.VMEM), pl.BlockSpec(memory_space=pl.ANY)
    shape = jax.ShapeDtypeStruct
    z_share = lat_len // n_z
    return pl.pallas_call(
        functools.partial(chain_kernel, n_z, n_dp, own),
        out_shape=[
            shape((n_dp, 2, mats.shape[0] * own, width), wire),
            shape((2, z_share // 2, width), bf_type),
            shape((lat_len, pad_width), bf_type),
            shape((3, 8, lat_len), fl_type),
            shape((z_share, width), fl_type),
            shape((n_cols, pad_width), fl_type),
            shape((8, width), fl_type),
        ],
        in_specs=[hbm] + [vmem] * 6,
        out_specs=[hbm] + [vmem] * 6,
        scratch_shapes=[
            pltpu.VMEM(mats.shape, bf_type),
            pltpu.VMEM((2, n_dp, 2, own, width), wire),
            pltpu.SemaphoreType.DMA((mats.shape[0],)),
            pltpu.SemaphoreType.DMA((2,)),
        ]
        + chain_bufs(lat_len, width, pad_width, n_cols),
        compiler_params=pltpu.CompilerParams(vmem_limit_bytes=62 * 2**20),
        name="latent_chain",
    )(mats, kt_one, lat, cot, gains, mean_rows, stat_rows)


def moments(weight, gradient, first_mom, second, sum_axes):
    first_new = 0.9 * first_mom + 0.1 * gradient
    second_new = 0.999 * second + 0.001 * gradient * gradient
    update = (
        first_new / first_fix / (jnp.sqrt(second_new / second_fix) + 1e-06) + decay_rate * weight
    )
    return (
        first_new,
        second_new,
        update,
        jnp.sum(weight * weight, sum_axes),
        jnp.sum(update * update, sum_axes),
    )


def local(
    latents,
    pixels,
    pix_counts,
    cotangent,
    weight_mats,
    kv_weights,
    norm_gains,
    input_gain,
    mats_first,
    mats_second,
    kv_first,
    kv_second,
    gains_first,
    gains_second,
    input_first,
    input_second,
):
    item_count, lat_len, model_width = latents.shape
    pix_dev, pix_width = pixels.shape[1:]
    n_mats, own_width = weight_mats.shape[:2]
    n_dp, n_z = lax.axis_size("dp"), lax.axis_size("z")
    z_rank, core = lax.axis_index("z"), lax.axis_index("core")
    pad_width = round_up(round_up(pix_width, 8) + 8, 128)

    kv_cols = jnp.swapaxes(kv_weights, 1, 2)
    gain_at = round_up(pix_width, 8)
    first_block = jnp.concatenate(
        [
            weight_mats[0],
            jnp.pad(kv_cols[0], ((0, 0), (0, pad_width - pix_width))),
            jnp.pad(kv_cols[1], ((0, 0), (0, gain_at - pix_width))),
            norm_gains.T,
            jnp.zeros((own_width, pad_width - gain_at - 4), fl_type),
        ],
        axis=1,
    ).astype(bf_type)
    rest_block = weight_mats[1:].astype(bf_type)
    if own_width % 16:
        first_block = lax.all_gather(first_block, ALL, axis=0, tiled=True)
        w_rest = lax.all_gather(rest_block, ALL, axis=1, tiled=True)
        rest_block = None
    outs = forward_call(
        first_block, rest_block, pixels, latents, pix_counts, input_gain, n_z, n_dp * n_z * 2
    )
    first_all, gathered = outs[:2]
    xn, exp_low, peak_loc, qk_both, q_own, gain_rows, mean_rows, stat_rows = outs[2:]
    if gathered is not None:
        w_rest = gathered
    def own_of(both):
        return lax.dynamic_index_in_dim(both, core, 0, keepdims=False)

    early, block_rows, gk_own, stats_own, cross_rows, term_k_one, gain_sums = chain_call(
        n_z,
        n_dp,
        own_width,
        w_rest,
        first_all[:, model_width + pad_width :],
        own_of(latents),
        own_of(cotangent),
        gain_rows,
        mean_rows,
        stat_rows,
    )
    block_out, latent_grad, pixel_grad, wide_grad, kv_grad, gains_grad, small = backward_call(
        n_z,
        n_dp,
        (
            gk_own,
            stats_own,
            early,
            block_rows,
            xn,
            exp_low,
            peak_loc,
            qk_both,
            pixels,
            input_gain.reshape(1, pix_width),
            latents,
            first_all,
            gain_rows,
            q_own,
            cross_rows,
            term_k_one,
            gain_sums,
            weight_mats,
            mats_first,
            mats_second,
            kv_weights,
            kv_first,
            kv_second,
            norm_gains,
            gains_first,
            gains_second,
        ),
    )

    mats_first_new, mats_second_new, mats_update, mats_wsum, mats_usum = moments(
        weight_mats, wide_grad, mats_first, mats_second, (1, 2)
    )
    kv_first_new, kv_second_new, kv_update, kv_wsum, kv_usum = moments(
        kv_weights, kv_grad, kv_first, kv_second, (1, 2)
    )
    gains_first_new, gains_second_new, gains_update, gains_wsum, gains_usum = moments(
        norm_gains, gains_grad, gains_first, gains_second, (1,)
    )
    square_w, square_u, input_grad = small[0, :16], small[1, :16], small[2, :pix_width]
    trust = jnp.sqrt(square_w) / (jnp.sqrt(square_u) + 1e-06)
    mats_new = weight_mats - step_rate * trust[0:10, None, None] * mats_update
    kv_new = kv_weights - step_rate * trust[10:12, None, None] * kv_update
    gains_new = norm_gains - step_rate * trust[12:16, None] * gains_update
    input_first_new, input_second_new, input_update, input_wsum, input_usum = moments(
        input_gain, input_grad, input_first, input_second, (0,)
    )
    input_trust = jnp.sqrt(input_wsum) / (jnp.sqrt(input_usum) + 1e-06)
    input_new = input_gain - step_rate * input_trust * input_update
    return (
        block_out,
        latent_grad,
        pixel_grad,
        wide_grad,
        kv_grad,
        gains_grad,
        input_grad,
        mats_new,
        mats_first_new,
        mats_second_new,
        kv_new,
        kv_first_new,
        kv_second_new,
        gains_new,
        gains_first_new,
        gains_second_new,
        input_new,
        input_first_new,
        input_second_new,
    )


def solution(mesh):
    n_dp, n_rows = mesh.devices.shape
    split_mesh = Mesh(mesh.devices.reshape(n_dp, n_rows // 2, 2), ALL)
    rows = ("z", "core")
    items = P("dp", None, None)
    pix = P("dp", rows, None)
    mats = P(None, ALL, None)
    pairs = P(None, None, ALL)
    gains = P(None, ALL)
    in_specs = (
        items,
        pix,
        P("dp"),
        items,
        mats,
        pairs,
        gains,
        P(),
        mats,
        mats,
        pairs,
        pairs,
        gains,
        gains,
        P(),
        P(),
    )
    out_specs = (
        pix,
        pix,
        pix,
        mats,
        pairs,
        gains,
        P(),
        mats,
        mats,
        mats,
        pairs,
        pairs,
        pairs,
        gains,
        gains,
        gains,
        P(),
        P(),
        P(),
    )
    return jax.shard_map(
        local, mesh=split_mesh, in_specs=in_specs, out_specs=out_specs, check_vma=False
    )
```

```python
import functools
import math

import jax
import jax.numpy as jnp
from jax import lax
from jax.experimental import pallas as pl
from jax.experimental.pallas import tpu as pltpu
from jax.sharding import Mesh, PartitionSpec as P

HEADS = 8
first_fix = 1.0 - 0.9**10
second_fix = 1.0 - 0.999**10
step_rate = 0.25
decay_rate = 0.01
bf_type = jnp.bfloat16
fl_type = jnp.float32
ALL = ("dp", "z", "core")
NT = (((1,), (1,)), ((), ()))
TN = (((0,), (0,)), ((), ()))
NN = (((1,), (0,)), ((), ()))
MESH = pl.DeviceIdType.MESH
PIECES = ((0, 1), (1, 3), (3, 5), (5, 7), (7, 9))


def dot(left_side, right_side, dims=NN):
    return lax.dot_general(left_side, right_side, dims, preferred_element_type=fl_type)


def round_up(value, unit):
    return -(-value // unit) * unit


def tile_of(rows, unit, most):
    best = unit
    for size in range(unit, most + 1, unit):
        if rows % size == 0:
            best = size
    return best


def meet(peers):
    barrier = pltpu.get_barrier_semaphore()
    for peer in peers:
        pl.semaphore_signal(barrier, inc=1, device_id=peer, device_id_type=MESH)
    pl.semaphore_wait(barrier, len(peers))


def lane_parts(total, size, body):
    def step(t, _):
        body(pl.multiple_of(t * size, size), size)
        return 0

    lax.fori_loop(0, total // size, step, 0)
    if total % size:
        body(total - total % size, total % size)


def remote(src, dst, sems, index, peer):
    return pltpu.make_async_remote_copy(
        src_ref=src,
        dst_ref=dst,
        send_sem=sems.at[0, index],
        recv_sem=sems.at[1, index],
        device_id=peer,
        device_id_type=MESH,
    )


class Gather:
    def __init__(self, mine, place, sems, n_z):
        self.mine, self.place, self.sems, self.n_z = mine, place, sems, n_z
        self.d, self.z, self.c = (lax.axis_index(name) for name in ALL)
        self.z_from = [lax.rem(self.z + n_z - i, n_z) for i in range(n_z)]
        self.z_to = [lax.rem(self.z + i, n_z) for i in range(n_z)]
        self.sent = []

    def slot(self, d, z, c):
        return self.place((d * self.n_z + z) * 2 + c)

    def copy(self, src, shard, kind, index, peer):
        return pltpu.make_async_remote_copy(
            src_ref=src,
            dst_ref=self.slot(*shard),
            send_sem=self.sems.at[0, kind, index],
            recv_sem=self.sems.at[1, kind, index],
            device_id=peer,
            device_id_type=MESH,
        )

    def send(self, src, shard, kind, index, peer):
        copy = self.copy(src, shard, kind, index, peer)
        copy.start()
        self.sent.append((kind, index))

    def arrived(self, shard, kind, index):
        self.copy(self.mine, shard, kind, index, (self.d, self.z, 1 - self.c)).wait_recv()

    def start_z(self):
        d, z, c = self.d, self.z, self.c
        shard = (d, z, c)
        for i in range(1, self.n_z):
            self.send(self.mine, shard, 0, i, (d, self.z_to[i], c))

    def start_plane(self, local_sems, local):
        d, z, c = self.d, self.z, self.c
        shard = (d, z, c)
        self.send(self.mine, shard, 1, 0, (d ^ 1, z, c))
        self.send(self.mine, shard, 2, 0, (d ^ 2, z, c))
        self.send(self.mine, shard, 4, 0, (d, z, 1 - c))
        self.local_sems, self.local = local_sems, local
        self.place_own().start()

    def place_own(self):
        slot = self.slot(self.d, self.z, self.c)
        return pltpu.make_async_copy(self.mine, slot, self.local_sems.at[self.local])

    def relay_z(self):
        d, z, c = self.d, self.z, self.c
        for i in range(1, self.n_z):
            shard = (d, self.z_from[i], c)
            self.arrived(shard, 0, i)
            src = self.slot(*shard)
            self.send(src, shard, 1, i, (d ^ 1, z, c))
            self.send(src, shard, 2, i, (d ^ 2, z, c))
            self.send(src, shard, 4, i, (d, z, 1 - c))

    def relay_plane(self):
        d, z, c = self.d, self.z, self.c
        for i in range(self.n_z):
            for kind, flip, onward in ((1, 1, 2), (2, 2, 1)):
                shard = (d ^ flip, self.z_from[i], c)
                self.arrived(shard, kind, i)
                src = self.slot(*shard)
                if (i < self.n_z // 2) == (kind == 1):
                    self.send(src, shard, 3, i, (d ^ onward, z, c))
                self.send(src, shard, 4 + kind, i, (d, z, 1 - c))

    def relay_far(self):
        d, z, c = self.d, self.z, self.c
        for i in range(self.n_z):
            shard = (d ^ 3, self.z_from[i], c)
            self.arrived(shard, 3, i)
            self.send(self.slot(*shard), shard, 7, i, (d, z, 1 - c))

    def finish(self):
        self.place_own().wait()
        for i in range(self.n_z):
            for kind, flip in ((4, 0), (5, 1), (6, 2), (7, 3)):
                self.arrived((self.d ^ flip, self.z_from[i], 1 - self.c), kind, i)

    def drain(self):
        shard = (self.d, self.z, self.c)
        for kind, index in self.sent:
            self.copy(self.mine, shard, kind, index, (self.d, self.z, 1 - self.c)).wait_send()


def forward(n_z, n_dp, gathers, pix_width, chunk, *refs):
    (counts, first_hbm, kone_hbm, rest_hbm, pix_hbm, lat_hbm, cot_hbm, gain_col) = refs[:8]
    (
        first_out, xn_out, pt_out, q_out, early_out,
        peak_ref, qk_ref, gains_ref, block_ref, gk_ref, stats_ref, cross_ref, k_one_ref, gterm_ref,
    ) = refs[8:22]
    (
        first_all, kone_all, mats, px_tx, px_rx, st_tx, st_rx, px2_tx, px2_rx, st2_tx, st2_rx,
        fin_tx, mean_ref, stat_ref, col_sems, local_sems,
    ) = refs[22:38]
    gather_sems = refs[38:]
    d, z, c = (lax.axis_index(name) for name in ALL)
    n_items, lat_len, width = lat_hbm.shape
    pix_dev, pad_width = xn_out.shape[1:]
    n_mats = mats.shape[0]
    own = width // (n_dp * n_z * 2)
    held = chunk * n_z
    peers = [(d, lax.rem(z + i, n_z), c) for i in range(1, n_z)] + [(d, z, 1 - c)]
    if gathers:
        peers += [(d ^ 1, z, c), (d ^ 2, z, c)]
    meet(peers)
    local = iter(range(1000))

    def copy_here(src, dst):
        copy = pltpu.make_async_copy(src, dst, local_sems.at[next(local)])
        copy.start()
        return copy

    if gathers:

        def rows_of(ref):
            return lambda rank: ref.at[pl.ds(pl.multiple_of(rank * own, own), own)]

        def mats_of(low, high):
            return lambda rank: mats.at[low:high, pl.ds(pl.multiple_of(rank * own, own), own)]

        blocks = [(first_hbm, rows_of(first_all)), (kone_hbm, rows_of(kone_all))]
        blocks += [(rest_hbm.at[low:high], mats_of(low, high)) for low, high in PIECES]
        pieces = [
            Gather(mine, place, gather_sems[index], n_z)
            for index, (mine, place) in enumerate(blocks)
        ]
        first = pieces[0]
        rest = pieces[1:]
        first.start_z()
        first.start_plane(local_sems, next(local))

        steps, groups, finished_at = [], [], []
        for t in range(len(rest) + 3):
            if 0 <= t - 3 < len(rest):
                steps.append(rest[t - 3].finish)
                finished_at.append(len(steps))
            if 0 <= t - 2 < len(rest):
                steps.append(rest[t - 2].relay_far)
            if 0 <= t - 1 < len(rest):
                steps.append(rest[t - 1].relay_plane)
            if t < len(rest):
                steps.append(rest[t].relay_z)
            groups.append(len(steps))
        done = [0]

        def run_steps(upto):
            while done[0] < upto:
                steps[done[0]]()
                done[0] += 1

        def pump(count):
            run_steps(groups[min(count, len(groups)) - 1])

        def weight(k):
            piece = [i for i, (low, high) in enumerate(PIECES) if low <= k - 1 < high][0] + 1
            run_steps(finished_at[piece])
            return mats.at[k - 1]

        def kt_one():
            run_steps(finished_at[0])
            return kone_all

    else:
        loads = {0: copy_here(first_hbm, first_all), -1: copy_here(kone_hbm, kone_all)}
        for k in range(n_mats):
            loads[k + 1] = copy_here(rest_hbm.at[k], mats.at[k])

        def pump(upto):
            pass

        def weight(k):
            if k in loads:
                loads.pop(k).wait()
            return kone_all if k < 0 else mats.at[k - 1]

        def kt_one():
            return weight(-1)

    def column_copy(src, dst, index, peer):
        return remote(src, dst, col_sems, index, peer)

    def pixel_phase(pix, lat, xn, pt, s_buf, q_all, px_own, xt):
        l_pix, l_lat = copy_here(pix_hbm, pix), copy_here(lat_hbm, lat)
        xt[...] = jnp.zeros(xt.shape, fl_type)
        rows = tile_of(pix_dev, 16, 256)
        tiles = pix_dev // rows

        def normalise(item):
            def part(start, size):
                values = pix[:, item, pl.ds(start, size)].astype(fl_type)
                centred = values - jnp.sum(values, 0, keepdims=True) * (1.0 / pix_width)
                var = jnp.sum(centred * centred, 0, keepdims=True) * (1.0 / pix_width)
                xt[:pix_width, :size] = centred * lax.rsqrt(var + 1e-05) * gain_col[...]
                turned = round_up(size, 128)
                low = xt[:, :turned].T.astype(bf_type)
                xn[item, pl.ds(start, size), :] = low[:size]

            lane_parts(pix_dev, 256, part)

        l_pix.wait()
        normalise(0)
        if gathers:
            first.relay_z()
            for piece in rest[:-1]:
                piece.start_z()
        for item in range(1, n_items):
            normalise(item)
        xn_copy = copy_here(xn, xn_out)
        if gathers:
            first.relay_plane()
            for piece in rest:
                piece.start_plane(local_sems, next(local))
            first.relay_far()
            first.finish()
            pump(2)
        else:
            loads.pop(0).wait()
        first_copy = copy_here(first_all, first_out)
        l_lat.wait()
        gain_at = round_up(pix_width, 8) - (pad_width - 128)
        tail = first_all[:, width + pad_width - 128 :].astype(fl_type).T
        gains_ref[...] = tail[gain_at : gain_at + 8]
        lat_rows = tile_of(lat_len, 128, 256)
        for item in range(n_items):

            def queries(t, _, item=item):
                at = pl.ds(pl.multiple_of(t * lat_rows, lat_rows), lat_rows)
                values = lat[item, at, :].astype(fl_type)
                centred = values - jnp.mean(values, -1, keepdims=True)
                var = jnp.mean(centred * centred, -1, keepdims=True)
                normal = (centred * lax.rsqrt(var + 1e-05) * gains_ref[:1]).astype(bf_type)
                q_low = dot(normal, first_all[:, :width]).astype(bf_type)
                q_all[item, at, :] = q_low
                raw = dot(q_low, first_all[:, width : width + pad_width])
                qk_ref[item, :, at] = (raw * width**-0.5).T.astype(bf_type)
                return 0

            lax.fori_loop(0, lat_len // lat_rows, queries, 0)
        pump(3)
        q_copy = copy_here(q_all.at[c], q_out)

        base = (z * 2 + c) * pix_dev
        for item in range(n_items):
            valid = counts[item] - base

            def score(t, most, item=item, valid=valid):
                at = pl.ds(pl.multiple_of(t * rows, rows), rows)
                values = dot(xn[item, at, :], qk_ref[item])
                place = lax.broadcasted_iota(jnp.int32, values.shape, 0) + t * rows
                values = jnp.where(place < valid, values, -1e30)
                s_buf[at, :] = values
                return jnp.maximum(most, jnp.max(values.reshape(rows // 8, 8, lat_len), 0))

            most = lax.fori_loop(0, tiles, score, jnp.full((8, lat_len), -1e30, fl_type))
            peak = jnp.max(most, 0, keepdims=True)

            def weigh(t, total, item=item, peak=peak):
                at = pl.ds(pl.multiple_of(t * rows, rows), rows)
                values = jnp.exp(s_buf[at, :] - peak)
                pt[item, at, :] = values.astype(bf_type)
                return total + jnp.sum(values.reshape(rows // 8, 8, lat_len), 0)

            total = lax.fori_loop(0, tiles, weigh, jnp.zeros((8, lat_len), fl_type))
            total = jnp.sum(total, 0, keepdims=True)
            peak_ref[item] = jnp.broadcast_to(peak, (8, lat_len))
            st_tx[item, :8] = jnp.broadcast_to(peak, (8, lat_len))
            st_tx[item, 8:] = jnp.broadcast_to(total, (8, lat_len))
            part = dot(xn[item], pt[item], TN)
            px_own[item, : part.shape[0]] = part
            if held > part.shape[0]:
                px_own[item, part.shape[0] :] = jnp.zeros((held - part.shape[0], lat_len), fl_type)
            px_tx[item] = px_own[item, :held].astype(bf_type)
        pt_copy = copy_here(pt, pt_out)
        pair = [
            column_copy(px_tx.at[1 - c], px_rx, 0, (d, z, 1 - c)),
            column_copy(st_tx.at[1 - c], st_rx, 1, (d, z, 1 - c)),
        ]
        for copy in pair:
            copy.start()
        pump(4)
        for copy in pair:
            copy.wait()
        peak_own, peak_rx = st_tx[c, :1], st_rx[:1]
        peak = jnp.maximum(peak_own, peak_rx)
        scale_own, scale_rx = jnp.exp(peak_own - peak), jnp.exp(peak_rx - peak)
        st2_tx[:8] = jnp.broadcast_to(peak, (8, lat_len))
        st2_tx[8:] = jnp.broadcast_to(
            scale_own * st_tx[c, 8:9] + scale_rx * st_rx[8:9], (8, lat_len)
        )
        both = px_own[c, :held] * scale_own + px_rx[...].astype(fl_type) * scale_rx
        px2_tx[...] = both.astype(bf_type).reshape(n_z, chunk, lat_len)
        for copy in (xn_copy, first_copy, q_copy, pt_copy):
            copy.wait()

    pl.run_scoped(
        pixel_phase,
        pltpu.VMEM(pix_hbm.shape, bf_type),
        pltpu.VMEM(lat_hbm.shape, bf_type),
        pltpu.VMEM(xn_out.shape, bf_type),
        pltpu.VMEM(pt_out.shape, bf_type),
        pltpu.VMEM((pix_dev, lat_len), fl_type),
        pltpu.VMEM(lat_hbm.shape, bf_type),
        pltpu.VMEM((n_items, max(held, pad_width), lat_len), fl_type),
        pltpu.VMEM((pad_width, 256), fl_type),
    )

    copies = []
    for i in range(1, n_z):
        to = lax.rem(z + i, n_z)
        copies.append(column_copy(px2_tx.at[to], px2_rx.at[z], 2 * i, (d, to, c)))
        copies.append(column_copy(st2_tx, st2_rx.at[z], 2 * i + 1, (d, to, c)))
    for copy in copies:
        copy.start()
    if gathers:
        rest[-1].start_z()
    for copy in copies:
        copy.wait()
    peak = st2_tx[:1]
    froms = [lax.rem(z + n_z - i, n_z) for i in range(1, n_z)]
    for other in froms:
        peak = jnp.maximum(peak, st2_rx[other, :1])
    scale = jnp.exp(st2_tx[:1] - peak)
    total = scale * st2_tx[8:9]
    mean = scale * px2_tx[z].astype(fl_type)
    for other in froms:
        scale = jnp.exp(st2_rx[other, :1] - peak)
        total = total + scale * st2_rx[other, 8:9]
        mean = mean + scale * px2_rx[other].astype(fl_type)
    stat_ref[:8] = jnp.broadcast_to(peak, (8, lat_len))
    stat_ref[8:] = jnp.broadcast_to(total, (8, lat_len))
    fin_tx[...] = (mean / total).astype(bf_type)
    own_rows = pl.ds(pl.multiple_of(z * chunk, chunk), chunk)
    copies = []
    for i in range(1, n_z):
        to = lax.rem(z + i, n_z)
        copies.append(column_copy(fin_tx, mean_ref.at[own_rows], 2 * n_z + i, (d, to, c)))
    for copy in copies:
        copy.start()
    pump(5)
    for copy in copies:
        copy.wait()
    mean_ref[own_rows] = fin_tx[...]

    def chain_phase(lat, cot, stage, *bufs):
        l_lat, l_cot = copy_here(lat_hbm.at[c], lat), copy_here(cot_hbm.at[c], cot)
        flying = []
        put_sems = [next(local), next(local)]

        def early_put(k, term):
            buffer = len(flying) % 2
            if len(flying) >= 2:
                flying[-2].wait()
            stage[buffer] = term.astype(stage.dtype).reshape(stage.shape[1:])
            copy = pltpu.make_async_copy(
                stage.at[buffer],
                early_out.at[:, :, pl.ds((k - 1) * own, own)],
                local_sems.at[put_sems[buffer]],
            )
            copy.start()
            flying.append(copy)

        outs = (early_put, block_ref, gk_ref, stats_ref, cross_ref, k_one_ref, gterm_ref)
        l_lat.wait()
        l_cot.wait()
        latent_chain(
            n_z, n_dp, own, weight, kt_one, pump, lat, cot, gains_ref, mean_ref, stat_ref, outs, bufs
        )
        for copy in flying[-2:]:
            copy.wait()

    wire = early_out.dtype
    one_item = pltpu.VMEM((lat_len, width), bf_type)
    n_cols = n_dp * 2 * own
    pl.run_scoped(
        chain_phase,
        one_item,
        one_item,
        pltpu.VMEM((2, n_dp, 2, own, width), wire),
        *chain_bufs(lat_len, width, pad_width, n_cols),
    )
    if gathers:
        run_steps(len(steps))
        for piece in pieces:
            piece.drain()


def forward_call(n_z, n_dp, first, kone, rest, counts, pix_turned, latents, cotangent, gain_col):
    n_items, lat_len, width = latents.shape
    pix_width, _, pix_dev = pix_turned.shape
    own = width // (n_dp * n_z * 2)
    gathers = first.shape[0] == own
    n_mats = rest.shape[0]
    pad_width = kone.shape[1]
    wire = bf_type if own % 16 == 0 else fl_type
    chunk = round_up(-(-pix_width // n_z), 16)
    held = chunk * n_z
    z_share = lat_len // n_z
    n_cols = n_dp * 2 * own
    vmem, hbm = pl.BlockSpec(memory_space=pltpu.VMEM), pl.BlockSpec(memory_space=pl.ANY)
    shape, buf = jax.ShapeDtypeStruct, pltpu.VMEM
    out_shape = [
        shape((width, first.shape[1]), bf_type),
        shape((n_items, pix_dev, pad_width), bf_type),
        shape((n_items, pix_dev, lat_len), bf_type),
        shape((lat_len, width), bf_type),
        shape((n_dp, 2, n_mats * own, width), wire),
        shape((n_items, 8, lat_len), fl_type),
        shape((n_items, pad_width, lat_len), bf_type),
        shape((8, width), fl_type),
        shape((2, z_share // 2, width), bf_type),
        shape((pad_width, lat_len), bf_type),
        shape((3, 8, lat_len), fl_type),
        shape((z_share, width), fl_type),
        shape((n_cols, pad_width), fl_type),
        shape((8, width), fl_type),
    ]
    scratch = [
        buf((width, first.shape[1]), bf_type),
        buf((width, pad_width), bf_type),
        buf((n_mats, width, width), bf_type),
        buf((n_items, held, lat_len), bf_type),
        buf((held, lat_len), bf_type),
        buf((n_items, 16, lat_len), fl_type),
        buf((16, lat_len), fl_type),
        buf((n_z, chunk, lat_len), bf_type),
        buf((n_z, chunk, lat_len), bf_type),
        buf((16, lat_len), fl_type),
        buf((n_z, 16, lat_len), fl_type),
        buf((chunk, lat_len), bf_type),
        buf((held, lat_len), bf_type),
        buf((16, lat_len), fl_type),
        pltpu.SemaphoreType.DMA((2, 3 * n_z)),
        pltpu.SemaphoreType.DMA((32,)),
    ]
    if gathers:
        scratch += [pltpu.SemaphoreType.DMA((2, 8, n_z))] * (2 + len(PIECES))
    return pl.pallas_call(
        functools.partial(forward, n_z, n_dp, gathers, pix_width, chunk),
        out_shape=out_shape,
        in_specs=[pl.BlockSpec(memory_space=pltpu.SMEM)] + [hbm] * 6 + [vmem],
        out_specs=[hbm] * 5 + [vmem] * 9,
        scratch_shapes=scratch,
        compiler_params=pltpu.CompilerParams(
            collective_id=0, has_side_effects=True, vmem_limit_bytes=62 * 2**20
        ),
        name="forward",
    )(counts, first, kone, rest, pix_turned, latents, cotangent, gain_col)


def row_loop(total, body, rows=32):
    def step(t, _):
        body(pl.ds(pl.multiple_of(t * rows, rows), rows))
        return 0

    lax.fori_loop(0, total // rows, step, 0)


def tanh_gelu(values):
    factor, cubic = (2.0 / math.pi) ** 0.5, 0.044715
    square = values * values
    bent = jnp.tanh(factor * values * (1.0 + cubic * square))
    half = 0.5 * (1.0 + bent)
    slope = half + 0.5 * values * (1.0 - bent * bent) * factor * (1.0 + 3.0 * cubic * square)
    return values * half, slope


def choose(sel_ref, n_dp, n_z, pair_width):
    width, n_cols = sel_ref.shape
    z = lax.axis_index("z")
    wanted = lax.broadcasted_iota(jnp.int32, (width, n_cols), 1)
    wanted = (lax.div(wanted, pair_width) * n_z + z) * pair_width + lax.rem(wanted, pair_width)
    place = lax.broadcasted_iota(jnp.int32, (width, n_cols), 0)
    sel_ref[...] = jnp.where(place == wanted, 1.0, 0.0).astype(bf_type)


def latent_chain(n_z, n_dp, own, weight, kt_one, pump, lat, cot, gains, mean_ref, stat_ref, outs, bufs):
    early_put, block_ref, gk_ref, stats_ref, cross_ref, k_one_ref, gterm_ref = outs
    (
        run, x_buf, hat_c, hat_s, hat_f, inv, slope_c, slope_f,
        att, norm_c, gelu_c, norm_s, q_s, k_s, v_s, mixed, norm_f, gelu_f, probs, sel, mean_pad,
    ) = bufs
    lat_len, width = lat.shape
    pad_width = mean_pad.shape[1]
    head_dim = width // HEADS
    z = lax.axis_index("z")
    z_share = lat_len // n_z
    z_rows = pl.ds(pl.multiple_of(z * z_share, z_share), z_share)
    choose(sel, n_dp, n_z, 2 * own)
    tmp = lat

    def add_norm(base, gain, hat, which, normal):
        def body(at):
            values = base(at) + x_buf[at, :]
            run[at, :] = values
            centred = values - jnp.mean(values, -1, keepdims=True)
            scale = lax.rsqrt(jnp.mean(centred * centred, -1, keepdims=True) + 1e-05)
            standard_values = centred * scale
            hat[at, :] = standard_values
            inv[which, at, :] = jnp.broadcast_to(scale, (scale.shape[0], 128))
            normal[at, :] = (standard_values * gains[gain : gain + 1]).astype(bf_type)

        row_loop(lat_len, body)

    def activate(slope, low):
        def body(at):
            value, grad = tanh_gelu(x_buf[at, :])
            low[at, :] = value.astype(bf_type)
            slope[at, :] = grad

        row_loop(lat_len, body)

    def times_slope(slope, low):
        def body(at):
            low[at, :] = (x_buf[at, :] * slope[at, :]).astype(bf_type)

        row_loop(lat_len, body)

    def pull_norm(base, gain, hat, which, low):
        def body(t, sums):
            at = pl.ds(pl.multiple_of(t * 32, 32), 32)
            grad = x_buf[at, :]
            normal = hat[at, :]
            sums = sums + jnp.sum((normal * grad).reshape(4, 8, width), 0)
            grad = grad * gains[gain : gain + 1]
            mean = jnp.mean(grad, -1, keepdims=True)
            along = jnp.mean(grad * normal, -1, keepdims=True)
            value = base(at) + (grad - mean - normal * along) * inv[which, at, :1]
            run[at, :] = value
            low[at, :] = value.astype(bf_type)
            return sums

        sums = lax.fori_loop(0, lat_len // 32, body, jnp.zeros((8, width), fl_type))
        gterm_ref[gain : gain + 1] = jnp.sum(sums, 0, keepdims=True)

    def matrix_term(k, left, right):
        early_put(k, dot(dot(left[...], sel[...]).astype(bf_type), right[...], TN))

    def head(h):
        return pl.ds(pl.multiple_of(h * head_dim, head_dim), head_dim)

    head_scale = head_dim**-0.5
    gterm_ref[...] = jnp.zeros(gterm_ref.shape, fl_type)

    mean_pad[...] = jnp.zeros(mean_pad.shape, bf_type)
    held = min(mean_ref.shape[0], pad_width)
    mean_pad[:, :held] = mean_ref[:held].astype(fl_type).T.astype(bf_type)
    att[...] = dot(mean_pad[...], kt_one()[...], NT).astype(bf_type)
    x_buf[...] = dot(att[...], weight(1)[...])
    add_norm(lambda at: lat[at, :].astype(fl_type), 1, hat_c, 0, norm_c)
    pump(6)
    x_buf[...] = dot(norm_c[...], weight(2)[...])
    activate(slope_c, gelu_c)
    x_buf[...] = dot(gelu_c[...], weight(3)[...])
    add_norm(lambda at: run[at, :], 2, hat_s, 1, norm_s)
    pump(7)
    q_s[...] = dot(norm_s[...], weight(4)[...]).astype(bf_type)
    k_s[...] = dot(norm_s[...], weight(5)[...]).astype(bf_type)
    pump(8)
    v_s[...] = dot(norm_s[...], weight(6)[...]).astype(bf_type)

    def attend(h, _):
        at = head(h)
        scores = dot(k_s[:, at], q_s[:, at], NT) * head_scale
        weights = jnp.exp(scores - jnp.max(scores, 0, keepdims=True))
        weights = weights * (1.0 / jnp.sum(weights, 0, keepdims=True))
        low = weights.astype(bf_type)
        probs[h] = low
        mixed[:, at] = dot(low, v_s[:, at], TN).astype(bf_type)
        return 0

    lax.fori_loop(0, HEADS, attend, 0)
    pump(9)
    x_buf[...] = dot(mixed[...], weight(7)[...])
    add_norm(lambda at: run[at, :], 3, hat_f, 2, norm_f)
    x_buf[...] = dot(norm_f[...], weight(8)[...])
    activate(slope_f, gelu_f)
    final = run[z_rows, :] + dot(gelu_f[z_rows, :], weight(9)[...])
    block_ref[...] = final.astype(bf_type).reshape(block_ref.shape)

    matrix_term(9, gelu_f, cot)
    x_buf[...] = dot(cot[...], weight(9)[...], NT)
    times_slope(slope_f, tmp)
    matrix_term(8, norm_f, tmp)
    x_buf[...] = dot(tmp[...], weight(8)[...], NT)
    pull_norm(lambda at: cot[at, :].astype(fl_type), 3, hat_f, 2, tmp)
    matrix_term(7, mixed, tmp)
    grad_mixed = gelu_f
    grad_mixed[...] = dot(tmp[...], weight(7)[...], NT).astype(bf_type)

    def attend_back(h, _):
        at = head(h)
        q_h, k_h, v_h, grad_h = q_s[:, at], k_s[:, at], v_s[:, at], grad_mixed[:, at]
        low = probs[h]
        weights = low.astype(fl_type)
        grad_weights = dot(v_h, grad_h, NT)
        along = jnp.sum(weights * grad_weights, 0, keepdims=True)
        grad_scores = (weights * (grad_weights - along)).astype(bf_type)
        q_s[:, at] = (dot(grad_scores, k_h, TN) * head_scale).astype(bf_type)
        k_s[:, at] = (dot(grad_scores, q_h) * head_scale).astype(bf_type)
        v_s[:, at] = dot(low, grad_h).astype(bf_type)
        return 0

    lax.fori_loop(0, HEADS, attend_back, 0)
    matrix_term(4, norm_s, q_s)
    matrix_term(5, norm_s, k_s)
    matrix_term(6, norm_s, v_s)
    x_buf[...] = dot(q_s[...], weight(4)[...], NT)
    x_buf[...] += dot(k_s[...], weight(5)[...], NT)
    x_buf[...] += dot(v_s[...], weight(6)[...], NT)
    pull_norm(lambda at: run[at, :], 2, hat_s, 1, tmp)
    matrix_term(3, gelu_c, tmp)
    x_buf[...] = dot(tmp[...], weight(3)[...], NT)
    times_slope(slope_c, tmp)
    matrix_term(2, norm_c, tmp)
    x_buf[...] = dot(tmp[...], weight(2)[...], NT)
    pull_norm(lambda at: run[at, :], 1, hat_c, 0, tmp)
    matrix_term(1, att, tmp)
    cross_ref[...] = run[z_rows, :]
    grad_att = gelu_f
    grad_att[...] = dot(tmp[...], weight(1)[...], NT).astype(bf_type)
    low = dot(grad_att[...], kt_one()[...]).T.astype(bf_type)
    gk_ref[...] = low
    delta = jnp.sum(low[:held].astype(fl_type) * mean_ref[:held].astype(fl_type), 0, keepdims=True)
    stats_ref[0] = stat_ref[:8]
    stats_ref[1] = stat_ref[8:]
    stats_ref[2] = jnp.broadcast_to(delta, stats_ref.shape[1:])
    k_one_ref[...] = dot(dot(grad_att[...], sel[...]).astype(bf_type), mean_pad[...], TN)


def chain_bufs(lat_len, width, pad_width, n_cols):
    wide = pltpu.VMEM((lat_len, width), fl_type)
    low = pltpu.VMEM((lat_len, width), bf_type)
    return (
        [wide] * 5
        + [pltpu.VMEM((3, lat_len, 128), fl_type)]
        + [wide] * 2
        + [low] * 10
        + [
            pltpu.VMEM((HEADS, lat_len, lat_len), bf_type),
            pltpu.VMEM((width, n_cols), bf_type),
            pltpu.VMEM((lat_len, pad_width), bf_type),
        ]
    )


def backward(n_z, n_dp, pix_width, chunk, *refs):
    (
        gk_ref,
        stats_ref,
        early_ref,
        block_ref,
        xn_hbm,
        pt_hbm,
        peak_ref,
        qk_ref,
        pix_hbm,
        gain_ref,
        lat_hbm,
        first_hbm,
        gains_ref,
        q_hbm,
        cross_ref,
        k_one_ref,
        gterm_ref,
        mats_hbm,
        mfirst_hbm,
        msecond_hbm,
        kv_ref,
        kfirst_ref,
        ksecond_ref,
        ng_ref,
        gfirst_ref,
        gsecond_ref,
        block_out,
        lat_out,
        pix_out,
        mats_out,
        kv_out,
        gains_out,
        small_out,
        xn,
        pt,
        pix,
        lat,
        first,
        q_own,
        mats,
        mfirst,
        msecond,
        gk_all,
        stats_rx,
        ds,
        pl_low,
        part_tx,
        part_own,
        part_rx,
        col_tx,
        col_rx,
        fin_tx,
        fin_rx,
        dst_full,
        early_own,
        early_rx,
        early_tx,
        early_sum,
        early_far,
        pix_buf,
        hat,
        inv,
        norm,
        dq,
        da,
        sel,
        lat_tx,
        late,
        late_rx,
        late_tx,
        late_own,
        late_far,
        small_tx,
        small_col,
        small_far_tx,
        small_far,
        input_acc,
        sems,
        loads,
    ) = refs
    d, z, c = (lax.axis_index(name) for name in ALL)
    oc = 1 - c
    n_items, pix_dev, pad_width = xn.shape
    gain_col = gain_ref
    lat_len, width = lat.shape[1:]
    own = kv_out.shape[1]
    far = [lax.rem(d + i, n_dp) for i in range(1, n_dp)]
    far_from = [lax.rem(d + n_dp - i, n_dp) for i in range(1, n_dp)]
    z_to = [lax.rem(z + i, n_z) for i in range(1, n_z)]
    z_from = [lax.rem(z + n_z - i, n_z) for i in range(1, n_z)]
    partner = (d, z, oc)
    column = [(i, 0) for i in range(1, n_z)] + [(i, 1) for i in range(n_z)]

    def in_column(i, j):
        return (d, lax.rem(z + i, n_z), lax.rem(c + j, 2))

    meet([in_column(i, j) for i, j in column] + [(to, z, c) for to in far])

    slot = iter(range(1000))

    def send(src, dst, peer):
        copy = remote(src, dst, sems, next(slot), peer)
        copy.start()
        return copy

    pair = [
        send(gk_ref, gk_all.at[c], partner),
        send(stats_ref, stats_rx, partner),
    ]
    out_pair = send(block_ref.at[oc], block_out.at[c], partner)
    early_pair = send(early_ref.at[:, oc], early_rx, partner)
    load_slot = iter(range(1000))

    def load(src, dst):
        copy = pltpu.make_async_copy(src, dst, loads.at[next(load_slot)])
        copy.start()
        return copy

    l_xn = load(xn_hbm, xn)
    l_pt = load(pt_hbm, pt)
    l_pix = load(pix_hbm, pix)
    l_lat = load(lat_hbm.at[c], lat.at[0])
    l_first = load(first_hbm, first)
    l_q = load(q_hbm, q_own)
    l_early = load(early_ref.at[:, c], early_own)
    l_mats = [load(mats_hbm, mats), load(mfirst_hbm, mfirst), load(msecond_hbm, msecond)]
    block_out[c] = block_ref[c]
    gk_all[c] = gk_ref[...]

    rows = tile_of(pix_dev, 16, 256)
    tiles = pix_dev // rows
    held = chunk * n_z
    l_pt.wait()
    l_xn.wait()
    for copy in pair:
        copy.wait()

    def score_side(item, gk, stats):
        scale = jnp.exp(peak_ref[item, :1] - stats[0, :1]) / stats[1, :1]
        delta = stats[2, :1]

        def body(t, _):
            at = pl.ds(pl.multiple_of(t * rows, rows), rows)
            probs = pt[item, at, :].astype(fl_type) * scale
            grad_probs = dot(xn[item, at, :], gk[...])
            ds[item, at, :] = (probs * (grad_probs - delta)).astype(bf_type)
            pl_low[item, at, :] = probs.astype(bf_type)
            return 0

        lax.fori_loop(0, tiles, body, 0)
        return dot(xn[item], ds[item], TN)

    part_tx[...] = score_side(oc, gk_all.at[oc], stats_rx)[: part_tx.shape[0]].astype(part_tx.dtype)
    px_pair = send(part_tx, part_rx, partner)
    part_own[...] = score_side(c, gk_ref, stats_ref)
    l_early.wait()
    early_pair.wait()

    n_rows = early_own.shape[1]

    def pair_sum(t, _):
        both = early_own[t].astype(fl_type) + early_rx[t].astype(fl_type)
        early_tx[t] = both.astype(early_tx.dtype)
        return 0

    lax.fori_loop(0, n_dp, pair_sum, 0)
    early_sum[...] = early_own[d].astype(fl_type) + early_rx[d].astype(fl_type)
    px_pair.wait()
    both = part_own[: part_rx.shape[0]] + part_rx[...].astype(fl_type)
    if held > both.shape[0]:
        both = jnp.concatenate([both, jnp.zeros((held - both.shape[0], lat_len), fl_type)], 0)
    col_tx[...] = both[:held].astype(col_tx.dtype).reshape(n_z, chunk, lat_len)
    col = [
        send(col_tx.at[to], col_rx.at[z], (d, to, c)) for to in z_to
    ]
    early_out = [send(early_tx.at[to], early_far.at[d], (to, z, c)) for to in far]

    l_pix.wait()
    input_acc[...] = jnp.zeros(input_acc.shape, fl_type)

    def pixel_side(item, gk):
        def part(start, size):
            at = pl.ds(start, size)
            grad = dot(qk_ref[item], ds[item, at, :], NT) + dot(gk[...], pl_low[item, at, :], NT)
            grad = grad[:pix_width]
            values = pix[:, item, at].astype(fl_type)
            centred = values - jnp.sum(values, 0, keepdims=True) * (1.0 / pix_width)
            var = jnp.sum(centred * centred, 0, keepdims=True) * (1.0 / pix_width)
            scale = lax.rsqrt(var + 1e-05)
            normal = centred * scale
            along = normal * grad
            for low in range(0, size, 128):
                high = min(low + 128, size)
                input_acc[:pix_width, : high - low] += along[:, low:high]
            grad = grad * gain_col[...]
            mean = jnp.sum(grad, 0, keepdims=True) * (1.0 / pix_width)
            along = jnp.sum(grad * normal, 0, keepdims=True) * (1.0 / pix_width)
            pix_buf[:, item, at] = (grad - mean - normal * along) * scale

        lane_parts(pix_dev, 256, part)

    pixel_side(0, gk_all.at[0])

    for copy in col:
        copy.wait()
    mean = col_tx[z].astype(fl_type)
    for other in z_from:
        mean = mean + col_rx[other].astype(fl_type)
    fin_tx[...] = mean.astype(fin_tx.dtype)
    fin = [send(fin_tx, fin_rx.at[z], (d, to, c)) for to in z_to]

    pixel_side(1, gk_all.at[1])
    stores = [load(pix_buf, pix_out)]

    l_lat.wait()
    l_first.wait()
    l_q.wait()
    pair_width = 2 * own
    n_cols = n_dp * pair_width
    wanted = lax.broadcasted_iota(jnp.int32, (width, n_cols), 1)
    wanted = (lax.div(wanted, pair_width) * n_z + z) * pair_width + lax.rem(wanted, pair_width)
    place = lax.broadcasted_iota(jnp.int32, (width, n_cols), 0)
    sel[...] = jnp.where(place == wanted, 1.0, 0.0).astype(bf_type)
    values = lat[0].astype(fl_type)
    centred = values - jnp.mean(values, -1, keepdims=True)
    scale = lax.rsqrt(jnp.mean(centred * centred, -1, keepdims=True) + 1e-05)
    hat[...] = centred * scale
    inv[...] = jnp.broadcast_to(scale, inv.shape)
    norm[...] = dot((hat[...] * gains_ref[:1]).astype(bf_type), sel[...]).astype(bf_type)

    for copy in fin:
        copy.wait()
    dst_full[...] = jnp.zeros(dst_full.shape, fl_type)
    for other in z_from:
        dst_full[pl.ds(other * chunk, chunk)] = fin_rx[other].astype(fl_type)
    dst_full[pl.ds(z * chunk, chunk)] = fin_tx[...].astype(fl_type)
    summed = dst_full[:pad_width].T.astype(bf_type)
    kt_zero = first[:, width : width + pad_width]
    dq[...] = (dot(summed, kt_zero, NT) * width**-0.5).astype(bf_type)
    da[...] = dot(dq[...], first[:, :width], NT)
    term_zero = dot(norm[...], dq[...], TN)
    q_sel = dot(q_own[...], sel[...]).astype(bf_type)
    term_k = dot(q_sel, summed, TN) * width**-0.5
    gain_at = round_up(pix_width, 8) - (pad_width - 128)
    gain_zero = jnp.sum(hat[...] * da[...], 0, keepdims=True)
    place = lax.broadcasted_iota(jnp.int32, (8, width), 0)
    gain_sums = jnp.where(place == 0, gain_zero, gterm_ref[...]).astype(bf_type)
    gain_cols = dot(gain_sums, sel[...])
    gain_cols = jnp.concatenate(
        [
            jnp.zeros((gain_at, n_cols), fl_type),
            gain_cols,
            jnp.zeros((128 - gain_at - 8, n_cols), fl_type),
        ],
        0,
    ).T
    late[:, :, :, :width] = term_zero.astype(late.dtype).reshape(n_dp, 2, own, width)
    late[:, :, :, width : width + pad_width] = term_k.astype(late.dtype).reshape(
        n_dp, 2, own, pad_width
    )
    ones = k_one_ref[...]
    late[:, :, :, width + pad_width : width + 2 * pad_width - 128] = (
        ones[:, : pad_width - 128].astype(late.dtype).reshape(n_dp, 2, own, pad_width - 128)
    )
    late[:, :, :, width + 2 * pad_width - 128 :] = (
        (ones[:, pad_width - 128 :] + gain_cols).astype(late.dtype).reshape(n_dp, 2, own, 128)
    )
    late_pair = send(late.at[:, oc], late_rx, partner)

    z_share = lat_len // n_z
    at = pl.ds(pl.multiple_of(z * z_share, z_share), z_share)
    grad = da[at, :] * gains_ref[:1]
    normal = hat[at, :]
    mean = jnp.mean(grad, -1, keepdims=True)
    along = jnp.mean(grad * normal, -1, keepdims=True)
    lat_grad = cross_ref[...] + (grad - mean - normal * along) * inv[at, :1]
    lat_tx[...] = lat_grad.reshape(2, z_share // 2, width)
    lat_pair = send(lat_tx.at[oc], lat_out.at[c], partner)
    lat_out[c] = lat_tx[c]

    late_pair.wait()
    late_sum = late[:, c].astype(fl_type) + late_rx[...].astype(fl_type)
    late_tx[...] = late_sum.astype(late_tx.dtype)
    late_out = [send(late_tx.at[to], late_far.at[d], (to, z, c)) for to in far]
    late_own[...] = late[d, c].astype(fl_type) + late_rx[d].astype(fl_type)

    for copy in early_out:
        copy.wait()
    for copy in l_mats:
        copy.wait()
    lane = lax.broadcasted_iota(jnp.int32, (1, 128), 1)

    def norms(weight, gradient, first_mom, second):
        first_new = 0.9 * first_mom + 0.1 * gradient
        second_new = 0.999 * second + 0.001 * gradient * gradient
        update = (
            first_new / first_fix / (jnp.sqrt(second_new / second_fix) + 1e-06)
            + decay_rate * weight
        )
        return (weight * weight, update * update)

    def total(values):
        return jnp.sum(jnp.sum(values, 0, keepdims=True), 1, keepdims=True)

    def matrix(k, sums):
        at = pl.ds(pl.multiple_of((k - 1) * own, own), own)
        gradient = early_sum[at, :]
        for other in far_from:
            gradient = gradient + early_far[other, at, :].astype(fl_type)
        mats_out[k] = gradient
        w_sq, u_sq = norms(mats[k], gradient, mfirst[k], msecond[k])
        here = lane == k
        return (
            sums[0] + jnp.where(here, total(w_sq), 0.0),
            sums[1] + jnp.where(here, total(u_sq), 0.0),
        )

    zero = jnp.zeros((1, 128), fl_type)
    sums = lax.fori_loop(1, mats.shape[0], matrix, (zero, zero))

    for copy in late_out:
        copy.wait()
    for other in far_from:
        late_own[...] += late_far[other].astype(fl_type)
    mats_out[0] = late_own[:, :width]
    grads = [(mats[0], late_own[:, :width], mfirst[0], msecond[0], 0)]
    for k in range(2):
        cols = late_own[:, width + k * pad_width : width + k * pad_width + pix_width]
        kv_out[k] = cols
        grads.append((kv_ref[k], cols, kfirst_ref[k], ksecond_ref[k], 10 + k))
    gain_grad = late_own[:, width + 2 * pad_width - 128 :].T[gain_at : gain_at + 8]
    gains_out[...] = gain_grad[:4]
    w_sum, u_sum = sums
    for weight, gradient, first_mom, second, k in grads:
        w_sq, u_sq = norms(weight, gradient, first_mom, second)
        w_sum = w_sum + jnp.where(lane == k, total(w_sq), 0.0)
        u_sum = u_sum + jnp.where(lane == k, total(u_sq), 0.0)
    w_sq, u_sq = norms(ng_ref[...], gain_grad[:4], gfirst_ref[...], gsecond_ref[...])
    w_sq, u_sq = jnp.sum(w_sq, 1, keepdims=True), jnp.sum(u_sq, 1, keepdims=True)
    for k in range(4):
        w_sum = w_sum + jnp.where(lane == 12 + k, w_sq[k : k + 1], 0.0)
        u_sum = u_sum + jnp.where(lane == 12 + k, u_sq[k : k + 1], 0.0)
    small_tx[...] = jnp.zeros(small_tx.shape, fl_type)
    small_tx[0:1, :128] = w_sum
    small_tx[1:2, :128] = u_sum
    small_tx[2:3, :] = jnp.sum(input_acc[...].T, 0, keepdims=True)
    copies = [
        send(small_tx, small_col.at[n], in_column(i, j)) for n, (i, j) in enumerate(column)
    ]
    for copy in copies:
        copy.wait()
    all_sum = small_tx[...]
    for n in range(len(column)):
        all_sum = all_sum + small_col[n]
    small_far_tx[...] = all_sum
    copies = [
        send(small_far_tx, small_far.at[n], (to, z, c)) for n, to in enumerate(far)
    ]
    for copy in copies:
        copy.wait()
    for n in range(len(far)):
        all_sum = all_sum + small_far[n]
    small_out[...] = all_sum
    for copy in [out_pair, lat_pair] + stores:
        copy.wait()


def backward_call(n_z, n_dp, args):
    (gk, stats, early, _, xn, pt, _, _, pixels, _, latents, first) = args[:12]
    mats, kv, gains = args[17], args[20], args[23]
    pix_width = pixels.shape[0]
    n_items, lat_len, width = latents.shape
    own = mats.shape[1]
    pad_width = xn.shape[2]
    early_rows = early.shape[2]
    wire = early.dtype
    chunk = round_up(-(-pix_width // n_z), 16)
    held = chunk * n_z
    cut = min(held, pad_width)
    z_share = lat_len // n_z
    n_cols = n_dp * 2 * own
    vmem, hbm = pl.BlockSpec(memory_space=pltpu.VMEM), pl.BlockSpec(memory_space=pl.ANY)
    places = {2, 4, 5, 8, 10, 11, 13, 17, 18, 19}
    in_specs = [hbm if index in places else vmem for index in range(len(args))]
    shape, buf = jax.ShapeDtypeStruct, pltpu.VMEM
    out_shape = [
        shape((n_items, z_share // 2, width), bf_type),
        shape((n_items, z_share // 2, width), fl_type),
        shape(pixels.shape, fl_type),
        shape(mats.shape, fl_type),
        shape(kv.shape, fl_type),
        shape(gains.shape, fl_type),
        shape((8, pad_width), fl_type),
    ]
    out_specs = [vmem, vmem, hbm, vmem, vmem, vmem, vmem]
    late_width = width + 2 * pad_width
    scratch = [
        buf(xn.shape, bf_type),
        buf(pt.shape, bf_type),
        buf(pixels.shape, bf_type),
        buf((1, lat_len, width), bf_type),
        buf(first.shape, bf_type),
        buf((lat_len, width), bf_type),
        buf(mats.shape, fl_type),
        buf(mats.shape, fl_type),
        buf(mats.shape, fl_type),
        buf((n_items,) + gk.shape, bf_type),
        buf(stats.shape, fl_type),
        buf(pt.shape, bf_type),
        buf(pt.shape, bf_type),
        buf((cut, lat_len), bf_type),
        buf((pad_width, lat_len), fl_type),
        buf((cut, lat_len), bf_type),
        buf((n_z, chunk, lat_len), bf_type),
        buf((n_z, chunk, lat_len), bf_type),
        buf((chunk, lat_len), bf_type),
        buf((n_z, chunk, lat_len), bf_type),
        buf((max(held, pad_width), lat_len), fl_type),
        buf((n_dp, early_rows, width), wire),
        buf((n_dp, early_rows, width), wire),
        buf((n_dp, early_rows, width), wire),
        buf((early_rows, width), fl_type),
        buf((n_dp, early_rows, width), wire),
        buf(pixels.shape, fl_type),
        buf((lat_len, width), fl_type),
        buf((lat_len, 128), fl_type),
        buf((lat_len, n_cols), bf_type),
        buf((lat_len, width), bf_type),
        buf((lat_len, width), fl_type),
        buf((width, n_cols), bf_type),
        buf((2, z_share // 2, width), fl_type),
        buf((n_dp, 2, own, late_width), wire),
        buf((n_dp, own, late_width), wire),
        buf((n_dp, own, late_width), wire),
        buf((own, late_width), fl_type),
        buf((n_dp, own, late_width), wire),
        buf((8, pad_width), fl_type),
        buf((2 * n_z - 1, 8, pad_width), fl_type),
        buf((8, pad_width), fl_type),
        buf((n_dp - 1, 8, pad_width), fl_type),
        buf((pad_width, 128), fl_type),
        pltpu.SemaphoreType.DMA((2, 20 + 6 * n_z + 3 * n_dp)),
        pltpu.SemaphoreType.DMA((16,)),
    ]
    return pl.pallas_call(
        functools.partial(backward, n_z, n_dp, pix_width, chunk),
        out_shape=out_shape,
        in_specs=in_specs,
        out_specs=out_specs,
        scratch_shapes=scratch,
        compiler_params=pltpu.CompilerParams(
            collective_id=1, has_side_effects=True, vmem_limit_bytes=60 * 2**20
        ),
        name="backward",
    )(*args)


def lamb(n_mats, *refs):
    (
        mg, kg, gg, small, mw, mf, ms, kw, kf, ks, gw, gf, gs, iw, i_f, i_s,
        mg_out, kg_out, gg_out, ig_out,
        mw_out, mf_out, ms_out, kw_out, kf_out, ks_out, gw_out, gf_out, gs_out, iw_out, if_out, is_out,
        g_buf, w_buf, f_buf, s_buf, w_new, f_new, s_new, in_sems, out_sems,
    ) = refs
    loads = []
    for k in range(n_mats):
        loads.append(
            [
                pltpu.make_async_copy(src.at[k], dst.at[k], in_sems.at[n, k])
                for n, (src, dst) in enumerate(
                    ((mg, g_buf), (mw, w_buf), (mf, f_buf), (ms, s_buf))
                )
            ]
        )
        for copy in loads[-1]:
            copy.start()
    lane = lax.broadcasted_iota(jnp.int32, (1, 128), 1)

    def ratio(w_sq, u_sq):
        return jnp.sqrt(w_sq) / (jnp.sqrt(u_sq) + 1e-06)

    trust = ratio(small[0:1, :128], small[1:2, :128])

    def scalar(k):
        return jnp.sum(jnp.where(lane == k, trust, 0.0), 1, keepdims=True)

    def update(weight, gradient, first_mom, second):
        first_new = 0.9 * first_mom + 0.1 * gradient
        second_new = 0.999 * second + 0.001 * gradient * gradient
        step = (
            first_new / first_fix / (jnp.sqrt(second_new / second_fix) + 1e-06)
            + decay_rate * weight
        )
        return first_new, second_new, step

    kg_out[...] = kg[...]
    gg_out[...] = gg[...]
    for k in range(2):
        kf_out[k], ks_out[k], step = update(kw[k], kg[k], kf[k], ks[k])
        kw_out[k] = kw[k] - step_rate * scalar(n_mats + k) * step
    first_new, second_new, step = update(gw[...], gg[...], gf[...], gs[...])
    gf_out[...] = first_new
    gs_out[...] = second_new
    row = lax.broadcasted_iota(jnp.int32, (4, 1), 0)
    rates = jnp.zeros((4, 1), fl_type)
    for k in range(4):
        rates = rates + jnp.where(row == k, scalar(n_mats + 2 + k), 0.0)
    gw_out[...] = gw[...] - step_rate * rates * step
    in_grad = small[2:3, : iw.shape[1]]
    ig_out[...] = in_grad
    first_new, second_new, step = update(iw[...], in_grad, i_f[...], i_s[...])
    if_out[...] = first_new
    is_out[...] = second_new
    in_trust = ratio(
        jnp.sum(iw[...] * iw[...], 1, keepdims=True), jnp.sum(step * step, 1, keepdims=True)
    )
    iw_out[...] = iw[...] - step_rate * in_trust * step
    stores = []
    for k in range(n_mats):
        for copy in loads[k]:
            copy.wait()
        first_new, second_new, step = update(w_buf[k], g_buf[k], f_buf[k], s_buf[k])
        f_new[k] = first_new
        s_new[k] = second_new
        w_new[k] = w_buf[k] - step_rate * scalar(k) * step
        for n, (src, dst) in enumerate(
            ((g_buf, mg_out), (w_new, mw_out), (f_new, mf_out), (s_new, ms_out))
        ):
            copy = pltpu.make_async_copy(src.at[k], dst.at[k], out_sems.at[n, k])
            copy.start()
            stores.append(copy)
    for copy in stores:
        copy.wait()


def lamb_call(args):
    n_mats = args[0].shape[0]
    vmem, hbm = pl.BlockSpec(memory_space=pltpu.VMEM), pl.BlockSpec(memory_space=pl.ANY)
    mats, kv, gains = args[:3]
    row = args[13]
    shape = jax.ShapeDtypeStruct

    def like(value):
        return shape(value.shape, value.dtype)

    out_shape = [like(v) for v in (mats, kv, gains, row)]
    out_shape += [like(mats)] * 3 + [like(kv)] * 3 + [like(gains)] * 3 + [like(row)] * 3
    return pl.pallas_call(
        functools.partial(lamb, n_mats),
        out_shape=out_shape,
        in_specs=[hbm] + [vmem] * 3 + [hbm] * 3 + [vmem] * 9,
        out_specs=[hbm] + [vmem] * 3 + [hbm] * 3 + [vmem] * 9,
        scratch_shapes=[pltpu.VMEM(mats.shape, fl_type)] * 7
        + [
            pltpu.SemaphoreType.DMA((4, n_mats)),
            pltpu.SemaphoreType.DMA((4, n_mats)),
        ],
        compiler_params=pltpu.CompilerParams(vmem_limit_bytes=62 * 2**20),
        name="lamb",
    )(*args)


def local(
    latents,
    pixels,
    pix_counts,
    cotangent,
    weight_mats,
    kv_weights,
    norm_gains,
    input_gain,
    mats_first,
    mats_second,
    kv_first,
    kv_second,
    gains_first,
    gains_second,
    input_first,
    input_second,
):
    pix_width = pixels.shape[2]
    model_width = latents.shape[2]
    own_width = weight_mats.shape[1]
    n_dp, n_z = lax.axis_size("dp"), lax.axis_size("z")
    gain_at = round_up(pix_width, 8)
    pad_width = round_up(gain_at + 8, 128)

    def turned(value):
        return jnp.swapaxes(value, 1, 2)

    kv_cols = turned(kv_weights)
    first = jnp.concatenate(
        [
            weight_mats[0],
            jnp.pad(kv_cols[0], ((0, 0), (0, gain_at - pix_width))),
            norm_gains.T,
            jnp.zeros((own_width, pad_width - gain_at - 4), fl_type),
        ],
        axis=1,
    ).astype(bf_type)
    kone = jnp.pad(kv_cols[1], ((0, 0), (0, pad_width - pix_width))).astype(bf_type)
    rest = weight_mats[1:].astype(bf_type)
    if own_width % 16:
        first = lax.all_gather(first, ALL, axis=0, tiled=True)
        kone = lax.all_gather(kone, ALL, axis=0, tiled=True)
        rest = lax.all_gather(rest, ALL, axis=1, tiled=True)
    pix_turned = jnp.transpose(pixels, (2, 0, 1))
    gain_col = input_gain.reshape(pix_width, 1)
    (
        first_all, xn, pt, q_own, early, peak, qk, gains, block_rows, gk, stats, cross_rows, k_one, gterm,
    ) = forward_call(
        n_z, n_dp, first, kone, rest, pix_counts, pix_turned, latents, cotangent, gain_col
    )
    summed = backward_call(
        n_z,
        n_dp,
        (
            gk,
            stats,
            early,
            block_rows,
            xn,
            pt,
            peak,
            qk,
            pix_turned,
            gain_col,
            latents,
            first_all,
            gains,
            q_own,
            cross_rows,
            k_one,
            gterm,
            weight_mats,
            mats_first,
            mats_second,
            kv_cols,
            turned(kv_first),
            turned(kv_second),
            norm_gains,
            gains_first,
            gains_second,
        ),
    )
    row = (1, pix_width)
    outs = lamb_call(
        (
            *summed[3:],
            weight_mats,
            mats_first,
            mats_second,
            kv_cols,
            turned(kv_first),
            turned(kv_second),
            norm_gains,
            gains_first,
            gains_second,
            input_gain.reshape(row),
            input_first.reshape(row),
            input_second.reshape(row),
        )
    )
    outs = list(summed[:3]) + list(outs)
    outs[2] = jnp.transpose(outs[2], (1, 2, 0))
    for index in (4, 10, 11, 12):
        outs[index] = turned(outs[index])
    for index in (6, 16, 17, 18):
        outs[index] = outs[index].reshape(pix_width)
    return tuple(outs)


def solution(mesh):
    n_dp, n_rows = mesh.devices.shape
    split_mesh = Mesh(mesh.devices.reshape(n_dp, n_rows // 2, 2), ALL)
    rows = ("z", "core")
    items = P("dp", None, None)
    pix = P("dp", rows, None)
    mats = P(None, ALL, None)
    pairs = P(None, None, ALL)
    gains = P(None, ALL)
    in_specs = (
        items,
        pix,
        P("dp"),
        items,
        mats,
        pairs,
        gains,
        P(),
        mats,
        mats,
        pairs,
        pairs,
        gains,
        gains,
        P(),
        P(),
    )
    out_specs = (
        pix,
        pix,
        pix,
        mats,
        pairs,
        gains,
        P(),
        mats,
        mats,
        mats,
        pairs,
        pairs,
        pairs,
        gains,
        gains,
        gains,
        P(),
        P(),
        P(),
    )
    return jax.shard_map(
        local, mesh=split_mesh, in_specs=in_specs, out_specs=out_specs, check_vma=False
    )
```

```python
import functools
import math

import jax
import jax.numpy as jnp
from jax import lax
from jax.experimental import pallas as pl
from jax.experimental.pallas import tpu as pltpu
from jax.sharding import Mesh, PartitionSpec as P

HEADS = 8
first_fix = 1.0 - 0.9**10
second_fix = 1.0 - 0.999**10
step_rate = 0.25
decay_rate = 0.01
bf_type = jnp.bfloat16
fl_type = jnp.float32
ALL = ("dp", "z", "core")
NT = (((1,), (1,)), ((), ()))
TN = (((0,), (0,)), ((), ()))
NN = (((1,), (0,)), ((), ()))
MESH = pl.DeviceIdType.MESH
PIECES = ((2, 4), (4, 6), (6, 8), (8, 10))


def dot(left_side, right_side, dims=NN):
    return lax.dot_general(left_side, right_side, dims, preferred_element_type=fl_type)


def round_up(value, unit):
    return -(-value // unit) * unit


def tile_of(rows, unit, most):
    best = unit
    for size in range(unit, most + 1, unit):
        if rows % size == 0:
            best = size
    return best


def meet(peers):
    barrier = pltpu.get_barrier_semaphore()
    for peer in peers:
        pl.semaphore_signal(barrier, inc=1, device_id=peer, device_id_type=MESH)
    pl.semaphore_wait(barrier, len(peers))


def lane_parts(total, size, body):
    def step(t, _):
        body(pl.multiple_of(t * size, size), size)
        return 0

    lax.fori_loop(0, total // size, step, 0)
    if total % size:
        body(total - total % size, total % size)


def remote(src, dst, sems, index, peer):
    return pltpu.make_async_remote_copy(
        src_ref=src,
        dst_ref=dst,
        send_sem=sems.at[0, index],
        recv_sem=sems.at[1, index],
        device_id=peer,
        device_id_type=MESH,
    )


class Gather:
    def __init__(self, whole, lead, sems, n_z):
        self.whole, self.lead, self.sems, self.n_z = whole, lead, sems, n_z
        self.d, self.z, self.c = (lax.axis_index(name) for name in ALL)
        self.z_from = [lax.rem(self.z + n_z - i, n_z) for i in range(n_z)]
        self.z_to = [lax.rem(self.z + i, n_z) for i in range(n_z)]
        self.across = (self.d, self.z, 1 - self.c)
        self.sent = []

    def region(self, flip, start, count, core):
        chips = pl.ds((self.d ^ flip) * self.n_z + start, count)
        return self.whole.at[(*self.lead, chips, core)]

    def copy(self, region, kind, index, peer):
        return pltpu.make_async_remote_copy(
            src_ref=region,
            dst_ref=region,
            send_sem=self.sems.at[0, kind, index],
            recv_sem=self.sems.at[1, kind, index],
            device_id=peer,
            device_id_type=MESH,
        )

    def send(self, region, kind, index, peer, count=1):
        self.copy(region, kind, index, peer).start()
        self.sent.append((kind, index, count))

    def arrived(self, region, kind, index):
        self.copy(region, kind, index, self.across).wait_recv()

    def start_z(self):
        mine = self.region(0, self.z, 1, self.c)
        for i in range(1, self.n_z):
            self.send(mine, 0, i, (self.d, self.z_to[i], self.c))

    def to_plane(self, region, index):
        self.send(region, 1, index, (self.d ^ 1, self.z, self.c))
        self.send(region, 2, index, (self.d ^ 2, self.z, self.c))

    def start_plane(self):
        self.to_plane(self.region(0, self.z, 1, self.c), 0)

    def relay_z(self):
        for i in range(1, self.n_z):
            region = self.region(0, self.z_from[i], 1, self.c)
            self.arrived(region, 0, i)
            self.to_plane(region, i)
        self.send(self.region(0, 0, self.n_z, self.c), 4, 0, self.across, self.n_z)

    def relay_plane(self):
        half = self.n_z // 2
        for kind, flip, onward, start in ((1, 1, 2, 0), (2, 2, 1, half)):
            for i in range(self.n_z):
                self.arrived(self.region(flip, self.z_from[i], 1, self.c), kind, i)
            region = self.region(flip, start, half, self.c)
            self.send(region, 3, kind - 1, (self.d ^ onward, self.z, self.c), half)
        for kind, flip in ((1, 1), (2, 2)):
            region = self.region(flip, 0, self.n_z, self.c)
            self.send(region, 4 + kind, 0, self.across, self.n_z)

    def relay_far(self):
        half = self.n_z // 2
        self.arrived(self.region(3, 0, half, self.c), 3, 0)
        self.arrived(self.region(3, half, half, self.c), 3, 1)
        self.send(self.region(3, 0, self.n_z, self.c), 7, 0, self.across, self.n_z)

    def finish(self):
        for flip in range(4):
            self.arrived(self.region(flip, 0, self.n_z, 1 - self.c), 4 + flip, 0)

    def drain(self):
        for kind, index, count in self.sent:
            self.copy(self.region(0, 0, count, self.c), kind, index, self.across).wait_send()


class Whole:
    def __init__(self, ref, low, high):
        self.ref, self.low, self.high = ref, low, high

    def __getitem__(self, _):
        return self.ref[..., self.low : self.high].reshape(-1, self.high - self.low)


def forward(n_z, n_dp, gathers, pix_width, chunk, *refs):
    counts, first_in, second_in, rest_in, pix_hbm, lat_hbm, cot_hbm, gain_ref = refs[:8]
    (
        first_out, xn_out, pt_out, q_out, early_out,
        peak_ref, qk_ref, gains_ref, block_ref, gk_ref, stats_ref, cross_ref, k_one_ref, gterm_ref,
        gain_cols,
    ) = refs[8:23]
    (
        first_all, second_all, mats, px_tx, px_rx, st_tx, st_rx, px2_tx, px2_rx, st2_tx, st2_rx,
        fin_tx, mean_ref, stat_ref, col_sems, local_sems,
    ) = refs[23:39]
    gather_sems = refs[39:]
    d, z, c = (lax.axis_index(name) for name in ALL)
    n_items, lat_len, width = lat_hbm.shape
    pix_dev, pad_width = xn_out.shape[1:]
    own = width // (n_dp * n_z * 2)
    held = chunk * n_z
    peers = [(d, lax.rem(z + i, n_z), c) for i in range(1, n_z)] + [(d, z, 1 - c)]
    if gathers:
        peers += [(d ^ 1, z, c), (d ^ 2, z, c)]
    local = iter(range(1000))

    def copy_here(src, dst):
        copy = pltpu.make_async_copy(src, dst, local_sems.at[next(local)])
        copy.start()
        return copy

    if gathers:
        first = Gather(first_all, (), gather_sems[0], n_z)
        rest = [Gather(second_all, (), gather_sems[1], n_z)]
        for index, (low, high) in enumerate(PIECES):
            rest.append(Gather(mats, (pl.ds(low - 2, high - low),), gather_sems[2 + index], n_z))
        ready = [(21, 30, 35, 38), (33, 42, 48, 51), (44, 54, 60, 63), (57, 67, 73, 76), (70, 79, 85, 88)]
        steps = []
        for piece, times in zip(rest, ready, strict=True):
            relays = (piece.relay_z, piece.relay_plane, piece.relay_far, piece.finish)
            steps += list(zip(times, relays, strict=True))
        steps.sort(key=lambda step: step[0])
        done = [0]

        def pump(time):
            while done[0] < len(steps) and steps[done[0]][0] <= time:
                steps[done[0]][1]()
                done[0] += 1

        def weight(k):
            piece = [n for n, (low, high) in enumerate(PIECES) if low <= k < high]
            pump(ready[piece[0] + 1 if piece else 0][3])
            return Whole(mats.at[k - 2] if piece else second_all, 0, width)

    else:
        loads = {0: copy_here(first_in, first_all), 1: copy_here(second_in, second_all)}
        for k in range(2, mats.shape[0] + 2):
            loads[k] = copy_here(rest_in.at[k - 2], mats.at[k - 2])

        def pump(time):
            pass

        def weight(k):
            if k in loads:
                loads.pop(k).wait()
            return Whole(mats.at[k - 2] if k > 1 else second_all, 0, width)

    def kt_one():
        weight(1)
        return Whole(second_all, width, width + pad_width)

    def column_copy(src, dst, index, peer):
        return remote(src, dst, col_sems, index, peer)

    def pixel_phase(pix, lat, xn, pt, s_buf, q_all, px_own, xt, turn, *own_bufs):
        l_pix, l_lat = copy_here(pix_hbm, pix), copy_here(lat_hbm, lat)
        if gathers:
            own_mats, own_cols = own_bufs
            l_own = copy_here(first_in, own_mats)
        turn[...] = jnp.zeros(turn.shape, fl_type)
        turn[0:1, :pix_width] = gain_ref[...].reshape(1, pix_width)
        gain_cols[...] = turn[...].T
        gain_col = gain_cols[:pix_width, :1]
        meet(peers)
        if gathers:
            me = d * n_z + z
            gain_at = round_up(pix_width, 8) - (pad_width - 128)
            turn[...] = jnp.zeros(turn.shape, fl_type)
            turn[gain_at : gain_at + 4, :own] = rest_in[...]
            l_own.wait()
            for k, whole in ((0, first_all), (1, second_all)):
                own_cols[...] = jnp.zeros(own_cols.shape, fl_type)
                own_cols[:, :pix_width] = second_in[k]
                if k == 0:
                    own_cols[:, pad_width - 128 :] += turn[:, :128].T[:own]
                whole[me, c, :, :width] = own_mats[k].astype(bf_type)
                whole[me, c, :, width:] = own_cols[...].astype(bf_type)
                if k == 0:
                    first.start_z()
                    first.start_plane()
            for k in range(mats.shape[0]):
                mats[k, me, c] = own_mats[k + 2].astype(bf_type)
            for piece in rest[:-1]:
                piece.start_z()
            for piece in rest[:2]:
                piece.start_plane()
        xt[...] = jnp.zeros(xt.shape, fl_type)
        rows = tile_of(pix_dev, 16, 256)
        tiles = pix_dev // rows

        def normalise(item):
            def part(start, size):
                values = pix[:, item, pl.ds(start, size)].astype(fl_type)
                centred = values - jnp.sum(values, 0, keepdims=True) * (1.0 / pix_width)
                var = jnp.sum(centred * centred, 0, keepdims=True) * (1.0 / pix_width)
                xt[:pix_width, :size] = centred * lax.rsqrt(var + 1e-05) * gain_col
                turned = round_up(size, 128)
                low = xt[:, :turned].T.astype(bf_type)
                xn[item, pl.ds(start, size), :] = low[:size]

            lane_parts(pix_dev, 256, part)

        l_pix.wait()
        normalise(0)
        if gathers:
            first.relay_z()
        for item in range(1, n_items):
            normalise(item)
        xn_copy = copy_here(xn, xn_out)
        if gathers:
            first.relay_plane()
            for piece in rest[2:]:
                piece.start_plane()
            first.relay_far()
            pump(21)
            first.finish()
        else:
            loads.pop(0).wait()
        first_copy = copy_here(first_all, first_out)
        l_lat.wait()
        gain_at = round_up(pix_width, 8) - (pad_width - 128)
        tail = Whole(first_all, width + pad_width - 128, width + pad_width)[...]
        tail = tail.astype(fl_type).T
        gains_ref[...] = tail[gain_at : gain_at + 8]
        lat_rows = tile_of(lat_len, 128, 256)
        for item in range(n_items):

            def queries(t, _, item=item):
                at = pl.ds(pl.multiple_of(t * lat_rows, lat_rows), lat_rows)
                values = lat[item, at, :].astype(fl_type)
                centred = values - jnp.mean(values, -1, keepdims=True)
                var = jnp.mean(centred * centred, -1, keepdims=True)
                normal = (centred * lax.rsqrt(var + 1e-05) * gains_ref[:1]).astype(bf_type)
                q_low = dot(normal, Whole(first_all, 0, width)[...]).astype(bf_type)
                q_all[item, at, :] = q_low
                raw = dot(q_low, Whole(first_all, width, width + pad_width)[...])
                qk_ref[item, :, at] = (raw * width**-0.5).T.astype(bf_type)
                return 0

            lax.fori_loop(0, lat_len // lat_rows, queries, 0)
            pump(31 + 3 * item)
        q_copy = copy_here(q_all.at[c], q_out)

        base = (z * 2 + c) * pix_dev
        for item in range(n_items):
            valid = counts[item] - base

            def score(t, most, item=item, valid=valid):
                at = pl.ds(pl.multiple_of(t * rows, rows), rows)
                values = dot(xn[item, at, :], qk_ref[item])
                place = lax.broadcasted_iota(jnp.int32, values.shape, 0) + t * rows
                values = jnp.where(place < valid, values, -1e30)
                s_buf[at, :] = values
                return jnp.maximum(most, jnp.max(values.reshape(rows // 8, 8, lat_len), 0))

            most = lax.fori_loop(0, tiles, score, jnp.full((8, lat_len), -1e30, fl_type))
            peak = jnp.max(most, 0, keepdims=True)
            pump(36 + 6 * item)

            def weigh(t, total, item=item, peak=peak):
                at = pl.ds(pl.multiple_of(t * rows, rows), rows)
                values = jnp.exp(s_buf[at, :] - peak)
                pt[item, at, :] = values.astype(bf_type)
                return total + jnp.sum(values.reshape(rows // 8, 8, lat_len), 0)

            total = lax.fori_loop(0, tiles, weigh, jnp.zeros((8, lat_len), fl_type))
            total = jnp.sum(total, 0, keepdims=True)
            peak_ref[item] = jnp.broadcast_to(peak, (8, lat_len))
            st_tx[item, :4] = jnp.broadcast_to(peak, (4, lat_len))
            st_tx[item, 4:] = jnp.broadcast_to(total, (4, lat_len))
            part = dot(xn[item], pt[item], TN)
            px_own[item, : part.shape[0]] = part
            if held > part.shape[0]:
                px_own[item, part.shape[0] :] = jnp.zeros((held - part.shape[0], lat_len), fl_type)
            px_tx[item] = px_own[item, :held].astype(bf_type)
            pump(39 + 5 * item)
        pt_copy = copy_here(pt, pt_out)
        pair = [
            column_copy(px_tx.at[1 - c], px_rx, 0, (d, z, 1 - c)),
            column_copy(st_tx.at[1 - c], st_rx, 1, (d, z, 1 - c)),
        ]
        for copy in pair:
            copy.start()
        for copy in pair:
            copy.wait()
        peak_own, peak_rx = st_tx[c, :1], st_rx[:1]
        peak = jnp.maximum(peak_own, peak_rx)
        scale_own, scale_rx = jnp.exp(peak_own - peak), jnp.exp(peak_rx - peak)
        st2_tx[:4] = jnp.broadcast_to(peak, (4, lat_len))
        st2_tx[4:] = jnp.broadcast_to(
            scale_own * st_tx[c, 4:5] + scale_rx * st_rx[4:5], (4, lat_len)
        )
        both = px_own[c, :held] * scale_own + px_rx[...].astype(fl_type) * scale_rx
        px2_tx[...] = both.astype(bf_type).reshape(n_z, chunk, lat_len)
        for copy in (xn_copy, first_copy, q_copy, pt_copy):
            copy.wait()

    own_bufs = []
    if gathers:
        own_bufs = [pltpu.VMEM(first_in.shape, fl_type), pltpu.VMEM((own, pad_width), fl_type)]
    pl.run_scoped(
        pixel_phase,
        pltpu.VMEM(pix_hbm.shape, bf_type),
        pltpu.VMEM(lat_hbm.shape, bf_type),
        pltpu.VMEM(xn_out.shape, bf_type),
        pltpu.VMEM(pt_out.shape, bf_type),
        pltpu.VMEM((pix_dev, lat_len), fl_type),
        pltpu.VMEM(lat_hbm.shape, bf_type),
        pltpu.VMEM((n_items, max(held, pad_width), lat_len), fl_type),
        pltpu.VMEM((pad_width, 256), fl_type),
        pltpu.VMEM((128, pad_width), fl_type),
        *own_bufs,
    )

    copies = []
    for i in range(1, n_z):
        to = lax.rem(z + i, n_z)
        copies.append(column_copy(px2_tx.at[to], px2_rx.at[z], 2 * i, (d, to, c)))
        copies.append(column_copy(st2_tx, st2_rx.at[z], 2 * i + 1, (d, to, c)))
    for copy in copies:
        copy.start()
    if gathers:
        rest[-1].start_z()
    pump(50)
    for copy in copies:
        copy.wait()
    pump(57)
    peak = st2_tx[:1]
    froms = [lax.rem(z + n_z - i, n_z) for i in range(1, n_z)]
    for other in froms:
        peak = jnp.maximum(peak, st2_rx[other, :1])
    scale = jnp.exp(st2_tx[:1] - peak)
    total = scale * st2_tx[4:5]
    mean = scale * px2_tx[z].astype(fl_type)
    for other in froms:
        scale = jnp.exp(st2_rx[other, :1] - peak)
        total = total + scale * st2_rx[other, 4:5]
        mean = mean + scale * px2_rx[other].astype(fl_type)
    stat_ref[:8] = jnp.broadcast_to(peak, (8, lat_len))
    stat_ref[8:] = jnp.broadcast_to(total, (8, lat_len))
    fin_tx[...] = (mean / total).astype(bf_type)
    own_rows = pl.ds(pl.multiple_of(z * chunk, chunk), chunk)
    copies = []
    for i in range(1, n_z):
        to = lax.rem(z + i, n_z)
        copies.append(column_copy(fin_tx, mean_ref.at[own_rows], 2 * n_z + i, (d, to, c)))
    for copy in copies:
        copy.start()
    pump(60)
    for copy in copies:
        copy.wait()
    mean_ref[own_rows] = fin_tx[...]

    def chain_phase(lat, cot, stage, *bufs):
        l_lat, l_cot = copy_here(lat_hbm.at[c], lat), copy_here(cot_hbm.at[c], cot)
        flying = []
        put_sems = [next(local), next(local)]

        def early_put(k, term):
            buffer = len(flying) % 2
            if len(flying) >= 2:
                flying[-2].wait()
            stage[buffer] = term.astype(stage.dtype).reshape(stage.shape[1:])
            copy = pltpu.make_async_copy(
                stage.at[buffer],
                early_out.at[:, :, pl.ds((k - 1) * own, own)],
                local_sems.at[put_sems[buffer]],
            )
            copy.start()
            flying.append(copy)

        outs = (early_put, block_ref, gk_ref, stats_ref, cross_ref, k_one_ref, gterm_ref)
        l_lat.wait()
        l_cot.wait()
        latent_chain(
            n_z, n_dp, own, weight, kt_one, pump, lat, cot, gains_ref, mean_ref, stat_ref, outs, bufs
        )
        for copy in flying[-2:]:
            copy.wait()

    wire = early_out.dtype
    one_item = pltpu.VMEM((lat_len, width), bf_type)
    n_cols = n_dp * 2 * own
    pl.run_scoped(
        chain_phase,
        one_item,
        one_item,
        pltpu.VMEM((2, n_dp, 2, own, width), wire),
        *chain_bufs(lat_len, width, pad_width, n_cols),
    )
    if gathers:
        pump(1000)
        for piece in [first] + rest:
            piece.drain()


def forward_call(n_z, n_dp, gathers, first, second, rest, counts, pix_turned, latents, cotangent, gain):
    n_items, lat_len, width = latents.shape
    pix_width, _, pix_dev = pix_turned.shape
    own = width // (n_dp * n_z * 2)
    blocks = (n_dp * n_z, 2, own) if gathers else (1, 1, width)
    n_rest = 8
    pad_width = round_up(round_up(pix_width, 8) + 8, 128)
    wire = bf_type if own % 16 == 0 else fl_type
    chunk = round_up(-(-pix_width // n_z), 16)
    held = chunk * n_z
    z_share = lat_len // n_z
    n_cols = n_dp * 2 * own
    vmem, hbm = pl.BlockSpec(memory_space=pltpu.VMEM), pl.BlockSpec(memory_space=pl.ANY)
    shape, buf = jax.ShapeDtypeStruct, pltpu.VMEM
    out_shape = [
        shape((*blocks, width + pad_width), bf_type),
        shape((n_items, pix_dev, pad_width), bf_type),
        shape((n_items, pix_dev, lat_len), bf_type),
        shape((lat_len, width), bf_type),
        shape((n_dp, 2, (n_rest + 1) * own, width), wire),
        shape((n_items, 8, lat_len), fl_type),
        shape((n_items, pad_width, lat_len), bf_type),
        shape((8, width), fl_type),
        shape((2, z_share // 2, width), bf_type),
        shape((pad_width, lat_len), bf_type),
        shape((3, 8, lat_len), fl_type),
        shape((z_share, width), fl_type),
        shape((n_cols, pad_width), fl_type),
        shape((8, width), fl_type),
        shape((pad_width, 128), fl_type),
    ]
    scratch = [
        buf((*blocks, width + pad_width), bf_type),
        buf((*blocks, width + pad_width), bf_type),
        buf((n_rest, *blocks, width), bf_type),
        buf((n_items, held, lat_len), bf_type),
        buf((held, lat_len), bf_type),
        buf((n_items, 8, lat_len), fl_type),
        buf((8, lat_len), fl_type),
        buf((n_z, chunk, lat_len), bf_type),
        buf((n_z, chunk, lat_len), bf_type),
        buf((8, lat_len), fl_type),
        buf((n_z, 8, lat_len), fl_type),
        buf((chunk, lat_len), bf_type),
        buf((held, lat_len), bf_type),
        buf((16, lat_len), fl_type),
        pltpu.SemaphoreType.DMA((2, 3 * n_z)),
        pltpu.SemaphoreType.DMA((32,)),
    ]
    if gathers:
        scratch += [pltpu.SemaphoreType.DMA((2, 8, n_z))] * (2 + len(PIECES))
    weight_specs = [hbm, vmem, vmem] if gathers else [hbm] * 3
    return pl.pallas_call(
        functools.partial(forward, n_z, n_dp, gathers, pix_width, chunk),
        out_shape=out_shape,
        in_specs=[pl.BlockSpec(memory_space=pltpu.SMEM)] + weight_specs + [hbm] * 3 + [vmem],
        out_specs=[hbm] * 5 + [vmem] * 10,
        scratch_shapes=scratch,
        compiler_params=pltpu.CompilerParams(
            collective_id=0, has_side_effects=True, vmem_limit_bytes=62 * 2**20
        ),
        name="forward",
    )(counts, first, second, rest, pix_turned, latents, cotangent, gain)


def row_loop(total, body, rows=128):
    def step(t, _):
        body(pl.ds(pl.multiple_of(t * rows, rows), rows))
        return 0

    lax.fori_loop(0, total // rows, step, 0)


def tanh_gelu(values):
    factor, cubic = (2.0 / math.pi) ** 0.5, 0.044715
    square = values * values
    bent = jnp.tanh(factor * values * (1.0 + cubic * square))
    half = 0.5 * (1.0 + bent)
    slope = half + 0.5 * values * (1.0 - bent * bent) * factor * (1.0 + 3.0 * cubic * square)
    return values * half, slope


def choose(sel_ref, n_dp, n_z, pair_width):
    width, n_cols = sel_ref.shape
    z = lax.axis_index("z")
    wanted = lax.broadcasted_iota(jnp.int32, (width, n_cols), 1)
    wanted = (lax.div(wanted, pair_width) * n_z + z) * pair_width + lax.rem(wanted, pair_width)
    place = lax.broadcasted_iota(jnp.int32, (width, n_cols), 0)
    sel_ref[...] = jnp.where(place == wanted, 1.0, 0.0).astype(bf_type)


def latent_chain(n_z, n_dp, own, weight, kt_one, pump, lat, cot, gains, mean_ref, stat_ref, outs, bufs):
    early_put, block_ref, gk_ref, stats_ref, cross_ref, k_one_ref, gterm_ref = outs
    (
        run, x_buf, hat_c, hat_s, hat_f, inv, slope_c, slope_f,
        att, norm_c, gelu_c, norm_s, q_s, k_s, v_s, mixed, norm_f, gelu_f, probs, sel, mean_pad,
    ) = bufs
    lat_len, width = lat.shape
    pad_width = mean_pad.shape[1]
    head_dim = width // HEADS
    z = lax.axis_index("z")
    z_share = lat_len // n_z
    z_rows = pl.ds(pl.multiple_of(z * z_share, z_share), z_share)
    choose(sel, n_dp, n_z, 2 * own)
    tmp = lat

    def add_norm(base, gain, hat, which, normal):
        def body(at):
            values = base(at) + x_buf[at, :]
            run[at, :] = values
            centred = values - jnp.mean(values, -1, keepdims=True)
            scale = lax.rsqrt(jnp.mean(centred * centred, -1, keepdims=True) + 1e-05)
            standard_values = centred * scale
            hat[at, :] = standard_values
            inv[which, at, :] = jnp.broadcast_to(scale, (scale.shape[0], 128))
            normal[at, :] = (standard_values * gains[gain : gain + 1]).astype(bf_type)

        row_loop(lat_len, body)

    def activate(slope, low):
        def body(at):
            value, grad = tanh_gelu(x_buf[at, :])
            low[at, :] = value.astype(bf_type)
            slope[at, :] = grad

        row_loop(lat_len, body)

    def times_slope(slope, low):
        def body(at):
            low[at, :] = (x_buf[at, :] * slope[at, :]).astype(bf_type)

        row_loop(lat_len, body)

    def pull_norm(base, gain, hat, which, low):
        def body(t, sums):
            at = pl.ds(pl.multiple_of(t * 128, 128), 128)
            grad = x_buf[at, :]
            normal = hat[at, :]
            sums = sums + jnp.sum((normal * grad).reshape(16, 8, width), 0)
            grad = grad * gains[gain : gain + 1]
            mean = jnp.mean(grad, -1, keepdims=True)
            along = jnp.mean(grad * normal, -1, keepdims=True)
            value = base(at) + (grad - mean - normal * along) * inv[which, at, :1]
            run[at, :] = value
            low[at, :] = value.astype(bf_type)
            return sums

        sums = lax.fori_loop(0, lat_len // 128, body, jnp.zeros((8, width), fl_type))
        gterm_ref[gain : gain + 1] = jnp.sum(sums, 0, keepdims=True)

    def matrix_term(k, left, right):
        early_put(k, dot(dot(left[...], sel[...]).astype(bf_type), right[...], TN))

    def head(h):
        return slice(h * head_dim, (h + 1) * head_dim)

    head_scale = head_dim**-0.5
    gterm_ref[...] = jnp.zeros(gterm_ref.shape, fl_type)

    pump(65)
    mean_pad[...] = jnp.zeros(mean_pad.shape, bf_type)
    held = min(mean_ref.shape[0], pad_width)
    mean_pad[:, :held] = mean_ref[:held].astype(fl_type).T.astype(bf_type)
    att[...] = dot(mean_pad[...], kt_one()[...], NT).astype(bf_type)
    x_buf[...] = dot(att[...], weight(1)[...])
    add_norm(lambda at: lat[at, :].astype(fl_type), 1, hat_c, 0, norm_c)
    pump(70)
    x_buf[...] = dot(norm_c[...], weight(2)[...])
    activate(slope_c, gelu_c)
    pump(73)
    x_buf[...] = dot(gelu_c[...], weight(3)[...])
    add_norm(lambda at: run[at, :], 2, hat_s, 1, norm_s)
    pump(75)
    q_s[...] = dot(norm_s[...], weight(4)[...]).astype(bf_type)
    k_s[...] = dot(norm_s[...], weight(5)[...]).astype(bf_type)
    pump(77)
    v_s[...] = dot(norm_s[...], weight(6)[...]).astype(bf_type)

    def attend(h):
        at = head(h)
        scores = dot(k_s[:, at], q_s[:, at], NT) * head_scale
        weights = jnp.exp(scores - jnp.max(scores, 0, keepdims=True))
        weights = weights * (1.0 / jnp.sum(weights, 0, keepdims=True))
        low = weights.astype(bf_type)
        probs[h] = low
        mixed[:, at] = dot(low, v_s[:, at], TN).astype(bf_type)

    for h in range(HEADS):
        attend(h)
    pump(85)
    x_buf[...] = dot(mixed[...], weight(7)[...])
    add_norm(lambda at: run[at, :], 3, hat_f, 2, norm_f)
    x_buf[...] = dot(norm_f[...], weight(8)[...])
    activate(slope_f, gelu_f)
    final = run[z_rows, :] + dot(gelu_f[z_rows, :], weight(9)[...])
    block_ref[...] = final.astype(bf_type).reshape(block_ref.shape)

    matrix_term(9, gelu_f, cot)
    x_buf[...] = dot(cot[...], weight(9)[...], NT)
    times_slope(slope_f, tmp)
    matrix_term(8, norm_f, tmp)
    x_buf[...] = dot(tmp[...], weight(8)[...], NT)
    pull_norm(lambda at: cot[at, :].astype(fl_type), 3, hat_f, 2, tmp)
    matrix_term(7, mixed, tmp)
    grad_mixed = gelu_f
    grad_mixed[...] = dot(tmp[...], weight(7)[...], NT).astype(bf_type)

    def attend_back(h):
        at = head(h)
        q_h, k_h, v_h, grad_h = q_s[:, at], k_s[:, at], v_s[:, at], grad_mixed[:, at]
        low = probs[h]
        weights = low.astype(fl_type)
        grad_weights = dot(v_h, grad_h, NT)
        along = jnp.sum(weights * grad_weights, 0, keepdims=True)
        grad_scores = (weights * (grad_weights - along)).astype(bf_type)
        q_s[:, at] = (dot(grad_scores, k_h, TN) * head_scale).astype(bf_type)
        k_s[:, at] = (dot(grad_scores, q_h) * head_scale).astype(bf_type)
        v_s[:, at] = dot(low, grad_h).astype(bf_type)

    for h in range(HEADS):
        attend_back(h)
    matrix_term(4, norm_s, q_s)
    matrix_term(5, norm_s, k_s)
    matrix_term(6, norm_s, v_s)
    x_buf[...] = dot(q_s[...], weight(4)[...], NT)
    x_buf[...] += dot(k_s[...], weight(5)[...], NT)
    x_buf[...] += dot(v_s[...], weight(6)[...], NT)
    pull_norm(lambda at: run[at, :], 2, hat_s, 1, tmp)
    matrix_term(3, gelu_c, tmp)
    x_buf[...] = dot(tmp[...], weight(3)[...], NT)
    times_slope(slope_c, tmp)
    matrix_term(2, norm_c, tmp)
    x_buf[...] = dot(tmp[...], weight(2)[...], NT)
    pull_norm(lambda at: run[at, :], 1, hat_c, 0, tmp)
    matrix_term(1, att, tmp)
    cross_ref[...] = run[z_rows, :]
    grad_att = gelu_f
    grad_att[...] = dot(tmp[...], weight(1)[...], NT).astype(bf_type)
    low = dot(grad_att[...], kt_one()[...]).T.astype(bf_type)
    gk_ref[...] = low
    delta = jnp.sum(low[:held].astype(fl_type) * mean_ref[:held].astype(fl_type), 0, keepdims=True)
    stats_ref[0] = stat_ref[:8]
    stats_ref[1] = stat_ref[8:]
    stats_ref[2] = jnp.broadcast_to(delta, stats_ref.shape[1:])
    k_one_ref[...] = dot(dot(grad_att[...], sel[...]).astype(bf_type), mean_pad[...], TN)


def chain_bufs(lat_len, width, pad_width, n_cols):
    wide = pltpu.VMEM((lat_len, width), fl_type)
    low = pltpu.VMEM((lat_len, width), bf_type)
    return (
        [wide] * 5
        + [pltpu.VMEM((3, lat_len, 128), fl_type)]
        + [wide] * 2
        + [low] * 10
        + [
            pltpu.VMEM((HEADS, lat_len, lat_len), bf_type),
            pltpu.VMEM((width, n_cols), bf_type),
            pltpu.VMEM((lat_len, pad_width), bf_type),
        ]
    )


def backward(n_z, n_dp, pix_width, chunk, *refs):
    (
        gk_ref,
        stats_ref,
        early_ref,
        block_ref,
        xn_hbm,
        pt_hbm,
        peak_ref,
        qk_ref,
        pix_hbm,
        gain_ref,
        lat_hbm,
        first_hbm,
        gains_ref,
        q_hbm,
        cross_ref,
        k_one_ref,
        gterm_ref,
        mats_hbm,
        mfirst_hbm,
        msecond_hbm,
        kv_ref,
        kfirst_ref,
        ksecond_ref,
        ng_ref,
        gfirst_ref,
        gsecond_ref,
        block_out,
        lat_out,
        pix_out,
        mats_out,
        kv_out,
        gains_out,
        small_out,
        xn,
        pt,
        pix,
        lat,
        first,
        q_own,
        mats,
        mfirst,
        msecond,
        gk_all,
        stats_rx,
        ds,
        pl_low,
        part_tx,
        part_own,
        part_rx,
        col_tx,
        col_rx,
        fin_tx,
        fin_rx,
        dst_full,
        early_own,
        early_rx,
        early_tx,
        early_sum,
        early_far,
        pix_buf,
        hat,
        inv,
        norm,
        dq,
        da,
        sel,
        lat_tx,
        late,
        late_rx,
        late_tx,
        late_own,
        late_far,
        small_tx,
        small_col,
        small_far_tx,
        small_far,
        input_acc,
        sems,
        loads,
    ) = refs
    d, z, c = (lax.axis_index(name) for name in ALL)
    oc = 1 - c
    n_items, pix_dev, pad_width = xn.shape
    gain_col = gain_ref[:pix_width, :1]
    lat_len, width = lat.shape[1:]
    own = kv_out.shape[1]
    far = [lax.rem(d + i, n_dp) for i in range(1, n_dp)]
    far_from = [lax.rem(d + n_dp - i, n_dp) for i in range(1, n_dp)]
    z_to = [lax.rem(z + i, n_z) for i in range(1, n_z)]
    z_from = [lax.rem(z + n_z - i, n_z) for i in range(1, n_z)]
    partner = (d, z, oc)
    column = [(i, 0) for i in range(1, n_z)] + [(i, 1) for i in range(n_z)]

    def in_column(i, j):
        return (d, lax.rem(z + i, n_z), lax.rem(c + j, 2))

    meet([in_column(i, j) for i, j in column] + [(to, z, c) for to in far])

    slot = iter(range(1000))

    def send(src, dst, peer):
        copy = remote(src, dst, sems, next(slot), peer)
        copy.start()
        return copy

    pair = [
        send(gk_ref, gk_all.at[c], partner),
        send(stats_ref, stats_rx, partner),
    ]
    out_pair = send(block_ref.at[oc], block_out.at[c], partner)
    early_pair = send(early_ref.at[:, oc], early_rx, partner)
    load_slot = iter(range(1000))

    def load(src, dst):
        copy = pltpu.make_async_copy(src, dst, loads.at[next(load_slot)])
        copy.start()
        return copy

    l_xn = load(xn_hbm, xn)
    l_pt = load(pt_hbm, pt)
    l_pix = load(pix_hbm, pix)
    l_lat = load(lat_hbm.at[c], lat.at[0])
    l_first = load(first_hbm, first)
    l_q = load(q_hbm, q_own)
    l_early = load(early_ref.at[:, c], early_own)
    l_mats = [load(mats_hbm, mats), load(mfirst_hbm, mfirst), load(msecond_hbm, msecond)]
    block_out[c] = block_ref[c]
    gk_all[c] = gk_ref[...]

    rows = tile_of(pix_dev, 16, 256)
    tiles = pix_dev // rows
    held = chunk * n_z
    l_pt.wait()
    l_xn.wait()
    for copy in pair:
        copy.wait()

    def score_side(item, gk, stats):
        scale = jnp.exp(peak_ref[item, :1] - stats[0, :1]) / stats[1, :1]
        delta = stats[2, :1]

        def body(t, _):
            at = pl.ds(pl.multiple_of(t * rows, rows), rows)
            probs = pt[item, at, :].astype(fl_type) * scale
            grad_probs = dot(xn[item, at, :], gk[...])
            ds[item, at, :] = (probs * (grad_probs - delta)).astype(bf_type)
            pl_low[item, at, :] = probs.astype(bf_type)
            return 0

        lax.fori_loop(0, tiles, body, 0)
        return dot(xn[item], ds[item], TN)

    part_tx[...] = score_side(oc, gk_all.at[oc], stats_rx)[: part_tx.shape[0]].astype(part_tx.dtype)
    px_pair = send(part_tx, part_rx, partner)
    part_own[...] = score_side(c, gk_ref, stats_ref)
    l_early.wait()
    early_pair.wait()

    n_rows = early_own.shape[1]

    def pair_sum(t, _):
        both = early_own[t].astype(fl_type) + early_rx[t].astype(fl_type)
        early_tx[t] = both.astype(early_tx.dtype)
        return 0

    lax.fori_loop(0, n_dp, pair_sum, 0)
    early_sum[...] = early_own[d].astype(fl_type) + early_rx[d].astype(fl_type)
    px_pair.wait()
    both = part_own[: part_rx.shape[0]] + part_rx[...].astype(fl_type)
    if held > both.shape[0]:
        both = jnp.concatenate([both, jnp.zeros((held - both.shape[0], lat_len), fl_type)], 0)
    col_tx[...] = both[:held].astype(col_tx.dtype).reshape(n_z, chunk, lat_len)
    col = [
        send(col_tx.at[to], col_rx.at[z], (d, to, c)) for to in z_to
    ]
    early_out = [send(early_tx.at[to], early_far.at[d], (to, z, c)) for to in far]

    l_pix.wait()
    input_acc[...] = jnp.zeros(input_acc.shape, fl_type)

    def pixel_side(item, gk):
        def part(start, size):
            at = pl.ds(start, size)
            grad = dot(qk_ref[item], ds[item, at, :], NT) + dot(gk[...], pl_low[item, at, :], NT)
            grad = grad[:pix_width]
            values = pix[:, item, at].astype(fl_type)
            centred = values - jnp.sum(values, 0, keepdims=True) * (1.0 / pix_width)
            var = jnp.sum(centred * centred, 0, keepdims=True) * (1.0 / pix_width)
            scale = lax.rsqrt(var + 1e-05)
            normal = centred * scale
            along = normal * grad
            for low in range(0, size, 128):
                high = min(low + 128, size)
                input_acc[:pix_width, : high - low] += along[:, low:high]
            grad = grad * gain_col
            mean = jnp.sum(grad, 0, keepdims=True) * (1.0 / pix_width)
            along = jnp.sum(grad * normal, 0, keepdims=True) * (1.0 / pix_width)
            pix_buf[:, item, at] = (grad - mean - normal * along) * scale

        lane_parts(pix_dev, 256, part)

    pixel_side(0, gk_all.at[0])

    for copy in col:
        copy.wait()
    mean = col_tx[z].astype(fl_type)
    for other in z_from:
        mean = mean + col_rx[other].astype(fl_type)
    fin_tx[...] = mean.astype(fin_tx.dtype)
    fin = [send(fin_tx, fin_rx.at[z], (d, to, c)) for to in z_to]

    pixel_side(1, gk_all.at[1])
    stores = [load(pix_buf, pix_out)]

    l_lat.wait()
    l_first.wait()
    l_q.wait()
    pair_width = 2 * own
    n_cols = n_dp * pair_width
    wanted = lax.broadcasted_iota(jnp.int32, (width, n_cols), 1)
    wanted = (lax.div(wanted, pair_width) * n_z + z) * pair_width + lax.rem(wanted, pair_width)
    place = lax.broadcasted_iota(jnp.int32, (width, n_cols), 0)
    sel[...] = jnp.where(place == wanted, 1.0, 0.0).astype(bf_type)
    values = lat[0].astype(fl_type)
    centred = values - jnp.mean(values, -1, keepdims=True)
    scale = lax.rsqrt(jnp.mean(centred * centred, -1, keepdims=True) + 1e-05)
    hat[...] = centred * scale
    inv[...] = jnp.broadcast_to(scale, inv.shape)
    norm[...] = dot((hat[...] * gains_ref[:1]).astype(bf_type), sel[...]).astype(bf_type)

    for copy in fin:
        copy.wait()
    dst_full[...] = jnp.zeros(dst_full.shape, fl_type)
    for other in z_from:
        dst_full[pl.ds(other * chunk, chunk)] = fin_rx[other].astype(fl_type)
    dst_full[pl.ds(z * chunk, chunk)] = fin_tx[...].astype(fl_type)
    summed = dst_full[:pad_width].T.astype(bf_type)
    kt_zero = first[:, width : width + pad_width]
    dq[...] = (dot(summed, kt_zero, NT) * width**-0.5).astype(bf_type)
    da[...] = dot(dq[...], first[:, :width], NT)
    term_zero = dot(norm[...], dq[...], TN)
    q_sel = dot(q_own[...], sel[...]).astype(bf_type)
    term_k = dot(q_sel, summed, TN) * width**-0.5
    gain_at = round_up(pix_width, 8) - (pad_width - 128)
    gain_zero = jnp.sum(hat[...] * da[...], 0, keepdims=True)
    place = lax.broadcasted_iota(jnp.int32, (8, width), 0)
    gain_sums = jnp.where(place == 0, gain_zero, gterm_ref[...]).astype(bf_type)
    gain_cols = dot(gain_sums, sel[...])
    gain_cols = jnp.concatenate(
        [
            jnp.zeros((gain_at, n_cols), fl_type),
            gain_cols,
            jnp.zeros((128 - gain_at - 8, n_cols), fl_type),
        ],
        0,
    ).T
    late[:, :, :, :width] = term_zero.astype(late.dtype).reshape(n_dp, 2, own, width)
    late[:, :, :, width : width + pad_width] = term_k.astype(late.dtype).reshape(
        n_dp, 2, own, pad_width
    )
    ones = k_one_ref[...]
    late[:, :, :, width + pad_width : width + 2 * pad_width - 128] = (
        ones[:, : pad_width - 128].astype(late.dtype).reshape(n_dp, 2, own, pad_width - 128)
    )
    late[:, :, :, width + 2 * pad_width - 128 :] = (
        (ones[:, pad_width - 128 :] + gain_cols).astype(late.dtype).reshape(n_dp, 2, own, 128)
    )
    late_pair = send(late.at[:, oc], late_rx, partner)

    z_share = lat_len // n_z
    at = pl.ds(pl.multiple_of(z * z_share, z_share), z_share)
    grad = da[at, :] * gains_ref[:1]
    normal = hat[at, :]
    mean = jnp.mean(grad, -1, keepdims=True)
    along = jnp.mean(grad * normal, -1, keepdims=True)
    lat_grad = cross_ref[...] + (grad - mean - normal * along) * inv[at, :1]
    lat_tx[...] = lat_grad.reshape(2, z_share // 2, width)
    lat_pair = send(lat_tx.at[oc], lat_out.at[c], partner)
    lat_out[c] = lat_tx[c]

    late_pair.wait()
    late_sum = late[:, c].astype(fl_type) + late_rx[...].astype(fl_type)
    late_tx[...] = late_sum.astype(late_tx.dtype)
    late_out = [send(late_tx.at[to], late_far.at[d], (to, z, c)) for to in far]
    late_own[...] = late[d, c].astype(fl_type) + late_rx[d].astype(fl_type)

    for copy in early_out:
        copy.wait()
    for copy in l_mats:
        copy.wait()
    lane = lax.broadcasted_iota(jnp.int32, (1, 128), 1)

    def norms(weight, gradient, first_mom, second):
        first_new = 0.9 * first_mom + 0.1 * gradient
        second_new = 0.999 * second + 0.001 * gradient * gradient
        update = (
            first_new / first_fix / (jnp.sqrt(second_new / second_fix) + 1e-06)
            + decay_rate * weight
        )
        return (weight * weight, update * update)

    def total(values):
        return jnp.sum(jnp.sum(values, 0, keepdims=True), 1, keepdims=True)

    def matrix(k, sums):
        at = pl.ds(pl.multiple_of((k - 1) * own, own), own)
        gradient = early_sum[at, :]
        for other in far_from:
            gradient = gradient + early_far[other, at, :].astype(fl_type)
        mats_out[k] = gradient
        w_sq, u_sq = norms(mats[k], gradient, mfirst[k], msecond[k])
        here = lane == k
        return (
            sums[0] + jnp.where(here, total(w_sq), 0.0),
            sums[1] + jnp.where(here, total(u_sq), 0.0),
        )

    zero = jnp.zeros((1, 128), fl_type)
    sums = lax.fori_loop(1, mats.shape[0], matrix, (zero, zero))

    for copy in late_out:
        copy.wait()
    for other in far_from:
        late_own[...] += late_far[other].astype(fl_type)
    mats_out[0] = late_own[:, :width]
    grads = [(mats[0], late_own[:, :width], mfirst[0], msecond[0], 0)]
    for k in range(2):
        cols = late_own[:, width + k * pad_width : width + k * pad_width + pix_width]
        kv_out[k] = cols
        grads.append((kv_ref[k], cols, kfirst_ref[k], ksecond_ref[k], 10 + k))
    gain_grad = late_own[:, width + 2 * pad_width - 128 :].T[gain_at : gain_at + 8]
    gains_out[...] = gain_grad[:4]
    w_sum, u_sum = sums
    for weight, gradient, first_mom, second, k in grads:
        w_sq, u_sq = norms(weight, gradient, first_mom, second)
        w_sum = w_sum + jnp.where(lane == k, total(w_sq), 0.0)
        u_sum = u_sum + jnp.where(lane == k, total(u_sq), 0.0)
    w_sq, u_sq = norms(ng_ref[...], gain_grad[:4], gfirst_ref[...], gsecond_ref[...])
    w_sq, u_sq = jnp.sum(w_sq, 1, keepdims=True), jnp.sum(u_sq, 1, keepdims=True)
    for k in range(4):
        w_sum = w_sum + jnp.where(lane == 12 + k, w_sq[k : k + 1], 0.0)
        u_sum = u_sum + jnp.where(lane == 12 + k, u_sq[k : k + 1], 0.0)
    small_tx[...] = jnp.zeros(small_tx.shape, fl_type)
    small_tx[0:1, :128] = w_sum
    small_tx[1:2, :128] = u_sum
    small_tx[2:3, :] = jnp.sum(input_acc[...].T, 0, keepdims=True)
    copies = [
        send(small_tx, small_col.at[n], in_column(i, j)) for n, (i, j) in enumerate(column)
    ]
    for copy in copies:
        copy.wait()
    all_sum = small_tx[...]
    for n in range(len(column)):
        all_sum = all_sum + small_col[n]
    small_far_tx[...] = all_sum
    copies = [
        send(small_far_tx, small_far.at[n], (to, z, c)) for n, to in enumerate(far)
    ]
    for copy in copies:
        copy.wait()
    for n in range(len(far)):
        all_sum = all_sum + small_far[n]
    small_out[...] = all_sum
    for copy in [out_pair, lat_pair] + stores:
        copy.wait()


def backward_call(n_z, n_dp, args):
    (gk, stats, early, _, xn, pt, _, _, pixels, _, latents, first) = args[:12]
    mats, kv, gains = args[17], args[20], args[23]
    pix_width = pixels.shape[0]
    n_items, lat_len, width = latents.shape
    own = mats.shape[1]
    pad_width = xn.shape[2]
    early_rows = early.shape[2]
    wire = early.dtype
    chunk = round_up(-(-pix_width // n_z), 16)
    held = chunk * n_z
    cut = min(held, pad_width)
    z_share = lat_len // n_z
    n_cols = n_dp * 2 * own
    vmem, hbm = pl.BlockSpec(memory_space=pltpu.VMEM), pl.BlockSpec(memory_space=pl.ANY)
    places = {2, 4, 5, 8, 10, 11, 13, 17, 18, 19}
    in_specs = [hbm if index in places else vmem for index in range(len(args))]
    shape, buf = jax.ShapeDtypeStruct, pltpu.VMEM
    out_shape = [
        shape((n_items, z_share // 2, width), bf_type),
        shape((n_items, z_share // 2, width), fl_type),
        shape(pixels.shape, fl_type),
        shape(mats.shape, fl_type),
        shape(kv.shape, fl_type),
        shape(gains.shape, fl_type),
        shape((8, pad_width), fl_type),
    ]
    out_specs = [vmem, vmem, hbm, vmem, vmem, vmem, vmem]
    late_width = width + 2 * pad_width
    scratch = [
        buf(xn.shape, bf_type),
        buf(pt.shape, bf_type),
        buf(pixels.shape, bf_type),
        buf((1, lat_len, width), bf_type),
        buf(first.shape, bf_type),
        buf((lat_len, width), bf_type),
        buf(mats.shape, fl_type),
        buf(mats.shape, fl_type),
        buf(mats.shape, fl_type),
        buf((n_items,) + gk.shape, bf_type),
        buf(stats.shape, fl_type),
        buf(pt.shape, bf_type),
        buf(pt.shape, bf_type),
        buf((cut, lat_len), bf_type),
        buf((pad_width, lat_len), fl_type),
        buf((cut, lat_len), bf_type),
        buf((n_z, chunk, lat_len), bf_type),
        buf((n_z, chunk, lat_len), bf_type),
        buf((chunk, lat_len), bf_type),
        buf((n_z, chunk, lat_len), bf_type),
        buf((max(held, pad_width), lat_len), fl_type),
        buf((n_dp, early_rows, width), wire),
        buf((n_dp, early_rows, width), wire),
        buf((n_dp, early_rows, width), wire),
        buf((early_rows, width), fl_type),
        buf((n_dp, early_rows, width), wire),
        buf(pixels.shape, fl_type),
        buf((lat_len, width), fl_type),
        buf((lat_len, 128), fl_type),
        buf((lat_len, n_cols), bf_type),
        buf((lat_len, width), bf_type),
        buf((lat_len, width), fl_type),
        buf((width, n_cols), bf_type),
        buf((2, z_share // 2, width), fl_type),
        buf((n_dp, 2, own, late_width), wire),
        buf((n_dp, own, late_width), wire),
        buf((n_dp, own, late_width), wire),
        buf((own, late_width), fl_type),
        buf((n_dp, own, late_width), wire),
        buf((8, pad_width), fl_type),
        buf((2 * n_z - 1, 8, pad_width), fl_type),
        buf((8, pad_width), fl_type),
        buf((n_dp - 1, 8, pad_width), fl_type),
        buf((pad_width, 128), fl_type),
        pltpu.SemaphoreType.DMA((2, 20 + 6 * n_z + 3 * n_dp)),
        pltpu.SemaphoreType.DMA((16,)),
    ]
    return pl.pallas_call(
        functools.partial(backward, n_z, n_dp, pix_width, chunk),
        out_shape=out_shape,
        in_specs=in_specs,
        out_specs=out_specs,
        scratch_shapes=scratch,
        compiler_params=pltpu.CompilerParams(
            collective_id=1, has_side_effects=True, vmem_limit_bytes=60 * 2**20
        ),
        name="backward",
    )(*args)


def lamb(n_mats, *refs):
    (
        block_in, lat_in, pix_in, mg, kg, gg, small, mw, mf, ms, kw, kf, ks, gw, gf, gs, iw, i_f, i_s,
        block_out, lat_out, pix_out, mg_out, kg_out, gg_out, ig_out,
        mw_out, mf_out, ms_out, kw_out, kf_out, ks_out, gw_out, gf_out, gs_out, iw_out, if_out, is_out,
        g_buf, w_buf, f_buf, s_buf, w_new, f_new, s_new, pix_buf, in_sems, out_sems, pix_sems,
    ) = refs
    loads = []
    for k in range(n_mats):
        loads.append(
            [
                pltpu.make_async_copy(src.at[k], dst.at[k], in_sems.at[n, k])
                for n, (src, dst) in enumerate(
                    ((mg, g_buf), (mw, w_buf), (mf, f_buf), (ms, s_buf))
                )
            ]
        )
        for copy in loads[-1]:
            copy.start()
    parts = [(low, min(low + 88, pix_in.shape[0])) for low in range(0, pix_in.shape[0], 88)]

    def pix_copy(n, back):
        low, high = parts[n]
        src, dst = pix_in.at[low:high], pix_buf.at[low:high]
        if back:
            src, dst = dst, pix_out.at[low:high]
        return pltpu.make_async_copy(src, dst, pix_sems.at[int(back), n])

    for n in range(len(parts)):
        pix_copy(n, False).start()
    block_out[...] = block_in[...]
    lat_out[...] = lat_in[...]
    lane = lax.broadcasted_iota(jnp.int32, (1, 128), 1)

    def ratio(w_sq, u_sq):
        return jnp.sqrt(w_sq) / (jnp.sqrt(u_sq) + 1e-06)

    trust = ratio(small[0:1, :128], small[1:2, :128])

    def scalar(k):
        return jnp.sum(jnp.where(lane == k, trust, 0.0), 1, keepdims=True)

    def update(weight, gradient, first_mom, second):
        first_new = 0.9 * first_mom + 0.1 * gradient
        second_new = 0.999 * second + 0.001 * gradient * gradient
        step = (
            first_new / first_fix / (jnp.sqrt(second_new / second_fix) + 1e-06)
            + decay_rate * weight
        )
        return first_new, second_new, step

    kg_out[...] = kg[...]
    gg_out[...] = gg[...]
    for k in range(2):
        kf_out[k], ks_out[k], step = update(kw[k], kg[k], kf[k], ks[k])
        kw_out[k] = kw[k] - step_rate * scalar(n_mats + k) * step
    first_new, second_new, step = update(gw[...], gg[...], gf[...], gs[...])
    gf_out[...] = first_new
    gs_out[...] = second_new
    row = lax.broadcasted_iota(jnp.int32, (4, 1), 0)
    rates = jnp.zeros((4, 1), fl_type)
    for k in range(4):
        rates = rates + jnp.where(row == k, scalar(n_mats + 2 + k), 0.0)
    gw_out[...] = gw[...] - step_rate * rates * step
    pix_width = iw.shape[0]
    row = (1, pix_width)
    in_grad = small[2:3, :pix_width]
    weight = iw[...].reshape(row)
    first_new, second_new, step = update(
        weight, in_grad, i_f[...].reshape(row), i_s[...].reshape(row)
    )
    in_trust = ratio(
        jnp.sum(weight * weight, 1, keepdims=True), jnp.sum(step * step, 1, keepdims=True)
    )
    ig_out[...] = in_grad.reshape(pix_width)
    if_out[...] = first_new.reshape(pix_width)
    is_out[...] = second_new.reshape(pix_width)
    iw_out[...] = (weight - step_rate * in_trust * step).reshape(pix_width)
    stores = []
    for k in range(n_mats):
        for copy in loads[k]:
            copy.wait()
        first_new, second_new, step = update(w_buf[k], g_buf[k], f_buf[k], s_buf[k])
        f_new[k] = first_new
        s_new[k] = second_new
        w_new[k] = w_buf[k] - step_rate * scalar(k) * step
        for n, (src, dst) in enumerate(
            ((g_buf, mg_out), (w_new, mw_out), (f_new, mf_out), (s_new, ms_out))
        ):
            copy = pltpu.make_async_copy(src.at[k], dst.at[k], out_sems.at[n, k])
            copy.start()
            stores.append(copy)
    for n in range(len(parts)):
        pix_copy(n, False).wait()
        pix_copy(n, True).start()
    for copy in stores + [pix_copy(n, True) for n in range(len(parts))]:
        copy.wait()


def lamb_call(args):
    n_mats = args[3].shape[0]
    vmem, hbm = pl.BlockSpec(memory_space=pltpu.VMEM), pl.BlockSpec(memory_space=pl.ANY)
    block, lat, pix, mats, kv, gains = args[:6]
    row = args[16]
    shape = jax.ShapeDtypeStruct

    def like(value):
        return shape(value.shape, value.dtype)

    out_shape = [like(v) for v in (block, lat, pix, mats, kv, gains, row)]
    out_shape += [like(mats)] * 3 + [like(kv)] * 3 + [like(gains)] * 3 + [like(row)] * 3
    return pl.pallas_call(
        functools.partial(lamb, n_mats),
        out_shape=out_shape,
        in_specs=[vmem] * 2 + [hbm] * 2 + [vmem] * 3 + [hbm] * 3 + [vmem] * 9,
        out_specs=[vmem] * 2 + [hbm] * 2 + [vmem] * 3 + [hbm] * 3 + [vmem] * 9,
        scratch_shapes=[pltpu.VMEM(mats.shape, fl_type)] * 7
        + [
            pltpu.VMEM(pix.shape, fl_type),
            pltpu.SemaphoreType.DMA((4, n_mats)),
            pltpu.SemaphoreType.DMA((4, n_mats)),
            pltpu.SemaphoreType.DMA((2, 4)),
        ],
        compiler_params=pltpu.CompilerParams(vmem_limit_bytes=62 * 2**20),
        name="lamb",
    )(*args)


def local(
    latents,
    pixels,
    pix_counts,
    cotangent,
    weight_mats,
    kv_weights,
    norm_gains,
    input_gain,
    mats_first,
    mats_second,
    kv_first,
    kv_second,
    gains_first,
    gains_second,
    input_first,
    input_second,
):
    pix_width = pixels.shape[2]
    model_width = latents.shape[2]
    own_width = weight_mats.shape[1]
    n_dp, n_z = lax.axis_size("dp"), lax.axis_size("z")
    gain_at = round_up(pix_width, 8)
    pad_width = round_up(gain_at + 8, 128)

    def turned(value):
        return jnp.swapaxes(value, 1, 2)

    kv_cols = turned(kv_weights)
    pix_turned = jnp.transpose(pixels, (2, 0, 1))
    gathers = own_width % 16 == 0 and n_dp == 4 and n_z % 2 == 0
    if gathers:
        weights = (weight_mats, kv_cols, norm_gains)
    else:
        extra = jnp.zeros((own_width, pad_width - gain_at - 4), fl_type)
        keys = [jnp.pad(kv_cols[0], ((0, 0), (0, gain_at - pix_width))), norm_gains.T, extra]
        values = jnp.pad(kv_cols[1], ((0, 0), (0, pad_width - pix_width)))
        both = jnp.stack(
            [
                jnp.concatenate([weight_mats[0]] + keys, 1),
                jnp.concatenate([weight_mats[1], values], 1),
            ]
        ).astype(bf_type)
        both = lax.all_gather(both, ALL, axis=1, tiled=True)
        others = lax.all_gather(weight_mats[2:].astype(bf_type), ALL, axis=1, tiled=True)
        weights = (both[0][None, None], both[1][None, None], others[:, None, None])
    (
        first_all, xn, pt, q_own, early, peak, qk, gains, block_rows, gk, stats, cross_rows, k_one, gterm,
        gain_cols,
    ) = forward_call(
        n_z, n_dp, gathers, *weights, pix_counts, pix_turned, latents, cotangent, input_gain
    )
    first_all = first_all.reshape(model_width, model_width + pad_width)
    summed = backward_call(
        n_z,
        n_dp,
        (
            gk,
            stats,
            early,
            block_rows,
            xn,
            pt,
            peak,
            qk,
            pix_turned,
            gain_cols,
            latents,
            first_all,
            gains,
            q_own,
            cross_rows,
            k_one,
            gterm,
            weight_mats,
            mats_first,
            mats_second,
            kv_cols,
            turned(kv_first),
            turned(kv_second),
            norm_gains,
            gains_first,
            gains_second,
        ),
    )
    outs = lamb_call(
        (
            *summed,
            weight_mats,
            mats_first,
            mats_second,
            kv_cols,
            turned(kv_first),
            turned(kv_second),
            norm_gains,
            gains_first,
            gains_second,
            input_gain,
            input_first,
            input_second,
        )
    )
    outs = list(outs)
    outs[2] = jnp.transpose(outs[2], (1, 2, 0))
    for index in (4, 10, 11, 12):
        outs[index] = turned(outs[index])
    return tuple(outs)


def solution(mesh):
    n_dp, n_rows = mesh.devices.shape
    split_mesh = Mesh(mesh.devices.reshape(n_dp, n_rows // 2, 2), ALL)
    rows = ("z", "core")
    items = P("dp", None, None)
    pix = P("dp", rows, None)
    mats = P(None, ALL, None)
    pairs = P(None, None, ALL)
    gains = P(None, ALL)
    in_specs = (
        items,
        pix,
        P("dp"),
        items,
        mats,
        pairs,
        gains,
        P(),
        mats,
        mats,
        pairs,
        pairs,
        gains,
        gains,
        P(),
        P(),
    )
    out_specs = (
        pix,
        pix,
        pix,
        mats,
        pairs,
        gains,
        P(),
        mats,
        mats,
        mats,
        pairs,
        pairs,
        pairs,
        gains,
        gains,
        gains,
        P(),
        P(),
        P(),
    )
    return jax.shard_map(
        local, mesh=split_mesh, in_specs=in_specs, out_specs=out_specs, check_vma=False
    )
```

```python
import functools
import math

import jax
import jax.numpy as jnp
from jax import lax
from jax.experimental import pallas as pl
from jax.experimental.pallas import tpu as pltpu
from jax.sharding import Mesh, PartitionSpec as P

HEADS = 8
first_fix = 1.0 - 0.9**10
second_fix = 1.0 - 0.999**10
step_rate = 0.25
decay_rate = 0.01
bf_type = jnp.bfloat16
fl_type = jnp.float32
ALL = ("dp", "z", "core")
NT = (((1,), (1,)), ((), ()))
TN = (((0,), (0,)), ((), ()))
NN = (((1,), (0,)), ((), ()))
MESH = pl.DeviceIdType.MESH
PIECES = ((2, 4), (4, 6), (6, 8), (8, 10))
LAST = 6


def dot(left_side, right_side, dims=NN):
    return lax.dot_general(left_side, right_side, dims, preferred_element_type=fl_type)


def round_up(value, unit):
    return -(-value // unit) * unit


def tile_of(rows, unit, most):
    best = unit
    for size in range(unit, most + 1, unit):
        if rows % size == 0:
            best = size
    return best


def meet(peers):
    barrier = pltpu.get_barrier_semaphore()
    for peer in peers:
        pl.semaphore_signal(barrier, inc=1, device_id=peer, device_id_type=MESH)
    pl.semaphore_wait(barrier, len(peers))


def lane_parts(total, size, body):
    def step(t, _):
        body(pl.multiple_of(t * size, size), size)
        return 0

    lax.fori_loop(0, total // size, step, 0)
    if total % size:
        body(total - total % size, total % size)


def remote(src, dst, sems, index, peer):
    return pltpu.make_async_remote_copy(
        src_ref=src,
        dst_ref=dst,
        send_sem=sems.at[0, index],
        recv_sem=sems.at[1, index],
        device_id=peer,
        device_id_type=MESH,
    )


class Gather:
    def __init__(self, whole, lead, sems, n_z):
        self.whole, self.lead, self.sems, self.n_z = whole, lead, sems, n_z
        self.d, self.z, self.c = (lax.axis_index(name) for name in ALL)
        self.z_from = [lax.rem(self.z + n_z - i, n_z) for i in range(n_z)]
        self.z_to = [lax.rem(self.z + i, n_z) for i in range(n_z)]
        self.across = (self.d, self.z, 1 - self.c)
        self.sent = []

    def region(self, flip, start, count, core):
        chips = pl.ds((self.d ^ flip) * self.n_z + start, count)
        return self.whole.at[(*self.lead, chips, core)]

    def copy(self, region, kind, index, peer):
        return pltpu.make_async_remote_copy(
            src_ref=region,
            dst_ref=region,
            send_sem=self.sems.at[0, kind, index],
            recv_sem=self.sems.at[1, kind, index],
            device_id=peer,
            device_id_type=MESH,
        )

    def send(self, region, kind, index, peer, count=1):
        self.copy(region, kind, index, peer).start()
        self.sent.append((kind, index, count))

    def arrived(self, region, kind, index):
        self.copy(region, kind, index, self.across).wait_recv()

    def start_z(self):
        mine = self.region(0, self.z, 1, self.c)
        for i in range(1, self.n_z):
            self.send(mine, 0, i, (self.d, self.z_to[i], self.c))

    def to_plane(self, region, index):
        self.send(region, 1, index, (self.d ^ 1, self.z, self.c))
        self.send(region, 2, index, (self.d ^ 2, self.z, self.c))

    def start_plane(self):
        self.to_plane(self.region(0, self.z, 1, self.c), 0)

    def relay_z(self):
        for i in range(1, self.n_z):
            region = self.region(0, self.z_from[i], 1, self.c)
            self.arrived(region, 0, i)
            self.to_plane(region, i)
        self.send(self.region(0, 0, self.n_z, self.c), 4, 0, self.across, self.n_z)

    def relay_plane(self):
        half = self.n_z // 2
        for kind, flip, onward, start in ((1, 1, 2, 0), (2, 2, 1, half)):
            for i in range(self.n_z):
                self.arrived(self.region(flip, self.z_from[i], 1, self.c), kind, i)
            region = self.region(flip, start, half, self.c)
            self.send(region, 3, kind - 1, (self.d ^ onward, self.z, self.c), half)
        for kind, flip in ((1, 1), (2, 2)):
            region = self.region(flip, 0, self.n_z, self.c)
            self.send(region, 4 + kind, 0, self.across, self.n_z)

    def relay_far(self):
        half = self.n_z // 2
        self.arrived(self.region(3, 0, half, self.c), 3, 0)
        self.arrived(self.region(3, half, half, self.c), 3, 1)
        self.send(self.region(3, 0, self.n_z, self.c), 7, 0, self.across, self.n_z)

    def finish(self):
        for flip in range(4):
            self.arrived(self.region(flip, 0, self.n_z, 1 - self.c), 4 + flip, 0)

    def drain(self):
        for kind, index, count in self.sent:
            self.copy(self.region(0, 0, count, self.c), kind, index, self.across).wait_send()


class Whole:
    def __init__(self, ref, low, high):
        self.ref, self.low, self.high = ref, low, high

    def __getitem__(self, _):
        return self.ref[..., self.low : self.high].reshape(-1, self.high - self.low)


def forward(n_z, n_dp, gathers, pix_width, chunk, *refs):
    counts, first_in, second_in, rest_in, pix_hbm, lat_hbm, cot_hbm, gain_ref = refs[:8]
    (
        first_out, xn_out, pt_out, q_out, early_out,
        peak_ref, qk_ref, gains_ref, block_ref, gk_both, stats_both, cross_ref, k_one_ref, gterm_ref,
        gain_cols, done_sum, done_far,
    ) = refs[8:25]
    (
        first_all, second_all, mats, px_tx, px_rx, st_tx, st_rx, px2_tx, px2_rx, st2_tx, st2_rx,
        fin_tx, mean_ref, stat_ref, col_sems, term_sems, local_sems,
    ) = refs[25:42]
    gather_sems = refs[42:]
    d, z, c = (lax.axis_index(name) for name in ALL)
    n_items, lat_len, width = lat_hbm.shape
    pix_dev, pad_width = xn_out.shape[1:]
    own = width // (n_dp * n_z * 2)
    held = chunk * n_z
    peers = [(d, lax.rem(z + i, n_z), c) for i in range(1, n_z)] + [(d, z, 1 - c)]
    if gathers:
        peers += [(d ^ 1, z, c), (d ^ 2, z, c)]
    local = iter(range(1000))

    def copy_here(src, dst):
        copy = pltpu.make_async_copy(src, dst, local_sems.at[next(local)])
        copy.start()
        return copy

    if gathers:
        first = Gather(first_all, (), gather_sems[0], n_z)
        rest = [Gather(second_all, (), gather_sems[1], n_z)]
        for index, (low, high) in enumerate(PIECES):
            rest.append(Gather(mats, (pl.ds(low - 2, high - low),), gather_sems[2 + index], n_z))
        ready = [(21, 30, 35, 38), (31, 42, 46, 50), (39, 49, 57, 59), (45, 60, 66, 72), (58, 71, 80, 88)]
        steps = []
        for piece, times in zip(rest, ready, strict=True):
            relays = (piece.relay_z, piece.relay_plane, piece.relay_far, piece.finish)
            steps += list(zip(times, relays, strict=True))
        steps.sort(key=lambda step: step[0])
        done = [0]

        def pump(time):
            while done[0] < len(steps) and steps[done[0]][0] <= time:
                steps[done[0]][1]()
                done[0] += 1

        def weight(k):
            piece = [n for n, (low, high) in enumerate(PIECES) if low <= k < high]
            pump(ready[piece[0] + 1 if piece else 0][3])
            return Whole(mats.at[k - 2] if piece else second_all, 0, width)

    else:
        loads = {0: copy_here(first_in, first_all), 1: copy_here(second_in, second_all)}
        for k in range(2, mats.shape[0] + 2):
            loads[k] = copy_here(rest_in.at[k - 2], mats.at[k - 2])

        def pump(time):
            pass

        def weight(k):
            if k in loads:
                loads.pop(k).wait()
            return Whole(mats.at[k - 2] if k > 1 else second_all, 0, width)

    def kt_one():
        weight(1)
        return Whole(second_all, width, width + pad_width)

    def column_copy(src, dst, index, peer):
        return remote(src, dst, col_sems, index, peer)

    def pixel_phase(pix, lat, xn, pt, s_buf, q_all, px_own, xt, turn, *own_bufs):
        l_pix, l_lat = copy_here(pix_hbm, pix), copy_here(lat_hbm, lat)
        if gathers:
            own_mats, own_cols = own_bufs
            l_own = copy_here(first_in, own_mats)
        turn[...] = jnp.zeros(turn.shape, fl_type)
        turn[0:1, :pix_width] = gain_ref[...].reshape(1, pix_width)
        gain_cols[...] = turn[...].T
        gain_col = gain_cols[:pix_width, :1]
        meet(peers)
        if gathers:
            me = d * n_z + z
            gain_at = round_up(pix_width, 8) - (pad_width - 128)
            turn[...] = jnp.zeros(turn.shape, fl_type)
            turn[gain_at : gain_at + 4, :own] = rest_in[...]
            l_own.wait()
            for k, whole in ((0, first_all), (1, second_all)):
                own_cols[...] = jnp.zeros(own_cols.shape, fl_type)
                own_cols[:, :pix_width] = second_in[k]
                if k == 0:
                    own_cols[:, pad_width - 128 :] += turn[:, :128].T[:own]
                whole[me, c, :, :width] = own_mats[k].astype(bf_type)
                whole[me, c, :, width:] = own_cols[...].astype(bf_type)
                if k == 0:
                    first.start_z()
                    first.start_plane()
            for k in range(mats.shape[0]):
                mats[k, me, c] = own_mats[k + 2].astype(bf_type)
            for piece in rest[:-1]:
                piece.start_z()
            for piece in rest[:2]:
                piece.start_plane()
        xt[...] = jnp.zeros(xt.shape, fl_type)
        rows = tile_of(pix_dev, 16, 256)
        tiles = pix_dev // rows

        def normalise(item):
            def part(start, size):
                values = pix[:, item, pl.ds(start, size)].astype(fl_type)
                centred = values - jnp.sum(values, 0, keepdims=True) * (1.0 / pix_width)
                var = jnp.sum(centred * centred, 0, keepdims=True) * (1.0 / pix_width)
                xt[:pix_width, :size] = centred * lax.rsqrt(var + 1e-05) * gain_col
                turned = round_up(size, 128)
                low = xt[:, :turned].T.astype(bf_type)
                xn[item, pl.ds(start, size), :] = low[:size]

            lane_parts(pix_dev, 256, part)

        l_pix.wait()
        normalise(0)
        if gathers:
            first.relay_z()
        for item in range(1, n_items):
            normalise(item)
        xn_copy = copy_here(xn, xn_out)
        if gathers:
            first.relay_plane()
            for piece in rest[2:]:
                piece.start_plane()
            first.relay_far()
            pump(21)
            first.finish()
        else:
            loads.pop(0).wait()
        first_copy = copy_here(first_all, first_out)
        l_lat.wait()
        gain_at = round_up(pix_width, 8) - (pad_width - 128)
        tail = Whole(first_all, width + pad_width - 128, width + pad_width)[...]
        tail = tail.astype(fl_type).T
        gains_ref[...] = tail[gain_at : gain_at + 8]
        lat_rows = tile_of(lat_len, 128, 256)
        for item in range(n_items):

            def queries(t, _, item=item):
                at = pl.ds(pl.multiple_of(t * lat_rows, lat_rows), lat_rows)
                values = lat[item, at, :].astype(fl_type)
                centred = values - jnp.mean(values, -1, keepdims=True)
                var = jnp.mean(centred * centred, -1, keepdims=True)
                normal = (centred * lax.rsqrt(var + 1e-05) * gains_ref[:1]).astype(bf_type)
                q_low = dot(normal, Whole(first_all, 0, width)[...]).astype(bf_type)
                q_all[item, at, :] = q_low
                raw = dot(q_low, Whole(first_all, width, width + pad_width)[...])
                qk_ref[item, :, at] = (raw * width**-0.5).T.astype(bf_type)
                return 0

            lax.fori_loop(0, lat_len // lat_rows, queries, 0)
            pump(31 + 3 * item)
        q_copy = copy_here(q_all.at[c], q_out)

        base = (z * 2 + c) * pix_dev
        for item in range(n_items):
            valid = counts[item] - base

            def score(t, most, item=item, valid=valid):
                at = pl.ds(pl.multiple_of(t * rows, rows), rows)
                values = dot(xn[item, at, :], qk_ref[item])
                place = lax.broadcasted_iota(jnp.int32, values.shape, 0) + t * rows
                values = jnp.where(place < valid, values, -1e30)
                s_buf[at, :] = values
                return jnp.maximum(most, jnp.max(values.reshape(rows // 8, 8, lat_len), 0))

            most = lax.fori_loop(0, tiles, score, jnp.full((8, lat_len), -1e30, fl_type))
            peak = jnp.max(most, 0, keepdims=True)
            pump(36 + 6 * item)

            def weigh(t, total, item=item, peak=peak):
                at = pl.ds(pl.multiple_of(t * rows, rows), rows)
                values = jnp.exp(s_buf[at, :] - peak)
                pt[item, at, :] = values.astype(bf_type)
                return total + jnp.sum(values.reshape(rows // 8, 8, lat_len), 0)

            total = lax.fori_loop(0, tiles, weigh, jnp.zeros((8, lat_len), fl_type))
            total = jnp.sum(total, 0, keepdims=True)
            peak_ref[item] = jnp.broadcast_to(peak, (8, lat_len))
            st_tx[item, :4] = jnp.broadcast_to(peak, (4, lat_len))
            st_tx[item, 4:] = jnp.broadcast_to(total, (4, lat_len))
            part = dot(xn[item], pt[item], TN)
            px_own[item, : part.shape[0]] = part
            if held > part.shape[0]:
                px_own[item, part.shape[0] :] = jnp.zeros((held - part.shape[0], lat_len), fl_type)
            px_tx[item] = px_own[item, :held].astype(bf_type)
            pump(39 + 5 * item)
        pt_copy = copy_here(pt, pt_out)
        pair = [
            column_copy(px_tx.at[1 - c], px_rx, 0, (d, z, 1 - c)),
            column_copy(st_tx.at[1 - c], st_rx, 1, (d, z, 1 - c)),
        ]
        for copy in pair:
            copy.start()
        for copy in pair:
            copy.wait()
        peak_own, peak_rx = st_tx[c, :1], st_rx[:1]
        peak = jnp.maximum(peak_own, peak_rx)
        scale_own, scale_rx = jnp.exp(peak_own - peak), jnp.exp(peak_rx - peak)
        st2_tx[:4] = jnp.broadcast_to(peak, (4, lat_len))
        st2_tx[4:] = jnp.broadcast_to(
            scale_own * st_tx[c, 4:5] + scale_rx * st_rx[4:5], (4, lat_len)
        )
        both = px_own[c, :held] * scale_own + px_rx[...].astype(fl_type) * scale_rx
        px2_tx[...] = both.astype(bf_type).reshape(n_z, chunk, lat_len)
        for copy in (xn_copy, first_copy, q_copy, pt_copy):
            copy.wait()

    own_bufs = []
    if gathers:
        own_bufs = [pltpu.VMEM(first_in.shape, fl_type), pltpu.VMEM((own, pad_width), fl_type)]
    pl.run_scoped(
        pixel_phase,
        pltpu.VMEM(pix_hbm.shape, bf_type),
        pltpu.VMEM(lat_hbm.shape, bf_type),
        pltpu.VMEM(xn_out.shape, bf_type),
        pltpu.VMEM(pt_out.shape, bf_type),
        pltpu.VMEM((pix_dev, lat_len), fl_type),
        pltpu.VMEM(lat_hbm.shape, bf_type),
        pltpu.VMEM((n_items, max(held, pad_width), lat_len), fl_type),
        pltpu.VMEM((pad_width, 256), fl_type),
        pltpu.VMEM((128, pad_width), fl_type),
        *own_bufs,
    )

    copies = []
    for i in range(1, n_z):
        to = lax.rem(z + i, n_z)
        copies.append(column_copy(px2_tx.at[to], px2_rx.at[z], 2 * i, (d, to, c)))
        copies.append(column_copy(st2_tx, st2_rx.at[z], 2 * i + 1, (d, to, c)))
    for copy in copies:
        copy.start()
    if gathers:
        rest[-1].start_z()
    pump(50)
    for copy in copies:
        copy.wait()
    pump(57)
    peak = st2_tx[:1]
    froms = [lax.rem(z + n_z - i, n_z) for i in range(1, n_z)]
    for other in froms:
        peak = jnp.maximum(peak, st2_rx[other, :1])
    scale = jnp.exp(st2_tx[:1] - peak)
    total = scale * st2_tx[4:5]
    mean = scale * px2_tx[z].astype(fl_type)
    for other in froms:
        scale = jnp.exp(st2_rx[other, :1] - peak)
        total = total + scale * st2_rx[other, 4:5]
        mean = mean + scale * px2_rx[other].astype(fl_type)
    stat_ref[:8] = jnp.broadcast_to(peak, (8, lat_len))
    stat_ref[8:] = jnp.broadcast_to(total, (8, lat_len))
    fin_tx[...] = (mean / total).astype(bf_type)
    own_rows = pl.ds(pl.multiple_of(z * chunk, chunk), chunk)
    copies = []
    for i in range(1, n_z):
        to = lax.rem(z + i, n_z)
        copies.append(column_copy(fin_tx, mean_ref.at[own_rows], 2 * n_z + i, (d, to, c)))
    for copy in copies:
        copy.start()
    pump(60)
    for copy in copies:
        copy.wait()
    mean_ref[own_rows] = fin_tx[...]
    if gathers:
        first.drain()

    def chain_phase(lat, cot, stage, *bufs):
        l_lat, l_cot = copy_here(lat_hbm.at[c], lat), copy_here(cot_hbm.at[c], cot)
        stages, lead = stage.shape[0], len(stage.shape) - 3
        put_sems = [next(local) for _ in range(stages)]
        order, pending, flying, far_flying = [], [], [None] * stages, []
        far = [lax.rem(d + i, n_dp) for i in range(1, n_dp)]

        def place(k):
            return first_all.at[pl.ds(2 * (k - 1 - LAST), 2), :, :, :width]

        def settle(k, buffer, copy):
            copy.wait()
            index = (lax.div(d, 2), lax.rem(d, 2))
            rows = pl.ds((k - 1 - LAST) * own, own)
            whole = place(k)
            mine = stage[(buffer, *index, c)].astype(fl_type) + whole[index].astype(fl_type)
            done_sum[rows, :] = mine
            both = stage[buffer, :, :, c].astype(fl_type) + whole[...].astype(fl_type)
            whole[...] = both.astype(bf_type)
            for n, to in enumerate(far):
                copy = remote(
                    whole.at[lax.div(to, 2), lax.rem(to, 2)],
                    done_far.at[d, rows],
                    term_sems,
                    8 + 3 * (k - 1 - LAST) + n,
                    (to, z, c),
                )
                copy.start()
                far_flying.append(copy)

        def put(k):
            while len(pending) > 1:
                settle(*pending.pop(0))
            buffer = len(order) % stages
            order.append(k)
            if flying[buffer] is not None:
                flying[buffer].wait()
                flying[buffer] = None
            if any(entry[1] == buffer for entry in pending):
                settle(*pending.pop(0))

            def start():
                if gathers and k > LAST:
                    source = stage.at[buffer, :, :, 1 - c]
                    copy = remote(source, place(k), term_sems, k - 1 - LAST, (d, z, 1 - c))
                    copy.start()
                    pending.append((k, buffer, copy))
                else:
                    at = (slice(None),) * lead + (pl.ds((k - 1) * own, own),)
                    copy = pltpu.make_async_copy(
                        stage.at[buffer], early_out.at[at], local_sems.at[put_sems[buffer]]
                    )
                    copy.start()
                    flying[buffer] = copy

            return stage.at[buffer], start

        outs = (
            put,
            block_ref,
            gk_both.at[c],
            stats_both.at[c],
            cross_ref,
            k_one_ref,
            gterm_ref,
        )
        l_lat.wait()
        l_cot.wait()
        latent_chain(
            n_z, n_dp, own, weight, kt_one, pump, lat, cot, gains_ref, mean_ref, stat_ref, outs, bufs
        )
        pair = [
            column_copy(gk_both.at[c], gk_both.at[c], 3 * n_z, (d, z, 1 - c)),
            column_copy(stats_both.at[c], stats_both.at[c], 3 * n_z + 1, (d, z, 1 - c)),
        ]
        for copy in pair:
            copy.start()
        while pending:
            settle(*pending.pop(0))
        for copy in [copy for copy in flying if copy is not None] + pair + far_flying:
            copy.wait()

    wire = early_out.dtype
    one_item = pltpu.VMEM((lat_len, width), bf_type)
    n_cols = n_dp * 2 * own
    pl.run_scoped(
        chain_phase,
        one_item,
        one_item,
        pltpu.VMEM((3, *early_out.shape[:-2], own, width), wire),
        *chain_bufs(lat_len, width, pad_width, n_cols),
    )
    if gathers:
        pump(1000)
        for piece in rest:
            piece.drain()


def forward_call(n_z, n_dp, gathers, first, second, rest, counts, pix_turned, latents, cotangent, gain):
    n_items, lat_len, width = latents.shape
    pix_width, _, pix_dev = pix_turned.shape
    own = width // (n_dp * n_z * 2)
    blocks = (n_dp * n_z, 2, own) if gathers else (1, 1, width)
    n_rest = 8
    pad_width = round_up(round_up(pix_width, 8) + 8, 128)
    wire = bf_type if own % 16 == 0 else fl_type
    chunk = round_up(-(-pix_width // n_z), 16)
    held = chunk * n_z
    z_share = lat_len // n_z
    n_cols = n_dp * 2 * own
    vmem, hbm = pl.BlockSpec(memory_space=pltpu.VMEM), pl.BlockSpec(memory_space=pl.ANY)
    shape, buf = jax.ShapeDtypeStruct, pltpu.VMEM
    out_shape = [
        shape((*blocks, width + pad_width), bf_type),
        shape((n_items, pix_dev, pad_width), bf_type),
        shape((n_items, pix_dev, lat_len), bf_type),
        shape((lat_len, width), bf_type),
        shape((2, 2, 2, LAST * own, width) if gathers else (n_dp, 2, 9 * own, width), wire),
        shape((n_items, 8, lat_len), fl_type),
        shape((n_items, pad_width, lat_len), bf_type),
        shape((8, width), fl_type),
        shape((2, z_share // 2, width), bf_type),
        shape((n_items, pad_width, lat_len), bf_type),
        shape((n_items, 3, 8, lat_len), fl_type),
        shape((z_share, width), fl_type),
        shape((n_cols, pad_width), fl_type),
        shape((8, width), fl_type),
        shape((pad_width, 128), fl_type),
        shape(((9 - LAST) * own, width), fl_type),
        shape((n_dp, (9 - LAST) * own, width), wire),
    ]
    scratch = [
        buf((*blocks, width + pad_width), bf_type),
        buf((*blocks, width + pad_width), bf_type),
        buf((n_rest, *blocks, width), bf_type),
        buf((n_items, held, lat_len), bf_type),
        buf((held, lat_len), bf_type),
        buf((n_items, 8, lat_len), fl_type),
        buf((8, lat_len), fl_type),
        buf((n_z, chunk, lat_len), bf_type),
        buf((n_z, chunk, lat_len), bf_type),
        buf((8, lat_len), fl_type),
        buf((n_z, 8, lat_len), fl_type),
        buf((chunk, lat_len), bf_type),
        buf((held, lat_len), bf_type),
        buf((16, lat_len), fl_type),
        pltpu.SemaphoreType.DMA((2, 3 * n_z + 2)),
        pltpu.SemaphoreType.DMA((2, 32)),
        pltpu.SemaphoreType.DMA((32,)),
    ]
    if gathers:
        scratch += [pltpu.SemaphoreType.DMA((2, 8, n_z))] * (2 + len(PIECES))
    weight_specs = [hbm, vmem, vmem] if gathers else [hbm] * 3
    return pl.pallas_call(
        functools.partial(forward, n_z, n_dp, gathers, pix_width, chunk),
        out_shape=out_shape,
        in_specs=[pl.BlockSpec(memory_space=pltpu.SMEM)] + weight_specs + [hbm] * 3 + [vmem],
        out_specs=[hbm] * 5 + [vmem] * 11 + [hbm],
        scratch_shapes=scratch,
        compiler_params=pltpu.CompilerParams(
            collective_id=0, has_side_effects=True, vmem_limit_bytes=62 * 2**20
        ),
        name="forward",
    )(counts, first, second, rest, pix_turned, latents, cotangent, gain)


def row_loop(total, body, rows=128):
    def step(t, _):
        body(pl.ds(pl.multiple_of(t * rows, rows), rows))
        return 0

    lax.fori_loop(0, total // rows, step, 0)


def tanh_gelu(values):
    factor, cubic = (2.0 / math.pi) ** 0.5, 0.044715
    square = values * values
    bent = jnp.tanh(factor * values * (1.0 + cubic * square))
    half = 0.5 * (1.0 + bent)
    slope = half + 0.5 * values * (1.0 - bent * bent) * factor * (1.0 + 3.0 * cubic * square)
    return values * half, slope


def choose(sel_ref, n_dp, n_z, pair_width):
    width, n_cols = sel_ref.shape
    z = lax.axis_index("z")
    wanted = lax.broadcasted_iota(jnp.int32, (width, n_cols), 1)
    wanted = (lax.div(wanted, pair_width) * n_z + z) * pair_width + lax.rem(wanted, pair_width)
    place = lax.broadcasted_iota(jnp.int32, (width, n_cols), 0)
    sel_ref[...] = jnp.where(place == wanted, 1.0, 0.0).astype(bf_type)


def latent_chain(n_z, n_dp, own, weight, kt_one, pump, lat, cot, gains, mean_ref, stat_ref, outs, bufs):
    put, block_ref, gk_ref, stats_ref, cross_ref, k_one_ref, gterm_ref = outs
    (
        run, x_buf, hat_c, hat_s, hat_f, inv, slope_c, slope_f,
        even, odd, q_s, k_s, v_s, probs, sel, mean_pad, picks,
    ) = bufs
    lat_len, width = lat.shape
    pad_width = mean_pad.shape[1]
    head_dim = width // HEADS
    z = lax.axis_index("z")
    z_share = lat_len // n_z
    z_rows = pl.ds(pl.multiple_of(z * z_share, z_share), z_share)
    choose(sel, n_dp, n_z, 2 * own)
    att = gelu_c = mixed = gelu_f = even
    norm_c = norm_s = norm_f = odd
    tmp = lat

    def add_norm(base, gain, hat, which, normal):
        def body(at):
            values = base(at) + x_buf[at, :]
            run[at, :] = values
            centred = values - jnp.mean(values, -1, keepdims=True)
            scale = lax.rsqrt(jnp.mean(centred * centred, -1, keepdims=True) + 1e-05)
            standard_values = centred * scale
            hat[at, :] = standard_values
            inv[which, at, :] = jnp.broadcast_to(scale, (scale.shape[0], 128))
            normal[at, :] = (standard_values * gains[gain : gain + 1]).astype(bf_type)

        row_loop(lat_len, body)

    def activate(slope, low):
        def body(at):
            value, grad = tanh_gelu(x_buf[at, :])
            low[at, :] = value.astype(bf_type)
            slope[at, :] = grad

        row_loop(lat_len, body)

    parts = lat_len // 128
    part_cols = width // parts

    def pick(n, ref):
        picks[n] = dot(ref[...], sel[...]).astype(bf_type)

    def terms(*wanted):
        staged = [(put(k), n, right) for k, n, right in wanted]

        def part(t):
            cols = pl.ds(pl.multiple_of(t * part_cols, part_cols), part_cols)
            for (buffer, _), n, right in staged:
                term = dot(picks[n], right[:, cols], TN).astype(buffer.dtype)
                buffer[..., cols] = term.reshape(*buffer.shape[:-1], part_cols)

        def send():
            for (_, start), _, _ in staged:
                start()

        return part, send

    def times_slope(slope, low, beside):
        def body(t, _):
            at = pl.ds(pl.multiple_of(t * 128, 128), 128)
            beside[0](t)
            low[at, :] = (x_buf[at, :] * slope[at, :]).astype(bf_type)
            return 0

        lax.fori_loop(0, parts, body, 0)
        beside[1]()

    def pull_norm(base, gain, hat, which, low, beside):
        def body(t, sums):
            at = pl.ds(pl.multiple_of(t * 128, 128), 128)
            beside[0](t)
            grad = x_buf[at, :]
            normal = hat[at, :]
            sums = sums + jnp.sum((normal * grad).reshape(16, 8, width), 0)
            grad = grad * gains[gain : gain + 1]
            mean = jnp.mean(grad, -1, keepdims=True)
            along = jnp.mean(grad * normal, -1, keepdims=True)
            value = base(at) + (grad - mean - normal * along) * inv[which, at, :1]
            run[at, :] = value
            low[at, :] = value.astype(bf_type)
            return sums

        sums = lax.fori_loop(0, parts, body, jnp.zeros((8, width), fl_type))
        beside[1]()
        gterm_ref[gain : gain + 1] = jnp.sum(sums, 0, keepdims=True)

    def matrix_term(k, n, right):
        buffer, start = put(k)
        buffer[...] = dot(picks[n], right[...], TN).astype(buffer.dtype).reshape(buffer.shape)
        start()

    def head(h):
        return slice(h * head_dim, (h + 1) * head_dim)

    head_scale = head_dim**-0.5
    gterm_ref[...] = jnp.zeros(gterm_ref.shape, fl_type)

    pump(65)
    mean_pad[...] = jnp.zeros(mean_pad.shape, bf_type)
    held = min(mean_ref.shape[0], pad_width)
    mean_pad[:, :held] = mean_ref[:held].astype(fl_type).T.astype(bf_type)
    att[...] = dot(mean_pad[...], kt_one()[...], NT).astype(bf_type)
    x_buf[...] = dot(att[...], weight(1)[...])
    pick(0, att)
    add_norm(lambda at: lat[at, :].astype(fl_type), 1, hat_c, 0, norm_c)
    pump(70)
    x_buf[...] = dot(norm_c[...], weight(2)[...])
    pick(1, norm_c)
    activate(slope_c, gelu_c)
    pump(73)
    x_buf[...] = dot(gelu_c[...], weight(3)[...])
    pick(2, gelu_c)
    add_norm(lambda at: run[at, :], 2, hat_s, 1, norm_s)
    pump(75)
    q_s[...] = dot(norm_s[...], weight(4)[...]).astype(bf_type)
    k_s[...] = dot(norm_s[...], weight(5)[...]).astype(bf_type)
    pump(77)
    v_s[...] = dot(norm_s[...], weight(6)[...]).astype(bf_type)
    pick(3, norm_s)

    def attend(h):
        at = head(h)
        scores = dot(k_s[:, at], q_s[:, at], NT) * head_scale
        weights = jnp.exp(scores - jnp.max(scores, 0, keepdims=True))
        weights = weights * (1.0 / jnp.sum(weights, 0, keepdims=True))
        low = weights.astype(bf_type)
        probs[h] = low
        mixed[:, at] = dot(low, v_s[:, at], TN).astype(bf_type)

    for h in range(HEADS):
        attend(h)
    pump(85)
    x_buf[...] = dot(mixed[...], weight(7)[...])
    pick(4, mixed)
    add_norm(lambda at: run[at, :], 3, hat_f, 2, norm_f)
    x_buf[...] = dot(norm_f[...], weight(8)[...])
    pick(5, norm_f)
    activate(slope_f, gelu_f)
    final = run[z_rows, :] + dot(gelu_f[z_rows, :], weight(9)[...])
    block_ref[...] = final.astype(bf_type).reshape(block_ref.shape)

    pick(6, gelu_f)

    x_buf[...] = dot(cot[...], weight(9)[...], NT)
    times_slope(slope_f, tmp, terms((9, 6, cot)))
    x_buf[...] = dot(tmp[...], weight(8)[...], NT)
    pull_norm(lambda at: cot[at, :].astype(fl_type), 3, hat_f, 2, odd, terms((8, 5, tmp)))
    grad_mixed = even
    grad_mixed[...] = dot(odd[...], weight(7)[...], NT).astype(bf_type)
    matrix_term(7, 4, odd)

    def attend_back(h):
        at = head(h)
        q_h, k_h, v_h, grad_h = q_s[:, at], k_s[:, at], v_s[:, at], grad_mixed[:, at]
        low = probs[h]
        weights = low.astype(fl_type)
        grad_weights = dot(v_h, grad_h, NT)
        along = jnp.sum(weights * grad_weights, 0, keepdims=True)
        grad_scores = (weights * (grad_weights - along)).astype(bf_type)
        q_s[:, at] = (dot(grad_scores, k_h, TN) * head_scale).astype(bf_type)
        k_s[:, at] = (dot(grad_scores, q_h) * head_scale).astype(bf_type)
        v_s[:, at] = dot(low, grad_h).astype(bf_type)

    for h in range(HEADS):
        attend_back(h)
    x_buf[...] = dot(q_s[...], weight(4)[...], NT)
    x_buf[...] += dot(k_s[...], weight(5)[...], NT)
    x_buf[...] += dot(v_s[...], weight(6)[...], NT)
    selves = terms((4, 3, q_s), (5, 3, k_s), (6, 3, v_s))
    pull_norm(lambda at: run[at, :], 2, hat_s, 1, tmp, selves)
    x_buf[...] = dot(tmp[...], weight(3)[...], NT)
    times_slope(slope_c, odd, terms((3, 2, tmp)))
    x_buf[...] = dot(odd[...], weight(2)[...], NT)
    pull_norm(lambda at: run[at, :], 1, hat_c, 0, tmp, terms((2, 1, odd)))
    grad_att = even
    grad_att[...] = dot(tmp[...], weight(1)[...], NT).astype(bf_type)
    matrix_term(1, 0, tmp)
    cross_ref[...] = run[z_rows, :]
    low = dot(grad_att[...], kt_one()[...]).T.astype(bf_type)
    gk_ref[...] = low
    delta = jnp.sum(low[:held].astype(fl_type) * mean_ref[:held].astype(fl_type), 0, keepdims=True)
    stats_ref[0] = stat_ref[:8]
    stats_ref[1] = stat_ref[8:]
    stats_ref[2] = jnp.broadcast_to(delta, stats_ref.shape[1:])
    k_one_ref[...] = dot(dot(grad_att[...], sel[...]).astype(bf_type), mean_pad[...], TN)


def chain_bufs(lat_len, width, pad_width, n_cols):
    wide = pltpu.VMEM((lat_len, width), fl_type)
    low = pltpu.VMEM((lat_len, width), bf_type)
    return (
        [wide] * 5
        + [pltpu.VMEM((3, lat_len, 128), fl_type)]
        + [wide] * 2
        + [low] * 5
        + [
            pltpu.VMEM((HEADS, lat_len, lat_len), bf_type),
            pltpu.VMEM((width, n_cols), bf_type),
            pltpu.VMEM((lat_len, pad_width), bf_type),
            pltpu.VMEM((7, lat_len, n_cols), bf_type),
        ]
    )


def backward(n_z, n_dp, pix_width, chunk, *refs):
    (
        gk_all,
        stats_all,
        early_ref,
        block_ref,
        xn_hbm,
        pt_hbm,
        peak_ref,
        qk_ref,
        pix_hbm,
        gain_ref,
        lat_hbm,
        first_hbm,
        gains_ref,
        q_hbm,
        cross_ref,
        k_one_ref,
        gterm_ref,
        done_sum_hbm,
        done_far_hbm,
        mats_hbm,
        mfirst_hbm,
        msecond_hbm,
        kv_ref,
        kfirst_ref,
        ksecond_ref,
        ng_ref,
        gfirst_ref,
        gsecond_ref,
        block_out,
        lat_out,
        pix_out,
        mats_out,
        kv_out,
        gains_out,
        small_out,
        xn,
        pt,
        pix,
        lat,
        first,
        q_own,
        mats,
        mfirst,
        msecond,
        ds,
        pl_low,
        part_tx,
        part_own,
        part_rx,
        col_tx,
        col_rx,
        fin_tx,
        fin_rx,
        dst_full,
        early_own,
        early_rx,
        early_tx,
        early_sum,
        early_far,
        done_sum,
        done_far,
        pix_buf,
        hat,
        inv,
        norm,
        dq,
        da,
        sel,
        lat_tx,
        late,
        late_rx,
        late_tx,
        late_own,
        late_far,
        small_tx,
        small_col,
        small_far_tx,
        small_far,
        input_acc,
        sems,
        loads,
    ) = refs
    d, z, c = (lax.axis_index(name) for name in ALL)
    oc = 1 - c
    n_items, pix_dev, pad_width = xn.shape
    gain_col = gain_ref[:pix_width, :1]
    lat_len, width = lat.shape[1:]
    own = kv_out.shape[1]
    far = [lax.rem(d + i, n_dp) for i in range(1, n_dp)]
    far_from = [lax.rem(d + n_dp - i, n_dp) for i in range(1, n_dp)]
    z_to = [lax.rem(z + i, n_z) for i in range(1, n_z)]
    z_from = [lax.rem(z + n_z - i, n_z) for i in range(1, n_z)]
    partner = (d, z, oc)
    column = [(i, 0) for i in range(1, n_z)] + [(i, 1) for i in range(n_z)]

    def in_column(i, j):
        return (d, lax.rem(z + i, n_z), lax.rem(c + j, 2))

    peers = [in_column(i, j) for i, j in column] + [(to, z, c) for to in far]
    barrier = pltpu.get_barrier_semaphore()
    for peer in peers:
        pl.semaphore_signal(barrier, inc=1, device_id=peer, device_id_type=MESH)

    slot = iter(range(1000))

    def send(src, dst, peer):
        copy = remote(src, dst, sems, next(slot), peer)
        copy.start()
        return copy

    load_slot = iter(range(1000))

    def load(src, dst):
        copy = pltpu.make_async_copy(src, dst, loads.at[next(load_slot)])
        copy.start()
        return copy

    l_xn = load(xn_hbm, xn)
    l_pt = load(pt_hbm, pt)
    l_pix = load(pix_hbm, pix)
    l_lat = load(lat_hbm.at[c], lat.at[0])
    l_first = load(first_hbm, first)
    l_q = load(q_hbm, q_own)
    l_early = load(early_ref.at[:, c], early_own)
    n_early = early_own.shape[1] // own
    l_done = []
    if n_early < mats.shape[0] - 1:
        l_done = [load(done_sum_hbm, done_sum), load(done_far_hbm, done_far)]
    l_mats = [load(mats_hbm, mats), load(mfirst_hbm, mfirst), load(msecond_hbm, msecond)]
    block_out[c] = block_ref[c]

    rows = tile_of(pix_dev, 16, 256)
    tiles = pix_dev // rows
    held = chunk * n_z
    l_pt.wait()
    l_xn.wait()

    def score_side(item):
        gk = gk_all.at[item]
        scale = jnp.exp(peak_ref[item, :1] - stats_all[item, 0, :1]) / stats_all[item, 1, :1]
        delta = stats_all[item, 2, :1]

        def body(t, _):
            at = pl.ds(pl.multiple_of(t * rows, rows), rows)
            probs = pt[item, at, :].astype(fl_type) * scale
            grad_probs = dot(xn[item, at, :], gk[...])
            ds[item, at, :] = (probs * (grad_probs - delta)).astype(bf_type)
            pl_low[item, at, :] = probs.astype(bf_type)
            return 0

        lax.fori_loop(0, tiles, body, 0)
        return dot(xn[item], ds[item], TN)

    part_tx[...] = score_side(oc)[: part_tx.shape[0]].astype(part_tx.dtype)
    pl.semaphore_wait(barrier, len(peers))
    px_pair = send(part_tx, part_rx, partner)
    out_pair = send(block_ref.at[oc], block_out.at[c], partner)
    early_pair = send(early_ref.at[:, oc], early_rx, partner)
    part_own[...] = score_side(c)
    px_pair.wait()
    both = part_own[: part_rx.shape[0]] + part_rx[...].astype(fl_type)
    if held > both.shape[0]:
        both = jnp.concatenate([both, jnp.zeros((held - both.shape[0], lat_len), fl_type)], 0)
    col_tx[...] = both[:held].astype(col_tx.dtype).reshape(n_z, chunk, lat_len)
    col = [send(col_tx.at[to], col_rx.at[z], (d, to, c)) for to in z_to]

    l_early.wait()
    early_pair.wait()

    def pair_sum(t, _):
        both = early_own[t].astype(fl_type) + early_rx[t].astype(fl_type)
        early_tx[t] = both.astype(early_tx.dtype)
        return 0

    lax.fori_loop(0, n_dp, pair_sum, 0)
    early_out = [send(early_tx.at[to], early_far.at[d], (to, z, c)) for to in far]
    early_sum[...] = early_own[d].astype(fl_type) + early_rx[d].astype(fl_type)

    l_pix.wait()
    input_acc[...] = jnp.zeros(input_acc.shape, fl_type)

    def pixel_side(item, gk):
        def part(start, size):
            at = pl.ds(start, size)
            grad = dot(qk_ref[item], ds[item, at, :], NT) + dot(gk[...], pl_low[item, at, :], NT)
            grad = grad[:pix_width]
            values = pix[:, item, at].astype(fl_type)
            centred = values - jnp.sum(values, 0, keepdims=True) * (1.0 / pix_width)
            var = jnp.sum(centred * centred, 0, keepdims=True) * (1.0 / pix_width)
            scale = lax.rsqrt(var + 1e-05)
            normal = centred * scale
            along = normal * grad
            for low in range(0, size, 128):
                high = min(low + 128, size)
                input_acc[:pix_width, : high - low] += along[:, low:high]
            grad = grad * gain_col
            mean = jnp.sum(grad, 0, keepdims=True) * (1.0 / pix_width)
            along = jnp.sum(grad * normal, 0, keepdims=True) * (1.0 / pix_width)
            pix_buf[:, item, at] = (grad - mean - normal * along) * scale

        lane_parts(pix_dev, 256, part)

    pixel_side(0, gk_all.at[0])

    for copy in col:
        copy.wait()
    mean = col_tx[z].astype(fl_type)
    for other in z_from:
        mean = mean + col_rx[other].astype(fl_type)
    fin_tx[...] = mean.astype(fin_tx.dtype)
    fin = [send(fin_tx, fin_rx.at[z], (d, to, c)) for to in z_to]

    pixel_side(1, gk_all.at[1])
    stores = [load(pix_buf, pix_out)]

    l_lat.wait()
    l_first.wait()
    l_q.wait()
    pair_width = 2 * own
    n_cols = n_dp * pair_width
    wanted = lax.broadcasted_iota(jnp.int32, (width, n_cols), 1)
    wanted = (lax.div(wanted, pair_width) * n_z + z) * pair_width + lax.rem(wanted, pair_width)
    place = lax.broadcasted_iota(jnp.int32, (width, n_cols), 0)
    sel[...] = jnp.where(place == wanted, 1.0, 0.0).astype(bf_type)
    values = lat[0].astype(fl_type)
    centred = values - jnp.mean(values, -1, keepdims=True)
    scale = lax.rsqrt(jnp.mean(centred * centred, -1, keepdims=True) + 1e-05)
    hat[...] = centred * scale
    inv[...] = jnp.broadcast_to(scale, inv.shape)
    norm[...] = dot((hat[...] * gains_ref[:1]).astype(bf_type), sel[...]).astype(bf_type)

    for copy in fin:
        copy.wait()
    dst_full[...] = jnp.zeros(dst_full.shape, fl_type)
    for other in z_from:
        dst_full[pl.ds(other * chunk, chunk)] = fin_rx[other].astype(fl_type)
    dst_full[pl.ds(z * chunk, chunk)] = fin_tx[...].astype(fl_type)
    summed = dst_full[:pad_width].T.astype(bf_type)
    kt_zero = first[:, width : width + pad_width]
    dq[...] = (dot(summed, kt_zero, NT) * width**-0.5).astype(bf_type)
    da[...] = dot(dq[...], first[:, :width], NT)
    term_zero = dot(norm[...], dq[...], TN)
    q_sel = dot(q_own[...], sel[...]).astype(bf_type)
    term_k = dot(q_sel, summed, TN) * width**-0.5
    gain_at = round_up(pix_width, 8) - (pad_width - 128)
    gain_zero = jnp.sum(hat[...] * da[...], 0, keepdims=True)
    place = lax.broadcasted_iota(jnp.int32, (8, width), 0)
    gain_sums = jnp.where(place == 0, gain_zero, gterm_ref[...]).astype(bf_type)
    gain_cols = dot(gain_sums, sel[...])
    gain_cols = jnp.concatenate(
        [
            jnp.zeros((gain_at, n_cols), fl_type),
            gain_cols,
            jnp.zeros((128 - gain_at - 8, n_cols), fl_type),
        ],
        0,
    ).T
    late[:, :, :, :width] = term_zero.astype(late.dtype).reshape(n_dp, 2, own, width)
    late[:, :, :, width : width + pad_width] = term_k.astype(late.dtype).reshape(
        n_dp, 2, own, pad_width
    )
    ones = k_one_ref[...]
    late[:, :, :, width + pad_width : width + 2 * pad_width - 128] = (
        ones[:, : pad_width - 128].astype(late.dtype).reshape(n_dp, 2, own, pad_width - 128)
    )
    late[:, :, :, width + 2 * pad_width - 128 :] = (
        (ones[:, pad_width - 128 :] + gain_cols).astype(late.dtype).reshape(n_dp, 2, own, 128)
    )
    late_pair = send(late.at[:, oc], late_rx, partner)

    z_share = lat_len // n_z
    at = pl.ds(pl.multiple_of(z * z_share, z_share), z_share)
    grad = da[at, :] * gains_ref[:1]
    normal = hat[at, :]
    mean = jnp.mean(grad, -1, keepdims=True)
    along = jnp.mean(grad * normal, -1, keepdims=True)
    lat_grad = cross_ref[...] + (grad - mean - normal * along) * inv[at, :1]
    lat_tx[...] = lat_grad.reshape(2, z_share // 2, width)
    lat_pair = send(lat_tx.at[oc], lat_out.at[c], partner)
    lat_out[c] = lat_tx[c]

    late_pair.wait()
    late_sum = late[:, c].astype(fl_type) + late_rx[...].astype(fl_type)
    late_tx[...] = late_sum.astype(late_tx.dtype)
    late_out = [send(late_tx.at[to], late_far.at[d], (to, z, c)) for to in far]
    late_own[...] = late[d, c].astype(fl_type) + late_rx[d].astype(fl_type)

    for copy in early_out:
        copy.wait()
    for copy in l_mats + l_done:
        copy.wait()
    lane = lax.broadcasted_iota(jnp.int32, (1, 128), 1)

    def norms(weight, gradient, first_mom, second):
        first_new = 0.9 * first_mom + 0.1 * gradient
        second_new = 0.999 * second + 0.001 * gradient * gradient
        update = (
            first_new / first_fix / (jnp.sqrt(second_new / second_fix) + 1e-06)
            + decay_rate * weight
        )
        return (weight * weight, update * update)

    def total(values):
        return jnp.sum(jnp.sum(values, 0, keepdims=True), 1, keepdims=True)

    def matrix(k, sums, early=True):
        if early:
            at = pl.ds(pl.multiple_of((k - 1) * own, own), own)
            mine, others = early_sum, early_far
        else:
            at = pl.ds(pl.multiple_of((k - 1 - n_early) * own, own), own)
            mine, others = done_sum, done_far
        gradient = mine[at, :]
        for other in far_from:
            gradient = gradient + others[other, at, :].astype(fl_type)
        mats_out[k] = gradient
        w_sq, u_sq = norms(mats[k], gradient, mfirst[k], msecond[k])
        here = lane == k
        return (
            sums[0] + jnp.where(here, total(w_sq), 0.0),
            sums[1] + jnp.where(here, total(u_sq), 0.0),
        )

    zero = jnp.zeros((1, 128), fl_type)
    sums = lax.fori_loop(1, 1 + n_early, matrix, (zero, zero))
    if n_early < mats.shape[0] - 1:
        late_matrix = functools.partial(matrix, early=False)
        sums = lax.fori_loop(1 + n_early, mats.shape[0], late_matrix, sums)

    for copy in late_out:
        copy.wait()
    for other in far_from:
        late_own[...] += late_far[other].astype(fl_type)
    mats_out[0] = late_own[:, :width]
    grads = [(mats[0], late_own[:, :width], mfirst[0], msecond[0], 0)]
    for k in range(2):
        cols = late_own[:, width + k * pad_width : width + k * pad_width + pix_width]
        kv_out[k] = cols
        grads.append((kv_ref[k], cols, kfirst_ref[k], ksecond_ref[k], 10 + k))
    gain_grad = late_own[:, width + 2 * pad_width - 128 :].T[gain_at : gain_at + 8]
    gains_out[...] = gain_grad[:4]
    w_sum, u_sum = sums
    for weight, gradient, first_mom, second, k in grads:
        w_sq, u_sq = norms(weight, gradient, first_mom, second)
        w_sum = w_sum + jnp.where(lane == k, total(w_sq), 0.0)
        u_sum = u_sum + jnp.where(lane == k, total(u_sq), 0.0)
    w_sq, u_sq = norms(ng_ref[...], gain_grad[:4], gfirst_ref[...], gsecond_ref[...])
    w_sq, u_sq = jnp.sum(w_sq, 1, keepdims=True), jnp.sum(u_sq, 1, keepdims=True)
    for k in range(4):
        w_sum = w_sum + jnp.where(lane == 12 + k, w_sq[k : k + 1], 0.0)
        u_sum = u_sum + jnp.where(lane == 12 + k, u_sq[k : k + 1], 0.0)
    small_tx[...] = jnp.zeros(small_tx.shape, fl_type)
    small_tx[0:1] = w_sum
    small_tx[1:2] = u_sum
    input_row = jnp.sum(input_acc[...].T, 0, keepdims=True)
    for n in range(pad_width // 128):
        small_tx[2 + n : 3 + n] = input_row[:, n * 128 : (n + 1) * 128]
    copies = [
        send(small_tx, small_col.at[n], in_column(i, j)) for n, (i, j) in enumerate(column)
    ]
    for copy in copies:
        copy.wait()
    all_sum = small_tx[...]
    for n in range(len(column)):
        all_sum = all_sum + small_col[n]
    small_far_tx[...] = all_sum
    copies = [
        send(small_far_tx, small_far.at[n], (to, z, c)) for n, to in enumerate(far)
    ]
    for copy in copies:
        copy.wait()
    for n in range(len(far)):
        all_sum = all_sum + small_far[n]
    small_out[...] = all_sum
    for copy in [out_pair, lat_pair] + stores:
        copy.wait()


def backward_call(n_z, n_dp, args):
    (gk, stats, early, _, xn, pt, _, _, pixels, _, latents, first) = args[:12]
    mats, kv, gains = args[19], args[22], args[25]
    pix_width = pixels.shape[0]
    n_items, lat_len, width = latents.shape
    own = mats.shape[1]
    pad_width = xn.shape[2]
    early_rows = early.shape[2]
    wire = early.dtype
    chunk = round_up(-(-pix_width // n_z), 16)
    held = chunk * n_z
    cut = min(held, pad_width)
    z_share = lat_len // n_z
    n_cols = n_dp * 2 * own
    vmem, hbm = pl.BlockSpec(memory_space=pltpu.VMEM), pl.BlockSpec(memory_space=pl.ANY)
    places = {2, 4, 5, 8, 10, 11, 13, 17, 18, 19, 20, 21}
    in_specs = [hbm if index in places else vmem for index in range(len(args))]
    shape, buf = jax.ShapeDtypeStruct, pltpu.VMEM
    out_shape = [
        shape((n_items, z_share // 2, width), bf_type),
        shape((n_items, z_share // 2, width), fl_type),
        shape(pixels.shape, fl_type),
        shape(mats.shape, fl_type),
        shape(kv.shape, fl_type),
        shape(gains.shape, fl_type),
        shape((8, 128), fl_type),
    ]
    out_specs = [vmem, vmem, hbm, vmem, vmem, vmem, vmem]
    late_width = width + 2 * pad_width
    scratch = [
        buf(xn.shape, bf_type),
        buf(pt.shape, bf_type),
        buf(pixels.shape, bf_type),
        buf((1, lat_len, width), bf_type),
        buf(first.shape, bf_type),
        buf((lat_len, width), bf_type),
        buf(mats.shape, fl_type),
        buf(mats.shape, fl_type),
        buf(mats.shape, fl_type),
        buf(pt.shape, bf_type),
        buf(pt.shape, bf_type),
        buf((cut, lat_len), bf_type),
        buf((pad_width, lat_len), fl_type),
        buf((cut, lat_len), bf_type),
        buf((n_z, chunk, lat_len), bf_type),
        buf((n_z, chunk, lat_len), bf_type),
        buf((chunk, lat_len), bf_type),
        buf((n_z, chunk, lat_len), bf_type),
        buf((max(held, pad_width), lat_len), fl_type),
        buf((n_dp, early_rows, width), wire),
        buf((n_dp, early_rows, width), wire),
        buf((n_dp, early_rows, width), wire),
        buf((early_rows, width), fl_type),
        buf((n_dp, early_rows, width), wire),
        buf(args[17].shape, fl_type),
        buf(args[18].shape, wire),
        buf(pixels.shape, fl_type),
        buf((lat_len, width), fl_type),
        buf((lat_len, 128), fl_type),
        buf((lat_len, n_cols), bf_type),
        buf((lat_len, width), bf_type),
        buf((lat_len, width), fl_type),
        buf((width, n_cols), bf_type),
        buf((2, z_share // 2, width), fl_type),
        buf((n_dp, 2, own, late_width), wire),
        buf((n_dp, own, late_width), wire),
        buf((n_dp, own, late_width), wire),
        buf((own, late_width), fl_type),
        buf((n_dp, own, late_width), wire),
        buf((8, 128), fl_type),
        buf((2 * n_z - 1, 8, 128), fl_type),
        buf((8, 128), fl_type),
        buf((n_dp - 1, 8, 128), fl_type),
        buf((pad_width, 128), fl_type),
        pltpu.SemaphoreType.DMA((2, 20 + 6 * n_z + 3 * n_dp)),
        pltpu.SemaphoreType.DMA((16,)),
    ]
    return pl.pallas_call(
        functools.partial(backward, n_z, n_dp, pix_width, chunk),
        out_shape=out_shape,
        in_specs=in_specs,
        out_specs=out_specs,
        scratch_shapes=scratch,
        compiler_params=pltpu.CompilerParams(
            collective_id=1, has_side_effects=True, vmem_limit_bytes=60 * 2**20
        ),
        name="backward",
    )(*args)


def lamb(n_mats, *refs):
    (
        block_in, lat_in, pix_in, mg, kg, gg, small, mw, mf, ms, kw, kf, ks, gw, gf, gs, iw, i_f, i_s,
        block_out, lat_out, pix_out, mg_out, kg_out, gg_out, ig_out,
        mw_out, mf_out, ms_out, kw_out, kf_out, ks_out, gw_out, gf_out, gs_out, iw_out, if_out, is_out,
        g_buf, w_buf, f_buf, s_buf, w_new, f_new, s_new, pix_buf, in_sems, out_sems, pix_sems,
    ) = refs
    spans = [(low, min(low + 2, n_mats)) for low in range(0, n_mats, 2)]
    loads = []
    for k, (low, high) in enumerate(spans):
        loads.append(
            [
                pltpu.make_async_copy(src.at[low:high], dst.at[low:high], in_sems.at[n, k])
                for n, (src, dst) in enumerate(
                    ((mg, g_buf), (mw, w_buf), (mf, f_buf), (ms, s_buf))
                )
            ]
        )
        for copy in loads[-1]:
            copy.start()
    parts = [(low, min(low + 88, pix_in.shape[0])) for low in range(0, pix_in.shape[0], 88)]

    def pix_copy(n, back):
        low, high = parts[n]
        src, dst = pix_in.at[low:high], pix_buf.at[low:high]
        if back:
            src, dst = dst, pix_out.at[low:high]
        return pltpu.make_async_copy(src, dst, pix_sems.at[int(back), n])

    for n in range(len(parts)):
        pix_copy(n, False).start()
    block_out[...] = block_in[...]
    lat_out[...] = lat_in[...]
    lane = lax.broadcasted_iota(jnp.int32, (1, 128), 1)

    def ratio(w_sq, u_sq):
        return jnp.sqrt(w_sq) / (jnp.sqrt(u_sq) + 1e-06)

    trust = ratio(small[0:1], small[1:2])

    def scalar(k):
        return jnp.sum(jnp.where(lane == k, trust, 0.0), 1, keepdims=True)

    def update(weight, gradient, first_mom, second):
        first_new = 0.9 * first_mom + 0.1 * gradient
        second_new = 0.999 * second + 0.001 * gradient * gradient
        step = (
            first_new / first_fix / (jnp.sqrt(second_new / second_fix) + 1e-06)
            + decay_rate * weight
        )
        return first_new, second_new, step

    kg_out[...] = kg[...]
    gg_out[...] = gg[...]
    for k in range(2):
        kf_out[k], ks_out[k], step = update(kw[k], kg[k], kf[k], ks[k])
        kw_out[k] = kw[k] - step_rate * scalar(n_mats + k) * step
    first_new, second_new, step = update(gw[...], gg[...], gf[...], gs[...])
    gf_out[...] = first_new
    gs_out[...] = second_new
    row = lax.broadcasted_iota(jnp.int32, (4, 1), 0)
    rates = jnp.zeros((4, 1), fl_type)
    for k in range(4):
        rates = rates + jnp.where(row == k, scalar(n_mats + 2 + k), 0.0)
    gw_out[...] = gw[...] - step_rate * rates * step
    pix_width = iw.shape[0]
    row = (1, pix_width)
    rows = [small[n : n + 1] for n in range(2, 2 + -(-pix_width // 128))]
    in_grad = jnp.concatenate(rows, 1)[:, :pix_width]
    weight = iw[...].reshape(row)
    first_new, second_new, step = update(
        weight, in_grad, i_f[...].reshape(row), i_s[...].reshape(row)
    )
    in_trust = ratio(
        jnp.sum(weight * weight, 1, keepdims=True), jnp.sum(step * step, 1, keepdims=True)
    )
    ig_out[...] = in_grad.reshape(pix_width)
    if_out[...] = first_new.reshape(pix_width)
    is_out[...] = second_new.reshape(pix_width)
    iw_out[...] = (weight - step_rate * in_trust * step).reshape(pix_width)
    stores = []
    for n_span, (low, high) in enumerate(spans):
        for copy in loads[n_span]:
            copy.wait()
        for k in range(low, high):
            first_new, second_new, step = update(w_buf[k], g_buf[k], f_buf[k], s_buf[k])
            f_new[k] = first_new
            s_new[k] = second_new
            w_new[k] = w_buf[k] - step_rate * scalar(k) * step
        for n, (src, dst) in enumerate(
            ((g_buf, mg_out), (w_new, mw_out), (f_new, mf_out), (s_new, ms_out))
        ):
            copy = pltpu.make_async_copy(
                src.at[low:high], dst.at[low:high], out_sems.at[n, n_span]
            )
            copy.start()
            stores.append(copy)
    for n in range(len(parts)):
        pix_copy(n, False).wait()
        pix_copy(n, True).start()
    for copy in stores + [pix_copy(n, True) for n in range(len(parts))]:
        copy.wait()


def lamb_call(args):
    n_mats = args[3].shape[0]
    vmem, hbm = pl.BlockSpec(memory_space=pltpu.VMEM), pl.BlockSpec(memory_space=pl.ANY)
    block, lat, pix, mats, kv, gains = args[:6]
    row = args[16]
    shape = jax.ShapeDtypeStruct

    def like(value):
        return shape(value.shape, value.dtype)

    out_shape = [like(v) for v in (block, lat, pix, mats, kv, gains, row)]
    out_shape += [like(mats)] * 3 + [like(kv)] * 3 + [like(gains)] * 3 + [like(row)] * 3
    return pl.pallas_call(
        functools.partial(lamb, n_mats),
        out_shape=out_shape,
        in_specs=[vmem] * 2 + [hbm] * 2 + [vmem] * 3 + [hbm] * 3 + [vmem] * 9,
        out_specs=[vmem] * 2 + [hbm] * 2 + [vmem] * 3 + [hbm] * 3 + [vmem] * 9,
        scratch_shapes=[pltpu.VMEM(mats.shape, fl_type)] * 7
        + [
            pltpu.VMEM(pix.shape, fl_type),
            pltpu.SemaphoreType.DMA((4, n_mats)),
            pltpu.SemaphoreType.DMA((4, n_mats)),
            pltpu.SemaphoreType.DMA((2, 4)),
        ],
        compiler_params=pltpu.CompilerParams(vmem_limit_bytes=62 * 2**20),
        name="lamb",
    )(*args)


def local(
    latents,
    pixels,
    pix_counts,
    cotangent,
    weight_mats,
    kv_weights,
    norm_gains,
    input_gain,
    mats_first,
    mats_second,
    kv_first,
    kv_second,
    gains_first,
    gains_second,
    input_first,
    input_second,
):
    pix_width = pixels.shape[2]
    model_width = latents.shape[2]
    own_width = weight_mats.shape[1]
    n_dp, n_z = lax.axis_size("dp"), lax.axis_size("z")
    gain_at = round_up(pix_width, 8)
    pad_width = round_up(gain_at + 8, 128)

    def turned(value):
        return jnp.swapaxes(value, 1, 2)

    kv_cols = turned(kv_weights)
    pix_turned = jnp.transpose(pixels, (2, 0, 1))
    gathers = own_width % 16 == 0 and n_dp == 4 and n_z % 2 == 0 and n_z >= 4
    if gathers:
        weights = (weight_mats, kv_cols, norm_gains)
    else:
        extra = jnp.zeros((own_width, pad_width - gain_at - 4), fl_type)
        keys = [jnp.pad(kv_cols[0], ((0, 0), (0, gain_at - pix_width))), norm_gains.T, extra]
        values = jnp.pad(kv_cols[1], ((0, 0), (0, pad_width - pix_width)))
        both = jnp.stack(
            [
                jnp.concatenate([weight_mats[0]] + keys, 1),
                jnp.concatenate([weight_mats[1], values], 1),
            ]
        ).astype(bf_type)
        both = lax.all_gather(both, ALL, axis=1, tiled=True)
        others = lax.all_gather(weight_mats[2:].astype(bf_type), ALL, axis=1, tiled=True)
        weights = (both[0][None, None], both[1][None, None], others[:, None, None])
    (
        first_all, xn, pt, q_own, early, peak, qk, gains, block_rows, gk, stats, cross_rows, k_one, gterm,
        gain_cols, done_sum, done_far,
    ) = forward_call(
        n_z, n_dp, gathers, *weights, pix_counts, pix_turned, latents, cotangent, input_gain
    )
    first_all = first_all.reshape(model_width, model_width + pad_width)
    early = early.reshape(n_dp, 2, -1, model_width)
    summed = backward_call(
        n_z,
        n_dp,
        (
            gk,
            stats,
            early,
            block_rows,
            xn,
            pt,
            peak,
            qk,
            pix_turned,
            gain_cols,
            latents,
            first_all,
            gains,
            q_own,
            cross_rows,
            k_one,
            gterm,
            done_sum,
            done_far,
            weight_mats,
            mats_first,
            mats_second,
            kv_cols,
            turned(kv_first),
            turned(kv_second),
            norm_gains,
            gains_first,
            gains_second,
        ),
    )
    outs = lamb_call(
        (
            *summed,
            weight_mats,
            mats_first,
            mats_second,
            kv_cols,
            turned(kv_first),
            turned(kv_second),
            norm_gains,
            gains_first,
            gains_second,
            input_gain,
            input_first,
            input_second,
        )
    )
    outs = list(outs)
    outs[2] = jnp.transpose(outs[2], (1, 2, 0))
    for index in (4, 10, 11, 12):
        outs[index] = turned(outs[index])
    return tuple(outs)


def solution(mesh):
    n_dp, n_rows = mesh.devices.shape
    split_mesh = Mesh(mesh.devices.reshape(n_dp, n_rows // 2, 2), ALL)
    rows = ("z", "core")
    items = P("dp", None, None)
    pix = P("dp", rows, None)
    mats = P(None, ALL, None)
    pairs = P(None, None, ALL)
    gains = P(None, ALL)
    in_specs = (
        items,
        pix,
        P("dp"),
        items,
        mats,
        pairs,
        gains,
        P(),
        mats,
        mats,
        pairs,
        pairs,
        gains,
        gains,
        P(),
        P(),
    )
    out_specs = (
        pix,
        pix,
        pix,
        mats,
        pairs,
        gains,
        P(),
        mats,
        mats,
        mats,
        pairs,
        pairs,
        pairs,
        gains,
        gains,
        gains,
        P(),
        P(),
        P(),
    )
    return jax.shard_map(
        local, mesh=split_mesh, in_specs=in_specs, out_specs=out_specs, check_vma=False
    )
```

```python
import functools
import math

import jax
import jax.numpy as jnp
from jax import lax
from jax.experimental import pallas as pl
from jax.experimental.pallas import tpu as pltpu
from jax.sharding import Mesh, PartitionSpec as P

HEADS = 8
first_fix = 1.0 - 0.9**10
second_fix = 1.0 - 0.999**10
step_rate = 0.25
decay_rate = 0.01
bf_type = jnp.bfloat16
fl_type = jnp.float32
ALL = ("dp", "z", "core")
NT = (((1,), (1,)), ((), ()))
TN = (((0,), (0,)), ((), ()))
NN = (((1,), (0,)), ((), ()))
MESH = pl.DeviceIdType.MESH
PIECES = ((2, 4), (4, 6), (6, 8), (8, 10))
LAST = 6


def dot(left_side, right_side, dims=NN):
    return lax.dot_general(left_side, right_side, dims, preferred_element_type=fl_type)


def round_up(value, unit):
    return -(-value // unit) * unit


def tile_of(rows, unit, most):
    best = unit
    for size in range(unit, most + 1, unit):
        if rows % size == 0:
            best = size
    return best


def meet(peers):
    barrier = pltpu.get_barrier_semaphore()
    for peer in peers:
        pl.semaphore_signal(barrier, inc=1, device_id=peer, device_id_type=MESH)
    pl.semaphore_wait(barrier, len(peers))


def lane_parts(total, size, body):
    def step(t, _):
        body(pl.multiple_of(t * size, size), size)
        return 0

    lax.fori_loop(0, total // size, step, 0)
    if total % size:
        body(total - total % size, total % size)


def remote(src, dst, sems, index, peer):
    return pltpu.make_async_remote_copy(
        src_ref=src,
        dst_ref=dst,
        send_sem=sems.at[0, index],
        recv_sem=sems.at[1, index],
        device_id=peer,
        device_id_type=MESH,
    )


class Gather:
    def __init__(self, whole, lead, sems, n_z):
        self.whole, self.lead, self.sems, self.n_z = whole, lead, sems, n_z
        self.d, self.z, self.c = (lax.axis_index(name) for name in ALL)
        self.z_from = [lax.rem(self.z + n_z - i, n_z) for i in range(n_z)]
        self.z_to = [lax.rem(self.z + i, n_z) for i in range(n_z)]
        self.across = (self.d, self.z, 1 - self.c)
        self.sent = []

    def region(self, flip, start, count, core):
        chips = pl.ds((self.d ^ flip) * self.n_z + start, count)
        return self.whole.at[(*self.lead, chips, core)]

    def copy(self, region, kind, index, peer):
        return pltpu.make_async_remote_copy(
            src_ref=region,
            dst_ref=region,
            send_sem=self.sems.at[0, kind, index],
            recv_sem=self.sems.at[1, kind, index],
            device_id=peer,
            device_id_type=MESH,
        )

    def send(self, region, kind, index, peer, count=1):
        self.copy(region, kind, index, peer).start()
        self.sent.append((kind, index, count))

    def arrived(self, region, kind, index):
        self.copy(region, kind, index, self.across).wait_recv()

    def start_z(self):
        mine = self.region(0, self.z, 1, self.c)
        for i in range(1, self.n_z):
            self.send(mine, 0, i, (self.d, self.z_to[i], self.c))

    def to_plane(self, region, index):
        self.send(region, 1, index, (self.d ^ 1, self.z, self.c))
        self.send(region, 2, index, (self.d ^ 2, self.z, self.c))

    def start_plane(self):
        self.to_plane(self.region(0, self.z, 1, self.c), 0)

    def relay_z(self):
        for i in range(1, self.n_z):
            region = self.region(0, self.z_from[i], 1, self.c)
            self.arrived(region, 0, i)
            self.to_plane(region, i)
        self.send(self.region(0, 0, self.n_z, self.c), 4, 0, self.across, self.n_z)

    def relay_plane(self):
        half = self.n_z // 2
        for kind, flip, onward, start in ((1, 1, 2, 0), (2, 2, 1, half)):
            for i in range(self.n_z):
                self.arrived(self.region(flip, self.z_from[i], 1, self.c), kind, i)
            region = self.region(flip, start, half, self.c)
            self.send(region, 3, kind - 1, (self.d ^ onward, self.z, self.c), half)
        for kind, flip in ((1, 1), (2, 2)):
            region = self.region(flip, 0, self.n_z, self.c)
            self.send(region, 4 + kind, 0, self.across, self.n_z)

    def relay_far(self):
        half = self.n_z // 2
        self.arrived(self.region(3, 0, half, self.c), 3, 0)
        self.arrived(self.region(3, half, half, self.c), 3, 1)
        self.send(self.region(3, 0, self.n_z, self.c), 7, 0, self.across, self.n_z)

    def finish(self):
        for flip in range(4):
            self.arrived(self.region(flip, 0, self.n_z, 1 - self.c), 4 + flip, 0)

    def drain(self):
        for kind, index, count in self.sent:
            self.copy(self.region(0, 0, count, self.c), kind, index, self.across).wait_send()


class Whole:
    def __init__(self, ref, low, high):
        self.ref, self.low, self.high = ref, low, high

    def __getitem__(self, _):
        return self.ref[..., self.low : self.high].reshape(-1, self.high - self.low)


def forward(n_z, n_dp, gathers, pix_width, chunk, *refs):
    counts, first_in, second_in, rest_in, pix_hbm, lat_hbm, cot_hbm, gain_ref = refs[:8]
    (
        first_out, xn_out, pt_out, q_out, early_out,
        peak_ref, qk_ref, gains_ref, block_ref, gk_both, stats_both, cross_ref, k_one_ref, gterm_ref,
        gain_cols, done_sum, done_far,
    ) = refs[8:25]
    (
        first_all, second_all, mats, px_tx, px_rx, st_tx, st_rx, px2_tx, px2_rx, st2_tx, st2_rx,
        fin_tx, mean_ref, stat_ref, col_sems, term_sems, local_sems,
    ) = refs[25:42]
    gather_sems = refs[42:]
    d, z, c = (lax.axis_index(name) for name in ALL)
    n_items, lat_len, width = lat_hbm.shape
    pix_dev, pad_width = xn_out.shape[1:]
    own = width // (n_dp * n_z * 2)
    held = chunk * n_z
    peers = [(d, lax.rem(z + i, n_z), c) for i in range(1, n_z)] + [(d, z, 1 - c)]
    if gathers:
        peers += [(d ^ 1, z, c), (d ^ 2, z, c)]
    local = iter(range(1000))

    def copy_here(src, dst):
        copy = pltpu.make_async_copy(src, dst, local_sems.at[next(local)])
        copy.start()
        return copy

    if gathers:
        first = Gather(first_all, (), gather_sems[0], n_z)
        rest = [Gather(second_all, (), gather_sems[1], n_z)]
        for index, (low, high) in enumerate(PIECES):
            rest.append(Gather(mats, (pl.ds(low - 2, high - low),), gather_sems[2 + index], n_z))
        ready = [(21, 30, 42), (31, 42, 57), (39, 50, 65), (45, 60, 73), (58, 73, 85)]
        steps = []
        for piece, times in zip(rest, ready, strict=True):
            relays = (piece.relay_z, piece.relay_plane, piece.relay_far)
            steps += list(zip(times, relays, strict=True))
        steps.sort(key=lambda step: step[0])
        done, whole_now = [0], set()

        def pump(time):
            while done[0] < len(steps) and steps[done[0]][0] <= time:
                steps[done[0]][1]()
                done[0] += 1

        def weight(k):
            piece = sum(low <= k for low, _ in PIECES)
            if piece not in whole_now:
                pump(ready[piece][2])
                rest[piece].finish()
                whole_now.add(piece)
            return Whole(mats.at[k - 2] if piece else second_all, 0, width)

    else:
        loads = {0: copy_here(first_in, first_all), 1: copy_here(second_in, second_all)}
        for k in range(2, mats.shape[0] + 2):
            loads[k] = copy_here(rest_in.at[k - 2], mats.at[k - 2])

        def pump(time):
            pass

        def weight(k):
            if k in loads:
                loads.pop(k).wait()
            return Whole(mats.at[k - 2] if k > 1 else second_all, 0, width)

    def kt_one():
        weight(1)
        return Whole(second_all, width, width + pad_width)

    def column_copy(src, dst, index, peer):
        return remote(src, dst, col_sems, index, peer)

    def pixel_phase(pix, lat, xn, pt, s_buf, q_all, px_own, xt, turn, *own_bufs):
        l_pix, l_lat = copy_here(pix_hbm, pix), copy_here(lat_hbm, lat)
        if gathers:
            own_mats, own_cols = own_bufs
            l_own = copy_here(first_in, own_mats)
        turn[...] = jnp.zeros(turn.shape, fl_type)
        turn[0:1, :pix_width] = gain_ref[...].reshape(1, pix_width)
        gain_cols[...] = turn[...].T
        gain_col = gain_cols[:pix_width, :1]
        meet(peers)
        if gathers:
            me = d * n_z + z
            gain_at = round_up(pix_width, 8) - (pad_width - 128)
            turn[...] = jnp.zeros(turn.shape, fl_type)
            turn[gain_at : gain_at + 4, :own] = rest_in[...]
            l_own.wait()
            for k, whole in ((0, first_all), (1, second_all)):
                own_cols[...] = jnp.zeros(own_cols.shape, fl_type)
                own_cols[:, :pix_width] = second_in[k]
                if k == 0:
                    own_cols[:, pad_width - 128 :] += turn[:, :128].T[:own]
                whole[me, c, :, :width] = own_mats[k].astype(bf_type)
                whole[me, c, :, width:] = own_cols[...].astype(bf_type)
                if k == 0:
                    first.start_z()
                    first.start_plane()
            for k in range(mats.shape[0]):
                mats[k, me, c] = own_mats[k + 2].astype(bf_type)
            for piece in rest[:-1]:
                piece.start_z()
            for piece in rest[:2]:
                piece.start_plane()
        xt[...] = jnp.zeros(xt.shape, fl_type)
        rows = tile_of(pix_dev, 16, 256)
        tiles = pix_dev // rows

        def normalise(item):
            def part(start, size):
                values = pix[:, item, pl.ds(start, size)].astype(fl_type)
                centred = values - jnp.sum(values, 0, keepdims=True) * (1.0 / pix_width)
                var = jnp.sum(centred * centred, 0, keepdims=True) * (1.0 / pix_width)
                xt[:pix_width, :size] = centred * lax.rsqrt(var + 1e-05) * gain_col
                turned = round_up(size, 128)
                low = xt[:, :turned].T.astype(bf_type)
                xn[item, pl.ds(start, size), :] = low[:size]

            lane_parts(pix_dev, 256, part)

        l_pix.wait()
        normalise(0)
        if gathers:
            first.relay_z()
        for item in range(1, n_items):
            normalise(item)
        xn_copy = copy_here(xn, xn_out)
        if gathers:
            first.relay_plane()
            for piece in rest[2:]:
                piece.start_plane()
            first.relay_far()
            pump(21)
            first.finish()
        else:
            loads.pop(0).wait()
        first_copy = copy_here(first_all, first_out)
        l_lat.wait()
        gain_at = round_up(pix_width, 8) - (pad_width - 128)
        tail = Whole(first_all, width + pad_width - 128, width + pad_width)[...]
        tail = tail.astype(fl_type).T
        gains_ref[...] = tail[gain_at : gain_at + 8]
        lat_rows = tile_of(lat_len, 128, 256)
        for item in range(n_items):

            def queries(t, _, item=item):
                at = pl.ds(pl.multiple_of(t * lat_rows, lat_rows), lat_rows)
                values = lat[item, at, :].astype(fl_type)
                centred = values - jnp.mean(values, -1, keepdims=True)
                var = jnp.mean(centred * centred, -1, keepdims=True)
                normal = (centred * lax.rsqrt(var + 1e-05) * gains_ref[:1]).astype(bf_type)
                q_low = dot(normal, Whole(first_all, 0, width)[...]).astype(bf_type)
                q_all[item, at, :] = q_low
                raw = dot(q_low, Whole(first_all, width, width + pad_width)[...])
                qk_ref[item, :, at] = (raw * width**-0.5).T.astype(bf_type)
                return 0

            lax.fori_loop(0, lat_len // lat_rows, queries, 0)
            pump(31 + 3 * item)
        q_copy = copy_here(q_all.at[c], q_out)

        base = (z * 2 + c) * pix_dev
        for item in range(n_items):
            valid = counts[item] - base

            def score(t, most, item=item, valid=valid):
                at = pl.ds(pl.multiple_of(t * rows, rows), rows)
                values = dot(xn[item, at, :], qk_ref[item])
                place = lax.broadcasted_iota(jnp.int32, values.shape, 0) + t * rows
                values = jnp.where(place < valid, values, -1e30)
                s_buf[at, :] = values
                return jnp.maximum(most, jnp.max(values.reshape(rows // 8, 8, lat_len), 0))

            most = lax.fori_loop(0, tiles, score, jnp.full((8, lat_len), -1e30, fl_type))
            peak = jnp.max(most, 0, keepdims=True)
            pump(36 + 6 * item)

            def weigh(t, total, item=item, peak=peak):
                at = pl.ds(pl.multiple_of(t * rows, rows), rows)
                values = jnp.exp(s_buf[at, :] - peak)
                pt[item, at, :] = values.astype(bf_type)
                return total + jnp.sum(values.reshape(rows // 8, 8, lat_len), 0)

            total = lax.fori_loop(0, tiles, weigh, jnp.zeros((8, lat_len), fl_type))
            total = jnp.sum(total, 0, keepdims=True)
            peak_ref[item] = jnp.broadcast_to(peak, (8, lat_len))
            st_tx[item, :4] = jnp.broadcast_to(peak, (4, lat_len))
            st_tx[item, 4:] = jnp.broadcast_to(total, (4, lat_len))
            part = dot(xn[item], pt[item], TN)
            px_own[item, : part.shape[0]] = part
            if held > part.shape[0]:
                px_own[item, part.shape[0] :] = jnp.zeros((held - part.shape[0], lat_len), fl_type)
            px_tx[item] = px_own[item, :held].astype(bf_type)
            pump(39 + 5 * item)
        pt_copy = copy_here(pt, pt_out)
        pair = [
            column_copy(px_tx.at[1 - c], px_rx, 0, (d, z, 1 - c)),
            column_copy(st_tx.at[1 - c], st_rx, 1, (d, z, 1 - c)),
        ]
        for copy in pair:
            copy.start()
        for copy in pair:
            copy.wait()
        peak_own, peak_rx = st_tx[c, :1], st_rx[:1]
        peak = jnp.maximum(peak_own, peak_rx)
        scale_own, scale_rx = jnp.exp(peak_own - peak), jnp.exp(peak_rx - peak)
        st2_tx[:4] = jnp.broadcast_to(peak, (4, lat_len))
        st2_tx[4:] = jnp.broadcast_to(
            scale_own * st_tx[c, 4:5] + scale_rx * st_rx[4:5], (4, lat_len)
        )
        both = px_own[c, :held] * scale_own + px_rx[...].astype(fl_type) * scale_rx
        px2_tx[...] = both.astype(bf_type).reshape(n_z, chunk, lat_len)
        for copy in (xn_copy, first_copy, q_copy, pt_copy):
            copy.wait()

    own_bufs = []
    if gathers:
        own_bufs = [pltpu.VMEM(first_in.shape, fl_type), pltpu.VMEM((own, pad_width), fl_type)]
    pl.run_scoped(
        pixel_phase,
        pltpu.VMEM(pix_hbm.shape, bf_type),
        pltpu.VMEM(lat_hbm.shape, bf_type),
        pltpu.VMEM(xn_out.shape, bf_type),
        pltpu.VMEM(pt_out.shape, bf_type),
        pltpu.VMEM((pix_dev, lat_len), fl_type),
        pltpu.VMEM(lat_hbm.shape, bf_type),
        pltpu.VMEM((n_items, max(held, pad_width), lat_len), fl_type),
        pltpu.VMEM((pad_width, 256), fl_type),
        pltpu.VMEM((128, pad_width), fl_type),
        *own_bufs,
    )

    copies = []
    for i in range(1, n_z):
        to = lax.rem(z + i, n_z)
        copies.append(column_copy(px2_tx.at[to], px2_rx.at[z], 2 * i, (d, to, c)))
        copies.append(column_copy(st2_tx, st2_rx.at[z], 2 * i + 1, (d, to, c)))
    for copy in copies:
        copy.start()
    if gathers:
        rest[-1].start_z()
    pump(50)
    for copy in copies:
        copy.wait()
    pump(57)
    peak = st2_tx[:1]
    froms = [lax.rem(z + n_z - i, n_z) for i in range(1, n_z)]
    for other in froms:
        peak = jnp.maximum(peak, st2_rx[other, :1])
    scale = jnp.exp(st2_tx[:1] - peak)
    total = scale * st2_tx[4:5]
    mean = scale * px2_tx[z].astype(fl_type)
    for other in froms:
        scale = jnp.exp(st2_rx[other, :1] - peak)
        total = total + scale * st2_rx[other, 4:5]
        mean = mean + scale * px2_rx[other].astype(fl_type)
    stat_ref[:8] = jnp.broadcast_to(peak, (8, lat_len))
    stat_ref[8:] = jnp.broadcast_to(total, (8, lat_len))
    fin_tx[...] = (mean / total).astype(bf_type)
    own_rows = pl.ds(pl.multiple_of(z * chunk, chunk), chunk)
    copies = []
    for i in range(1, n_z):
        to = lax.rem(z + i, n_z)
        copies.append(column_copy(fin_tx, mean_ref.at[own_rows], 2 * n_z + i, (d, to, c)))
    for copy in copies:
        copy.start()
    pump(60)
    for copy in copies:
        copy.wait()
    mean_ref[own_rows] = fin_tx[...]
    if gathers:
        first.drain()

    def chain_phase(lat, cot, stage, *bufs):
        l_lat, l_cot = copy_here(lat_hbm.at[c], lat), copy_here(cot_hbm.at[c], cot)
        stages, lead = stage.shape[0], len(stage.shape) - 3
        put_sems = [next(local) for _ in range(stages)]
        order, pending, flying, far_flying = [], [], [None] * stages, []
        far = [lax.rem(d + i, n_dp) for i in range(1, n_dp)]

        def place(k):
            return first_all.at[pl.ds(2 * (k - 1 - LAST), 2), :, :, :width]

        def settle(k, buffer, copy):
            copy.wait()
            index = (lax.div(d, 2), lax.rem(d, 2))
            rows = pl.ds((k - 1 - LAST) * own, own)
            whole = place(k)
            mine = stage[(buffer, *index, c)].astype(fl_type) + whole[index].astype(fl_type)
            done_sum[rows, :] = mine
            both = stage[buffer, :, :, c].astype(fl_type) + whole[...].astype(fl_type)
            whole[...] = both.astype(bf_type)
            for n, to in enumerate(far):
                copy = remote(
                    whole.at[lax.div(to, 2), lax.rem(to, 2)],
                    done_far.at[d, rows],
                    term_sems,
                    8 + 3 * (k - 1 - LAST) + n,
                    (to, z, c),
                )
                copy.start()
                far_flying.append(copy)

        def put(k):
            while len(pending) > 1:
                settle(*pending.pop(0))
            buffer = len(order) % stages
            order.append(k)
            if flying[buffer] is not None:
                flying[buffer].wait()
                flying[buffer] = None
            if any(entry[1] == buffer for entry in pending):
                settle(*pending.pop(0))

            def start():
                if gathers and k > LAST:
                    source = stage.at[buffer, :, :, 1 - c]
                    copy = remote(source, place(k), term_sems, k - 1 - LAST, (d, z, 1 - c))
                    copy.start()
                    pending.append((k, buffer, copy))
                else:
                    at = (slice(None),) * lead + (pl.ds((k - 1) * own, own),)
                    copy = pltpu.make_async_copy(
                        stage.at[buffer], early_out.at[at], local_sems.at[put_sems[buffer]]
                    )
                    copy.start()
                    flying[buffer] = copy

            return stage.at[buffer], start

        outs = (
            put,
            block_ref,
            gk_both.at[c],
            stats_both.at[c],
            cross_ref,
            k_one_ref,
            gterm_ref,
        )
        l_lat.wait()
        l_cot.wait()
        latent_chain(
            n_z, n_dp, own, weight, kt_one, pump, lat, cot, gains_ref, mean_ref, stat_ref, outs, bufs
        )
        pair = [
            column_copy(gk_both.at[c], gk_both.at[c], 3 * n_z, (d, z, 1 - c)),
            column_copy(stats_both.at[c], stats_both.at[c], 3 * n_z + 1, (d, z, 1 - c)),
        ]
        for copy in pair:
            copy.start()
        while pending:
            settle(*pending.pop(0))
        for copy in [copy for copy in flying if copy is not None] + pair + far_flying:
            copy.wait()

    wire = early_out.dtype
    one_item = pltpu.VMEM((lat_len, width), bf_type)
    n_cols = n_dp * 2 * own
    pl.run_scoped(
        chain_phase,
        one_item,
        one_item,
        pltpu.VMEM((3, *early_out.shape[:-2], own, width), wire),
        *chain_bufs(lat_len, width, pad_width, n_cols),
    )
    if gathers:
        pump(1000)
        for piece in rest:
            piece.drain()


def forward_call(n_z, n_dp, gathers, first, second, rest, counts, pix_turned, latents, cotangent, gain):
    n_items, lat_len, width = latents.shape
    pix_width, _, pix_dev = pix_turned.shape
    own = width // (n_dp * n_z * 2)
    blocks = (n_dp * n_z, 2, own) if gathers else (1, 1, width)
    n_rest = 8
    pad_width = round_up(round_up(pix_width, 8) + 8, 128)
    wire = bf_type if own % 16 == 0 else fl_type
    chunk = round_up(-(-pix_width // n_z), 16)
    held = chunk * n_z
    z_share = lat_len // n_z
    n_cols = n_dp * 2 * own
    vmem, hbm = pl.BlockSpec(memory_space=pltpu.VMEM), pl.BlockSpec(memory_space=pl.ANY)
    shape, buf = jax.ShapeDtypeStruct, pltpu.VMEM
    out_shape = [
        shape((*blocks, width + pad_width), bf_type),
        shape((n_items, pix_dev, pad_width), bf_type),
        shape((n_items, pix_dev, lat_len), bf_type),
        shape((lat_len, width), bf_type),
        shape((2, 2, 2, LAST * own, width) if gathers else (n_dp, 2, 9 * own, width), wire),
        shape((n_items, 8, lat_len), fl_type),
        shape((n_items, pad_width, lat_len), bf_type),
        shape((8, width), fl_type),
        shape((2, z_share // 2, width), bf_type),
        shape((n_items, pad_width, lat_len), bf_type),
        shape((n_items, 3, 8, lat_len), fl_type),
        shape((z_share, width), fl_type),
        shape((n_cols, pad_width), fl_type),
        shape((8, width), fl_type),
        shape((pad_width, 128), fl_type),
        shape(((9 - LAST) * own, width), fl_type),
        shape((n_dp, (9 - LAST) * own, width), wire),
    ]
    scratch = [
        buf((*blocks, width + pad_width), bf_type),
        buf((*blocks, width + pad_width), bf_type),
        buf((n_rest, *blocks, width), bf_type),
        buf((n_items, held, lat_len), bf_type),
        buf((held, lat_len), bf_type),
        buf((n_items, 8, lat_len), fl_type),
        buf((8, lat_len), fl_type),
        buf((n_z, chunk, lat_len), bf_type),
        buf((n_z, chunk, lat_len), bf_type),
        buf((8, lat_len), fl_type),
        buf((n_z, 8, lat_len), fl_type),
        buf((chunk, lat_len), bf_type),
        buf((held, lat_len), bf_type),
        buf((16, lat_len), fl_type),
        pltpu.SemaphoreType.DMA((2, 3 * n_z + 2)),
        pltpu.SemaphoreType.DMA((2, 32)),
        pltpu.SemaphoreType.DMA((32,)),
    ]
    if gathers:
        scratch += [pltpu.SemaphoreType.DMA((2, 8, n_z))] * (2 + len(PIECES))
    weight_specs = [hbm, vmem, vmem] if gathers else [hbm] * 3
    return pl.pallas_call(
        functools.partial(forward, n_z, n_dp, gathers, pix_width, chunk),
        out_shape=out_shape,
        in_specs=[pl.BlockSpec(memory_space=pltpu.SMEM)] + weight_specs + [hbm] * 3 + [vmem],
        out_specs=[hbm] * 5 + [vmem] * 11 + [hbm],
        scratch_shapes=scratch,
        compiler_params=pltpu.CompilerParams(
            collective_id=0, has_side_effects=True, vmem_limit_bytes=62 * 2**20
        ),
        name="forward",
    )(counts, first, second, rest, pix_turned, latents, cotangent, gain)


def row_loop(total, body, rows=128):
    def step(t, _):
        body(pl.ds(pl.multiple_of(t * rows, rows), rows))
        return 0

    lax.fori_loop(0, total // rows, step, 0)


def tanh_gelu(values):
    factor, cubic = (2.0 / math.pi) ** 0.5, 0.044715
    square = values * values
    bent = jnp.tanh(factor * values * (1.0 + cubic * square))
    half = 0.5 * (1.0 + bent)
    slope = half + 0.5 * values * (1.0 - bent * bent) * factor * (1.0 + 3.0 * cubic * square)
    return values * half, slope


def choose(sel_ref, n_dp, n_z, pair_width):
    width, n_cols = sel_ref.shape
    z = lax.axis_index("z")
    wanted = lax.broadcasted_iota(jnp.int32, (width, n_cols), 1)
    wanted = (lax.div(wanted, pair_width) * n_z + z) * pair_width + lax.rem(wanted, pair_width)
    place = lax.broadcasted_iota(jnp.int32, (width, n_cols), 0)
    sel_ref[...] = jnp.where(place == wanted, 1.0, 0.0).astype(bf_type)


def latent_chain(n_z, n_dp, own, weight, kt_one, pump, lat, cot, gains, mean_ref, stat_ref, outs, bufs):
    put, block_ref, gk_ref, stats_ref, cross_ref, k_one_ref, gterm_ref = outs
    (
        run, x_buf, hat_c, hat_s, hat_f, inv, slope_c, slope_f,
        even, odd, q_s, k_s, v_s, probs, sel, mean_pad, picks,
    ) = bufs
    lat_len, width = lat.shape
    pad_width = mean_pad.shape[1]
    head_dim = width // HEADS
    z = lax.axis_index("z")
    z_share = lat_len // n_z
    z_rows = pl.ds(pl.multiple_of(z * z_share, z_share), z_share)
    choose(sel, n_dp, n_z, 2 * own)
    att = gelu_c = mixed = gelu_f = even
    norm_c = norm_s = norm_f = odd
    tmp = lat

    def add_norm(base, gain, hat, which, normal):
        def body(at):
            values = base(at) + x_buf[at, :]
            run[at, :] = values
            centred = values - jnp.mean(values, -1, keepdims=True)
            scale = lax.rsqrt(jnp.mean(centred * centred, -1, keepdims=True) + 1e-05)
            standard_values = centred * scale
            hat[at, :] = standard_values
            inv[which, at, :] = jnp.broadcast_to(scale, (scale.shape[0], 128))
            normal[at, :] = (standard_values * gains[gain : gain + 1]).astype(bf_type)

        row_loop(lat_len, body)

    def activate(slope, low):
        def body(at):
            value, grad = tanh_gelu(x_buf[at, :])
            low[at, :] = value.astype(bf_type)
            slope[at, :] = grad

        row_loop(lat_len, body)

    parts = lat_len // 128
    part_cols = width // parts

    def pick(n, ref):
        picks[n] = dot(ref[...], sel[...]).astype(bf_type)

    def terms(*wanted):
        staged = [(put(k), n, right) for k, n, right in wanted]

        def part(t):
            cols = pl.ds(pl.multiple_of(t * part_cols, part_cols), part_cols)
            for (buffer, _), n, right in staged:
                term = dot(picks[n], right[:, cols], TN).astype(buffer.dtype)
                buffer[..., cols] = term.reshape(*buffer.shape[:-1], part_cols)

        def send():
            for (_, start), _, _ in staged:
                start()

        return part, send

    def times_slope(slope, low, beside):
        def body(t, _):
            at = pl.ds(pl.multiple_of(t * 128, 128), 128)
            beside[0](t)
            low[at, :] = (x_buf[at, :] * slope[at, :]).astype(bf_type)
            return 0

        lax.fori_loop(0, parts, body, 0)
        beside[1]()

    def pull_norm(base, gain, hat, which, low, beside):
        def body(t, sums):
            at = pl.ds(pl.multiple_of(t * 128, 128), 128)
            beside[0](t)
            grad = x_buf[at, :]
            normal = hat[at, :]
            sums = sums + jnp.sum((normal * grad).reshape(16, 8, width), 0)
            grad = grad * gains[gain : gain + 1]
            mean = jnp.mean(grad, -1, keepdims=True)
            along = jnp.mean(grad * normal, -1, keepdims=True)
            value = base(at) + (grad - mean - normal * along) * inv[which, at, :1]
            run[at, :] = value
            low[at, :] = value.astype(bf_type)
            return sums

        sums = lax.fori_loop(0, parts, body, jnp.zeros((8, width), fl_type))
        beside[1]()
        gterm_ref[gain : gain + 1] = jnp.sum(sums, 0, keepdims=True)

    def matrix_term(k, n, right):
        buffer, start = put(k)
        buffer[...] = dot(picks[n], right[...], TN).astype(buffer.dtype).reshape(buffer.shape)
        start()

    def head(h):
        return slice(h * head_dim, (h + 1) * head_dim)

    head_scale = head_dim**-0.5
    gterm_ref[...] = jnp.zeros(gterm_ref.shape, fl_type)

    pump(65)
    mean_pad[...] = jnp.zeros(mean_pad.shape, bf_type)
    held = min(mean_ref.shape[0], pad_width)
    mean_pad[:, :held] = mean_ref[:held].astype(fl_type).T.astype(bf_type)
    att[...] = dot(mean_pad[...], kt_one()[...], NT).astype(bf_type)
    x_buf[...] = dot(att[...], weight(1)[...])
    pick(0, att)
    add_norm(lambda at: lat[at, :].astype(fl_type), 1, hat_c, 0, norm_c)
    pump(70)
    x_buf[...] = dot(norm_c[...], weight(2)[...])
    pick(1, norm_c)
    activate(slope_c, gelu_c)
    pump(73)
    x_buf[...] = dot(gelu_c[...], weight(3)[...])
    pick(2, gelu_c)
    add_norm(lambda at: run[at, :], 2, hat_s, 1, norm_s)
    pump(75)
    q_s[...] = dot(norm_s[...], weight(4)[...]).astype(bf_type)
    k_s[...] = dot(norm_s[...], weight(5)[...]).astype(bf_type)
    pump(77)
    v_s[...] = dot(norm_s[...], weight(6)[...]).astype(bf_type)
    pick(3, norm_s)

    def attend(h):
        at = head(h)
        scores = dot(k_s[:, at], q_s[:, at], NT) * head_scale
        weights = jnp.exp(scores - jnp.max(scores, 0, keepdims=True))
        weights = weights * (1.0 / jnp.sum(weights, 0, keepdims=True))
        low = weights.astype(bf_type)
        probs[h] = low
        mixed[:, at] = dot(low, v_s[:, at], TN).astype(bf_type)

    for h in range(HEADS):
        attend(h)
    pump(85)
    x_buf[...] = dot(mixed[...], weight(7)[...])
    pick(4, mixed)
    add_norm(lambda at: run[at, :], 3, hat_f, 2, norm_f)
    x_buf[...] = dot(norm_f[...], weight(8)[...])
    pick(5, norm_f)
    activate(slope_f, gelu_f)
    final = run[z_rows, :] + dot(gelu_f[z_rows, :], weight(9)[...])
    block_ref[...] = final.astype(bf_type).reshape(block_ref.shape)

    pick(6, gelu_f)

    x_buf[...] = dot(cot[...], weight(9)[...], NT)
    times_slope(slope_f, tmp, terms((9, 6, cot)))
    x_buf[...] = dot(tmp[...], weight(8)[...], NT)
    pull_norm(lambda at: cot[at, :].astype(fl_type), 3, hat_f, 2, odd, terms((8, 5, tmp)))
    grad_mixed = even
    grad_mixed[...] = dot(odd[...], weight(7)[...], NT).astype(bf_type)
    matrix_term(7, 4, odd)

    def attend_back(h):
        at = head(h)
        q_h, k_h, v_h, grad_h = q_s[:, at], k_s[:, at], v_s[:, at], grad_mixed[:, at]
        low = probs[h]
        weights = low.astype(fl_type)
        grad_weights = dot(v_h, grad_h, NT)
        along = jnp.sum(weights * grad_weights, 0, keepdims=True)
        grad_scores = (weights * (grad_weights - along)).astype(bf_type)
        q_s[:, at] = (dot(grad_scores, k_h, TN) * head_scale).astype(bf_type)
        k_s[:, at] = (dot(grad_scores, q_h) * head_scale).astype(bf_type)
        v_s[:, at] = dot(low, grad_h).astype(bf_type)

    for h in range(HEADS):
        attend_back(h)
    x_buf[...] = dot(q_s[...], weight(4)[...], NT)
    x_buf[...] += dot(k_s[...], weight(5)[...], NT)
    x_buf[...] += dot(v_s[...], weight(6)[...], NT)
    selves = terms((4, 3, q_s), (5, 3, k_s), (6, 3, v_s))
    pull_norm(lambda at: run[at, :], 2, hat_s, 1, tmp, selves)
    x_buf[...] = dot(tmp[...], weight(3)[...], NT)
    times_slope(slope_c, odd, terms((3, 2, tmp)))
    x_buf[...] = dot(odd[...], weight(2)[...], NT)
    pull_norm(lambda at: run[at, :], 1, hat_c, 0, tmp, terms((2, 1, odd)))
    grad_att = even
    grad_att[...] = dot(tmp[...], weight(1)[...], NT).astype(bf_type)
    matrix_term(1, 0, tmp)
    cross_ref[...] = run[z_rows, :]
    low = dot(grad_att[...], kt_one()[...]).T.astype(bf_type)
    gk_ref[...] = low
    delta = jnp.sum(low[:held].astype(fl_type) * mean_ref[:held].astype(fl_type), 0, keepdims=True)
    stats_ref[0] = stat_ref[:8]
    stats_ref[1] = stat_ref[8:]
    stats_ref[2] = jnp.broadcast_to(delta, stats_ref.shape[1:])
    k_one_ref[...] = dot(dot(grad_att[...], sel[...]).astype(bf_type), mean_pad[...], TN)


def chain_bufs(lat_len, width, pad_width, n_cols):
    wide = pltpu.VMEM((lat_len, width), fl_type)
    low = pltpu.VMEM((lat_len, width), bf_type)
    return (
        [wide] * 5
        + [pltpu.VMEM((3, lat_len, 128), fl_type)]
        + [wide] * 2
        + [low] * 5
        + [
            pltpu.VMEM((HEADS, lat_len, lat_len), bf_type),
            pltpu.VMEM((width, n_cols), bf_type),
            pltpu.VMEM((lat_len, pad_width), bf_type),
            pltpu.VMEM((7, lat_len, n_cols), bf_type),
        ]
    )


def backward(n_z, n_dp, pix_width, chunk, *refs):
    (
        gk_all,
        stats_all,
        early_ref,
        block_ref,
        xn_hbm,
        pt_hbm,
        peak_ref,
        qk_ref,
        pix_hbm,
        gain_ref,
        lat_hbm,
        first_hbm,
        gains_ref,
        q_hbm,
        cross_ref,
        k_one_ref,
        gterm_ref,
        done_sum_hbm,
        done_far_hbm,
        mats_hbm,
        mfirst_hbm,
        msecond_hbm,
        kv_ref,
        kfirst_ref,
        ksecond_ref,
        ng_ref,
        gfirst_ref,
        gsecond_ref,
        block_out,
        lat_out,
        pix_out,
        mats_out,
        kv_out,
        gains_out,
        small_out,
        xn,
        pt,
        pix,
        lat,
        first,
        q_own,
        mats,
        mfirst,
        msecond,
        ds,
        pl_low,
        part_tx,
        part_own,
        part_rx,
        col_tx,
        col_rx,
        fin_tx,
        fin_rx,
        dst_full,
        early_own,
        early_rx,
        early_tx,
        early_sum,
        early_far,
        done_sum,
        done_far,
        pix_buf,
        hat,
        inv,
        norm,
        dq,
        da,
        sel,
        lat_tx,
        late,
        late_rx,
        late_tx,
        late_own,
        late_far,
        small_tx,
        small_col,
        small_far_tx,
        small_far,
        input_acc,
        sems,
        loads,
    ) = refs
    d, z, c = (lax.axis_index(name) for name in ALL)
    oc = 1 - c
    n_items, pix_dev, pad_width = xn.shape
    gain_col = gain_ref[:pix_width, :1]
    lat_len, width = lat.shape[1:]
    own = kv_out.shape[1]
    far = [lax.rem(d + i, n_dp) for i in range(1, n_dp)]
    far_from = [lax.rem(d + n_dp - i, n_dp) for i in range(1, n_dp)]
    z_to = [lax.rem(z + i, n_z) for i in range(1, n_z)]
    z_from = [lax.rem(z + n_z - i, n_z) for i in range(1, n_z)]
    partner = (d, z, oc)
    column = [(i, 0) for i in range(1, n_z)] + [(i, 1) for i in range(n_z)]

    def in_column(i, j):
        return (d, lax.rem(z + i, n_z), lax.rem(c + j, 2))

    peers = [in_column(i, j) for i, j in column] + [(to, z, c) for to in far]
    barrier = pltpu.get_barrier_semaphore()
    for peer in peers:
        pl.semaphore_signal(barrier, inc=1, device_id=peer, device_id_type=MESH)

    slot = iter(range(1000))

    def send(src, dst, peer):
        copy = remote(src, dst, sems, next(slot), peer)
        copy.start()
        return copy

    load_slot = iter(range(1000))

    def load(src, dst):
        copy = pltpu.make_async_copy(src, dst, loads.at[next(load_slot)])
        copy.start()
        return copy

    l_xn = load(xn_hbm, xn)
    l_pt = load(pt_hbm, pt)
    l_pix = load(pix_hbm, pix)
    l_lat = load(lat_hbm.at[c], lat.at[0])
    l_first = load(first_hbm, first)
    l_q = load(q_hbm, q_own)
    l_early = load(early_ref.at[:, c], early_own)
    n_early = early_own.shape[1] // own
    l_done = []
    if n_early < mats.shape[0] - 1:
        l_done = [load(done_sum_hbm, done_sum), load(done_far_hbm, done_far)]
    l_mats = [load(mats_hbm, mats), load(mfirst_hbm, mfirst), load(msecond_hbm, msecond)]
    block_out[c] = block_ref[c]

    rows = tile_of(pix_dev, 16, 256)
    tiles = pix_dev // rows
    held = chunk * n_z
    l_pt.wait()
    l_xn.wait()

    def score_side(item):
        gk = gk_all.at[item]
        scale = jnp.exp(peak_ref[item, :1] - stats_all[item, 0, :1]) / stats_all[item, 1, :1]
        delta = stats_all[item, 2, :1]

        def body(t, _):
            at = pl.ds(pl.multiple_of(t * rows, rows), rows)
            probs = pt[item, at, :].astype(fl_type) * scale
            grad_probs = dot(xn[item, at, :], gk[...])
            ds[item, at, :] = (probs * (grad_probs - delta)).astype(bf_type)
            pl_low[item, at, :] = probs.astype(bf_type)
            return 0

        lax.fori_loop(0, tiles, body, 0)
        return dot(xn[item], ds[item], TN)

    part_tx[...] = score_side(oc)[: part_tx.shape[0]].astype(part_tx.dtype)
    pl.semaphore_wait(barrier, len(peers))
    px_pair = send(part_tx, part_rx, partner)
    out_pair = send(block_ref.at[oc], block_out.at[c], partner)
    early_pair = send(early_ref.at[:, oc], early_rx, partner)
    part_own[...] = score_side(c)
    px_pair.wait()
    both = part_own[: part_rx.shape[0]] + part_rx[...].astype(fl_type)
    if held > both.shape[0]:
        both = jnp.concatenate([both, jnp.zeros((held - both.shape[0], lat_len), fl_type)], 0)
    col_tx[...] = both[:held].astype(col_tx.dtype).reshape(n_z, chunk, lat_len)
    col = [send(col_tx.at[to], col_rx.at[z], (d, to, c)) for to in z_to]

    l_early.wait()
    early_pair.wait()

    def pair_sum(t, _):
        both = early_own[t].astype(fl_type) + early_rx[t].astype(fl_type)
        early_tx[t] = both.astype(early_tx.dtype)
        return 0

    lax.fori_loop(0, n_dp, pair_sum, 0)
    early_out = [send(early_tx.at[to], early_far.at[d], (to, z, c)) for to in far]
    early_sum[...] = early_own[d].astype(fl_type) + early_rx[d].astype(fl_type)

    l_pix.wait()
    input_acc[...] = jnp.zeros(input_acc.shape, fl_type)

    def pixel_side(item, gk):
        def part(start, size):
            at = pl.ds(start, size)
            grad = dot(qk_ref[item], ds[item, at, :], NT) + dot(gk[...], pl_low[item, at, :], NT)
            grad = grad[:pix_width]
            values = pix[:, item, at].astype(fl_type)
            centred = values - jnp.sum(values, 0, keepdims=True) * (1.0 / pix_width)
            var = jnp.sum(centred * centred, 0, keepdims=True) * (1.0 / pix_width)
            scale = lax.rsqrt(var + 1e-05)
            normal = centred * scale
            along = normal * grad
            for low in range(0, size, 128):
                high = min(low + 128, size)
                input_acc[:pix_width, : high - low] += along[:, low:high]
            grad = grad * gain_col
            mean = jnp.sum(grad, 0, keepdims=True) * (1.0 / pix_width)
            along = jnp.sum(grad * normal, 0, keepdims=True) * (1.0 / pix_width)
            pix_buf[:, item, at] = (grad - mean - normal * along) * scale

        lane_parts(pix_dev, 256, part)

    pixel_side(0, gk_all.at[0])

    for copy in col:
        copy.wait()
    mean = col_tx[z].astype(fl_type)
    for other in z_from:
        mean = mean + col_rx[other].astype(fl_type)
    fin_tx[...] = mean.astype(fin_tx.dtype)
    fin = [send(fin_tx, fin_rx.at[z], (d, to, c)) for to in z_to]

    pixel_side(1, gk_all.at[1])
    stores = [load(pix_buf, pix_out)]

    l_lat.wait()
    l_first.wait()
    l_q.wait()
    pair_width = 2 * own
    n_cols = n_dp * pair_width
    wanted = lax.broadcasted_iota(jnp.int32, (width, n_cols), 1)
    wanted = (lax.div(wanted, pair_width) * n_z + z) * pair_width + lax.rem(wanted, pair_width)
    place = lax.broadcasted_iota(jnp.int32, (width, n_cols), 0)
    sel[...] = jnp.where(place == wanted, 1.0, 0.0).astype(bf_type)
    values = lat[0].astype(fl_type)
    centred = values - jnp.mean(values, -1, keepdims=True)
    scale = lax.rsqrt(jnp.mean(centred * centred, -1, keepdims=True) + 1e-05)
    hat[...] = centred * scale
    inv[...] = jnp.broadcast_to(scale, inv.shape)
    norm[...] = dot((hat[...] * gains_ref[:1]).astype(bf_type), sel[...]).astype(bf_type)

    for copy in fin:
        copy.wait()
    dst_full[...] = jnp.zeros(dst_full.shape, fl_type)
    for other in z_from:
        dst_full[pl.ds(other * chunk, chunk)] = fin_rx[other].astype(fl_type)
    dst_full[pl.ds(z * chunk, chunk)] = fin_tx[...].astype(fl_type)
    summed = dst_full[:pad_width].T.astype(bf_type)
    kt_zero = first[:, width : width + pad_width]
    dq[...] = (dot(summed, kt_zero, NT) * width**-0.5).astype(bf_type)
    da[...] = dot(dq[...], first[:, :width], NT)
    term_zero = dot(norm[...], dq[...], TN)
    q_sel = dot(q_own[...], sel[...]).astype(bf_type)
    term_k = dot(q_sel, summed, TN) * width**-0.5
    gain_at = round_up(pix_width, 8) - (pad_width - 128)
    gain_zero = jnp.sum(hat[...] * da[...], 0, keepdims=True)
    place = lax.broadcasted_iota(jnp.int32, (8, width), 0)
    gain_sums = jnp.where(place == 0, gain_zero, gterm_ref[...]).astype(bf_type)
    gain_cols = dot(gain_sums, sel[...])
    gain_cols = jnp.concatenate(
        [
            jnp.zeros((gain_at, n_cols), fl_type),
            gain_cols,
            jnp.zeros((128 - gain_at - 8, n_cols), fl_type),
        ],
        0,
    ).T
    late[:, :, :, :width] = term_zero.astype(late.dtype).reshape(n_dp, 2, own, width)
    late[:, :, :, width : width + pad_width] = term_k.astype(late.dtype).reshape(
        n_dp, 2, own, pad_width
    )
    ones = k_one_ref[...]
    late[:, :, :, width + pad_width : width + 2 * pad_width - 128] = (
        ones[:, : pad_width - 128].astype(late.dtype).reshape(n_dp, 2, own, pad_width - 128)
    )
    late[:, :, :, width + 2 * pad_width - 128 :] = (
        (ones[:, pad_width - 128 :] + gain_cols).astype(late.dtype).reshape(n_dp, 2, own, 128)
    )
    late_pair = send(late.at[:, oc], late_rx, partner)

    z_share = lat_len // n_z
    at = pl.ds(pl.multiple_of(z * z_share, z_share), z_share)
    grad = da[at, :] * gains_ref[:1]
    normal = hat[at, :]
    mean = jnp.mean(grad, -1, keepdims=True)
    along = jnp.mean(grad * normal, -1, keepdims=True)
    lat_grad = cross_ref[...] + (grad - mean - normal * along) * inv[at, :1]
    lat_tx[...] = lat_grad.reshape(2, z_share // 2, width)
    lat_pair = send(lat_tx.at[oc], lat_out.at[c], partner)
    lat_out[c] = lat_tx[c]

    late_pair.wait()
    late_sum = late[:, c].astype(fl_type) + late_rx[...].astype(fl_type)
    late_tx[...] = late_sum.astype(late_tx.dtype)
    late_out = [send(late_tx.at[to], late_far.at[d], (to, z, c)) for to in far]
    late_own[...] = late[d, c].astype(fl_type) + late_rx[d].astype(fl_type)

    for copy in early_out:
        copy.wait()
    for copy in l_mats + l_done:
        copy.wait()
    lane = lax.broadcasted_iota(jnp.int32, (1, 128), 1)

    def norms(weight, gradient, first_mom, second):
        first_new = 0.9 * first_mom + 0.1 * gradient
        second_new = 0.999 * second + 0.001 * gradient * gradient
        update = (
            first_new / first_fix / (jnp.sqrt(second_new / second_fix) + 1e-06)
            + decay_rate * weight
        )
        return (weight * weight, update * update)

    def total(values):
        return jnp.sum(jnp.sum(values, 0, keepdims=True), 1, keepdims=True)

    def matrix(k, sums, early=True):
        if early:
            at = pl.ds(pl.multiple_of((k - 1) * own, own), own)
            mine, others = early_sum, early_far
        else:
            at = pl.ds(pl.multiple_of((k - 1 - n_early) * own, own), own)
            mine, others = done_sum, done_far
        gradient = mine[at, :]
        for other in far_from:
            gradient = gradient + others[other, at, :].astype(fl_type)
        mats_out[k] = gradient
        w_sq, u_sq = norms(mats[k], gradient, mfirst[k], msecond[k])
        here = lane == k
        return (
            sums[0] + jnp.where(here, total(w_sq), 0.0),
            sums[1] + jnp.where(here, total(u_sq), 0.0),
        )

    zero = jnp.zeros((1, 128), fl_type)
    sums = lax.fori_loop(1, 1 + n_early, matrix, (zero, zero))
    if n_early < mats.shape[0] - 1:
        late_matrix = functools.partial(matrix, early=False)
        sums = lax.fori_loop(1 + n_early, mats.shape[0], late_matrix, sums)

    for copy in late_out:
        copy.wait()
    for other in far_from:
        late_own[...] += late_far[other].astype(fl_type)
    mats_out[0] = late_own[:, :width]
    grads = [(mats[0], late_own[:, :width], mfirst[0], msecond[0], 0)]
    for k in range(2):
        cols = late_own[:, width + k * pad_width : width + k * pad_width + pix_width]
        kv_out[k] = cols
        grads.append((kv_ref[k], cols, kfirst_ref[k], ksecond_ref[k], 10 + k))
    gain_grad = late_own[:, width + 2 * pad_width - 128 :].T[gain_at : gain_at + 8]
    gains_out[...] = gain_grad[:4]
    w_sum, u_sum = sums
    for weight, gradient, first_mom, second, k in grads:
        w_sq, u_sq = norms(weight, gradient, first_mom, second)
        w_sum = w_sum + jnp.where(lane == k, total(w_sq), 0.0)
        u_sum = u_sum + jnp.where(lane == k, total(u_sq), 0.0)
    w_sq, u_sq = norms(ng_ref[...], gain_grad[:4], gfirst_ref[...], gsecond_ref[...])
    w_sq, u_sq = jnp.sum(w_sq, 1, keepdims=True), jnp.sum(u_sq, 1, keepdims=True)
    for k in range(4):
        w_sum = w_sum + jnp.where(lane == 12 + k, w_sq[k : k + 1], 0.0)
        u_sum = u_sum + jnp.where(lane == 12 + k, u_sq[k : k + 1], 0.0)
    small_tx[...] = jnp.zeros(small_tx.shape, fl_type)
    small_tx[0:1] = w_sum
    small_tx[1:2] = u_sum
    input_row = jnp.sum(input_acc[...].T, 0, keepdims=True)
    for n in range(pad_width // 128):
        small_tx[2 + n : 3 + n] = input_row[:, n * 128 : (n + 1) * 128]
    copies = [
        send(small_tx, small_col.at[n], in_column(i, j)) for n, (i, j) in enumerate(column)
    ]
    for copy in copies:
        copy.wait()
    all_sum = small_tx[...]
    for n in range(len(column)):
        all_sum = all_sum + small_col[n]
    small_far_tx[...] = all_sum
    copies = [
        send(small_far_tx, small_far.at[n], (to, z, c)) for n, to in enumerate(far)
    ]
    for copy in copies:
        copy.wait()
    for n in range(len(far)):
        all_sum = all_sum + small_far[n]
    small_out[...] = all_sum
    for copy in [out_pair, lat_pair] + stores:
        copy.wait()


def backward_call(n_z, n_dp, args):
    (gk, stats, early, _, xn, pt, _, _, pixels, _, latents, first) = args[:12]
    mats, kv, gains = args[19], args[22], args[25]
    pix_width = pixels.shape[0]
    n_items, lat_len, width = latents.shape
    own = mats.shape[1]
    pad_width = xn.shape[2]
    early_rows = early.shape[2]
    wire = early.dtype
    chunk = round_up(-(-pix_width // n_z), 16)
    held = chunk * n_z
    cut = min(held, pad_width)
    z_share = lat_len // n_z
    n_cols = n_dp * 2 * own
    vmem, hbm = pl.BlockSpec(memory_space=pltpu.VMEM), pl.BlockSpec(memory_space=pl.ANY)
    places = {2, 4, 5, 8, 10, 11, 13, 17, 18, 19, 20, 21}
    in_specs = [hbm if index in places else vmem for index in range(len(args))]
    shape, buf = jax.ShapeDtypeStruct, pltpu.VMEM
    out_shape = [
        shape((n_items, z_share // 2, width), bf_type),
        shape((n_items, z_share // 2, width), fl_type),
        shape(pixels.shape, fl_type),
        shape(mats.shape, fl_type),
        shape(kv.shape, fl_type),
        shape(gains.shape, fl_type),
        shape((8, 128), fl_type),
    ]
    out_specs = [vmem, vmem, hbm, vmem, vmem, vmem, vmem]
    late_width = width + 2 * pad_width
    scratch = [
        buf(xn.shape, bf_type),
        buf(pt.shape, bf_type),
        buf(pixels.shape, bf_type),
        buf((1, lat_len, width), bf_type),
        buf(first.shape, bf_type),
        buf((lat_len, width), bf_type),
        buf(mats.shape, fl_type),
        buf(mats.shape, fl_type),
        buf(mats.shape, fl_type),
        buf(pt.shape, bf_type),
        buf(pt.shape, bf_type),
        buf((cut, lat_len), bf_type),
        buf((pad_width, lat_len), fl_type),
        buf((cut, lat_len), bf_type),
        buf((n_z, chunk, lat_len), bf_type),
        buf((n_z, chunk, lat_len), bf_type),
        buf((chunk, lat_len), bf_type),
        buf((n_z, chunk, lat_len), bf_type),
        buf((max(held, pad_width), lat_len), fl_type),
        buf((n_dp, early_rows, width), wire),
        buf((n_dp, early_rows, width), wire),
        buf((n_dp, early_rows, width), wire),
        buf((early_rows, width), fl_type),
        buf((n_dp, early_rows, width), wire),
        buf(args[17].shape, fl_type),
        buf(args[18].shape, wire),
        buf(pixels.shape, fl_type),
        buf((lat_len, width), fl_type),
        buf((lat_len, 128), fl_type),
        buf((lat_len, n_cols), bf_type),
        buf((lat_len, width), bf_type),
        buf((lat_len, width), fl_type),
        buf((width, n_cols), bf_type),
        buf((2, z_share // 2, width), fl_type),
        buf((n_dp, 2, own, late_width), wire),
        buf((n_dp, own, late_width), wire),
        buf((n_dp, own, late_width), wire),
        buf((own, late_width), fl_type),
        buf((n_dp, own, late_width), wire),
        buf((8, 128), fl_type),
        buf((2 * n_z - 1, 8, 128), fl_type),
        buf((8, 128), fl_type),
        buf((n_dp - 1, 8, 128), fl_type),
        buf((pad_width, 128), fl_type),
        pltpu.SemaphoreType.DMA((2, 20 + 6 * n_z + 3 * n_dp)),
        pltpu.SemaphoreType.DMA((16,)),
    ]
    return pl.pallas_call(
        functools.partial(backward, n_z, n_dp, pix_width, chunk),
        out_shape=out_shape,
        in_specs=in_specs,
        out_specs=out_specs,
        scratch_shapes=scratch,
        compiler_params=pltpu.CompilerParams(
            collective_id=1, has_side_effects=True, vmem_limit_bytes=60 * 2**20
        ),
        name="backward",
    )(*args)


def lamb(n_mats, *refs):
    (
        block_in, lat_in, pix_in, mg, kg, gg, small, mw, mf, ms, kw, kf, ks, gw, gf, gs, iw, i_f, i_s,
        block_out, lat_out, pix_out, mg_out, kg_out, gg_out, ig_out,
        mw_out, mf_out, ms_out, kw_out, kf_out, ks_out, gw_out, gf_out, gs_out, iw_out, if_out, is_out,
        g_buf, w_buf, f_buf, s_buf, w_new, f_new, s_new, pix_buf, in_sems, out_sems, pix_sems,
    ) = refs
    parts = [(low, min(low + 66, pix_in.shape[0])) for low in range(0, pix_in.shape[0], 66)]

    def pix_copy(n, back):
        low, high = parts[n]
        src, dst = pix_in.at[low:high], pix_buf.at[low:high]
        if back:
            src, dst = dst, pix_out.at[low:high]
        return pltpu.make_async_copy(src, dst, pix_sems.at[int(back), n])

    for n in range(len(parts)):
        pix_copy(n, False).start()
    spans = [(low, min(low + 2, n_mats)) for low in range(0, n_mats, 2)]
    loads = []
    for k, (low, high) in enumerate(spans):
        loads.append(
            [
                pltpu.make_async_copy(src.at[low:high], dst.at[low:high], in_sems.at[n, k])
                for n, (src, dst) in enumerate(
                    ((mg, g_buf), (mw, w_buf), (mf, f_buf), (ms, s_buf))
                )
            ]
        )
        for copy in loads[-1]:
            copy.start()
    block_out[...] = block_in[...]
    lat_out[...] = lat_in[...]
    lane = lax.broadcasted_iota(jnp.int32, (1, 128), 1)

    def ratio(w_sq, u_sq):
        return jnp.sqrt(w_sq) / (jnp.sqrt(u_sq) + 1e-06)

    trust = ratio(small[0:1], small[1:2])

    def scalar(k):
        return jnp.sum(jnp.where(lane == k, trust, 0.0), 1, keepdims=True)

    def update(weight, gradient, first_mom, second):
        first_new = 0.9 * first_mom + 0.1 * gradient
        second_new = 0.999 * second + 0.001 * gradient * gradient
        step = (
            first_new / first_fix / (jnp.sqrt(second_new / second_fix) + 1e-06)
            + decay_rate * weight
        )
        return first_new, second_new, step

    for n in range(len(parts)):
        pix_copy(n, False).wait()
        pix_copy(n, True).start()
    kg_out[...] = kg[...]
    gg_out[...] = gg[...]
    for k in range(2):
        kf_out[k], ks_out[k], step = update(kw[k], kg[k], kf[k], ks[k])
        kw_out[k] = kw[k] - step_rate * scalar(n_mats + k) * step
    first_new, second_new, step = update(gw[...], gg[...], gf[...], gs[...])
    gf_out[...] = first_new
    gs_out[...] = second_new
    row = lax.broadcasted_iota(jnp.int32, (4, 1), 0)
    rates = jnp.zeros((4, 1), fl_type)
    for k in range(4):
        rates = rates + jnp.where(row == k, scalar(n_mats + 2 + k), 0.0)
    gw_out[...] = gw[...] - step_rate * rates * step
    pix_width = iw.shape[0]
    row = (1, pix_width)
    rows = [small[n : n + 1] for n in range(2, 2 + -(-pix_width // 128))]
    in_grad = jnp.concatenate(rows, 1)[:, :pix_width]
    weight = iw[...].reshape(row)
    first_new, second_new, step = update(
        weight, in_grad, i_f[...].reshape(row), i_s[...].reshape(row)
    )
    in_trust = ratio(
        jnp.sum(weight * weight, 1, keepdims=True), jnp.sum(step * step, 1, keepdims=True)
    )
    ig_out[...] = in_grad.reshape(pix_width)
    if_out[...] = first_new.reshape(pix_width)
    is_out[...] = second_new.reshape(pix_width)
    iw_out[...] = (weight - step_rate * in_trust * step).reshape(pix_width)
    stores = []
    for n_span, (low, high) in enumerate(spans):
        for copy in loads[n_span]:
            copy.wait()
        for k in range(low, high):
            first_new, second_new, step = update(w_buf[k], g_buf[k], f_buf[k], s_buf[k])
            f_new[k] = first_new
            s_new[k] = second_new
            w_new[k] = w_buf[k] - step_rate * scalar(k) * step
        for n, (src, dst) in enumerate(
            ((g_buf, mg_out), (w_new, mw_out), (f_new, mf_out), (s_new, ms_out))
        ):
            copy = pltpu.make_async_copy(
                src.at[low:high], dst.at[low:high], out_sems.at[n, n_span]
            )
            copy.start()
            stores.append(copy)
    for copy in stores + [pix_copy(n, True) for n in range(len(parts))]:
        copy.wait()


def lamb_call(args):
    n_mats = args[3].shape[0]
    vmem, hbm = pl.BlockSpec(memory_space=pltpu.VMEM), pl.BlockSpec(memory_space=pl.ANY)
    block, lat, pix, mats, kv, gains = args[:6]
    row = args[16]
    shape = jax.ShapeDtypeStruct

    def like(value):
        return shape(value.shape, value.dtype)

    out_shape = [like(v) for v in (block, lat, pix, mats, kv, gains, row)]
    out_shape += [like(mats)] * 3 + [like(kv)] * 3 + [like(gains)] * 3 + [like(row)] * 3
    return pl.pallas_call(
        functools.partial(lamb, n_mats),
        out_shape=out_shape,
        in_specs=[vmem] * 2 + [hbm] * 2 + [vmem] * 3 + [hbm] * 3 + [vmem] * 9,
        out_specs=[vmem] * 2 + [hbm] * 2 + [vmem] * 3 + [hbm] * 3 + [vmem] * 9,
        scratch_shapes=[pltpu.VMEM(mats.shape, fl_type)] * 7
        + [
            pltpu.VMEM(pix.shape, fl_type),
            pltpu.SemaphoreType.DMA((4, n_mats)),
            pltpu.SemaphoreType.DMA((4, n_mats)),
            pltpu.SemaphoreType.DMA((2, 4)),
        ],
        compiler_params=pltpu.CompilerParams(vmem_limit_bytes=62 * 2**20),
        name="lamb",
    )(*args)


def local(
    latents,
    pixels,
    pix_counts,
    cotangent,
    weight_mats,
    kv_weights,
    norm_gains,
    input_gain,
    mats_first,
    mats_second,
    kv_first,
    kv_second,
    gains_first,
    gains_second,
    input_first,
    input_second,
):
    pix_width = pixels.shape[2]
    model_width = latents.shape[2]
    own_width = weight_mats.shape[1]
    n_dp, n_z = lax.axis_size("dp"), lax.axis_size("z")
    gain_at = round_up(pix_width, 8)
    pad_width = round_up(gain_at + 8, 128)

    def turned(value):
        return jnp.swapaxes(value, 1, 2)

    kv_cols = turned(kv_weights)
    pix_turned = jnp.transpose(pixels, (2, 0, 1))
    gathers = own_width % 16 == 0 and n_dp == 4 and n_z % 2 == 0 and n_z >= 4
    if gathers:
        weights = (weight_mats, kv_cols, norm_gains)
    else:
        extra = jnp.zeros((own_width, pad_width - gain_at - 4), fl_type)
        keys = [jnp.pad(kv_cols[0], ((0, 0), (0, gain_at - pix_width))), norm_gains.T, extra]
        values = jnp.pad(kv_cols[1], ((0, 0), (0, pad_width - pix_width)))
        both = jnp.stack(
            [
                jnp.concatenate([weight_mats[0]] + keys, 1),
                jnp.concatenate([weight_mats[1], values], 1),
            ]
        ).astype(bf_type)
        both = lax.all_gather(both, ALL, axis=1, tiled=True)
        others = lax.all_gather(weight_mats[2:].astype(bf_type), ALL, axis=1, tiled=True)
        weights = (both[0][None, None], both[1][None, None], others[:, None, None])
    (
        first_all, xn, pt, q_own, early, peak, qk, gains, block_rows, gk, stats, cross_rows, k_one, gterm,
        gain_cols, done_sum, done_far,
    ) = forward_call(
        n_z, n_dp, gathers, *weights, pix_counts, pix_turned, latents, cotangent, input_gain
    )
    first_all = first_all.reshape(model_width, model_width + pad_width)
    early = early.reshape(n_dp, 2, -1, model_width)
    summed = backward_call(
        n_z,
        n_dp,
        (
            gk,
            stats,
            early,
            block_rows,
            xn,
            pt,
            peak,
            qk,
            pix_turned,
            gain_cols,
            latents,
            first_all,
            gains,
            q_own,
            cross_rows,
            k_one,
            gterm,
            done_sum,
            done_far,
            weight_mats,
            mats_first,
            mats_second,
            kv_cols,
            turned(kv_first),
            turned(kv_second),
            norm_gains,
            gains_first,
            gains_second,
        ),
    )
    outs = lamb_call(
        (
            *summed,
            weight_mats,
            mats_first,
            mats_second,
            kv_cols,
            turned(kv_first),
            turned(kv_second),
            norm_gains,
            gains_first,
            gains_second,
            input_gain,
            input_first,
            input_second,
        )
    )
    outs = list(outs)
    outs[2] = jnp.transpose(outs[2], (1, 2, 0))
    for index in (4, 10, 11, 12):
        outs[index] = turned(outs[index])
    return tuple(outs)


def solution(mesh):
    n_dp, n_rows = mesh.devices.shape
    split_mesh = Mesh(mesh.devices.reshape(n_dp, n_rows // 2, 2), ALL)
    rows = ("z", "core")
    items = P("dp", None, None)
    pix = P("dp", rows, None)
    mats = P(None, ALL, None)
    pairs = P(None, None, ALL)
    gains = P(None, ALL)
    in_specs = (
        items,
        pix,
        P("dp"),
        items,
        mats,
        pairs,
        gains,
        P(),
        mats,
        mats,
        pairs,
        pairs,
        gains,
        gains,
        P(),
        P(),
    )
    out_specs = (
        pix,
        pix,
        pix,
        mats,
        pairs,
        gains,
        P(),
        mats,
        mats,
        mats,
        pairs,
        pairs,
        pairs,
        gains,
        gains,
        gains,
        P(),
        P(),
        P(),
    )
    return jax.shard_map(
        local, mesh=split_mesh, in_specs=in_specs, out_specs=out_specs, check_vma=False
    )
```

```python
import functools
import math

import jax
import jax.numpy as jnp
from jax import lax
from jax.experimental import pallas as pl
from jax.experimental.pallas import tpu as pltpu
from jax.sharding import Mesh, PartitionSpec as P

HEADS = 8
first_fix = 1.0 - 0.9**10
second_fix = 1.0 - 0.999**10
step_rate = 0.25
decay_rate = 0.01
bf_type = jnp.bfloat16
fl_type = jnp.float32
ALL = ("dp", "z", "core")
NT = (((1,), (1,)), ((), ()))
TN = (((0,), (0,)), ((), ()))
NN = (((1,), (0,)), ((), ()))
MESH = pl.DeviceIdType.MESH
PIECES = ((2, 4), (4, 6), (6, 8), (8, 10))
LAST = 6


def dot(left_side, right_side, dims=NN):
    return lax.dot_general(left_side, right_side, dims, preferred_element_type=fl_type)


def round_up(value, unit):
    return -(-value // unit) * unit


def tile_of(rows, unit, most):
    best = unit
    for size in range(unit, most + 1, unit):
        if rows % size == 0:
            best = size
    return best


def meet(peers):
    barrier = pltpu.get_barrier_semaphore()
    for peer in peers:
        pl.semaphore_signal(barrier, inc=1, device_id=peer, device_id_type=MESH)
    pl.semaphore_wait(barrier, len(peers))


def lane_parts(total, size, body):
    def step(t, _):
        body(pl.multiple_of(t * size, size), size)
        return 0

    lax.fori_loop(0, total // size, step, 0)
    if total % size:
        body(total - total % size, total % size)


def remote(src, dst, sems, index, peer):
    return pltpu.make_async_remote_copy(
        src_ref=src,
        dst_ref=dst,
        send_sem=sems.at[0, index],
        recv_sem=sems.at[1, index],
        device_id=peer,
        device_id_type=MESH,
    )


class Gather:
    def __init__(self, whole, lead, sems, n_z):
        self.whole, self.lead, self.sems, self.n_z = whole, lead, sems, n_z
        self.d, self.z, self.c = (lax.axis_index(name) for name in ALL)
        self.z_from = [lax.rem(self.z + n_z - i, n_z) for i in range(n_z)]
        self.z_to = [lax.rem(self.z + i, n_z) for i in range(n_z)]
        self.across = (self.d, self.z, 1 - self.c)
        self.sent = []

    def region(self, flip, start, count, core):
        chips = pl.ds((self.d ^ flip) * self.n_z + start, count)
        return self.whole.at[(*self.lead, chips, core)]

    def copy(self, region, kind, index, peer):
        return pltpu.make_async_remote_copy(
            src_ref=region,
            dst_ref=region,
            send_sem=self.sems.at[0, kind, index],
            recv_sem=self.sems.at[1, kind, index],
            device_id=peer,
            device_id_type=MESH,
        )

    def send(self, region, kind, index, peer, count=1):
        self.copy(region, kind, index, peer).start()
        self.sent.append((kind, index, count))

    def arrived(self, region, kind, index):
        self.copy(region, kind, index, self.across).wait_recv()

    def start_z(self):
        mine = self.region(0, self.z, 1, self.c)
        for i in range(1, self.n_z):
            self.send(mine, 0, i, (self.d, self.z_to[i], self.c))

    def to_plane(self, region, index):
        self.send(region, 1, index, (self.d ^ 1, self.z, self.c))
        self.send(region, 2, index, (self.d ^ 2, self.z, self.c))

    def start_plane(self):
        self.to_plane(self.region(0, self.z, 1, self.c), 0)

    def relay_z(self):
        for i in range(1, self.n_z):
            region = self.region(0, self.z_from[i], 1, self.c)
            self.arrived(region, 0, i)
            self.to_plane(region, i)
        self.send(self.region(0, 0, self.n_z, self.c), 4, 0, self.across, self.n_z)

    def relay_plane(self):
        half = self.n_z // 2
        for kind, flip, onward, start in ((1, 1, 2, 0), (2, 2, 1, half)):
            for i in range(self.n_z):
                self.arrived(self.region(flip, self.z_from[i], 1, self.c), kind, i)
            region = self.region(flip, start, half, self.c)
            self.send(region, 3, kind - 1, (self.d ^ onward, self.z, self.c), half)
        for kind, flip in ((1, 1), (2, 2)):
            region = self.region(flip, 0, self.n_z, self.c)
            self.send(region, 4 + kind, 0, self.across, self.n_z)

    def relay_far(self):
        half = self.n_z // 2
        self.arrived(self.region(3, 0, half, self.c), 3, 0)
        self.arrived(self.region(3, half, half, self.c), 3, 1)
        self.send(self.region(3, 0, self.n_z, self.c), 7, 0, self.across, self.n_z)

    def finish(self):
        for flip in range(4):
            self.arrived(self.region(flip, 0, self.n_z, 1 - self.c), 4 + flip, 0)

    def drain(self):
        for kind, index, count in self.sent:
            self.copy(self.region(0, 0, count, self.c), kind, index, self.across).wait_send()


class Whole:
    def __init__(self, ref, low, high):
        self.ref, self.low, self.high = ref, low, high

    def __getitem__(self, _):
        return self.ref[..., self.low : self.high].reshape(-1, self.high - self.low)


def forward(n_z, n_dp, gathers, pix_width, chunk, *refs):
    counts, first_in, second_in, rest_in, pix_hbm, lat_hbm, cot_hbm, gain_ref = refs[:8]
    (
        first_out, xn_out, pt_out, q_out, early_out,
        peak_ref, qk_ref, gains_ref, block_ref, gk_both, stats_both, cross_ref, k_one_ref, gterm_ref,
        gain_cols, done_sum, done_far,
    ) = refs[8:25]
    (
        first_all, second_all, mats, px_tx, px_rx, st_tx, st_rx, px2_tx, px2_rx, st2_tx, st2_rx,
        fin_tx, mean_ref, stat_ref, col_sems, term_sems, local_sems,
    ) = refs[25:42]
    gather_sems = refs[42:]
    d, z, c = (lax.axis_index(name) for name in ALL)
    n_items, lat_len, width = lat_hbm.shape
    pix_dev, pad_width = xn_out.shape[1:]
    own = width // (n_dp * n_z * 2)
    held = chunk * n_z
    peers = [(d, lax.rem(z + i, n_z), c) for i in range(1, n_z)] + [(d, z, 1 - c)]
    if gathers:
        peers += [(d ^ 1, z, c), (d ^ 2, z, c)]
    local = iter(range(1000))

    def copy_here(src, dst):
        copy = pltpu.make_async_copy(src, dst, local_sems.at[next(local)])
        copy.start()
        return copy

    if gathers:
        first = Gather(first_all, (), gather_sems[0], n_z)
        rest = [Gather(second_all, (), gather_sems[1], n_z)]
        for index, (low, high) in enumerate(PIECES):
            rest.append(Gather(mats, (pl.ds(low - 2, high - low),), gather_sems[2 + index], n_z))
        ready = [(21, 30, 50), (31, 42, 60), (39, 50, 70), (45, 60, 77), (58, 73, 85)]
        steps = []
        for piece, times in zip(rest, ready, strict=True):
            relays = (piece.relay_z, piece.relay_plane, piece.relay_far)
            steps += list(zip(times, relays, strict=True))
        steps.sort(key=lambda step: step[0])
        done, whole_now = [0], set()

        def pump(time):
            while done[0] < len(steps) and steps[done[0]][0] <= time:
                steps[done[0]][1]()
                done[0] += 1

        def weight(k):
            piece = sum(low <= k for low, _ in PIECES)
            if piece not in whole_now:
                pump(ready[piece][2])
                rest[piece].finish()
                whole_now.add(piece)
            return Whole(mats.at[k - 2] if piece else second_all, 0, width)

    else:
        loads = {0: copy_here(first_in, first_all), 1: copy_here(second_in, second_all)}
        for k in range(2, mats.shape[0] + 2):
            loads[k] = copy_here(rest_in.at[k - 2], mats.at[k - 2])

        def pump(time):
            pass

        def weight(k):
            if k in loads:
                loads.pop(k).wait()
            return Whole(mats.at[k - 2] if k > 1 else second_all, 0, width)

    def kt_one():
        weight(1)
        return Whole(second_all, width, width + pad_width)

    def column_copy(src, dst, index, peer):
        return remote(src, dst, col_sems, index, peer)

    def pixel_phase(pix, lat, xn, pt, s_buf, q_all, px_own, xt, turn, *own_bufs):
        l_pix, l_lat = copy_here(pix_hbm, pix), copy_here(lat_hbm, lat)
        if gathers:
            own_mats, own_cols = own_bufs
            l_own = copy_here(first_in, own_mats)
        turn[...] = jnp.zeros(turn.shape, fl_type)
        turn[0:1, :pix_width] = gain_ref[...].reshape(1, pix_width)
        gain_cols[...] = turn[...].T
        gain_col = gain_cols[:pix_width, :1]
        meet(peers)
        if gathers:
            me = d * n_z + z
            gain_at = round_up(pix_width, 8) - (pad_width - 128)
            turn[...] = jnp.zeros(turn.shape, fl_type)
            turn[gain_at : gain_at + 4, :own] = rest_in[...]
            l_own.wait()
            for k, whole in ((0, first_all), (1, second_all)):
                own_cols[...] = jnp.zeros(own_cols.shape, fl_type)
                own_cols[:, :pix_width] = second_in[k]
                if k == 0:
                    own_cols[:, pad_width - 128 :] += turn[:, :128].T[:own]
                whole[me, c, :, :width] = own_mats[k].astype(bf_type)
                whole[me, c, :, width:] = own_cols[...].astype(bf_type)
                if k == 0:
                    first.start_z()
                    first.start_plane()
            for k in range(mats.shape[0]):
                mats[k, me, c] = own_mats[k + 2].astype(bf_type)
            for piece in rest[:-1]:
                piece.start_z()
            for piece in rest[:2]:
                piece.start_plane()
        xt[...] = jnp.zeros(xt.shape, fl_type)
        rows = tile_of(pix_dev, 16, 256)
        tiles = pix_dev // rows

        def normalise(item):
            def part(start, size):
                values = pix[:, item, pl.ds(start, size)].astype(fl_type)
                centred = values - jnp.sum(values, 0, keepdims=True) * (1.0 / pix_width)
                var = jnp.sum(centred * centred, 0, keepdims=True) * (1.0 / pix_width)
                xt[:pix_width, :size] = centred * lax.rsqrt(var + 1e-05) * gain_col
                turned = round_up(size, 128)
                low = xt[:, :turned].T.astype(bf_type)
                xn[item, pl.ds(start, size), :] = low[:size]

            lane_parts(pix_dev, 256, part)

        l_pix.wait()
        normalise(0)
        if gathers:
            first.relay_z()
        for item in range(1, n_items):
            normalise(item)
        xn_copy = copy_here(xn, xn_out)
        if gathers:
            first.relay_plane()
            for piece in rest[2:]:
                piece.start_plane()
            first.relay_far()
            pump(21)
            first.finish()
        else:
            loads.pop(0).wait()
        first_copy = copy_here(first_all, first_out)
        l_lat.wait()
        gain_at = round_up(pix_width, 8) - (pad_width - 128)
        tail = Whole(first_all, width + pad_width - 128, width + pad_width)[...]
        tail = tail.astype(fl_type).T
        gains_ref[...] = tail[gain_at : gain_at + 8]
        lat_rows = tile_of(lat_len, 128, 256)
        for item in range(n_items):

            def queries(t, _, item=item):
                at = pl.ds(pl.multiple_of(t * lat_rows, lat_rows), lat_rows)
                values = lat[item, at, :].astype(fl_type)
                centred = values - jnp.mean(values, -1, keepdims=True)
                var = jnp.mean(centred * centred, -1, keepdims=True)
                normal = (centred * lax.rsqrt(var + 1e-05) * gains_ref[:1]).astype(bf_type)
                q_low = dot(normal, Whole(first_all, 0, width)[...]).astype(bf_type)
                q_all[item, at, :] = q_low
                raw = dot(q_low, Whole(first_all, width, width + pad_width)[...])
                qk_ref[item, :, at] = (raw * width**-0.5).T.astype(bf_type)
                return 0

            lax.fori_loop(0, lat_len // lat_rows, queries, 0)
            pump(31 + 3 * item)
        q_copy = copy_here(q_all.at[c], q_out)

        base = (z * 2 + c) * pix_dev
        for item in range(n_items):
            valid = counts[item] - base

            def score(t, most, item=item, valid=valid):
                at = pl.ds(pl.multiple_of(t * rows, rows), rows)
                values = dot(xn[item, at, :], qk_ref[item])
                place = lax.broadcasted_iota(jnp.int32, values.shape, 0) + t * rows
                values = jnp.where(place < valid, values, -1e30)
                s_buf[at, :] = values
                return jnp.maximum(most, jnp.max(values.reshape(rows // 8, 8, lat_len), 0))

            most = lax.fori_loop(0, tiles, score, jnp.full((8, lat_len), -1e30, fl_type))
            peak = jnp.max(most, 0, keepdims=True)
            pump(36 + 6 * item)

            def weigh(t, total, item=item, peak=peak):
                at = pl.ds(pl.multiple_of(t * rows, rows), rows)
                values = jnp.exp(s_buf[at, :] - peak)
                pt[item, at, :] = values.astype(bf_type)
                return total + jnp.sum(values.reshape(rows // 8, 8, lat_len), 0)

            total = lax.fori_loop(0, tiles, weigh, jnp.zeros((8, lat_len), fl_type))
            total = jnp.sum(total, 0, keepdims=True)
            peak_ref[item] = jnp.broadcast_to(peak, (8, lat_len))
            st_tx[item, :4] = jnp.broadcast_to(peak, (4, lat_len))
            st_tx[item, 4:] = jnp.broadcast_to(total, (4, lat_len))
            part = dot(xn[item], pt[item], TN)
            px_own[item, : part.shape[0]] = part
            if held > part.shape[0]:
                px_own[item, part.shape[0] :] = jnp.zeros((held - part.shape[0], lat_len), fl_type)
            px_tx[item] = px_own[item, :held].astype(bf_type)
            pump(39 + 5 * item)
        pt_copy = copy_here(pt, pt_out)
        pair = [
            column_copy(px_tx.at[1 - c], px_rx, 0, (d, z, 1 - c)),
            column_copy(st_tx.at[1 - c], st_rx, 1, (d, z, 1 - c)),
        ]
        for copy in pair:
            copy.start()
        for copy in pair:
            copy.wait()
        peak_own, peak_rx = st_tx[c, :1], st_rx[:1]
        peak = jnp.maximum(peak_own, peak_rx)
        scale_own, scale_rx = jnp.exp(peak_own - peak), jnp.exp(peak_rx - peak)
        st2_tx[:4] = jnp.broadcast_to(peak, (4, lat_len))
        st2_tx[4:] = jnp.broadcast_to(
            scale_own * st_tx[c, 4:5] + scale_rx * st_rx[4:5], (4, lat_len)
        )
        both = px_own[c, :held] * scale_own + px_rx[...].astype(fl_type) * scale_rx
        px2_tx[...] = both.astype(bf_type).reshape(n_z, chunk, lat_len)
        for copy in (xn_copy, first_copy, q_copy, pt_copy):
            copy.wait()

    own_bufs = []
    if gathers:
        own_bufs = [pltpu.VMEM(first_in.shape, fl_type), pltpu.VMEM((own, pad_width), fl_type)]
    pl.run_scoped(
        pixel_phase,
        pltpu.VMEM(pix_hbm.shape, bf_type),
        pltpu.VMEM(lat_hbm.shape, bf_type),
        pltpu.VMEM(xn_out.shape, bf_type),
        pltpu.VMEM(pt_out.shape, bf_type),
        pltpu.VMEM((pix_dev, lat_len), fl_type),
        pltpu.VMEM(lat_hbm.shape, bf_type),
        pltpu.VMEM((n_items, max(held, pad_width), lat_len), fl_type),
        pltpu.VMEM((pad_width, 256), fl_type),
        pltpu.VMEM((128, pad_width), fl_type),
        *own_bufs,
    )

    copies = []
    for i in range(1, n_z):
        to = lax.rem(z + i, n_z)
        copies.append(column_copy(px2_tx.at[to], px2_rx.at[z], 2 * i, (d, to, c)))
        copies.append(column_copy(st2_tx, st2_rx.at[z], 2 * i + 1, (d, to, c)))
    for copy in copies:
        copy.start()
    if gathers:
        rest[-1].start_z()
    pump(50)
    for copy in copies:
        copy.wait()
    pump(57)
    peak = st2_tx[:1]
    froms = [lax.rem(z + n_z - i, n_z) for i in range(1, n_z)]
    for other in froms:
        peak = jnp.maximum(peak, st2_rx[other, :1])
    scale = jnp.exp(st2_tx[:1] - peak)
    total = scale * st2_tx[4:5]
    mean = scale * px2_tx[z].astype(fl_type)
    for other in froms:
        scale = jnp.exp(st2_rx[other, :1] - peak)
        total = total + scale * st2_rx[other, 4:5]
        mean = mean + scale * px2_rx[other].astype(fl_type)
    stat_ref[:8] = jnp.broadcast_to(peak, (8, lat_len))
    stat_ref[8:] = jnp.broadcast_to(total, (8, lat_len))
    fin_tx[...] = (mean / total).astype(bf_type)
    own_rows = pl.ds(pl.multiple_of(z * chunk, chunk), chunk)
    copies = []
    for i in range(1, n_z):
        to = lax.rem(z + i, n_z)
        copies.append(column_copy(fin_tx, mean_ref.at[own_rows], 2 * n_z + i, (d, to, c)))
    for copy in copies:
        copy.start()
    pump(60)
    for copy in copies:
        copy.wait()
    mean_ref[own_rows] = fin_tx[...]
    if gathers:
        first.drain()

    def chain_phase(lat, cot, stage, *bufs):
        l_lat, l_cot = copy_here(lat_hbm.at[c], lat), copy_here(cot_hbm.at[c], cot)
        stages, lead = stage.shape[0], len(stage.shape) - 3
        put_sems = [next(local) for _ in range(stages)]
        order, pending, flying, far_flying = [], [], [None] * stages, []
        far = [lax.rem(d + i, n_dp) for i in range(1, n_dp)]

        def place(k):
            return first_all.at[pl.ds(2 * (k - 1 - LAST), 2), :, :, :width]

        def settle(k, buffer, copy):
            copy.wait()
            index = (lax.div(d, 2), lax.rem(d, 2))
            rows = pl.ds((k - 1 - LAST) * own, own)
            whole = place(k)
            mine = stage[(buffer, *index, c)].astype(fl_type) + whole[index].astype(fl_type)
            done_sum[rows, :] = mine
            both = stage[buffer, :, :, c].astype(fl_type) + whole[...].astype(fl_type)
            whole[...] = both.astype(bf_type)
            for n, to in enumerate(far):
                copy = remote(
                    whole.at[lax.div(to, 2), lax.rem(to, 2)],
                    done_far.at[d, rows],
                    term_sems,
                    8 + 3 * (k - 1 - LAST) + n,
                    (to, z, c),
                )
                copy.start()
                far_flying.append(copy)

        def put(k):
            while len(pending) > 1:
                settle(*pending.pop(0))
            buffer = len(order) % stages
            order.append(k)
            if flying[buffer] is not None:
                flying[buffer].wait()
                flying[buffer] = None
            if any(entry[1] == buffer for entry in pending):
                settle(*pending.pop(0))

            def start():
                if gathers and k > LAST:
                    source = stage.at[buffer, :, :, 1 - c]
                    copy = remote(source, place(k), term_sems, k - 1 - LAST, (d, z, 1 - c))
                    copy.start()
                    pending.append((k, buffer, copy))
                else:
                    at = (slice(None),) * lead + (pl.ds((k - 1) * own, own),)
                    copy = pltpu.make_async_copy(
                        stage.at[buffer], early_out.at[at], local_sems.at[put_sems[buffer]]
                    )
                    copy.start()
                    flying[buffer] = copy

            return stage.at[buffer], start

        outs = (
            put,
            block_ref,
            gk_both.at[c],
            stats_both.at[c],
            cross_ref,
            k_one_ref,
            gterm_ref,
        )
        l_lat.wait()
        l_cot.wait()
        latent_chain(
            n_z, n_dp, own, weight, kt_one, pump, lat, cot, gains_ref, mean_ref, stat_ref, outs, bufs
        )
        pair = [
            column_copy(gk_both.at[c], gk_both.at[c], 3 * n_z, (d, z, 1 - c)),
            column_copy(stats_both.at[c], stats_both.at[c], 3 * n_z + 1, (d, z, 1 - c)),
        ]
        for copy in pair:
            copy.start()
        while pending:
            settle(*pending.pop(0))
        for copy in [copy for copy in flying if copy is not None] + pair + far_flying:
            copy.wait()

    wire = early_out.dtype
    one_item = pltpu.VMEM((lat_len, width), bf_type)
    n_cols = n_dp * 2 * own
    pl.run_scoped(
        chain_phase,
        one_item,
        one_item,
        pltpu.VMEM((3, *early_out.shape[:-2], own, width), wire),
        *chain_bufs(lat_len, width, pad_width, n_cols),
    )
    if gathers:
        pump(1000)
        for piece in rest:
            piece.drain()


def forward_call(n_z, n_dp, gathers, first, second, rest, counts, pix_turned, latents, cotangent, gain):
    n_items, lat_len, width = latents.shape
    pix_width, _, pix_dev = pix_turned.shape
    own = width // (n_dp * n_z * 2)
    blocks = (n_dp * n_z, 2, own) if gathers else (1, 1, width)
    n_rest = 8
    pad_width = round_up(round_up(pix_width, 8) + 8, 128)
    wire = bf_type if own % 16 == 0 else fl_type
    chunk = round_up(-(-pix_width // n_z), 16)
    held = chunk * n_z
    z_share = lat_len // n_z
    n_cols = n_dp * 2 * own
    vmem, hbm = pl.BlockSpec(memory_space=pltpu.VMEM), pl.BlockSpec(memory_space=pl.ANY)
    shape, buf = jax.ShapeDtypeStruct, pltpu.VMEM
    out_shape = [
        shape((*blocks, width + pad_width), bf_type),
        shape((n_items, pix_dev, pad_width), bf_type),
        shape((n_items, pix_dev, lat_len), bf_type),
        shape((lat_len, width), bf_type),
        shape((2, 2, 2, LAST * own, width) if gathers else (n_dp, 2, 9 * own, width), wire),
        shape((n_items, 8, lat_len), fl_type),
        shape((n_items, pad_width, lat_len), bf_type),
        shape((8, width), fl_type),
        shape((2, z_share // 2, width), bf_type),
        shape((n_items, pad_width, lat_len), bf_type),
        shape((n_items, 3, 8, lat_len), fl_type),
        shape((z_share, width), fl_type),
        shape((n_cols, pad_width), fl_type),
        shape((8, width), fl_type),
        shape((pad_width, 128), fl_type),
        shape(((9 - LAST) * own, width), fl_type),
        shape((n_dp, (9 - LAST) * own, width), wire),
    ]
    scratch = [
        buf((*blocks, width + pad_width), bf_type),
        buf((*blocks, width + pad_width), bf_type),
        buf((n_rest, *blocks, width), bf_type),
        buf((n_items, held, lat_len), bf_type),
        buf((held, lat_len), bf_type),
        buf((n_items, 8, lat_len), fl_type),
        buf((8, lat_len), fl_type),
        buf((n_z, chunk, lat_len), bf_type),
        buf((n_z, chunk, lat_len), bf_type),
        buf((8, lat_len), fl_type),
        buf((n_z, 8, lat_len), fl_type),
        buf((chunk, lat_len), bf_type),
        buf((held, lat_len), bf_type),
        buf((16, lat_len), fl_type),
        pltpu.SemaphoreType.DMA((2, 3 * n_z + 2)),
        pltpu.SemaphoreType.DMA((2, 32)),
        pltpu.SemaphoreType.DMA((32,)),
    ]
    if gathers:
        scratch += [pltpu.SemaphoreType.DMA((2, 8, n_z))] * (2 + len(PIECES))
    weight_specs = [hbm, vmem, vmem] if gathers else [hbm] * 3
    return pl.pallas_call(
        functools.partial(forward, n_z, n_dp, gathers, pix_width, chunk),
        out_shape=out_shape,
        in_specs=[pl.BlockSpec(memory_space=pltpu.SMEM)] + weight_specs + [hbm] * 3 + [vmem],
        out_specs=[hbm] * 5 + [vmem] * 11 + [hbm],
        scratch_shapes=scratch,
        compiler_params=pltpu.CompilerParams(
            collective_id=0, has_side_effects=True, vmem_limit_bytes=62 * 2**20
        ),
        name="forward",
    )(counts, first, second, rest, pix_turned, latents, cotangent, gain)


def row_loop(total, body, rows=128):
    def step(t, _):
        body(pl.ds(pl.multiple_of(t * rows, rows), rows))
        return 0

    lax.fori_loop(0, total // rows, step, 0)


def tanh_gelu(values):
    factor, cubic = (2.0 / math.pi) ** 0.5, 0.044715
    square = values * values
    bent = jnp.tanh(factor * values * (1.0 + cubic * square))
    half = 0.5 * (1.0 + bent)
    slope = half + 0.5 * values * (1.0 - bent * bent) * factor * (1.0 + 3.0 * cubic * square)
    return values * half, slope


def choose(sel_ref, n_dp, n_z, pair_width):
    width, n_cols = sel_ref.shape
    z = lax.axis_index("z")
    wanted = lax.broadcasted_iota(jnp.int32, (width, n_cols), 1)
    wanted = (lax.div(wanted, pair_width) * n_z + z) * pair_width + lax.rem(wanted, pair_width)
    place = lax.broadcasted_iota(jnp.int32, (width, n_cols), 0)
    sel_ref[...] = jnp.where(place == wanted, 1.0, 0.0).astype(bf_type)


def latent_chain(n_z, n_dp, own, weight, kt_one, pump, lat, cot, gains, mean_ref, stat_ref, outs, bufs):
    put, block_ref, gk_ref, stats_ref, cross_ref, k_one_ref, gterm_ref = outs
    (
        run, x_buf, hat_c, hat_s, hat_f, inv, slope_c, slope_f,
        even, odd, q_s, k_s, v_s, probs, sel, mean_pad, picks,
    ) = bufs
    lat_len, width = lat.shape
    pad_width = mean_pad.shape[1]
    head_dim = width // HEADS
    z = lax.axis_index("z")
    z_share = lat_len // n_z
    z_rows = pl.ds(pl.multiple_of(z * z_share, z_share), z_share)
    choose(sel, n_dp, n_z, 2 * own)
    att = gelu_c = mixed = gelu_f = even
    norm_c = norm_s = norm_f = odd
    tmp = lat

    def add_norm(base, gain, hat, which, normal):
        def body(at):
            values = base(at) + x_buf[at, :]
            run[at, :] = values
            centred = values - jnp.mean(values, -1, keepdims=True)
            scale = lax.rsqrt(jnp.mean(centred * centred, -1, keepdims=True) + 1e-05)
            standard_values = centred * scale
            hat[at, :] = standard_values
            inv[which, at, :] = jnp.broadcast_to(scale, (scale.shape[0], 128))
            normal[at, :] = (standard_values * gains[gain : gain + 1]).astype(bf_type)

        row_loop(lat_len, body)

    def activate(slope, low):
        def body(at):
            value, grad = tanh_gelu(x_buf[at, :])
            low[at, :] = value.astype(bf_type)
            slope[at, :] = grad

        row_loop(lat_len, body)

    parts = lat_len // 128
    part_cols = width // parts

    def pick(n, ref):
        picks[n] = dot(ref[...], sel[...]).astype(bf_type)

    def terms(*wanted):
        staged = [(put(k), n, right) for k, n, right in wanted]

        def part(t):
            cols = pl.ds(pl.multiple_of(t * part_cols, part_cols), part_cols)
            for (buffer, _), n, right in staged:
                term = dot(picks[n], right[:, cols], TN).astype(buffer.dtype)
                buffer[..., cols] = term.reshape(*buffer.shape[:-1], part_cols)

        def send():
            for (_, start), _, _ in staged:
                start()

        return part, send

    def times_slope(slope, low, beside):
        def body(t, _):
            at = pl.ds(pl.multiple_of(t * 128, 128), 128)
            beside[0](t)
            low[at, :] = (x_buf[at, :] * slope[at, :]).astype(bf_type)
            return 0

        lax.fori_loop(0, parts, body, 0)
        beside[1]()

    def pull_norm(base, gain, hat, which, low, beside):
        def body(t, sums):
            at = pl.ds(pl.multiple_of(t * 128, 128), 128)
            beside[0](t)
            grad = x_buf[at, :]
            normal = hat[at, :]
            sums = sums + jnp.sum((normal * grad).reshape(16, 8, width), 0)
            grad = grad * gains[gain : gain + 1]
            mean = jnp.mean(grad, -1, keepdims=True)
            along = jnp.mean(grad * normal, -1, keepdims=True)
            value = base(at) + (grad - mean - normal * along) * inv[which, at, :1]
            run[at, :] = value
            low[at, :] = value.astype(bf_type)
            return sums

        sums = lax.fori_loop(0, parts, body, jnp.zeros((8, width), fl_type))
        beside[1]()
        gterm_ref[gain : gain + 1] = jnp.sum(sums, 0, keepdims=True)

    def matrix_term(k, n, right):
        buffer, start = put(k)
        buffer[...] = dot(picks[n], right[...], TN).astype(buffer.dtype).reshape(buffer.shape)
        start()

    def head(h):
        return slice(h * head_dim, (h + 1) * head_dim)

    head_scale = head_dim**-0.5
    gterm_ref[...] = jnp.zeros(gterm_ref.shape, fl_type)

    pump(65)
    mean_pad[...] = jnp.zeros(mean_pad.shape, bf_type)
    held = min(mean_ref.shape[0], pad_width)
    mean_pad[:, :held] = mean_ref[:held].astype(fl_type).T.astype(bf_type)
    att[...] = dot(mean_pad[...], kt_one()[...], NT).astype(bf_type)
    x_buf[...] = dot(att[...], weight(1)[...])
    pick(0, att)
    add_norm(lambda at: lat[at, :].astype(fl_type), 1, hat_c, 0, norm_c)
    pump(70)
    x_buf[...] = dot(norm_c[...], weight(2)[...])
    pick(1, norm_c)
    activate(slope_c, gelu_c)
    pump(73)
    x_buf[...] = dot(gelu_c[...], weight(3)[...])
    pick(2, gelu_c)
    add_norm(lambda at: run[at, :], 2, hat_s, 1, norm_s)
    pump(75)
    q_s[...] = dot(norm_s[...], weight(4)[...]).astype(bf_type)
    k_s[...] = dot(norm_s[...], weight(5)[...]).astype(bf_type)
    pump(77)
    v_s[...] = dot(norm_s[...], weight(6)[...]).astype(bf_type)
    pick(3, norm_s)

    def attend(h):
        at = head(h)
        scores = dot(k_s[:, at], q_s[:, at], NT) * head_scale
        weights = jnp.exp(scores - jnp.max(scores, 0, keepdims=True))
        weights = weights * (1.0 / jnp.sum(weights, 0, keepdims=True))
        low = weights.astype(bf_type)
        probs[h] = low
        mixed[:, at] = dot(low, v_s[:, at], TN).astype(bf_type)

    for h in range(HEADS):
        attend(h)
    pump(85)
    x_buf[...] = dot(mixed[...], weight(7)[...])
    pick(4, mixed)
    add_norm(lambda at: run[at, :], 3, hat_f, 2, norm_f)
    x_buf[...] = dot(norm_f[...], weight(8)[...])
    pick(5, norm_f)
    activate(slope_f, gelu_f)
    final = run[z_rows, :] + dot(gelu_f[z_rows, :], weight(9)[...])
    block_ref[...] = final.astype(bf_type).reshape(block_ref.shape)

    pick(6, gelu_f)

    x_buf[...] = dot(cot[...], weight(9)[...], NT)
    times_slope(slope_f, tmp, terms((9, 6, cot)))
    x_buf[...] = dot(tmp[...], weight(8)[...], NT)
    pull_norm(lambda at: cot[at, :].astype(fl_type), 3, hat_f, 2, odd, terms((8, 5, tmp)))
    grad_mixed = even
    grad_mixed[...] = dot(odd[...], weight(7)[...], NT).astype(bf_type)
    matrix_term(7, 4, odd)

    def attend_back(h):
        at = head(h)
        q_h, k_h, v_h, grad_h = q_s[:, at], k_s[:, at], v_s[:, at], grad_mixed[:, at]
        low = probs[h]
        weights = low.astype(fl_type)
        grad_weights = dot(v_h, grad_h, NT)
        along = jnp.sum(weights * grad_weights, 0, keepdims=True)
        grad_scores = (weights * (grad_weights - along)).astype(bf_type)
        q_s[:, at] = (dot(grad_scores, k_h, TN) * head_scale).astype(bf_type)
        k_s[:, at] = (dot(grad_scores, q_h) * head_scale).astype(bf_type)
        v_s[:, at] = dot(low, grad_h).astype(bf_type)

    for h in range(HEADS):
        attend_back(h)
    x_buf[...] = dot(q_s[...], weight(4)[...], NT)
    x_buf[...] += dot(k_s[...], weight(5)[...], NT)
    x_buf[...] += dot(v_s[...], weight(6)[...], NT)
    selves = terms((4, 3, q_s), (5, 3, k_s), (6, 3, v_s))
    pull_norm(lambda at: run[at, :], 2, hat_s, 1, tmp, selves)
    x_buf[...] = dot(tmp[...], weight(3)[...], NT)
    times_slope(slope_c, odd, terms((3, 2, tmp)))
    x_buf[...] = dot(odd[...], weight(2)[...], NT)
    pull_norm(lambda at: run[at, :], 1, hat_c, 0, tmp, terms((2, 1, odd)))
    grad_att = even
    grad_att[...] = dot(tmp[...], weight(1)[...], NT).astype(bf_type)
    matrix_term(1, 0, tmp)
    cross_ref[...] = run[z_rows, :]
    low = dot(grad_att[...], kt_one()[...]).T.astype(bf_type)
    gk_ref[...] = low
    delta = jnp.sum(low[:held].astype(fl_type) * mean_ref[:held].astype(fl_type), 0, keepdims=True)
    stats_ref[0] = stat_ref[:8]
    stats_ref[1] = stat_ref[8:]
    stats_ref[2] = jnp.broadcast_to(delta, stats_ref.shape[1:])
    k_one_ref[...] = dot(dot(grad_att[...], sel[...]).astype(bf_type), mean_pad[...], TN)


def chain_bufs(lat_len, width, pad_width, n_cols):
    wide = pltpu.VMEM((lat_len, width), fl_type)
    low = pltpu.VMEM((lat_len, width), bf_type)
    return (
        [wide] * 5
        + [pltpu.VMEM((3, lat_len, 128), fl_type)]
        + [wide] * 2
        + [low] * 5
        + [
            pltpu.VMEM((HEADS, lat_len, lat_len), bf_type),
            pltpu.VMEM((width, n_cols), bf_type),
            pltpu.VMEM((lat_len, pad_width), bf_type),
            pltpu.VMEM((7, lat_len, n_cols), bf_type),
        ]
    )


def backward(n_z, n_dp, pix_width, chunk, *refs):
    (
        gk_all,
        stats_all,
        early_ref,
        block_ref,
        xn_hbm,
        pt_hbm,
        peak_ref,
        qk_ref,
        pix_hbm,
        gain_ref,
        lat_hbm,
        first_hbm,
        gains_ref,
        q_hbm,
        cross_ref,
        k_one_ref,
        gterm_ref,
        done_sum_hbm,
        done_far_hbm,
        mats_hbm,
        mfirst_hbm,
        msecond_hbm,
        kv_ref,
        kfirst_ref,
        ksecond_ref,
        ng_ref,
        gfirst_ref,
        gsecond_ref,
        block_out,
        lat_out,
        pix_out,
        mats_out,
        kv_out,
        gains_out,
        small_out,
        xn,
        pt,
        pix,
        lat,
        first,
        q_own,
        mats,
        mfirst,
        msecond,
        ds,
        pl_low,
        part_tx,
        part_own,
        part_rx,
        col_tx,
        col_rx,
        fin_tx,
        fin_rx,
        dst_full,
        early_own,
        early_rx,
        early_tx,
        early_sum,
        early_far,
        done_sum,
        done_far,
        pix_buf,
        hat,
        inv,
        norm,
        dq,
        da,
        sel,
        lat_tx,
        late,
        late_rx,
        late_tx,
        late_own,
        late_far,
        small_tx,
        small_col,
        small_far_tx,
        small_far,
        input_acc,
        sems,
        loads,
    ) = refs
    d, z, c = (lax.axis_index(name) for name in ALL)
    oc = 1 - c
    n_items, pix_dev, pad_width = xn.shape
    gain_col = gain_ref[:pix_width, :1]
    lat_len, width = lat.shape[1:]
    own = kv_out.shape[1]
    far = [lax.rem(d + i, n_dp) for i in range(1, n_dp)]
    far_from = [lax.rem(d + n_dp - i, n_dp) for i in range(1, n_dp)]
    z_to = [lax.rem(z + i, n_z) for i in range(1, n_z)]
    z_from = [lax.rem(z + n_z - i, n_z) for i in range(1, n_z)]
    partner = (d, z, oc)
    column = [(i, 0) for i in range(1, n_z)] + [(i, 1) for i in range(n_z)]

    def in_column(i, j):
        return (d, lax.rem(z + i, n_z), lax.rem(c + j, 2))

    peers = [in_column(i, j) for i, j in column] + [(to, z, c) for to in far]
    barrier = pltpu.get_barrier_semaphore()
    for peer in peers:
        pl.semaphore_signal(barrier, inc=1, device_id=peer, device_id_type=MESH)

    slot = iter(range(1000))

    def send(src, dst, peer):
        copy = remote(src, dst, sems, next(slot), peer)
        copy.start()
        return copy

    load_slot = iter(range(1000))

    def load(src, dst):
        copy = pltpu.make_async_copy(src, dst, loads.at[next(load_slot)])
        copy.start()
        return copy

    l_xn = load(xn_hbm, xn)
    l_pt = load(pt_hbm, pt)
    l_pix = load(pix_hbm, pix)
    l_lat = load(lat_hbm.at[c], lat.at[0])
    l_first = load(first_hbm, first)
    l_q = load(q_hbm, q_own)
    l_early = load(early_ref.at[:, c], early_own)
    n_early = early_own.shape[1] // own
    l_done = []
    if n_early < mats.shape[0] - 1:
        l_done = [load(done_sum_hbm, done_sum), load(done_far_hbm, done_far)]
    l_mats = [load(mats_hbm, mats), load(mfirst_hbm, mfirst), load(msecond_hbm, msecond)]
    block_out[c] = block_ref[c]

    rows = tile_of(pix_dev, 16, 256)
    tiles = pix_dev // rows
    held = chunk * n_z
    l_pt.wait()
    l_xn.wait()

    def score_side(item):
        gk = gk_all.at[item]
        scale = jnp.exp(peak_ref[item, :1] - stats_all[item, 0, :1]) / stats_all[item, 1, :1]
        delta = stats_all[item, 2, :1]

        def body(t, _):
            at = pl.ds(pl.multiple_of(t * rows, rows), rows)
            probs = pt[item, at, :].astype(fl_type) * scale
            grad_probs = dot(xn[item, at, :], gk[...])
            ds[item, at, :] = (probs * (grad_probs - delta)).astype(bf_type)
            pl_low[item, at, :] = probs.astype(bf_type)
            return 0

        lax.fori_loop(0, tiles, body, 0)
        return dot(xn[item], ds[item], TN)

    part_tx[...] = score_side(oc)[: part_tx.shape[0]].astype(part_tx.dtype)
    pl.semaphore_wait(barrier, len(peers))
    px_pair = send(part_tx, part_rx, partner)
    out_pair = send(block_ref.at[oc], block_out.at[c], partner)
    early_pair = send(early_ref.at[:, oc], early_rx, partner)
    part_own[...] = score_side(c)
    px_pair.wait()
    both = part_own[: part_rx.shape[0]] + part_rx[...].astype(fl_type)
    if held > both.shape[0]:
        both = jnp.concatenate([both, jnp.zeros((held - both.shape[0], lat_len), fl_type)], 0)
    col_tx[...] = both[:held].astype(col_tx.dtype).reshape(n_z, chunk, lat_len)
    col = [send(col_tx.at[to], col_rx.at[z], (d, to, c)) for to in z_to]

    l_early.wait()
    early_pair.wait()

    def pair_sum(t, _):
        both = early_own[t].astype(fl_type) + early_rx[t].astype(fl_type)
        early_tx[t] = both.astype(early_tx.dtype)
        return 0

    lax.fori_loop(0, n_dp, pair_sum, 0)
    early_out = [send(early_tx.at[to], early_far.at[d], (to, z, c)) for to in far]
    early_sum[...] = early_own[d].astype(fl_type) + early_rx[d].astype(fl_type)

    l_pix.wait()
    input_acc[...] = jnp.zeros(input_acc.shape, fl_type)

    def pixel_side(item, gk):
        def part(start, size):
            at = pl.ds(start, size)
            grad = dot(qk_ref[item], ds[item, at, :], NT) + dot(gk[...], pl_low[item, at, :], NT)
            grad = grad[:pix_width]
            values = pix[:, item, at].astype(fl_type)
            centred = values - jnp.sum(values, 0, keepdims=True) * (1.0 / pix_width)
            var = jnp.sum(centred * centred, 0, keepdims=True) * (1.0 / pix_width)
            scale = lax.rsqrt(var + 1e-05)
            normal = centred * scale
            along = normal * grad
            for low in range(0, size, 128):
                high = min(low + 128, size)
                input_acc[:pix_width, : high - low] += along[:, low:high]
            grad = grad * gain_col
            mean = jnp.sum(grad, 0, keepdims=True) * (1.0 / pix_width)
            along = jnp.sum(grad * normal, 0, keepdims=True) * (1.0 / pix_width)
            pix_buf[:, item, at] = (grad - mean - normal * along) * scale

        lane_parts(pix_dev, 256, part)

    pixel_side(0, gk_all.at[0])

    for copy in col:
        copy.wait()
    mean = col_tx[z].astype(fl_type)
    for other in z_from:
        mean = mean + col_rx[other].astype(fl_type)
    fin_tx[...] = mean.astype(fin_tx.dtype)
    fin = [send(fin_tx, fin_rx.at[z], (d, to, c)) for to in z_to]

    pixel_side(1, gk_all.at[1])
    stores = [load(pix_buf, pix_out)]

    l_lat.wait()
    l_first.wait()
    l_q.wait()
    pair_width = 2 * own
    n_cols = n_dp * pair_width
    wanted = lax.broadcasted_iota(jnp.int32, (width, n_cols), 1)
    wanted = (lax.div(wanted, pair_width) * n_z + z) * pair_width + lax.rem(wanted, pair_width)
    place = lax.broadcasted_iota(jnp.int32, (width, n_cols), 0)
    sel[...] = jnp.where(place == wanted, 1.0, 0.0).astype(bf_type)
    values = lat[0].astype(fl_type)
    centred = values - jnp.mean(values, -1, keepdims=True)
    scale = lax.rsqrt(jnp.mean(centred * centred, -1, keepdims=True) + 1e-05)
    hat[...] = centred * scale
    inv[...] = jnp.broadcast_to(scale, inv.shape)
    norm[...] = dot((hat[...] * gains_ref[:1]).astype(bf_type), sel[...]).astype(bf_type)

    for copy in fin:
        copy.wait()
    dst_full[...] = jnp.zeros(dst_full.shape, fl_type)
    for other in z_from:
        dst_full[pl.ds(other * chunk, chunk)] = fin_rx[other].astype(fl_type)
    dst_full[pl.ds(z * chunk, chunk)] = fin_tx[...].astype(fl_type)
    summed = dst_full[:pad_width].T.astype(bf_type)
    kt_zero = first[:, width : width + pad_width]
    dq[...] = (dot(summed, kt_zero, NT) * width**-0.5).astype(bf_type)
    da[...] = dot(dq[...], first[:, :width], NT)
    term_zero = dot(norm[...], dq[...], TN)
    q_sel = dot(q_own[...], sel[...]).astype(bf_type)
    term_k = dot(q_sel, summed, TN) * width**-0.5
    gain_at = round_up(pix_width, 8) - (pad_width - 128)
    gain_zero = jnp.sum(hat[...] * da[...], 0, keepdims=True)
    place = lax.broadcasted_iota(jnp.int32, (8, width), 0)
    gain_sums = jnp.where(place == 0, gain_zero, gterm_ref[...]).astype(bf_type)
    gain_cols = dot(gain_sums, sel[...])
    gain_cols = jnp.concatenate(
        [
            jnp.zeros((gain_at, n_cols), fl_type),
            gain_cols,
            jnp.zeros((128 - gain_at - 8, n_cols), fl_type),
        ],
        0,
    ).T
    late[:, :, :, :width] = term_zero.astype(late.dtype).reshape(n_dp, 2, own, width)
    late[:, :, :, width : width + pad_width] = term_k.astype(late.dtype).reshape(
        n_dp, 2, own, pad_width
    )
    ones = k_one_ref[...]
    late[:, :, :, width + pad_width : width + 2 * pad_width - 128] = (
        ones[:, : pad_width - 128].astype(late.dtype).reshape(n_dp, 2, own, pad_width - 128)
    )
    late[:, :, :, width + 2 * pad_width - 128 :] = (
        (ones[:, pad_width - 128 :] + gain_cols).astype(late.dtype).reshape(n_dp, 2, own, 128)
    )
    late_pair = send(late.at[:, oc], late_rx, partner)

    z_share = lat_len // n_z
    at = pl.ds(pl.multiple_of(z * z_share, z_share), z_share)
    grad = da[at, :] * gains_ref[:1]
    normal = hat[at, :]
    mean = jnp.mean(grad, -1, keepdims=True)
    along = jnp.mean(grad * normal, -1, keepdims=True)
    lat_grad = cross_ref[...] + (grad - mean - normal * along) * inv[at, :1]
    lat_tx[...] = lat_grad.reshape(2, z_share // 2, width)
    lat_pair = send(lat_tx.at[oc], lat_out.at[c], partner)
    lat_out[c] = lat_tx[c]

    late_pair.wait()
    late_sum = late[:, c].astype(fl_type) + late_rx[...].astype(fl_type)
    late_tx[...] = late_sum.astype(late_tx.dtype)
    late_out = [send(late_tx.at[to], late_far.at[d], (to, z, c)) for to in far]
    late_own[...] = late[d, c].astype(fl_type) + late_rx[d].astype(fl_type)

    for copy in early_out:
        copy.wait()
    for copy in l_mats + l_done:
        copy.wait()
    lane = lax.broadcasted_iota(jnp.int32, (1, 128), 1)

    def norms(weight, gradient, first_mom, second):
        first_new = 0.9 * first_mom + 0.1 * gradient
        second_new = 0.999 * second + 0.001 * gradient * gradient
        update = (
            first_new / first_fix / (jnp.sqrt(second_new / second_fix) + 1e-06)
            + decay_rate * weight
        )
        return (weight * weight, update * update)

    def total(values):
        return jnp.sum(jnp.sum(values, 0, keepdims=True), 1, keepdims=True)

    def matrix(k, sums, early=True):
        if early:
            at = pl.ds(pl.multiple_of((k - 1) * own, own), own)
            mine, others = early_sum, early_far
        else:
            at = pl.ds(pl.multiple_of((k - 1 - n_early) * own, own), own)
            mine, others = done_sum, done_far
        gradient = mine[at, :]
        for other in far_from:
            gradient = gradient + others[other, at, :].astype(fl_type)
        mats_out[k] = gradient
        w_sq, u_sq = norms(mats[k], gradient, mfirst[k], msecond[k])
        here = lane == k
        return (
            sums[0] + jnp.where(here, total(w_sq), 0.0),
            sums[1] + jnp.where(here, total(u_sq), 0.0),
        )

    zero = jnp.zeros((1, 128), fl_type)
    sums = lax.fori_loop(1, 1 + n_early, matrix, (zero, zero))
    if n_early < mats.shape[0] - 1:
        late_matrix = functools.partial(matrix, early=False)
        sums = lax.fori_loop(1 + n_early, mats.shape[0], late_matrix, sums)

    for copy in late_out:
        copy.wait()
    for other in far_from:
        late_own[...] += late_far[other].astype(fl_type)
    mats_out[0] = late_own[:, :width]
    grads = [(mats[0], late_own[:, :width], mfirst[0], msecond[0], 0)]
    for k in range(2):
        cols = late_own[:, width + k * pad_width : width + k * pad_width + pix_width]
        kv_out[k] = cols
        grads.append((kv_ref[k], cols, kfirst_ref[k], ksecond_ref[k], 10 + k))
    gain_grad = late_own[:, width + 2 * pad_width - 128 :].T[gain_at : gain_at + 8]
    gains_out[...] = gain_grad[:4]
    w_sum, u_sum = sums
    for weight, gradient, first_mom, second, k in grads:
        w_sq, u_sq = norms(weight, gradient, first_mom, second)
        w_sum = w_sum + jnp.where(lane == k, total(w_sq), 0.0)
        u_sum = u_sum + jnp.where(lane == k, total(u_sq), 0.0)
    w_sq, u_sq = norms(ng_ref[...], gain_grad[:4], gfirst_ref[...], gsecond_ref[...])
    w_sq, u_sq = jnp.sum(w_sq, 1, keepdims=True), jnp.sum(u_sq, 1, keepdims=True)
    for k in range(4):
        w_sum = w_sum + jnp.where(lane == 12 + k, w_sq[k : k + 1], 0.0)
        u_sum = u_sum + jnp.where(lane == 12 + k, u_sq[k : k + 1], 0.0)
    small_tx[...] = jnp.zeros(small_tx.shape, fl_type)
    small_tx[0:1] = w_sum
    small_tx[1:2] = u_sum
    input_row = jnp.sum(input_acc[...].T, 0, keepdims=True)
    for n in range(pad_width // 128):
        small_tx[2 + n : 3 + n] = input_row[:, n * 128 : (n + 1) * 128]
    copies = [
        send(small_tx, small_col.at[n], in_column(i, j)) for n, (i, j) in enumerate(column)
    ]
    for copy in copies:
        copy.wait()
    all_sum = small_tx[...]
    for n in range(len(column)):
        all_sum = all_sum + small_col[n]
    small_far_tx[...] = all_sum
    copies = [
        send(small_far_tx, small_far.at[n], (to, z, c)) for n, to in enumerate(far)
    ]
    for copy in copies:
        copy.wait()
    for n in range(len(far)):
        all_sum = all_sum + small_far[n]
    small_out[...] = all_sum
    for copy in [out_pair, lat_pair] + stores:
        copy.wait()


def backward_call(n_z, n_dp, args):
    (gk, stats, early, _, xn, pt, _, _, pixels, _, latents, first) = args[:12]
    mats, kv, gains = args[19], args[22], args[25]
    pix_width = pixels.shape[0]
    n_items, lat_len, width = latents.shape
    own = mats.shape[1]
    pad_width = xn.shape[2]
    early_rows = early.shape[2]
    wire = early.dtype
    chunk = round_up(-(-pix_width // n_z), 16)
    held = chunk * n_z
    cut = min(held, pad_width)
    z_share = lat_len // n_z
    n_cols = n_dp * 2 * own
    vmem, hbm = pl.BlockSpec(memory_space=pltpu.VMEM), pl.BlockSpec(memory_space=pl.ANY)
    places = {2, 4, 5, 8, 10, 11, 13, 17, 18, 19, 20, 21}
    in_specs = [hbm if index in places else vmem for index in range(len(args))]
    shape, buf = jax.ShapeDtypeStruct, pltpu.VMEM
    out_shape = [
        shape((n_items, z_share // 2, width), bf_type),
        shape((n_items, z_share // 2, width), fl_type),
        shape(pixels.shape, fl_type),
        shape(mats.shape, fl_type),
        shape(kv.shape, fl_type),
        shape(gains.shape, fl_type),
        shape((8, 128), fl_type),
    ]
    out_specs = [vmem, vmem, hbm, vmem, vmem, vmem, vmem]
    late_width = width + 2 * pad_width
    scratch = [
        buf(xn.shape, bf_type),
        buf(pt.shape, bf_type),
        buf(pixels.shape, bf_type),
        buf((1, lat_len, width), bf_type),
        buf(first.shape, bf_type),
        buf((lat_len, width), bf_type),
        buf(mats.shape, fl_type),
        buf(mats.shape, fl_type),
        buf(mats.shape, fl_type),
        buf(pt.shape, bf_type),
        buf(pt.shape, bf_type),
        buf((cut, lat_len), bf_type),
        buf((pad_width, lat_len), fl_type),
        buf((cut, lat_len), bf_type),
        buf((n_z, chunk, lat_len), bf_type),
        buf((n_z, chunk, lat_len), bf_type),
        buf((chunk, lat_len), bf_type),
        buf((n_z, chunk, lat_len), bf_type),
        buf((max(held, pad_width), lat_len), fl_type),
        buf((n_dp, early_rows, width), wire),
        buf((n_dp, early_rows, width), wire),
        buf((n_dp, early_rows, width), wire),
        buf((early_rows, width), fl_type),
        buf((n_dp, early_rows, width), wire),
        buf(args[17].shape, fl_type),
        buf(args[18].shape, wire),
        buf(pixels.shape, fl_type),
        buf((lat_len, width), fl_type),
        buf((lat_len, 128), fl_type),
        buf((lat_len, n_cols), bf_type),
        buf((lat_len, width), bf_type),
        buf((lat_len, width), fl_type),
        buf((width, n_cols), bf_type),
        buf((2, z_share // 2, width), fl_type),
        buf((n_dp, 2, own, late_width), wire),
        buf((n_dp, own, late_width), wire),
        buf((n_dp, own, late_width), wire),
        buf((own, late_width), fl_type),
        buf((n_dp, own, late_width), wire),
        buf((8, 128), fl_type),
        buf((2 * n_z - 1, 8, 128), fl_type),
        buf((8, 128), fl_type),
        buf((n_dp - 1, 8, 128), fl_type),
        buf((pad_width, 128), fl_type),
        pltpu.SemaphoreType.DMA((2, 20 + 6 * n_z + 3 * n_dp)),
        pltpu.SemaphoreType.DMA((16,)),
    ]
    return pl.pallas_call(
        functools.partial(backward, n_z, n_dp, pix_width, chunk),
        out_shape=out_shape,
        in_specs=in_specs,
        out_specs=out_specs,
        scratch_shapes=scratch,
        compiler_params=pltpu.CompilerParams(
            collective_id=1, has_side_effects=True, vmem_limit_bytes=60 * 2**20
        ),
        name="backward",
    )(*args)


def lamb(n_mats, *refs):
    (
        block_in, lat_in, pix_in, mg, kg, gg, small, mw, mf, ms, kw, kf, ks, gw, gf, gs, iw, i_f, i_s,
        block_out, lat_out, pix_out, mg_out, kg_out, gg_out, ig_out,
        mw_out, mf_out, ms_out, kw_out, kf_out, ks_out, gw_out, gf_out, gs_out, iw_out, if_out, is_out,
        g_buf, w_buf, f_buf, s_buf, w_new, f_new, s_new, pix_buf, in_sems, out_sems, pix_sems,
    ) = refs
    parts = [(low, min(low + 66, pix_in.shape[0])) for low in range(0, pix_in.shape[0], 66)]

    def pix_copy(n, back):
        low, high = parts[n]
        src, dst = pix_in.at[low:high], pix_buf.at[low:high]
        if back:
            src, dst = dst, pix_out.at[low:high]
        return pltpu.make_async_copy(src, dst, pix_sems.at[int(back), n])

    for n in range(len(parts)):
        pix_copy(n, False).start()
    spans = [(low, min(low + 2, n_mats)) for low in range(0, n_mats, 2)]
    loads = []
    for k, (low, high) in enumerate(spans):
        loads.append(
            [
                pltpu.make_async_copy(src.at[low:high], dst.at[low:high], in_sems.at[n, k])
                for n, (src, dst) in enumerate(
                    ((mg, g_buf), (mw, w_buf), (mf, f_buf), (ms, s_buf))
                )
            ]
        )
        for copy in loads[-1]:
            copy.start()
    block_out[...] = block_in[...]
    lat_out[...] = lat_in[...]
    lane = lax.broadcasted_iota(jnp.int32, (1, 128), 1)

    def ratio(w_sq, u_sq):
        return jnp.sqrt(w_sq) / (jnp.sqrt(u_sq) + 1e-06)

    trust = ratio(small[0:1], small[1:2])

    def scalar(k):
        return jnp.sum(jnp.where(lane == k, trust, 0.0), 1, keepdims=True)

    def update(weight, gradient, first_mom, second):
        first_new = 0.9 * first_mom + 0.1 * gradient
        second_new = 0.999 * second + 0.001 * gradient * gradient
        step = (
            first_new / first_fix / (jnp.sqrt(second_new / second_fix) + 1e-06)
            + decay_rate * weight
        )
        return first_new, second_new, step

    for n in range(len(parts)):
        pix_copy(n, False).wait()
        pix_copy(n, True).start()
    kg_out[...] = kg[...]
    gg_out[...] = gg[...]
    for k in range(2):
        kf_out[k], ks_out[k], step = update(kw[k], kg[k], kf[k], ks[k])
        kw_out[k] = kw[k] - step_rate * scalar(n_mats + k) * step
    first_new, second_new, step = update(gw[...], gg[...], gf[...], gs[...])
    gf_out[...] = first_new
    gs_out[...] = second_new
    row = lax.broadcasted_iota(jnp.int32, (4, 1), 0)
    rates = jnp.zeros((4, 1), fl_type)
    for k in range(4):
        rates = rates + jnp.where(row == k, scalar(n_mats + 2 + k), 0.0)
    gw_out[...] = gw[...] - step_rate * rates * step
    pix_width = iw.shape[0]
    row = (1, pix_width)
    rows = [small[n : n + 1] for n in range(2, 2 + -(-pix_width // 128))]
    in_grad = jnp.concatenate(rows, 1)[:, :pix_width]
    weight = iw[...].reshape(row)
    first_new, second_new, step = update(
        weight, in_grad, i_f[...].reshape(row), i_s[...].reshape(row)
    )
    in_trust = ratio(
        jnp.sum(weight * weight, 1, keepdims=True), jnp.sum(step * step, 1, keepdims=True)
    )
    ig_out[...] = in_grad.reshape(pix_width)
    if_out[...] = first_new.reshape(pix_width)
    is_out[...] = second_new.reshape(pix_width)
    iw_out[...] = (weight - step_rate * in_trust * step).reshape(pix_width)
    stores = []
    for n_span, (low, high) in enumerate(spans):
        for copy in loads[n_span]:
            copy.wait()
        for k in range(low, high):
            first_new, second_new, step = update(w_buf[k], g_buf[k], f_buf[k], s_buf[k])
            f_new[k] = first_new
            s_new[k] = second_new
            w_new[k] = w_buf[k] - step_rate * scalar(k) * step
        for n, (src, dst) in enumerate(
            ((g_buf, mg_out), (w_new, mw_out), (f_new, mf_out), (s_new, ms_out))
        ):
            copy = pltpu.make_async_copy(
                src.at[low:high], dst.at[low:high], out_sems.at[n, n_span]
            )
            copy.start()
            stores.append(copy)
    for copy in stores + [pix_copy(n, True) for n in range(len(parts))]:
        copy.wait()


def lamb_call(args):
    n_mats = args[3].shape[0]
    vmem, hbm = pl.BlockSpec(memory_space=pltpu.VMEM), pl.BlockSpec(memory_space=pl.ANY)
    block, lat, pix, mats, kv, gains = args[:6]
    row = args[16]
    shape = jax.ShapeDtypeStruct

    def like(value):
        return shape(value.shape, value.dtype)

    out_shape = [like(v) for v in (block, lat, pix, mats, kv, gains, row)]
    out_shape += [like(mats)] * 3 + [like(kv)] * 3 + [like(gains)] * 3 + [like(row)] * 3
    return pl.pallas_call(
        functools.partial(lamb, n_mats),
        out_shape=out_shape,
        in_specs=[vmem] * 2 + [hbm] * 2 + [vmem] * 3 + [hbm] * 3 + [vmem] * 9,
        out_specs=[vmem] * 2 + [hbm] * 2 + [vmem] * 3 + [hbm] * 3 + [vmem] * 9,
        scratch_shapes=[pltpu.VMEM(mats.shape, fl_type)] * 7
        + [
            pltpu.VMEM(pix.shape, fl_type),
            pltpu.SemaphoreType.DMA((4, n_mats)),
            pltpu.SemaphoreType.DMA((4, n_mats)),
            pltpu.SemaphoreType.DMA((2, 4)),
        ],
        compiler_params=pltpu.CompilerParams(vmem_limit_bytes=62 * 2**20),
        name="lamb",
    )(*args)


def local(
    latents,
    pixels,
    pix_counts,
    cotangent,
    weight_mats,
    kv_weights,
    norm_gains,
    input_gain,
    mats_first,
    mats_second,
    kv_first,
    kv_second,
    gains_first,
    gains_second,
    input_first,
    input_second,
):
    pix_width = pixels.shape[2]
    model_width = latents.shape[2]
    own_width = weight_mats.shape[1]
    n_dp, n_z = lax.axis_size("dp"), lax.axis_size("z")
    gain_at = round_up(pix_width, 8)
    pad_width = round_up(gain_at + 8, 128)

    def turned(value):
        return jnp.swapaxes(value, 1, 2)

    kv_cols = turned(kv_weights)
    pix_turned = jnp.transpose(pixels, (2, 0, 1))
    gathers = own_width % 16 == 0 and n_dp == 4 and n_z % 2 == 0 and n_z >= 4
    if gathers:
        weights = (weight_mats, kv_cols, norm_gains)
    else:
        extra = jnp.zeros((own_width, pad_width - gain_at - 4), fl_type)
        keys = [jnp.pad(kv_cols[0], ((0, 0), (0, gain_at - pix_width))), norm_gains.T, extra]
        values = jnp.pad(kv_cols[1], ((0, 0), (0, pad_width - pix_width)))
        both = jnp.stack(
            [
                jnp.concatenate([weight_mats[0]] + keys, 1),
                jnp.concatenate([weight_mats[1], values], 1),
            ]
        ).astype(bf_type)
        both = lax.all_gather(both, ALL, axis=1, tiled=True)
        others = lax.all_gather(weight_mats[2:].astype(bf_type), ALL, axis=1, tiled=True)
        weights = (both[0][None, None], both[1][None, None], others[:, None, None])
    (
        first_all, xn, pt, q_own, early, peak, qk, gains, block_rows, gk, stats, cross_rows, k_one, gterm,
        gain_cols, done_sum, done_far,
    ) = forward_call(
        n_z, n_dp, gathers, *weights, pix_counts, pix_turned, latents, cotangent, input_gain
    )
    first_all = first_all.reshape(model_width, model_width + pad_width)
    early = early.reshape(n_dp, 2, -1, model_width)
    summed = backward_call(
        n_z,
        n_dp,
        (
            gk,
            stats,
            early,
            block_rows,
            xn,
            pt,
            peak,
            qk,
            pix_turned,
            gain_cols,
            latents,
            first_all,
            gains,
            q_own,
            cross_rows,
            k_one,
            gterm,
            done_sum,
            done_far,
            weight_mats,
            mats_first,
            mats_second,
            kv_cols,
            turned(kv_first),
            turned(kv_second),
            norm_gains,
            gains_first,
            gains_second,
        ),
    )
    outs = lamb_call(
        (
            *summed,
            weight_mats,
            mats_first,
            mats_second,
            kv_cols,
            turned(kv_first),
            turned(kv_second),
            norm_gains,
            gains_first,
            gains_second,
            input_gain,
            input_first,
            input_second,
        )
    )
    outs = list(outs)
    outs[2] = jnp.transpose(outs[2], (1, 2, 0))
    for index in (4, 10, 11, 12):
        outs[index] = turned(outs[index])
    return tuple(outs)


def solution(mesh):
    n_dp, n_rows = mesh.devices.shape
    split_mesh = Mesh(mesh.devices.reshape(n_dp, n_rows // 2, 2), ALL)
    rows = ("z", "core")
    items = P("dp", None, None)
    pix = P("dp", rows, None)
    mats = P(None, ALL, None)
    pairs = P(None, None, ALL)
    gains = P(None, ALL)
    in_specs = (
        items,
        pix,
        P("dp"),
        items,
        mats,
        pairs,
        gains,
        P(),
        mats,
        mats,
        pairs,
        pairs,
        gains,
        gains,
        P(),
        P(),
    )
    out_specs = (
        pix,
        pix,
        pix,
        mats,
        pairs,
        gains,
        P(),
        mats,
        mats,
        mats,
        pairs,
        pairs,
        pairs,
        gains,
        gains,
        gains,
        P(),
        P(),
        P(),
    )
    return jax.shard_map(
        local, mesh=split_mesh, in_specs=in_specs, out_specs=out_specs, check_vma=False
    )
```
